32 devices in a mesh: groups: 2 (over x), sky: 16 (over z, y, core).
Axes of the slice: x: 2, y: 2, z: 4, core: 2. Of those that a mesh axis runs over, the one named last changes fastest.
Arguments:
- image: bfloat16 [32, 512, 128], P(('groups', 'sky')), parts along dimension 0, may hold values from -6 to 6
- row_taps: bfloat16 [40, 31], replicated, may hold values from -1 to 1
- col_taps: bfloat16 [40, 31], replicated, may hold values from -1 to 1
- mix_coeff: float32 [32, 3, 40], P(('groups', 'sky')), parts along dimension 0, may hold values from -1 to 1
- shift_frac: float32 [32, 2], P(('groups', 'sky')), parts along dimension 0, may hold values from 0.05 to 0.95
- ccd_visit: int32 [32], P(('groups', 'sky')), parts along dimension 0, may hold values from 0 to 3
- visit_weight: bfloat16 [8], P('groups'), parts along dimension 0, may hold values from 0.25 to 4
- tile_block: int32 [2048], P(('groups', 'sky')), parts along dimension 0, may hold values from 0 to 255, as said below
- tile_offset: int32 [2048], P(('groups', 'sky')), parts along dimension 0, may hold values from 0 to 7
Outputs:
- coadd: float32 [4096, 128], P(('groups', 'sky')), parts along dimension 0
- weight_map: float32 [4096], P(('groups', 'sky')), parts along dimension 0
The draws below stay inside these ranges and needn't reach their ends.
There are 2 independent parts, one for each index of `groups`. The reference program is written for one: setup_inputs(seed, part) draws one part's arguments, and reference() takes and returns one part's arrays. A program takes and returns all parts, laid end to end along the dimension named above; an argument that names none is the same for every part. Nothing has to cross between parts.
Inputs may be any that keep to these rules, and one draw needn't show every extreme that they name: `tile_block`: the owner of sky block b is device b // 16 of the sky axis. The 64 tiles of one window go to exactly 16 distinct owners, 4 tiles to each; at least four owners receive 4 tiles from every window.
All inputs are finite; a program needn't handle non-finite values.
Results may differ from the reference program's by a relative error of at most 0.0041.
Values may be sent and summed in bfloat16 or wider, within the bound.
No kernel may reach another device: no remote copies, remote signals or barrier semaphores. Data moves between devices by JAX's collectives and lax.ppermute only.
A program may use at most 64 MiB of HBM per device.

```python
import math
import jax
import jax.numpy as jnp
from jax import lax

K = 40
TAPS = 31
VISITS = 4
TILE_R = 8
WC = 128
WR = 512
TILES_DEV = 64
CAP = 4
BLK_DEV = 16
SKY_HOLDERS = 16
CCDS = 16
TILES = 1024
SKY_ROWS = 2048


def draw_tile_block(key, part):
    keys = jax.random.split(jax.random.fold_in(key, 17), 5)
    dest_count = TILES_DEV // CAP
    demand_tally = jax.random.randint(keys[0], (SKY_HOLDERS,), 0, 2 ** 20)
    central_ranking = jax.random.permutation(keys[1], SKY_HOLDERS)
    central_reward = jnp.where(central_ranking < 4, 2 ** 22, 0)
    random_perturbation = jax.random.randint(keys[2], (SKY_HOLDERS, SKY_HOLDERS), 0, 2 ** 20)
    priority_values = (demand_tally[None, :] + central_reward[None, :] + random_perturbation) * SKY_HOLDERS + jnp.arange(SKY_HOLDERS)[None, :]
    priority_values = priority_values.astype(jnp.int32)
    unused_values, chosen = lax.top_k(priority_values, dest_count)
    shuffles = jax.vmap(lambda derived_random_key: jax.random.permutation(derived_random_key, TILES_DEV))(jax.random.split(keys[3], SKY_HOLDERS))
    owners = jnp.take_along_axis(chosen, shuffles // CAP, axis=1)
    local_block = jax.random.randint(keys[4], (SKY_HOLDERS, TILES_DEV), 0, BLK_DEV)
    return (owners * BLK_DEV + local_block).reshape(-1).astype(jnp.int32)


def plant(array, key, low, largest):
    extent = array.shape
    spot = [jax.random.randint(jax.random.fold_in(key, axis), (), 0, extent[axis]) for axis in range(len(extent))]
    array = array.at[tuple(spot)].set(low)
    longest = extent.index(max(extent))
    spot[longest] = (spot[longest] + 1) % extent[longest]
    return array.at[tuple(spot)].set(largest)


def steps_of(rng, dims, shards, smallest, largest):
    def one(position, blocks):
        steps = jax.random.uniform(jax.random.fold_in(jax.random.fold_in(rng, 6), position), (blocks,), jnp.float32, smallest / len(shards), largest / len(shards))
        return jnp.repeat(jnp.exp(steps), dims[position] // blocks).reshape((-1,) + (1,) * (len(dims) - position - 1))

    level = one(*shards[0])
    for cut in shards[1:]:
        level = level * one(*cut)
    return level


def bell_draw(rng, dims, deviation, reach, shards=(), held_as=jnp.bfloat16):
    values = jax.random.normal(rng, dims, jnp.float32) * deviation
    if len(shards) > 0:
        values = steps_of(rng, dims, shards, -0.22, 0.18) * values
    return jnp.clip(values, min=-reach, max=reach).astype(held_as)


def setup_inputs(seed: int = 0, part: int = 0) -> dict:
    streams_of = jax.random.split(jax.random.key(seed), 10)
    part_splits = jax.random.split(jax.random.fold_in(streams_of[9], part), 10)
    image = bell_draw(part_splits[0], (CCDS, WR, WC), 1.0, 6.0, ((0, 16),))
    row_taps = bell_draw(streams_of[1], (K, TAPS), TAPS ** -0.5, 1.0)
    col_taps = bell_draw(streams_of[2], (K, TAPS), TAPS ** -0.5, 1.0)
    mix_coeff = bell_draw(part_splits[3], (CCDS, 3, K), K ** -0.5, 1.0, ((0, 16),), jnp.float32)
    shift_frac = jnp.clip(0.05 + 0.9 * jax.random.uniform(part_splits[4], (CCDS, 2), jnp.float32) ** steps_of(part_splits[4], (CCDS, 2), ((0, 16),), -0.2, 0.2), 0.05, 0.95)
    ccd_visit = plant(jax.random.randint(part_splits[5], (CCDS,), 0, VISITS), jax.random.fold_in(part_splits[5], 1), 0, VISITS - 1).astype(jnp.int32)
    visit_weight = jnp.clip(jnp.exp(jax.random.uniform(part_splits[6], (VISITS,), jnp.float32, math.log(0.25), math.log(4.0))), 0.25, 4.0).astype(jnp.bfloat16)
    tile_block = draw_tile_block(jax.random.fold_in(jax.random.fold_in(streams_of[9], part), 71), part)
    tile_offset = plant(jax.random.randint(part_splits[8], (TILES,), 0, TILE_R), jax.random.fold_in(part_splits[8], 1), 0, TILE_R - 1).astype(jnp.int32)
    return {"image": image, "row_taps": row_taps, "col_taps": col_taps, "mix_coeff": mix_coeff, "shift_frac": shift_frac, "ccd_visit": ccd_visit, "visit_weight": visit_weight, "tile_block": tile_block, "tile_offset": tile_offset}


def lanczos_taps(fraction):
    positions = jnp.arange(-2, 4).astype(jnp.float32)
    offsets = positions[None, :] - fraction[:, None]
    angles = jnp.pi * offsets
    kernel = jnp.sin(angles) / angles * (jnp.sin(angles / 3.0) / (angles / 3.0))
    return kernel / jnp.sum(kernel, axis=1, keepdims=True)


def match_window(window, row_taps, col_taps, coefficients):
    half_taps = (TAPS - 1) // 2
    pixels = window.astype(jnp.float32)[None, None]
    kernel_row = row_taps.astype(jnp.float32)[:, None, None, :]
    smoothed = lax.conv_general_dilated(pixels, kernel_row, (1, 1), ((0, 0), (half_taps, half_taps)), dimension_numbers=("NCHW", "OIHW", "NCHW"), precision=lax.Precision.HIGHEST)
    smoothed = lax.optimization_barrier(smoothed.astype(jnp.bfloat16)).astype(jnp.float32)
    kernel_col = col_taps.astype(jnp.float32)[:, None, :, None]
    vertical = lax.conv_general_dilated(smoothed, kernel_col, (1, 1), ((half_taps, half_taps), (0, 0)), dimension_numbers=("NCHW", "OIHW", "NCHW"), feature_group_count=K, precision=lax.Precision.HIGHEST)[0]
    column_pos = (2.0 * jnp.arange(WC).astype(jnp.float32) + 1.0) / WC - 1.0
    row_pos = (2.0 * jnp.arange(WR).astype(jnp.float32) + 1.0) / WR - 1.0
    weights = coefficients[0][:, None, None] + coefficients[1][:, None, None] * column_pos[None, None, :] + coefficients[2][:, None, None] * row_pos[None, :, None]
    return jnp.sum(weights * vertical, axis=0)


def warp_window(matched, fraction):
    taps_across = lanczos_taps(fraction[1:2])[0]
    taps_down = lanczos_taps(fraction[0:1])[0]
    padded = jnp.pad(matched, ((0, 0), (2, 3)))
    spread = taps_across[0] * padded[:, 0:WC]
    for offset_index in range(1, 6):
        spread = spread + taps_across[offset_index] * padded[:, offset_index:offset_index + WC]
    padded = jnp.pad(spread, ((2, 3), (0, 0)))
    warped = taps_down[0] * padded[0:WR]
    for offset_index in range(1, 6):
        warped = warped + taps_down[offset_index] * padded[offset_index:offset_index + WR]
    return warped.astype(jnp.bfloat16)


def reference(image, row_taps, col_taps, mix_coeff, shift_frac, ccd_visit, visit_weight, tile_block, tile_offset):
    def one_window(packed):
        window, coefficients, fraction = packed
        return warp_window(match_window(window, row_taps, col_taps, coefficients), fraction)

    warped = lax.map(one_window, (image, mix_coeff, shift_frac))
    visit_match = ccd_visit[:, None] == jnp.arange(VISITS)[None, :]
    ccd_weight = jnp.sum(jnp.where(visit_match, visit_weight.astype(jnp.float32)[None, :], 0.0), axis=1)
    tile_weight = jnp.repeat(ccd_weight, TILES_DEV)
    tile_pixels = warped.reshape(CCDS * TILES_DEV, TILE_R, WC).astype(jnp.float32)
    weighted = tile_pixels * tile_weight[:, None, None]
    row_index = (tile_block[:, None] * TILE_R + tile_offset[:, None] + jnp.arange(TILE_R)[None, :]).astype(jnp.int32)
    sky_sum = jax.ops.segment_sum(weighted.reshape(-1, WC), row_index.reshape(-1), num_segments=SKY_ROWS + TILE_R)[:SKY_ROWS]
    row_weight = jnp.broadcast_to(tile_weight[:, None], (CCDS * TILES_DEV, TILE_R))
    weight_map = jax.ops.segment_sum(row_weight.reshape(-1), row_index.reshape(-1), num_segments=SKY_ROWS + TILE_R)[:SKY_ROWS]
    coadd = sky_sum / jnp.maximum(weight_map, 1.0)[:, None]
    return coadd, weight_map
```

```python
import functools

import jax
import jax.numpy as jnp
from jax import lax
from jax.experimental import pallas as pl
from jax.experimental.pallas import tpu as pltpu
from jax.sharding import PartitionSpec as P

BLK_DEV = 16
SUB = 8
TAIL = 16
EMPTY = -64
TAPS_DOWN = 6


def iota(shape, axis):
    return lax.broadcasted_iota(jnp.int32, shape, axis)


def weight_of(visit_ref, weight_ref):
    values = weight_ref[...].astype(jnp.float32)
    chosen = jnp.where(iota(values.shape, 1) == visit_ref[0], values, 0.0)
    return jnp.sum(chosen, axis=1, keepdims=True)


def assign_slots(capacity, block_ref, offset_ref, slot_of, starts, counts):
    tiles = slot_of.shape[0]
    owners = counts.shape[0]

    @pl.loop(0, owners)
    def _(owner):
        counts[owner] = 0

    if owners * capacity > tiles:

        @pl.loop(0, owners * capacity)
        def _(slot):
            starts[slot] = EMPTY

    def assign(tile, carry):
        block = block_ref[tile]
        owner = lax.div(block, BLK_DEV)
        rank = counts[owner]
        counts[owner] = rank + 1
        slot = owner * capacity + rank
        slot_of[tile] = slot
        starts[slot] = (block - owner * BLK_DEV) * SUB + offset_ref[tile]
        return carry

    lax.fori_loop(0, tiles, assign, 0, unroll=8)


def lanczos_rows(frac_ref, cols):
    row = iota((2 * SUB, cols), 0)
    tap = jnp.where(row < SUB, row, row - SUB)
    fraction = jnp.where(row < SUB, frac_ref[0, 1], frac_ref[0, 0])
    angles = jnp.pi * ((tap - 2).astype(jnp.float32) - fraction)
    third = angles / 3.0
    kernel = jnp.sin(angles) / angles * (jnp.sin(third) / third)
    kernel = jnp.where(tap < TAPS_DOWN, kernel, 0.0)
    across, down = kernel[:SUB], kernel[SUB:]
    across = across / jnp.sum(across, axis=0, keepdims=True)
    down = down / jnp.sum(down, axis=0, keepdims=True)
    return across, down


def combined_taps(row_ref, col_ref, mix_ref, base):
    basis, taps = row_ref.shape
    cols = base.shape[2]
    half = taps // 2
    s, l = iota((taps, cols), 0), iota((taps, cols), 1)
    turned = ((s + l == half) | (s + l == half + cols)).astype(jnp.float32).astype(jnp.bfloat16)
    moved = (l == s + 1).astype(jnp.float32).astype(jnp.bfloat16)
    across = jnp.dot(row_ref[...], turned, preferred_element_type=jnp.float32).astype(jnp.bfloat16)
    down = jnp.dot(col_ref[...], moved, preferred_element_type=jnp.float32)
    same = iota((basis, basis), 0) == iota((basis, basis), 1)
    over = functools.partial(
        lax.dot_general,
        dimension_numbers=(((0,), (0,)), ((), ())),
        preferred_element_type=jnp.float32,
    )
    found = []
    for term in range(3):
        coefficient = jnp.sum(
            jnp.where(same, mix_ref[0, term : term + 1, :], 0.0), axis=1, keepdims=True
        )
        scaled = down * coefficient
        high = scaled.astype(jnp.bfloat16)
        low = (scaled - high.astype(jnp.float32)).astype(jnp.bfloat16)
        found.append((over(high, across) + over(low, across))[: base.shape[1]])
    lane = iota(found[0].shape, 1)
    lane = jnp.where(lane < cols // 2, lane, lane - cols).astype(jnp.float32)
    base[0] = found[0] + (2.0 / cols) * lane * found[1]
    base[1] = found[1]
    base[2] = found[2]


def build_bands(base, band, half):
    cols = base.shape[2]
    fold = band.shape[0]
    blocks = cols // SUB
    sub = iota((SUB, cols), 0)
    lane = iota((SUB, cols), 1)
    first_u = (2.0 * sub.astype(jnp.float32) + 1.0) / cols - 1.0

    def spin(term, row):
        taps = jnp.broadcast_to(base[term, pl.ds(row, 1), :], (SUB, cols))
        return pltpu.roll(taps, 0, 1, stride=1, stride_axis=0)

    def keep(block, value):
        if block * SUB >= half and (block + 1) * SUB - 1 + half < cols:
            return value
        return jnp.where(jnp.abs(lane - sub - block * SUB) <= half, value, 0.0)

    @pl.loop(0, fold)
    def _(r):
        for part in range(2):
            row = r + fold * part
            slope = spin(1, row)
            level = spin(0, row) + first_u * slope
            rise = spin(2, row)
            for pair in range(blocks // 2):
                two = []
                for block in (2 * pair, 2 * pair + 1):
                    value = level + (2.0 * SUB * block / cols) * slope
                    value = keep(block, pltpu.roll(value, SUB * block, 1) if block else value)
                    other = keep(block, pltpu.roll(rise, SUB * block, 1) if block else rise)
                    two.append(jnp.concatenate([value, other], axis=1))
                first = part * cols + pair * 2 * SUB
                band[r, first : first + 2 * SUB, :] = jnp.concatenate(two, axis=0).astype(
                    jnp.bfloat16
                )


def window_kernel(
    capacity,
    image_ref,
    row_ref,
    col_ref,
    mix_ref,
    weight_ref,
    frac_ref,
    visit_ref,
    block_ref,
    offset_ref,
    out_ref,
    padded,
    base,
    band,
    total,
    spread,
    slots,
    slot_of,
    starts,
    counts,
):
    rows, cols = image_ref.shape[1:]
    half = row_ref.shape[1] // 2
    fold = band.shape[0]
    tiles = slot_of.shape[0]
    owners = out_ref.shape[0]
    data_rows = capacity * SUB
    owned = BLK_DEV * SUB

    assign_slots(capacity, block_ref, offset_ref, slot_of, starts, counts)
    across, down = lanczos_rows(frac_ref, cols)
    weight = weight_of(visit_ref, weight_ref)

    padded[:fold] = jnp.zeros((fold, cols), jnp.float32)
    padded[fold : fold + rows] = image_ref[0].astype(jnp.float32)
    padded[fold + rows :] = jnp.zeros((fold, cols), jnp.float32)
    combined_taps(row_ref, col_ref, mix_ref, base)
    build_bands(base, band, half)

    total[...] = jnp.zeros(total.shape, jnp.float32)

    @pl.loop(0, fold)
    def _(r):
        moved = padded[pl.ds(r, rows + fold), :].astype(jnp.bfloat16)
        pair = jnp.concatenate([moved[:rows], moved[fold:]], axis=1)
        total[...] += jnp.dot(pair, band[r], preferred_element_type=jnp.float32)

    lane = iota((1, cols), 1)
    taps_across = [
        jnp.where((lane + m - 2 >= 0) & (lane + m - 2 < cols), across[m : m + 1], 0.0)
        for m in range(TAPS_DOWN)
    ]
    spread[:SUB] = jnp.zeros((SUB, cols), jnp.float32)
    spread[SUB + rows :] = jnp.zeros((SUB, cols), jnp.float32)
    chunk = 64

    @pl.loop(0, rows // chunk)
    def _(index):
        first = pl.multiple_of(index * chunk, chunk)
        position = (2 * (iota((chunk, cols), 0) + first) + 1).astype(jnp.float32) / rows - 1.0
        both = total[pl.ds(first, chunk), :]
        matched = both[:, :cols] + position * both[:, cols:]
        result = taps_across[2] * matched
        for m in range(TAPS_DOWN):
            if m != 2:
                result = result + taps_across[m] * pltpu.roll(matched, (2 - m) % cols, 1)
        spread[pl.ds(first + SUB, chunk), :] = result

    if owners * capacity > tiles:
        slots[...] = jnp.zeros(slots.shape, jnp.float32)

    def warp(tile, carry):
        first = tile * SUB + SUB - 2
        result = down[0:1] * spread[pl.ds(first, SUB), :]
        for m in range(1, TAPS_DOWN):
            result = result + down[m : m + 1] * spread[pl.ds(first + m, SUB), :]
        slots[pl.ds(pl.multiple_of(slot_of[tile] * SUB, SUB), SUB), :] = result
        return carry

    lax.fori_loop(0, tiles, warp, 0, unroll=8)

    sub = iota((SUB, cols), 0)
    wide = iota((SUB, cols), 1)
    cap_bits = capacity.bit_length() - 1
    lane_row = wide & (SUB - 1)
    lane_slot = (wide >> 3) & (capacity - 1)
    spill_slot = wide & (capacity - 1)
    spill_row = wide >> cap_bits
    tile_weight = jnp.broadcast_to(weight, (SUB, cols))

    def message(owner, carry):
        previous = jnp.maximum(owner - 1, 0)
        first = owner * data_rows
        out_ref[owner, :data_rows, :] = slots[
            pl.ds(pl.multiple_of(first, data_rows), data_rows), :
        ].astype(jnp.bfloat16)
        spilled = jnp.zeros((SUB, cols), jnp.float32)
        over = jnp.zeros((SUB, cols), jnp.float32)
        target = jnp.zeros((SUB, cols), jnp.int32)
        for c in range(capacity):
            target = jnp.where(lane_slot == c, starts[owner * capacity + c] + lane_row, target)
            slot = previous * capacity + c
            start = starts[slot]
            past = jnp.where(owner > 0, start + SUB - owned, 0)
            tile = slots[pl.ds(pl.multiple_of(slot * SUB, SUB), SUB), :]
            tile = pltpu.roll(tile, start & (SUB - 1), 0)
            spilled = spilled + jnp.where(sub < past, tile, 0.0)
            over = jnp.where((spill_slot == c) & (spill_row < past), tile_weight, over)
        top = jnp.where(sub == SUB - 1, over, spilled * tile_weight)
        meta = jnp.where(sub == 0, target.astype(jnp.float32), tile_weight)
        out_ref[owner, data_rows:, :] = jnp.concatenate([top, meta], axis=0).astype(jnp.bfloat16)
        return carry

    lax.fori_loop(0, owners, message, 0, unroll=4)


def sky_kernel(capacity, got_ref, coadd_ref, map_ref):
    sources, message_rows, cols = got_ref.shape
    data_rows = capacity * SUB
    owned = coadd_ref.shape[0]
    per_chunk = cols // data_rows
    lane = iota((1, cols), 1)
    row = iota((owned, cols), 0)
    spilled = jnp.zeros((SUB, cols), jnp.float32)
    pieces = []
    for chunk in range(sources // per_chunk):
        target = jnp.zeros((1, cols), jnp.float32)
        weight = jnp.zeros((1, cols), jnp.float32)
        for k in range(per_chunk):
            tail = got_ref[chunk * per_chunk + k, data_rows:, :].astype(jnp.float32)
            spilled = spilled + tail[:SUB]
            here = (lane >= k * data_rows) & (lane < (k + 1) * data_rows)
            target = jnp.where(here, tail[SUB : SUB + 1], target)
            weight = jnp.where(here, tail[SUB + 1 : SUB + 2], weight)
        placed = jnp.where(row == target.astype(jnp.int32), weight, 0.0)
        pieces.append(placed.astype(jnp.bfloat16))
    placement = jnp.concatenate(pieces, axis=1)
    pixels = got_ref[:, :data_rows, :].reshape(sources * data_rows, cols)
    pixels = jnp.concatenate([pixels, jnp.ones(pixels.shape, jnp.bfloat16)], axis=1)
    sums = jnp.dot(placement, pixels, preferred_element_type=jnp.float32)
    sub = iota((SUB, cols), 0)
    wide = iota((SUB, cols), 1)
    last = sub == SUB - 1
    over = jnp.broadcast_to(spilled[SUB - 1 :], (SUB, cols))
    mine = ((wide >> (capacity.bit_length() - 1)) == sub) & ~last
    over = jnp.sum(jnp.where(mine, over, 0.0), axis=1, keepdims=True)
    rest = jnp.zeros((owned - SUB, cols), jnp.float32)
    pixel_sum = sums[:, :cols] + jnp.concatenate([jnp.where(last, 0.0, spilled), rest], axis=0)
    weight_sum = sums[:, cols:] + jnp.concatenate(
        [jnp.broadcast_to(over, (SUB, cols)), rest], axis=0
    )
    coadd_ref[...] = pixel_sum / jnp.maximum(weight_sum, 1.0)
    diagonal = jnp.where(row == iota((owned, cols), 1), weight_sum, 0.0)
    map_ref[...] = jnp.sum(diagonal, axis=0, keepdims=True)


def on_device(
    image,
    row_taps,
    col_taps,
    mix_coeff,
    shift_frac,
    ccd_visit,
    visit_weight,
    tile_block,
    tile_offset,
):
    rows, cols = image.shape[1:]
    tiles = tile_block.shape[0]
    sky = lax.axis_size("sky")
    capacity = max(2, tiles // sky)
    message_rows = capacity * SUB + TAIL
    fold = (row_taps.shape[1] + 1) // 2
    vmem = pl.BlockSpec(memory_space=pltpu.VMEM)
    smem = pl.BlockSpec(memory_space=pltpu.SMEM)
    messages = pl.pallas_call(
        functools.partial(window_kernel, capacity),
        out_shape=jax.ShapeDtypeStruct((sky, message_rows, cols), jnp.bfloat16),
        in_specs=[vmem] * 5 + [smem] * 4,
        out_specs=vmem,
        scratch_shapes=[
            pltpu.VMEM((rows + 2 * fold, cols), jnp.float32),
            pltpu.VMEM((3, 2 * fold, cols), jnp.float32),
            pltpu.VMEM((fold, 2 * cols, 2 * cols), jnp.bfloat16),
            pltpu.VMEM((rows, 2 * cols), jnp.float32),
            pltpu.VMEM((rows + 2 * SUB, cols), jnp.float32),
            pltpu.VMEM((sky * capacity * SUB, cols), jnp.float32),
            pltpu.SMEM((tiles,), jnp.int32),
            pltpu.SMEM((sky * capacity,), jnp.int32),
            pltpu.SMEM((sky,), jnp.int32),
        ],
        compiler_params=pltpu.CompilerParams(vmem_limit_bytes=32 * 1024 * 1024),
        name="match_warp_pack",
    )(
        image,
        row_taps,
        col_taps,
        mix_coeff,
        visit_weight.reshape(1, -1),
        shift_frac,
        ccd_visit,
        tile_block,
        tile_offset,
    )
    received = lax.all_to_all(messages, "sky", split_axis=0, concat_axis=0, tiled=True)
    coadd, weight_map = pl.pallas_call(
        functools.partial(sky_kernel, capacity),
        out_shape=(
            jax.ShapeDtypeStruct((BLK_DEV * SUB, cols), jnp.float32),
            jax.ShapeDtypeStruct((1, BLK_DEV * SUB), jnp.float32),
        ),
        in_specs=[vmem],
        out_specs=(vmem, vmem),
        compiler_params=pltpu.CompilerParams(vmem_limit_bytes=32 * 1024 * 1024),
        name="place_normalise",
    )(received)
    return coadd, weight_map.reshape(-1)


def solution(mesh):
    return jax.shard_map(
        on_device,
        mesh=mesh,
        in_specs=(
            P(("groups", "sky"), None, None),
            P(),
            P(),
            P(("groups", "sky"), None, None),
            P(("groups", "sky"), None),
            P(("groups", "sky")),
            P("groups"),
            P(("groups", "sky")),
            P(("groups", "sky")),
        ),
        out_specs=(P(("groups", "sky"), None), P(("groups", "sky"))),
        check_vma=False,
    )
```

```python
import functools

import jax
import jax.numpy as jnp
from jax import lax
from jax.experimental import pallas as pl
from jax.experimental.pallas import tpu as pltpu
from jax.sharding import PartitionSpec as P

BLK_DEV = 16
SUB = 8
LARGE_VMEM = 56 * 1024 * 1024
SMALL_VMEM = 16 * 1024 * 1024
EMPTY = -64
TAPS_DOWN = 6


def iota(shape, axis):
    return lax.broadcasted_iota(jnp.int32, shape, axis)


def weight_of(visit_ref, weight_ref):
    values = weight_ref[...].astype(jnp.float32)
    chosen = jnp.where(iota(values.shape, 1) == visit_ref[0], values, 0.0)
    return jnp.sum(chosen, axis=1, keepdims=True)


def lanczos_rows(frac_ref, cols):
    row = iota((2 * SUB, cols), 0)
    tap = jnp.where(row < SUB, row, row - SUB)
    fraction = jnp.where(row < SUB, frac_ref[0, 1], frac_ref[0, 0])
    angles = jnp.pi * ((tap - 2).astype(jnp.float32) - fraction)
    third = angles / 3.0
    kernel = jnp.sin(angles) / angles * (jnp.sin(third) / third)
    kernel = jnp.where(tap < TAPS_DOWN, kernel, 0.0)
    across, down = kernel[:SUB], kernel[SUB:]
    across = across / jnp.sum(across, axis=0, keepdims=True)
    down = down / jnp.sum(down, axis=0, keepdims=True)
    return across, down


def combined_taps(row_ref, col_ref, mix_ref, lifted, base):
    taps, basis = row_ref.shape
    count, cols = base.shape[1:]
    half = taps // 2
    l, s = iota((cols, taps), 0), iota((cols, taps), 1)
    turned = ((s + l == half) | (s + l == half + cols)).astype(jnp.float32).astype(jnp.bfloat16)
    across = jnp.dot(turned, row_ref[...], preferred_element_type=jnp.float32)
    across = across.astype(jnp.bfloat16)
    lifted[0:1] = jnp.zeros((1, basis), jnp.float32)
    lifted[1:] = col_ref[...].astype(jnp.float32)
    down = lifted[...]
    scaled = jnp.concatenate([down * mix_ref[term] for term in range(3)], axis=0)
    high = scaled.astype(jnp.bfloat16)
    low = (scaled - high.astype(jnp.float32)).astype(jnp.bfloat16)
    found = lax.dot_general(
        jnp.concatenate([high, low], axis=0),
        across,
        (((1,), (1,)), ((), ())),
        preferred_element_type=jnp.float32,
    )
    found = found[: 3 * count] + found[3 * count :]
    lane = iota((count, cols), 1)
    lane = jnp.where(lane < cols // 2, lane, lane - cols).astype(jnp.float32)
    base[0] = found[:count] + (2.0 / cols) * lane * found[count : 2 * count]
    base[1] = found[count : 2 * count]
    base[2] = found[2 * count :]


def build_band(base, row, half, band, first):
    cols = base.shape[2]
    blocks = cols // SUB
    sub = iota((SUB, cols), 0)
    lane = iota((SUB, cols), 1)
    first_u = (2.0 * sub.astype(jnp.float32) + 1.0) / cols - 1.0

    def spin(term):
        taps = jnp.broadcast_to(base[term, pl.ds(row, 1), :], (SUB, cols))
        return pltpu.roll(taps, 0, 1, stride=1, stride_axis=0)

    def keep(block, value):
        if block * SUB >= half and (block + 1) * SUB - 1 + half < cols:
            return value
        return jnp.where(jnp.abs(lane - sub - block * SUB) <= half, value, 0.0)

    slope = spin(1)
    level = spin(0) + first_u * slope
    rise = spin(2)
    for pair in range(blocks // 2):
        two = []
        for block in (2 * pair, 2 * pair + 1):
            value = level + (2.0 * SUB * block / cols) * slope
            value = keep(block, pltpu.roll(value, SUB * block, 1) if block else value)
            other = keep(block, pltpu.roll(rise, SUB * block, 1) if block else rise)
            two.append(jnp.concatenate([value, other], axis=1))
        at = first + pair * 2 * SUB
        band[at : at + 2 * SUB, :] = jnp.concatenate(two, axis=0).astype(jnp.bfloat16)


def window_kernel(
    capacity,
    image_hbm,
    row_hbm,
    col_hbm,
    mix_hbm,
    weight_hbm,
    frac_hbm,
    visit_hbm,
    block_hbm,
    offset_hbm,
    out_ref,
    image_ref,
    row_ref,
    col_ref,
    mix_ref,
    weight_ref,
    frac_ref,
    visit_ref,
    block_ref,
    offset_ref,
    copied,
    padded,
    lifted,
    base,
    band_a,
    band_b,
    moved_a,
    moved_b,
    total,
    spread,
    slots,
    slot_of,
    starts,
    counts,
):
    rows, cols = image_ref.shape[1:]
    half = row_ref.shape[0] // 2
    fold = half + 1
    tiles = slot_of.shape[0]
    owners = out_ref.shape[0]
    data_rows = capacity * SUB
    owned = BLK_DEV * SUB

    pairs = (
        (row_hbm, row_ref),
        (col_hbm, col_ref),
        (mix_hbm, mix_ref),
        (image_hbm, image_ref),
        (frac_hbm, frac_ref),
        (visit_hbm, visit_ref),
        (weight_hbm, weight_ref),
        (block_hbm, block_ref),
        (offset_hbm, offset_ref),
    )
    copies = [
        pltpu.make_async_copy(source, target, copied.at[index])
        for index, (source, target) in enumerate(pairs)
    ]
    for copy in copies:
        copy.start()

    @pl.loop(0, owners)
    def _(owner):
        counts[owner] = 0

    if owners * capacity > tiles:
        slots[...] = jnp.zeros(slots.shape, jnp.float32)

        @pl.loop(0, owners * capacity)
        def _(slot):
            starts[slot] = EMPTY

    padded[:fold] = jnp.zeros((fold, cols), jnp.float32)
    padded[fold + rows :] = jnp.zeros((fold, cols), jnp.float32)
    spread[:SUB] = jnp.zeros((SUB, cols), jnp.float32)
    spread[SUB + rows :] = jnp.zeros((SUB, cols), jnp.float32)
    total[...] = jnp.zeros(total.shape, jnp.float32)
    for copy in copies:
        copy.wait()

    combined_taps(row_ref, col_ref, mix_ref, lifted, base)
    padded[fold : fold + rows] = image_ref[0].astype(jnp.float32)
    across, down = lanczos_rows(frac_ref, cols)
    weight = weight_of(visit_ref, weight_ref)

    per_group = moved_a.shape[0]
    steps = fold // (2 * per_group)

    def build(group, band, moved):
        for index in range(per_group):
            r = group * per_group + index
            for part in range(2):
                build_band(base, r + part * fold, half, band, (2 * index + part) * cols)
            moved[index] = padded[pl.ds(r, rows + fold), :].astype(jnp.bfloat16)

    def multiply(band, moved):
        parts = []
        for index in range(per_group):
            parts += [moved[index, :rows, :], moved[index, fold:, :]]
        total[...] += jnp.dot(
            jnp.concatenate(parts, axis=1), band[...], preferred_element_type=jnp.float32
        )

    def assign(tile):
        block = block_ref[tile]
        owner = lax.div(block, BLK_DEV)
        rank = counts[owner]
        counts[owner] = rank + 1
        slot = owner * capacity + rank
        slot_of[tile] = slot
        starts[slot] = (block - owner * BLK_DEV) * SUB + offset_ref[tile]

    build(0, band_a, moved_a)

    @pl.loop(0, steps)
    def _(step):
        build(2 * step + 1, band_b, moved_b)
        multiply(band_a, moved_a)
        build(lax.rem(2 * step + 2, 2 * steps), band_a, moved_a)
        multiply(band_b, moved_b)
        for index in range(tiles // steps):
            assign(step * (tiles // steps) + index)

    lane = iota((1, cols), 1)
    taps_across = [
        jnp.where((lane + m - 2 >= 0) & (lane + m - 2 < cols), across[m : m + 1], 0.0)
        for m in range(TAPS_DOWN)
    ]
    chunk = 64
    for index in range(rows // chunk):
        first = index * chunk
        position = (2 * (iota((chunk, cols), 0) + first) + 1).astype(jnp.float32) / rows - 1.0
        both = total[first : first + chunk, :]
        matched = both[:, :cols] + position * both[:, cols:]
        result = taps_across[2] * matched
        for m in range(TAPS_DOWN):
            if m != 2:
                result = result + taps_across[m] * pltpu.roll(matched, (2 - m) % cols, 1)
        spread[first + SUB : first + SUB + chunk, :] = result

    for tile in range(tiles):
        first = tile * SUB + SUB - 2
        result = down[0:1] * spread[first : first + SUB, :]
        for m in range(1, TAPS_DOWN):
            result = result + down[m : m + 1] * spread[first + m : first + m + SUB, :]
        slots[pl.ds(pl.multiple_of(slot_of[tile] * SUB, SUB), SUB), :] = result

    sub = iota((SUB, cols), 0)
    wide = iota((SUB, cols), 1)
    segment = wide >> (data_rows.bit_length() - 1)
    lane_row = wide & (SUB - 1)
    lane_slot = (wide >> 3) & (capacity - 1)
    spill_slot = wide & (capacity - 1)
    spill_row = wide >> (capacity.bit_length() - 1)
    tile_weight = jnp.broadcast_to(weight, (SUB, cols))

    def message(owner, carry):
        previous = jnp.maximum(owner - 1, 0)
        first = owner * data_rows
        out_ref[owner, :data_rows, :] = slots[
            pl.ds(pl.multiple_of(first, data_rows), data_rows), :
        ].astype(jnp.bfloat16)
        spilled = jnp.zeros((SUB, cols), jnp.float32)
        over = jnp.zeros((SUB, cols), jnp.float32)
        target = jnp.zeros((SUB, cols), jnp.int32)
        for c in range(capacity):
            target = jnp.where(lane_slot == c, starts[owner * capacity + c] + lane_row, target)
            slot = previous * capacity + c
            start = starts[slot]
            past = jnp.where(owner > 0, start + SUB - owned, 0)
            tile = slots[pl.ds(pl.multiple_of(slot * SUB, SUB), SUB), :]
            tile = pltpu.roll(tile, start & (SUB - 1), 0)
            spilled = spilled + jnp.where(sub < past, tile, 0.0)
            over = jnp.where((spill_slot == c) & (spill_row < past), tile_weight, over)
        meta = jnp.where(segment == 1, target.astype(jnp.float32), tile_weight)
        meta = jnp.where(segment == 0, over, meta)
        tail = jnp.where(sub == SUB - 1, meta, spilled * tile_weight)
        out_ref[owner, data_rows:, :] = tail.astype(jnp.bfloat16)
        return carry

    lax.fori_loop(0, owners, message, 0, unroll=min(owners, 16))


def sky_kernel(capacity, got_ref, coadd_ref, map_ref):
    sources, message_rows, cols = got_ref.shape
    data_rows = capacity * SUB
    owned = coadd_ref.shape[0]
    per_chunk = cols // data_rows
    chunks = sources // per_chunk
    place = iota((chunks, cols), 0)
    wide = iota((chunks, cols), 1)
    row = iota((owned, cols), 0)
    spilled = jnp.zeros((SUB, cols), jnp.float32)
    target = jnp.zeros((chunks, cols), jnp.float32)
    weight = jnp.zeros((chunks, cols), jnp.float32)
    for k in range(per_chunk):
        heads = jnp.zeros((chunks, cols), jnp.float32)
        for chunk in range(chunks):
            tail = got_ref[chunk * per_chunk + k, data_rows:, :].astype(jnp.float32)
            spilled = spilled + tail
            heads = jnp.where(place == chunk, tail[SUB - 1 :], heads)
        here = (wide >= k * data_rows) & (wide < (k + 1) * data_rows)
        target = jnp.where(here, pltpu.roll(heads, (k - 1) * data_rows % cols, 1), target)
        weight = jnp.where(here, pltpu.roll(heads, (k - 2) * data_rows % cols, 1), weight)
    target = target.astype(jnp.int32)
    pieces = [
        jnp.where(row == target[chunk : chunk + 1], weight[chunk : chunk + 1], 0.0)
        for chunk in range(chunks)
    ]
    placement = jnp.concatenate(pieces, axis=1).astype(jnp.bfloat16)
    pixels = got_ref[:, :data_rows, :].reshape(sources * data_rows, cols)
    pixels = jnp.concatenate([pixels, jnp.ones(pixels.shape, jnp.bfloat16)], axis=1)
    sums = jnp.dot(placement, pixels, preferred_element_type=jnp.float32)
    sub = iota((SUB, cols), 0)
    wide = iota((SUB, cols), 1)
    last = sub == SUB - 1
    over = jnp.broadcast_to(spilled[SUB - 1 :], (SUB, cols))
    mine = ((wide >> (capacity.bit_length() - 1)) == sub) & ~last
    over = jnp.sum(jnp.where(mine, over, 0.0), axis=1, keepdims=True)
    rest = jnp.zeros((owned - SUB, cols), jnp.float32)
    pixel_sum = sums[:, :cols] + jnp.concatenate([jnp.where(last, 0.0, spilled), rest], axis=0)
    weight_sum = sums[:, cols:] + jnp.concatenate(
        [jnp.broadcast_to(over, (SUB, cols)), rest], axis=0
    )
    coadd_ref[...] = pixel_sum / jnp.maximum(weight_sum, 1.0)
    diagonal = jnp.where(row == iota((owned, cols), 1), weight_sum, 0.0)
    map_ref[...] = jnp.sum(diagonal, axis=0, keepdims=True)


def on_device(
    image,
    row_taps,
    col_taps,
    mix_coeff,
    shift_frac,
    ccd_visit,
    visit_weight,
    tile_block,
    tile_offset,
):
    rows, cols = image.shape[1:]
    tiles = tile_block.shape[0]
    sky = lax.axis_size("sky")
    capacity = max(2, tiles // sky)
    taps, basis = row_taps.shape[1], row_taps.shape[0]
    fold = taps // 2 + 1
    visits = visit_weight.shape[0]
    per_group = 2
    anywhere = pl.BlockSpec(memory_space=pl.ANY)
    vmem = pl.BlockSpec(memory_space=pltpu.VMEM)
    messages = pl.pallas_call(
        functools.partial(window_kernel, capacity),
        out_shape=jax.ShapeDtypeStruct((sky, capacity * SUB + SUB, cols), jnp.bfloat16),
        in_specs=[anywhere] * 9,
        out_specs=vmem,
        scratch_shapes=[
            pltpu.VMEM((1, rows, cols), jnp.bfloat16),
            pltpu.VMEM((taps, basis), jnp.bfloat16),
            pltpu.VMEM((taps, basis), jnp.bfloat16),
            pltpu.VMEM((3, 1, basis), jnp.float32),
            pltpu.VMEM((1, visits), jnp.bfloat16),
            pltpu.SMEM((1, 2), jnp.float32),
            pltpu.SMEM((1,), jnp.int32),
            pltpu.SMEM((tiles,), jnp.int32),
            pltpu.SMEM((tiles,), jnp.int32),
            pltpu.SemaphoreType.DMA((9,)),
            pltpu.VMEM((rows + 2 * fold, cols), jnp.float32),
            pltpu.VMEM((2 * fold, basis), jnp.float32),
            pltpu.VMEM((3, 2 * fold, cols), jnp.float32),
            pltpu.VMEM((per_group * 2 * cols, 2 * cols), jnp.bfloat16),
            pltpu.VMEM((per_group * 2 * cols, 2 * cols), jnp.bfloat16),
            pltpu.VMEM((per_group, rows + fold, cols), jnp.bfloat16),
            pltpu.VMEM((per_group, rows + fold, cols), jnp.bfloat16),
            pltpu.VMEM((rows, 2 * cols), jnp.float32),
            pltpu.VMEM((rows + 2 * SUB, cols), jnp.float32),
            pltpu.VMEM((sky * capacity * SUB, cols), jnp.float32),
            pltpu.SMEM((tiles,), jnp.int32),
            pltpu.SMEM((sky * capacity,), jnp.int32),
            pltpu.SMEM((sky,), jnp.int32),
        ],
        compiler_params=pltpu.CompilerParams(vmem_limit_bytes=LARGE_VMEM),
        name="match_warp_pack",
    )(
        image,
        row_taps.T,
        col_taps.T,
        mix_coeff.transpose(1, 0, 2),
        visit_weight.reshape(1, -1),
        shift_frac,
        ccd_visit,
        tile_block,
        tile_offset,
    )
    received = lax.all_to_all(messages, "sky", split_axis=0, concat_axis=0, tiled=True)
    coadd, weight_map = pl.pallas_call(
        functools.partial(sky_kernel, capacity),
        out_shape=(
            jax.ShapeDtypeStruct((BLK_DEV * SUB, cols), jnp.float32),
            jax.ShapeDtypeStruct((1, BLK_DEV * SUB), jnp.float32),
        ),
        in_specs=[vmem],
        out_specs=(vmem, vmem),
        compiler_params=pltpu.CompilerParams(vmem_limit_bytes=SMALL_VMEM),
        name="place_normalise",
    )(received)
    return coadd, weight_map.reshape(-1)


def solution(mesh):
    return jax.shard_map(
        on_device,
        mesh=mesh,
        in_specs=(
            P(("groups", "sky"), None, None),
            P(),
            P(),
            P(("groups", "sky"), None, None),
            P(("groups", "sky"), None),
            P(("groups", "sky")),
            P("groups"),
            P(("groups", "sky")),
            P(("groups", "sky")),
        ),
        out_specs=(P(("groups", "sky"), None), P(("groups", "sky"))),
        check_vma=False,
    )
```

```python
import functools

import jax
import jax.numpy as jnp
from jax import lax
from jax.experimental import pallas as pl
from jax.experimental.pallas import tpu as pltpu
from jax.sharding import PartitionSpec as P

BLK_DEV = 16
SUB = 8
LARGE_VMEM = 32 * 1024 * 1024
SMALL_VMEM = 16 * 1024 * 1024
EMPTY = -64
TAPS_DOWN = 6


def iota(shape, axis):
    return lax.broadcasted_iota(jnp.int32, shape, axis)


def weight_of(visit_ref, weight_ref):
    values = weight_ref[...].astype(jnp.float32)
    chosen = jnp.where(iota(values.shape, 1) == visit_ref[0], values, 0.0)
    return jnp.sum(chosen, axis=1, keepdims=True)


def lanczos_rows(frac_ref, cols):
    row = iota((2 * SUB, cols), 0)
    tap = jnp.where(row < SUB, row, row - SUB)
    fraction = jnp.where(row < SUB, frac_ref[0, 1], frac_ref[0, 0])
    angles = jnp.pi * ((tap - 2).astype(jnp.float32) - fraction)
    third = angles / 3.0
    kernel = jnp.sin(angles) / angles * (jnp.sin(third) / third)
    kernel = jnp.where(tap < TAPS_DOWN, kernel, 0.0)
    across, down = kernel[:SUB], kernel[SUB:]
    across = across / jnp.sum(across, axis=0, keepdims=True)
    down = down / jnp.sum(down, axis=0, keepdims=True)
    return across, down


def combined_taps(row_ref, col_ref, mix_ref, lifted, base):
    taps, basis = row_ref.shape
    count, cols = base.shape[1:]
    half = taps // 2
    l, s = iota((cols, taps), 0), iota((cols, taps), 1)
    turned = ((s + l == half) | (s + l == half + cols)).astype(jnp.float32).astype(jnp.bfloat16)
    across = jnp.dot(turned, row_ref[...], preferred_element_type=jnp.float32)
    across = across.astype(jnp.bfloat16)
    lifted[0:1] = jnp.zeros((1, basis), jnp.float32)
    lifted[1:] = col_ref[...].astype(jnp.float32)
    down = lifted[...]
    scaled = jnp.concatenate([down * mix_ref[term] for term in range(3)], axis=0)
    high = scaled.astype(jnp.bfloat16)
    low = (scaled - high.astype(jnp.float32)).astype(jnp.bfloat16)
    found = lax.dot_general(
        jnp.concatenate([high, low], axis=0),
        across,
        (((1,), (1,)), ((), ())),
        preferred_element_type=jnp.float32,
    )
    found = found[: 3 * count] + found[3 * count :]
    lane = iota((count, cols), 1)
    lane = jnp.where(lane < cols // 2, lane, lane - cols).astype(jnp.float32)
    base[0] = found[:count] + (2.0 / cols) * lane * found[count : 2 * count]
    base[1] = found[count : 2 * count]
    base[2] = found[2 * count :]


def build_band(base, row, half, band, first):
    cols = base.shape[2]
    blocks = cols // SUB
    sub = iota((SUB, cols), 0)
    lane = iota((SUB, cols), 1)
    first_u = (2.0 * sub.astype(jnp.float32) + 1.0) / cols - 1.0

    def spin(term):
        taps = jnp.broadcast_to(base[term, pl.ds(row, 1), :], (SUB, cols))
        return pltpu.roll(taps, 0, 1, stride=1, stride_axis=0)

    def keep(block, value):
        if block * SUB >= half and (block + 1) * SUB - 1 + half < cols:
            return value
        return jnp.where(jnp.abs(lane - sub - block * SUB) <= half, value, 0.0)

    slope = spin(1)
    level = spin(0) + first_u * slope
    rise = spin(2)
    for pair in range(blocks // 2):
        two = []
        for block in (2 * pair, 2 * pair + 1):
            value = level + (2.0 * SUB * block / cols) * slope
            value = keep(block, pltpu.roll(value, SUB * block, 1) if block else value)
            other = keep(block, pltpu.roll(rise, SUB * block, 1) if block else rise)
            two.append(jnp.concatenate([value, other], axis=1))
        at = first + pair * 2 * SUB
        band[at : at + 2 * SUB, :] = jnp.concatenate(two, axis=0).astype(jnp.bfloat16)


def window_kernel(
    capacity,
    image_hbm,
    row_hbm,
    col_hbm,
    mix_hbm,
    weight_hbm,
    frac_hbm,
    block_hbm,
    offset_hbm,
    visit_ref,
    out_ref,
    image_ref,
    row_ref,
    col_ref,
    mix_ref,
    weight_ref,
    frac_ref,
    block_ref,
    offset_ref,
    copied,
    padded,
    lifted,
    base,
    band_a,
    band_b,
    moved_a,
    moved_b,
    total,
    spread,
    slots,
    slot_of,
    starts,
    counts,
):
    rows, cols = image_ref.shape[1:]
    half = row_ref.shape[0] // 2
    fold = half + 1
    tiles = slot_of.shape[0]
    owners = out_ref.shape[0]
    data_rows = capacity * SUB
    owned = BLK_DEV * SUB

    pairs = (
        (row_hbm, row_ref),
        (col_hbm, col_ref),
        (mix_hbm, mix_ref),
        (image_hbm, image_ref),
        (frac_hbm, frac_ref),
        (weight_hbm, weight_ref),
        (block_hbm, block_ref),
        (offset_hbm, offset_ref),
    )
    copies = [
        pltpu.make_async_copy(source, target, copied.at[index])
        for index, (source, target) in enumerate(pairs)
    ]
    for copy in copies:
        copy.start()

    @pl.loop(0, owners)
    def _(owner):
        counts[owner] = 0

    if owners * capacity > tiles:
        slots[...] = jnp.zeros(slots.shape, jnp.float32)

        @pl.loop(0, owners * capacity)
        def _(slot):
            starts[slot] = EMPTY

    padded[:fold] = jnp.zeros((fold, cols), jnp.float32)
    padded[fold + rows :] = jnp.zeros((fold, cols), jnp.float32)
    spread[:SUB] = jnp.zeros((SUB, cols), jnp.float32)
    spread[SUB + rows :] = jnp.zeros((SUB, cols), jnp.float32)
    total[...] = jnp.zeros(total.shape, jnp.float32)
    for copy in copies:
        copy.wait()

    combined_taps(row_ref, col_ref, mix_ref, lifted, base)
    padded[fold : fold + rows] = image_ref[0].astype(jnp.float32)
    across, down = lanczos_rows(frac_ref, cols)
    weight = weight_of(visit_ref, weight_ref)

    per_group = moved_a.shape[0]
    steps = fold // (2 * per_group)

    def build(group, band, moved):
        for index in range(per_group):
            r = group * per_group + index
            for part in range(2):
                build_band(base, r + part * fold, half, band, (2 * index + part) * cols)
            moved[index] = padded[pl.ds(r, rows + fold), :].astype(jnp.bfloat16)

    def multiply(band, moved):
        parts = []
        for index in range(per_group):
            parts += [moved[index, :rows, :], moved[index, fold:, :]]
        total[...] += jnp.dot(
            jnp.concatenate(parts, axis=1), band[...], preferred_element_type=jnp.float32
        )

    def assign(tile):
        block = block_ref[tile]
        owner = lax.div(block, BLK_DEV)
        rank = counts[owner]
        counts[owner] = rank + 1
        slot = owner * capacity + rank
        slot_of[tile] = slot
        starts[slot] = (block - owner * BLK_DEV) * SUB + offset_ref[tile]

    build(0, band_a, moved_a)

    @pl.loop(0, steps)
    def _(step):
        build(2 * step + 1, band_b, moved_b)
        multiply(band_a, moved_a)
        build(lax.rem(2 * step + 2, 2 * steps), band_a, moved_a)
        multiply(band_b, moved_b)
        for index in range(tiles // steps):
            assign(step * (tiles // steps) + index)

    lane = iota((1, cols), 1)
    taps_across = [
        jnp.where((lane + m - 2 >= 0) & (lane + m - 2 < cols), across[m : m + 1], 0.0)
        for m in range(TAPS_DOWN)
    ]
    chunk = 64
    for index in range(rows // chunk):
        first = index * chunk
        position = (2 * (iota((chunk, cols), 0) + first) + 1).astype(jnp.float32) / rows - 1.0
        both = total[first : first + chunk, :]
        matched = both[:, :cols] + position * both[:, cols:]
        result = taps_across[2] * matched
        for m in range(TAPS_DOWN):
            if m != 2:
                result = result + taps_across[m] * pltpu.roll(matched, (2 - m) % cols, 1)
        spread[first + SUB : first + SUB + chunk, :] = result

    for tile in range(tiles):
        first = tile * SUB + SUB - 2
        result = down[0:1] * spread[first : first + SUB, :]
        for m in range(1, TAPS_DOWN):
            result = result + down[m : m + 1] * spread[first + m : first + m + SUB, :]
        slots[pl.ds(pl.multiple_of(slot_of[tile] * SUB, SUB), SUB), :] = result

    sub = iota((SUB, cols), 0)
    wide = iota((SUB, cols), 1)
    segment = wide >> (data_rows.bit_length() - 1)
    lane_row = wide & (SUB - 1)
    lane_slot = (wide >> 3) & (capacity - 1)
    spill_slot = wide & (capacity - 1)
    spill_row = wide >> (capacity.bit_length() - 1)
    tile_weight = jnp.broadcast_to(weight, (SUB, cols))

    def message(owner, carry):
        previous = jnp.maximum(owner - 1, 0)
        first = owner * data_rows
        out_ref[owner, :data_rows, :] = slots[
            pl.ds(pl.multiple_of(first, data_rows), data_rows), :
        ].astype(jnp.bfloat16)
        spilled = jnp.zeros((SUB, cols), jnp.float32)
        over = jnp.zeros((SUB, cols), jnp.float32)
        target = jnp.zeros((SUB, cols), jnp.int32)
        for c in range(capacity):
            target = jnp.where(lane_slot == c, starts[owner * capacity + c] + lane_row, target)
            slot = previous * capacity + c
            start = starts[slot]
            past = jnp.where(owner > 0, start + SUB - owned, 0)
            tile = slots[pl.ds(pl.multiple_of(slot * SUB, SUB), SUB), :]
            tile = pltpu.roll(tile, start & (SUB - 1), 0)
            spilled = spilled + jnp.where(sub < past, tile, 0.0)
            over = jnp.where((spill_slot == c) & (spill_row < past), tile_weight, over)
        meta = jnp.where(segment == 1, target.astype(jnp.float32), tile_weight)
        meta = jnp.where(segment == 0, over, meta)
        tail = jnp.where(sub == SUB - 1, meta, spilled * tile_weight)
        out_ref[owner, data_rows:, :] = tail.astype(jnp.bfloat16)
        return carry

    lax.fori_loop(0, owners, message, 0, unroll=min(owners, 16))


def sky_kernel(capacity, got_ref, coadd_ref, map_ref):
    sources, message_rows, cols = got_ref.shape
    data_rows = capacity * SUB
    owned = coadd_ref.shape[0]
    per_chunk = cols // data_rows
    chunks = sources // per_chunk
    place = iota((chunks, cols), 0)
    wide = iota((chunks, cols), 1)
    row = iota((owned, cols), 0)
    spilled = jnp.zeros((SUB, cols), jnp.float32)
    target = jnp.zeros((chunks, cols), jnp.float32)
    weight = jnp.zeros((chunks, cols), jnp.float32)
    for k in range(per_chunk):
        heads = jnp.zeros((chunks, cols), jnp.float32)
        for chunk in range(chunks):
            tail = got_ref[chunk * per_chunk + k, data_rows:, :].astype(jnp.float32)
            spilled = spilled + tail
            heads = jnp.where(place == chunk, tail[SUB - 1 :], heads)
        here = (wide >= k * data_rows) & (wide < (k + 1) * data_rows)
        target = jnp.where(here, pltpu.roll(heads, (k - 1) * data_rows % cols, 1), target)
        weight = jnp.where(here, pltpu.roll(heads, (k - 2) * data_rows % cols, 1), weight)
    target = target.astype(jnp.int32)
    pieces = [
        jnp.where(row == target[chunk : chunk + 1], weight[chunk : chunk + 1], 0.0)
        for chunk in range(chunks)
    ]
    placement = jnp.concatenate(pieces, axis=1).astype(jnp.bfloat16)
    pixels = got_ref[:, :data_rows, :].reshape(sources * data_rows, cols)
    pixels = jnp.concatenate([pixels, jnp.ones(pixels.shape, jnp.bfloat16)], axis=1)
    sums = jnp.dot(placement, pixels, preferred_element_type=jnp.float32)
    sub = iota((SUB, cols), 0)
    wide = iota((SUB, cols), 1)
    last = sub == SUB - 1
    over = jnp.broadcast_to(spilled[SUB - 1 :], (SUB, cols))
    mine = ((wide >> (capacity.bit_length() - 1)) == sub) & ~last
    over = jnp.sum(jnp.where(mine, over, 0.0), axis=1, keepdims=True)
    rest = jnp.zeros((owned - SUB, cols), jnp.float32)
    pixel_sum = sums[:, :cols] + jnp.concatenate([jnp.where(last, 0.0, spilled), rest], axis=0)
    weight_sum = sums[:, cols:] + jnp.concatenate(
        [jnp.broadcast_to(over, (SUB, cols)), rest], axis=0
    )
    coadd_ref[...] = pixel_sum / jnp.maximum(weight_sum, 1.0)
    diagonal = jnp.where(row == iota((owned, cols), 1), weight_sum, 0.0)
    map_ref[...] = jnp.sum(diagonal, axis=0, keepdims=True)


def on_device(
    image,
    row_taps,
    col_taps,
    mix_coeff,
    shift_frac,
    ccd_visit,
    visit_weight,
    tile_block,
    tile_offset,
):
    rows, cols = image.shape[1:]
    tiles = tile_block.shape[0]
    sky = lax.axis_size("sky")
    capacity = max(2, tiles // sky)
    taps, basis = row_taps.shape[1], row_taps.shape[0]
    fold = taps // 2 + 1
    visits = visit_weight.shape[0]
    per_group = 2
    anywhere = pl.BlockSpec(memory_space=pl.ANY)
    vmem = pl.BlockSpec(memory_space=pltpu.VMEM)
    messages = pl.pallas_call(
        functools.partial(window_kernel, capacity),
        out_shape=pltpu.VMEM((sky, capacity * SUB + SUB, cols), jnp.bfloat16),
        in_specs=[anywhere] * 8 + [pl.BlockSpec(memory_space=pltpu.SMEM)],
        out_specs=vmem,
        scratch_shapes=[
            pltpu.VMEM((1, rows, cols), jnp.bfloat16),
            pltpu.VMEM((taps, basis), jnp.bfloat16),
            pltpu.VMEM((taps, basis), jnp.bfloat16),
            pltpu.VMEM((3, 1, basis), jnp.float32),
            pltpu.VMEM((1, visits), jnp.bfloat16),
            pltpu.SMEM((1, 2), jnp.float32),
            pltpu.SMEM((tiles,), jnp.int32),
            pltpu.SMEM((tiles,), jnp.int32),
            pltpu.SemaphoreType.DMA((8,)),
            pltpu.VMEM((rows + 2 * fold, cols), jnp.float32),
            pltpu.VMEM((2 * fold, basis), jnp.float32),
            pltpu.VMEM((3, 2 * fold, cols), jnp.float32),
            pltpu.VMEM((per_group * 2 * cols, 2 * cols), jnp.bfloat16),
            pltpu.VMEM((per_group * 2 * cols, 2 * cols), jnp.bfloat16),
            pltpu.VMEM((per_group, rows + fold, cols), jnp.bfloat16),
            pltpu.VMEM((per_group, rows + fold, cols), jnp.bfloat16),
            pltpu.VMEM((rows, 2 * cols), jnp.float32),
            pltpu.VMEM((rows + 2 * SUB, cols), jnp.float32),
            pltpu.VMEM((sky * capacity * SUB, cols), jnp.float32),
            pltpu.SMEM((tiles,), jnp.int32),
            pltpu.SMEM((sky * capacity,), jnp.int32),
            pltpu.SMEM((sky,), jnp.int32),
        ],
        compiler_params=pltpu.CompilerParams(vmem_limit_bytes=LARGE_VMEM),
        name="match_warp_pack",
    )(
        *[
            pltpu.with_memory_space_constraint(value, pltpu.HBM)
            for value in (
                image,
                row_taps.T,
                col_taps.T,
                mix_coeff.transpose(1, 0, 2),
                visit_weight.reshape(1, -1),
                shift_frac,
                tile_block,
                tile_offset,
            )
        ],
        ccd_visit,
    )
    received = lax.all_to_all(messages, "sky", split_axis=0, concat_axis=0, tiled=True)
    coadd, weight_map = pl.pallas_call(
        functools.partial(sky_kernel, capacity),
        out_shape=(
            jax.ShapeDtypeStruct((BLK_DEV * SUB, cols), jnp.float32),
            jax.ShapeDtypeStruct((1, BLK_DEV * SUB), jnp.float32),
        ),
        in_specs=[vmem],
        out_specs=(vmem, vmem),
        compiler_params=pltpu.CompilerParams(vmem_limit_bytes=SMALL_VMEM),
        name="place_normalise",
    )(received)
    return coadd, weight_map.reshape(-1)


def solution(mesh):
    return jax.shard_map(
        on_device,
        mesh=mesh,
        in_specs=(
            P(("groups", "sky"), None, None),
            P(),
            P(),
            P(("groups", "sky"), None, None),
            P(("groups", "sky"), None),
            P(("groups", "sky")),
            P("groups"),
            P(("groups", "sky")),
            P(("groups", "sky")),
        ),
        out_specs=(P(("groups", "sky"), None), P(("groups", "sky"))),
        check_vma=False,
    )
```

```python
import functools

import jax
import jax.numpy as jnp
from jax import lax
from jax.experimental import pallas as pl
from jax.experimental.pallas import tpu as pltpu
from jax.sharding import PartitionSpec as P

BLK_DEV = 16
SUB = 8
LARGE_VMEM = 32 * 1024 * 1024
SMALL_VMEM = 16 * 1024 * 1024
EMPTY = -64
TAPS_DOWN = 6


def iota(shape, axis):
    return lax.broadcasted_iota(jnp.int32, shape, axis)


def weight_of(visit_ref, weight_ref):
    values = weight_ref[...].astype(jnp.float32)
    chosen = jnp.where(iota(values.shape, 1) == visit_ref[0], values, 0.0)
    return jnp.sum(chosen, axis=1, keepdims=True)


def lanczos_rows(frac_ref, cols):
    row = iota((2 * SUB, cols), 0)
    tap = jnp.where(row < SUB, row, row - SUB)
    fraction = jnp.where(row < SUB, frac_ref[0, 1], frac_ref[0, 0])
    angles = jnp.pi * ((tap - 2).astype(jnp.float32) - fraction)
    third = angles / 3.0
    kernel = jnp.sin(angles) / angles * (jnp.sin(third) / third)
    kernel = jnp.where(tap < TAPS_DOWN, kernel, 0.0)
    across, down = kernel[:SUB], kernel[SUB:]
    across = across / jnp.sum(across, axis=0, keepdims=True)
    down = down / jnp.sum(down, axis=0, keepdims=True)
    return across, down


def combined_taps(row_ref, col_ref, mix_ref, lifted, base):
    taps, basis = row_ref.shape
    count, cols = base.shape[1:]
    half = taps // 2
    l, s = iota((cols, taps), 0), iota((cols, taps), 1)
    turned = ((s + l == half) | (s + l == half + cols)).astype(jnp.float32).astype(jnp.bfloat16)
    across = jnp.dot(turned, row_ref[...], preferred_element_type=jnp.float32)
    across = across.astype(jnp.bfloat16)
    lifted[0:1] = jnp.zeros((1, basis), jnp.float32)
    lifted[1:] = col_ref[...].astype(jnp.float32)
    down = lifted[...]
    scaled = jnp.concatenate([down * mix_ref[term] for term in range(3)], axis=0)
    high = scaled.astype(jnp.bfloat16)
    low = (scaled - high.astype(jnp.float32)).astype(jnp.bfloat16)
    found = lax.dot_general(
        jnp.concatenate([high, low], axis=0),
        across,
        (((1,), (1,)), ((), ())),
        preferred_element_type=jnp.float32,
    )
    found = found[: 3 * count] + found[3 * count :]
    lane = iota((count, cols), 1)
    lane = jnp.where(lane < cols // 2, lane, lane - cols).astype(jnp.float32)
    base[0] = found[:count] + (2.0 / cols) * lane * found[count : 2 * count]
    base[1] = found[count : 2 * count]
    base[2] = found[2 * count :]


def build_band(base, row, half, band, first):
    cols = base.shape[2]
    blocks = cols // SUB
    sub = iota((SUB, cols), 0)
    lane = iota((SUB, cols), 1)
    first_u = (2.0 * sub.astype(jnp.float32) + 1.0) / cols - 1.0

    def spin(term):
        taps = jnp.broadcast_to(base[term, pl.ds(row, 1), :], (SUB, cols))
        return pltpu.roll(taps, 0, 1, stride=1, stride_axis=0)

    def keep(block, value):
        if block * SUB >= half and (block + 1) * SUB - 1 + half < cols:
            return value
        return jnp.where(jnp.abs(lane - sub - block * SUB) <= half, value, 0.0)

    slope = spin(1)
    level = spin(0) + first_u * slope
    rise = spin(2)
    for pair in range(blocks // 2):
        two = []
        for block in (2 * pair, 2 * pair + 1):
            value = level + (2.0 * SUB * block / cols) * slope
            value = keep(block, pltpu.roll(value, SUB * block, 1) if block else value)
            other = keep(block, pltpu.roll(rise, SUB * block, 1) if block else rise)
            two.append(jnp.concatenate([value, other], axis=1))
        at = first + pair * 2 * SUB
        band[at : at + 2 * SUB, :] = jnp.concatenate(two, axis=0).astype(jnp.bfloat16)


def window_kernel(
    capacity,
    image_hbm,
    row_hbm,
    col_hbm,
    mix_hbm,
    weight_hbm,
    frac_hbm,
    block_hbm,
    offset_hbm,
    visit_ref,
    out_ref,
    image_ref,
    row_ref,
    col_ref,
    mix_ref,
    weight_ref,
    frac_ref,
    block_ref,
    offset_ref,
    copied,
    padded,
    lifted,
    base,
    band_a,
    band_b,
    moved_a,
    moved_b,
    total,
    spread,
    sky,
    slot_of,
    starts,
    counts,
):
    rows, cols = image_ref.shape[1:]
    half = row_ref.shape[0] // 2
    fold = half + 1
    tiles = slot_of.shape[0]
    owners = out_ref.shape[0]
    owned = BLK_DEV * SUB

    pairs = (
        (row_hbm, row_ref),
        (col_hbm, col_ref),
        (mix_hbm, mix_ref),
        (image_hbm, image_ref),
        (frac_hbm, frac_ref),
        (weight_hbm, weight_ref),
        (block_hbm, block_ref),
        (offset_hbm, offset_ref),
    )
    copies = [
        pltpu.make_async_copy(source, target, copied.at[index])
        for index, (source, target) in enumerate(pairs)
    ]
    for copy in copies:
        copy.start()

    @pl.loop(0, owners)
    def _(owner):
        counts[owner] = 0

    if owners * capacity > tiles:

        @pl.loop(0, owners * capacity)
        def _(slot):
            starts[slot] = EMPTY

    padded[:fold] = jnp.zeros((fold, cols), jnp.float32)
    padded[fold + rows :] = jnp.zeros((fold, cols), jnp.float32)
    spread[:SUB] = jnp.zeros((SUB, cols), jnp.float32)
    spread[SUB + rows :] = jnp.zeros((SUB, cols), jnp.float32)
    total[...] = jnp.zeros(total.shape, jnp.float32)
    for copy in copies:
        copy.wait()

    combined_taps(row_ref, col_ref, mix_ref, lifted, base)
    padded[fold : fold + rows] = image_ref[0].astype(jnp.float32)
    across, down = lanczos_rows(frac_ref, cols)
    weight = weight_of(visit_ref, weight_ref)

    per_group = moved_a.shape[0]
    steps = fold // (2 * per_group)

    def build(group, band, moved):
        for index in range(per_group):
            r = group * per_group + index
            for part in range(2):
                build_band(base, r + part * fold, half, band, (2 * index + part) * cols)
            moved[index] = padded[pl.ds(r, rows + fold), :].astype(jnp.bfloat16)

    def multiply(band, moved):
        parts = []
        for index in range(per_group):
            parts += [moved[index, :rows, :], moved[index, fold:, :]]
        total[...] += jnp.dot(
            jnp.concatenate(parts, axis=1), band[...], preferred_element_type=jnp.float32
        )

    def assign(tile):
        block = block_ref[tile]
        owner = lax.div(block, BLK_DEV)
        rank = counts[owner]
        counts[owner] = rank + 1
        slot = owner * capacity + rank
        slot_of[tile] = block * SUB + offset_ref[tile]
        starts[slot] = (block - owner * BLK_DEV) * SUB + offset_ref[tile]

    build(0, band_a, moved_a)

    @pl.loop(0, steps)
    def _(step):
        build(2 * step + 1, band_b, moved_b)
        multiply(band_a, moved_a)
        build(lax.rem(2 * step + 2, 2 * steps), band_a, moved_a)
        multiply(band_b, moved_b)
        for index in range(tiles // steps):
            assign(step * (tiles // steps) + index)

    lane = iota((1, cols), 1)
    taps_across = [
        jnp.where((lane + m - 2 >= 0) & (lane + m - 2 < cols), across[m : m + 1], 0.0)
        for m in range(TAPS_DOWN)
    ]
    chunk = 64
    for index in range(rows // chunk):
        first = index * chunk
        position = (2 * (iota((chunk, cols), 0) + first) + 1).astype(jnp.float32) / rows - 1.0
        both = total[first : first + chunk, :]
        matched = both[:, :cols] + position * both[:, cols:]
        result = taps_across[2] * matched
        for m in range(TAPS_DOWN):
            if m != 2:
                result = result + taps_across[m] * pltpu.roll(matched, (2 - m) % cols, 1)
        spread[first + SUB : first + SUB + chunk, :] = result

    sky[...] = jnp.zeros(sky.shape, jnp.float32)
    for tile in range(tiles):
        first = tile * SUB + SUB - 2
        result = down[0:1] * spread[first : first + SUB, :]
        for m in range(1, TAPS_DOWN):
            result = result + down[m : m + 1] * spread[first + m : first + m + SUB, :]
        result = result.astype(jnp.bfloat16).astype(jnp.float32) * weight
        lands = pl.ds(slot_of[tile], SUB)
        sky[lands, :] = sky[lands, :] + result

    wide = iota((SUB, cols), 1)
    tile_weight = jnp.broadcast_to(weight, (SUB, cols))

    def message(owner, carry):
        first = pl.multiple_of(owner * owned, owned)
        out_ref[owner, :owned, :] = sky[pl.ds(first, owned), :]
        found = jnp.zeros((SUB, cols), jnp.float32)
        for c in range(capacity):
            start = starts[owner * capacity + c]
            found = found + jnp.where((wide >= start) & (wide < start + SUB), tile_weight, 0.0)
            start = starts[jnp.maximum(owner - 1, 0) * capacity + c] - owned
            start = jnp.where(owner > 0, start, EMPTY)
            found = found + jnp.where((wide >= start) & (wide < start + SUB), tile_weight, 0.0)
        out_ref[owner, owned:, :] = found
        return carry

    lax.fori_loop(0, owners, message, 0, unroll=min(owners, 16))


def sky_kernel(got_ref, coadd_ref, map_ref):
    owned, cols = coadd_ref.shape
    weights = got_ref[0, owned : owned + 1, :]
    column = jnp.transpose(jnp.broadcast_to(weights, (owned, cols)))
    coadd_ref[...] = got_ref[0, :owned, :] / jnp.maximum(column, 1.0)
    map_ref[...] = weights


def on_device(
    image,
    row_taps,
    col_taps,
    mix_coeff,
    shift_frac,
    ccd_visit,
    visit_weight,
    tile_block,
    tile_offset,
):
    rows, cols = image.shape[1:]
    tiles = tile_block.shape[0]
    sky = lax.axis_size("sky")
    capacity = max(2, tiles // sky)
    taps, basis = row_taps.shape[1], row_taps.shape[0]
    fold = taps // 2 + 1
    visits = visit_weight.shape[0]
    per_group = 2
    anywhere = pl.BlockSpec(memory_space=pl.ANY)
    vmem = pl.BlockSpec(memory_space=pltpu.VMEM)
    messages = pl.pallas_call(
        functools.partial(window_kernel, capacity),
        out_shape=jax.ShapeDtypeStruct((sky, BLK_DEV * SUB + SUB, cols), jnp.float32),
        in_specs=[anywhere] * 8 + [pl.BlockSpec(memory_space=pltpu.SMEM)],
        out_specs=vmem,
        scratch_shapes=[
            pltpu.VMEM((1, rows, cols), jnp.bfloat16),
            pltpu.VMEM((taps, basis), jnp.bfloat16),
            pltpu.VMEM((taps, basis), jnp.bfloat16),
            pltpu.VMEM((3, 1, basis), jnp.float32),
            pltpu.VMEM((1, visits), jnp.bfloat16),
            pltpu.SMEM((1, 2), jnp.float32),
            pltpu.SMEM((tiles,), jnp.int32),
            pltpu.SMEM((tiles,), jnp.int32),
            pltpu.SemaphoreType.DMA((8,)),
            pltpu.VMEM((rows + 2 * fold, cols), jnp.float32),
            pltpu.VMEM((2 * fold, basis), jnp.float32),
            pltpu.VMEM((3, 2 * fold, cols), jnp.float32),
            pltpu.VMEM((per_group * 2 * cols, 2 * cols), jnp.bfloat16),
            pltpu.VMEM((per_group * 2 * cols, 2 * cols), jnp.bfloat16),
            pltpu.VMEM((per_group, rows + fold, cols), jnp.bfloat16),
            pltpu.VMEM((per_group, rows + fold, cols), jnp.bfloat16),
            pltpu.VMEM((rows, 2 * cols), jnp.float32),
            pltpu.VMEM((rows + 2 * SUB, cols), jnp.float32),
            pltpu.VMEM((sky * BLK_DEV * SUB + SUB, cols), jnp.float32),
            pltpu.SMEM((tiles,), jnp.int32),
            pltpu.SMEM((sky * capacity,), jnp.int32),
            pltpu.SMEM((sky,), jnp.int32),
        ],
        compiler_params=pltpu.CompilerParams(vmem_limit_bytes=LARGE_VMEM),
        name="match_warp_pack",
    )(
        *[
            pltpu.with_memory_space_constraint(value, pltpu.HBM)
            for value in (
                image,
                row_taps.T,
                col_taps.T,
                mix_coeff.transpose(1, 0, 2),
                visit_weight.reshape(1, -1),
                shift_frac,
                tile_block,
                tile_offset,
            )
        ],
        ccd_visit,
    )
    received = lax.psum_scatter(messages, "sky", scatter_dimension=0, tiled=True)
    coadd, weight_map = pl.pallas_call(
        sky_kernel,
        out_shape=(
            jax.ShapeDtypeStruct((BLK_DEV * SUB, cols), jnp.float32),
            jax.ShapeDtypeStruct((1, BLK_DEV * SUB), jnp.float32),
        ),
        in_specs=[vmem],
        out_specs=(vmem, vmem),
        compiler_params=pltpu.CompilerParams(vmem_limit_bytes=SMALL_VMEM),
        name="place_normalise",
    )(received)
    return coadd, weight_map.reshape(-1)


def solution(mesh):
    return jax.shard_map(
        on_device,
        mesh=mesh,
        in_specs=(
            P(("groups", "sky"), None, None),
            P(),
            P(),
            P(("groups", "sky"), None, None),
            P(("groups", "sky"), None),
            P(("groups", "sky")),
            P("groups"),
            P(("groups", "sky")),
            P(("groups", "sky")),
        ),
        out_specs=(P(("groups", "sky"), None), P(("groups", "sky"))),
        check_vma=False,
    )
```

```python
import functools

import jax
import jax.numpy as jnp
from jax import lax
from jax.experimental import pallas as pl
from jax.experimental.pallas import tpu as pltpu
from jax.sharding import PartitionSpec as P

BLK_DEV = 16
SUB = 8
LARGE_VMEM = 32 * 1024 * 1024
SMALL_VMEM = 16 * 1024 * 1024
EMPTY = -64
TAPS_DOWN = 6


def iota(shape, axis):
    return lax.broadcasted_iota(jnp.int32, shape, axis)


def weight_of(visit_ref, weight_ref):
    values = weight_ref[...].astype(jnp.float32)
    chosen = jnp.where(iota(values.shape, 1) == visit_ref[0], values, 0.0)
    return jnp.sum(chosen, axis=1, keepdims=True)


def lanczos_rows(frac_ref, cols):
    row = iota((2 * SUB, cols), 0)
    tap = jnp.where(row < SUB, row, row - SUB)
    fraction = jnp.where(row < SUB, frac_ref[0, 1], frac_ref[0, 0])
    angles = jnp.pi * ((tap - 2).astype(jnp.float32) - fraction)
    third = angles / 3.0
    kernel = jnp.sin(angles) / angles * (jnp.sin(third) / third)
    kernel = jnp.where(tap < TAPS_DOWN, kernel, 0.0)
    across, down = kernel[:SUB], kernel[SUB:]
    across = across / jnp.sum(across, axis=0, keepdims=True)
    down = down / jnp.sum(down, axis=0, keepdims=True)
    return across, down


def combined_taps(row_ref, col_ref, mix_ref, lifted, base):
    taps, basis = row_ref.shape
    count, cols = base.shape[1:]
    half = taps // 2
    l, s = iota((cols, taps), 0), iota((cols, taps), 1)
    turned = ((s + l == half) | (s + l == half + cols)).astype(jnp.float32).astype(jnp.bfloat16)
    across = jnp.dot(turned, row_ref[...], preferred_element_type=jnp.float32)
    across = across.astype(jnp.bfloat16)
    lifted[0:1] = jnp.zeros((1, basis), jnp.float32)
    lifted[1:] = col_ref[...].astype(jnp.float32)
    down = lifted[...]
    scaled = jnp.concatenate([down * mix_ref[term] for term in range(3)], axis=0)
    high = scaled.astype(jnp.bfloat16)
    low = (scaled - high.astype(jnp.float32)).astype(jnp.bfloat16)
    found = lax.dot_general(
        jnp.concatenate([high, low], axis=0),
        across,
        (((1,), (1,)), ((), ())),
        preferred_element_type=jnp.float32,
    )
    found = found[: 3 * count] + found[3 * count :]
    lane = iota((count, cols), 1)
    lane = jnp.where(lane < cols // 2, lane, lane - cols).astype(jnp.float32)
    base[0] = found[:count] + (2.0 / cols) * lane * found[count : 2 * count]
    base[1] = found[count : 2 * count]
    base[2] = found[2 * count :]


def build_band(base, row, half, band, first):
    cols = base.shape[2]
    blocks = cols // SUB
    sub = iota((SUB, cols), 0)
    lane = iota((SUB, cols), 1)
    first_u = (2.0 * sub.astype(jnp.float32) + 1.0) / cols - 1.0

    def spin(term):
        taps = jnp.broadcast_to(base[term, pl.ds(row, 1), :], (SUB, cols))
        return pltpu.roll(taps, 0, 1, stride=1, stride_axis=0)

    def keep(block, value):
        if block * SUB >= half and (block + 1) * SUB - 1 + half < cols:
            return value
        return jnp.where(jnp.abs(lane - sub - block * SUB) <= half, value, 0.0)

    slope = spin(1)
    level = spin(0) + first_u * slope
    rise = spin(2)
    for pair in range(blocks // 2):
        two = []
        for block in (2 * pair, 2 * pair + 1):
            value = level + (2.0 * SUB * block / cols) * slope
            value = keep(block, pltpu.roll(value, SUB * block, 1) if block else value)
            other = keep(block, pltpu.roll(rise, SUB * block, 1) if block else rise)
            two.append(jnp.concatenate([value, other], axis=1))
        at = first + pair * 2 * SUB
        band[at : at + 2 * SUB, :] = jnp.concatenate(two, axis=0).astype(jnp.bfloat16)


def window_kernel(
    capacity,
    image_hbm,
    row_hbm,
    col_hbm,
    mix_hbm,
    weight_hbm,
    frac_hbm,
    block_hbm,
    offset_hbm,
    visit_ref,
    out_ref,
    image_ref,
    row_ref,
    col_ref,
    mix_ref,
    weight_ref,
    frac_ref,
    block_ref,
    offset_ref,
    copied,
    padded,
    lifted,
    base,
    band_a,
    band_b,
    moved_a,
    moved_b,
    total,
    spread,
    slots,
    slot_of,
    starts,
    counts,
):
    rows, cols = image_ref.shape[1:]
    half = row_ref.shape[0] // 2
    fold = half + 1
    tiles = slot_of.shape[0]
    owners = out_ref.shape[0]
    data_rows = capacity * SUB
    owned = BLK_DEV * SUB

    pairs = (
        (row_hbm, row_ref),
        (col_hbm, col_ref),
        (mix_hbm, mix_ref),
        (image_hbm, image_ref),
        (frac_hbm, frac_ref),
        (weight_hbm, weight_ref),
        (block_hbm, block_ref),
        (offset_hbm, offset_ref),
    )
    copies = [
        pltpu.make_async_copy(source, target, copied.at[index])
        for index, (source, target) in enumerate(pairs)
    ]
    for copy in copies:
        copy.start()

    @pl.loop(0, owners)
    def _(owner):
        counts[owner] = 0

    if owners * capacity > tiles:
        slots[...] = jnp.zeros(slots.shape, jnp.float32)

        @pl.loop(0, owners * capacity)
        def _(slot):
            starts[slot] = EMPTY

    padded[:fold] = jnp.zeros((fold, cols), jnp.float32)
    padded[fold + rows :] = jnp.zeros((fold, cols), jnp.float32)
    spread[:SUB] = jnp.zeros((SUB, cols), jnp.float32)
    spread[SUB + rows :] = jnp.zeros((SUB, cols), jnp.float32)
    total[...] = jnp.zeros(total.shape, jnp.float32)
    for copy in copies:
        copy.wait()

    combined_taps(row_ref, col_ref, mix_ref, lifted, base)
    padded[fold : fold + rows] = image_ref[0].astype(jnp.float32)
    across, down = lanczos_rows(frac_ref, cols)
    weight = weight_of(visit_ref, weight_ref)

    per_group = moved_a.shape[0]
    steps = fold // (2 * per_group)

    def build(group, band, moved):
        for index in range(per_group):
            r = group * per_group + index
            for part in range(2):
                build_band(base, r + part * fold, half, band, (2 * index + part) * cols)
            moved[index] = padded[pl.ds(r, rows + fold), :].astype(jnp.bfloat16)

    def multiply(band, moved):
        parts = []
        for index in range(per_group):
            parts += [moved[index, :rows, :], moved[index, fold:, :]]
        total[...] += jnp.dot(
            jnp.concatenate(parts, axis=1), band[...], preferred_element_type=jnp.float32
        )

    def assign(tile):
        block = block_ref[tile]
        owner = lax.div(block, BLK_DEV)
        rank = counts[owner]
        counts[owner] = rank + 1
        slot = owner * capacity + rank
        slot_of[tile] = slot
        starts[slot] = (block - owner * BLK_DEV) * SUB + offset_ref[tile]

    build(0, band_a, moved_a)

    @pl.loop(0, steps)
    def _(step):
        build(2 * step + 1, band_b, moved_b)
        multiply(band_a, moved_a)
        build(lax.rem(2 * step + 2, 2 * steps), band_a, moved_a)
        multiply(band_b, moved_b)
        for index in range(tiles // steps):
            assign(step * (tiles // steps) + index)

    lane = iota((1, cols), 1)
    taps_across = [
        jnp.where((lane + m - 2 >= 0) & (lane + m - 2 < cols), across[m : m + 1], 0.0)
        for m in range(TAPS_DOWN)
    ]
    chunk = 64
    for index in range(rows // chunk):
        first = index * chunk
        position = (2 * (iota((chunk, cols), 0) + first) + 1).astype(jnp.float32) / rows - 1.0
        both = total[first : first + chunk, :]
        matched = both[:, :cols] + position * both[:, cols:]
        result = taps_across[2] * matched
        for m in range(TAPS_DOWN):
            if m != 2:
                result = result + taps_across[m] * pltpu.roll(matched, (2 - m) % cols, 1)
        spread[first + SUB : first + SUB + chunk, :] = result

    for tile in range(tiles):
        first = tile * SUB + SUB - 2
        result = down[0:1] * spread[first : first + SUB, :]
        for m in range(1, TAPS_DOWN):
            result = result + down[m : m + 1] * spread[first + m : first + m + SUB, :]
        slots[pl.ds(pl.multiple_of(slot_of[tile] * SUB, SUB), SUB), :] = result

    sub = iota((SUB, cols), 0)
    wide = iota((SUB, cols), 1)
    segment = wide >> (data_rows.bit_length() - 1)
    lane_row = wide & (SUB - 1)
    lane_slot = (wide >> 3) & (capacity - 1)
    spill_slot = wide & (capacity - 1)
    spill_row = wide >> (capacity.bit_length() - 1)
    tile_weight = jnp.broadcast_to(weight, (SUB, cols))

    def message(owner, carry):
        previous = jnp.maximum(owner - 1, 0)
        first = owner * data_rows
        out_ref[owner, :data_rows, :] = slots[
            pl.ds(pl.multiple_of(first, data_rows), data_rows), :
        ].astype(jnp.bfloat16)
        spilled = jnp.zeros((SUB, cols), jnp.float32)
        over = jnp.zeros((SUB, cols), jnp.float32)
        target = jnp.zeros((SUB, cols), jnp.int32)
        for c in range(capacity):
            target = jnp.where(lane_slot == c, starts[owner * capacity + c] + lane_row, target)
            slot = previous * capacity + c
            start = starts[slot]
            past = jnp.where(owner > 0, start + SUB - owned, 0)
            tile = slots[pl.ds(pl.multiple_of(slot * SUB, SUB), SUB), :]
            tile = pltpu.roll(tile, start & (SUB - 1), 0)
            spilled = spilled + jnp.where(sub < past, tile, 0.0)
            over = jnp.where((spill_slot == c) & (spill_row < past), tile_weight, over)
        meta = jnp.where(segment == 1, target.astype(jnp.float32), tile_weight)
        meta = jnp.where(segment == 0, over, meta)
        tail = jnp.where(sub == SUB - 1, meta, spilled * tile_weight)
        out_ref[owner, data_rows:, :] = tail.astype(jnp.bfloat16)
        return carry

    lax.fori_loop(0, owners, message, 0, unroll=min(owners, 16))


def sky_kernel(capacity, got_ref, coadd_ref, map_ref):
    sources, message_rows, cols = got_ref.shape
    data_rows = capacity * SUB
    owned = coadd_ref.shape[0]
    per_chunk = cols // data_rows
    chunks = sources // per_chunk
    place = iota((chunks, cols), 0)
    wide = iota((chunks, cols), 1)
    row = iota((owned, cols), 0)
    spilled = jnp.zeros((SUB, cols), jnp.float32)
    target = jnp.zeros((chunks, cols), jnp.float32)
    weight = jnp.zeros((chunks, cols), jnp.float32)
    for k in range(per_chunk):
        heads = jnp.zeros((chunks, cols), jnp.float32)
        for chunk in range(chunks):
            tail = got_ref[chunk * per_chunk + k, data_rows:, :].astype(jnp.float32)
            spilled = spilled + tail
            heads = jnp.where(place == chunk, tail[SUB - 1 :], heads)
        here = (wide >= k * data_rows) & (wide < (k + 1) * data_rows)
        target = jnp.where(here, pltpu.roll(heads, (k - 1) * data_rows % cols, 1), target)
        weight = jnp.where(here, pltpu.roll(heads, (k - 2) * data_rows % cols, 1), weight)
    target = target.astype(jnp.int32)
    pieces = [
        jnp.where(row == target[chunk : chunk + 1], weight[chunk : chunk + 1], 0.0)
        for chunk in range(chunks)
    ]
    placement = jnp.concatenate(pieces, axis=1).astype(jnp.bfloat16)
    pixels = got_ref[:, :data_rows, :].reshape(sources * data_rows, cols)
    pixels = jnp.concatenate([pixels, jnp.ones(pixels.shape, jnp.bfloat16)], axis=1)
    sums = jnp.dot(placement, pixels, preferred_element_type=jnp.float32)
    sub = iota((SUB, cols), 0)
    wide = iota((SUB, cols), 1)
    last = sub == SUB - 1
    over = jnp.broadcast_to(spilled[SUB - 1 :], (SUB, cols))
    mine = ((wide >> (capacity.bit_length() - 1)) == sub) & ~last
    over = jnp.sum(jnp.where(mine, over, 0.0), axis=1, keepdims=True)
    rest = jnp.zeros((owned - SUB, cols), jnp.float32)
    pixel_sum = sums[:, :cols] + jnp.concatenate([jnp.where(last, 0.0, spilled), rest], axis=0)
    weight_sum = sums[:, cols:] + jnp.concatenate(
        [jnp.broadcast_to(over, (SUB, cols)), rest], axis=0
    )
    coadd_ref[...] = pixel_sum / jnp.maximum(weight_sum, 1.0)
    diagonal = jnp.where(row == iota((owned, cols), 1), weight_sum, 0.0)
    map_ref[...] = jnp.sum(diagonal, axis=0, keepdims=True)


def on_device(
    image,
    row_taps,
    col_taps,
    mix_coeff,
    shift_frac,
    ccd_visit,
    visit_weight,
    tile_block,
    tile_offset,
):
    rows, cols = image.shape[1:]
    tiles = tile_block.shape[0]
    sky = lax.axis_size("sky")
    capacity = max(2, tiles // sky)
    taps, basis = row_taps.shape[1], row_taps.shape[0]
    fold = taps // 2 + 1
    visits = visit_weight.shape[0]
    per_group = 4
    anywhere = pl.BlockSpec(memory_space=pl.ANY)
    vmem = pl.BlockSpec(memory_space=pltpu.VMEM)
    messages = pl.pallas_call(
        functools.partial(window_kernel, capacity),
        out_shape=pltpu.VMEM((sky, capacity * SUB + SUB, cols), jnp.bfloat16),
        in_specs=[anywhere] * 8 + [pl.BlockSpec(memory_space=pltpu.SMEM)],
        out_specs=vmem,
        scratch_shapes=[
            pltpu.VMEM((1, rows, cols), jnp.bfloat16),
            pltpu.VMEM((taps, basis), jnp.bfloat16),
            pltpu.VMEM((taps, basis), jnp.bfloat16),
            pltpu.VMEM((3, 1, basis), jnp.float32),
            pltpu.VMEM((1, visits), jnp.bfloat16),
            pltpu.SMEM((1, 2), jnp.float32),
            pltpu.SMEM((tiles,), jnp.int32),
            pltpu.SMEM((tiles,), jnp.int32),
            pltpu.SemaphoreType.DMA((8,)),
            pltpu.VMEM((rows + 2 * fold, cols), jnp.float32),
            pltpu.VMEM((2 * fold, basis), jnp.float32),
            pltpu.VMEM((3, 2 * fold, cols), jnp.float32),
            pltpu.VMEM((per_group * 2 * cols, 2 * cols), jnp.bfloat16),
            pltpu.VMEM((per_group * 2 * cols, 2 * cols), jnp.bfloat16),
            pltpu.VMEM((per_group, rows + fold, cols), jnp.bfloat16),
            pltpu.VMEM((per_group, rows + fold, cols), jnp.bfloat16),
            pltpu.VMEM((rows, 2 * cols), jnp.float32),
            pltpu.VMEM((rows + 2 * SUB, cols), jnp.float32),
            pltpu.VMEM((sky * capacity * SUB, cols), jnp.float32),
            pltpu.SMEM((tiles,), jnp.int32),
            pltpu.SMEM((sky * capacity,), jnp.int32),
            pltpu.SMEM((sky,), jnp.int32),
        ],
        compiler_params=pltpu.CompilerParams(vmem_limit_bytes=LARGE_VMEM),
        name="match_warp_pack",
    )(
        *[
            pltpu.with_memory_space_constraint(value, pltpu.HBM)
            for value in (
                image,
                row_taps.T,
                col_taps.T,
                mix_coeff.transpose(1, 0, 2),
                visit_weight.reshape(1, -1),
                shift_frac,
                tile_block,
                tile_offset,
            )
        ],
        ccd_visit,
    )
    received = lax.all_to_all(messages, "sky", split_axis=0, concat_axis=0, tiled=True)
    coadd, weight_map = pl.pallas_call(
        functools.partial(sky_kernel, capacity),
        out_shape=(
            jax.ShapeDtypeStruct((BLK_DEV * SUB, cols), jnp.float32),
            jax.ShapeDtypeStruct((1, BLK_DEV * SUB), jnp.float32),
        ),
        in_specs=[vmem],
        out_specs=(vmem, vmem),
        compiler_params=pltpu.CompilerParams(vmem_limit_bytes=SMALL_VMEM),
        name="place_normalise",
    )(received)
    return coadd, weight_map.reshape(-1)


def solution(mesh):
    return jax.shard_map(
        on_device,
        mesh=mesh,
        in_specs=(
            P(("groups", "sky"), None, None),
            P(),
            P(),
            P(("groups", "sky"), None, None),
            P(("groups", "sky"), None),
            P(("groups", "sky")),
            P("groups"),
            P(("groups", "sky")),
            P(("groups", "sky")),
        ),
        out_specs=(P(("groups", "sky"), None), P(("groups", "sky"))),
        check_vma=False,
    )
```

```python
import functools

import jax
import jax.numpy as jnp
from jax import lax
from jax.experimental import pallas as pl
from jax.experimental.pallas import tpu as pltpu
from jax.sharding import PartitionSpec as P

BLK_DEV = 16
SUB = 8
LARGE_VMEM = 32 * 1024 * 1024
SMALL_VMEM = 16 * 1024 * 1024
EMPTY = -64
TAPS_DOWN = 6


def iota(shape, axis):
    return lax.broadcasted_iota(jnp.int32, shape, axis)


def weight_of(visit_ref, weight_ref):
    values = weight_ref[...].astype(jnp.float32)
    chosen = jnp.where(iota(values.shape, 1) == visit_ref[0], values, 0.0)
    return jnp.sum(chosen, axis=1, keepdims=True)


def lanczos_rows(frac_ref, cols):
    row = iota((2 * SUB, cols), 0)
    tap = jnp.where(row < SUB, row, row - SUB)
    fraction = jnp.where(row < SUB, frac_ref[0, 1], frac_ref[0, 0])
    angles = jnp.pi * ((tap - 2).astype(jnp.float32) - fraction)
    third = angles / 3.0
    kernel = jnp.sin(angles) / angles * (jnp.sin(third) / third)
    kernel = jnp.where(tap < TAPS_DOWN, kernel, 0.0)
    across, down = kernel[:SUB], kernel[SUB:]
    across = across / jnp.sum(across, axis=0, keepdims=True)
    down = down / jnp.sum(down, axis=0, keepdims=True)
    return across, down


def combined_taps(row_ref, col_ref, mix_ref, lifted, base):
    taps, basis = row_ref.shape
    count, cols = base.shape[1:]
    half = taps // 2
    l, s = iota((cols, taps), 0), iota((cols, taps), 1)
    turned = ((s + l == half) | (s + l == half + cols)).astype(jnp.float32).astype(jnp.bfloat16)
    across = jnp.dot(turned, row_ref[...], preferred_element_type=jnp.float32)
    across = across.astype(jnp.bfloat16)
    lifted[0:1] = jnp.zeros((1, basis), jnp.float32)
    lifted[1:] = col_ref[...].astype(jnp.float32)
    down = lifted[...]
    scaled = jnp.concatenate([down * mix_ref[term] for term in range(3)], axis=0)
    high = scaled.astype(jnp.bfloat16)
    low = (scaled - high.astype(jnp.float32)).astype(jnp.bfloat16)
    found = lax.dot_general(
        jnp.concatenate([high, low], axis=0),
        across,
        (((1,), (1,)), ((), ())),
        preferred_element_type=jnp.float32,
    )
    found = found[: 3 * count] + found[3 * count :]
    lane = iota((count, cols), 1)
    lane = jnp.where(lane < cols // 2, lane, lane - cols).astype(jnp.float32)
    base[0] = found[:count] + (2.0 / cols) * lane * found[count : 2 * count]
    base[1] = found[count : 2 * count]
    base[2] = found[2 * count :]


def build_band(base, row, half, band, first):
    cols = base.shape[2]
    blocks = cols // SUB
    sub = iota((SUB, cols), 0)
    lane = iota((SUB, cols), 1)
    first_u = (2.0 * sub.astype(jnp.float32) + 1.0) / cols - 1.0

    def spin(term):
        taps = jnp.broadcast_to(base[term, pl.ds(row, 1), :], (SUB, cols))
        return pltpu.roll(taps, 0, 1, stride=1, stride_axis=0)

    def keep(block, value):
        if block * SUB >= half and (block + 1) * SUB - 1 + half < cols:
            return value
        return jnp.where(jnp.abs(lane - sub - block * SUB) <= half, value, 0.0)

    slope = spin(1)
    level = spin(0) + first_u * slope
    rise = spin(2)
    for pair in range(blocks // 2):
        two = []
        for block in (2 * pair, 2 * pair + 1):
            value = level + (2.0 * SUB * block / cols) * slope
            value = keep(block, pltpu.roll(value, SUB * block, 1) if block else value)
            other = keep(block, pltpu.roll(rise, SUB * block, 1) if block else rise)
            two.append(jnp.concatenate([value, other], axis=1))
        at = first + pair * 2 * SUB
        band[at : at + 2 * SUB, :] = jnp.concatenate(two, axis=0).astype(jnp.bfloat16)


def window_kernel(
    capacity,
    image_hbm,
    row_hbm,
    col_hbm,
    mix_hbm,
    weight_hbm,
    frac_hbm,
    block_hbm,
    offset_hbm,
    visit_ref,
    out_ref,
    image_ref,
    row_ref,
    col_ref,
    mix_ref,
    weight_ref,
    frac_ref,
    block_ref,
    offset_ref,
    copied,
    padded,
    lifted,
    base,
    band_a,
    band_b,
    moved_a,
    moved_b,
    total,
    spread,
    slots,
    slot_of,
    starts,
    counts,
):
    rows, cols = image_ref.shape[1:]
    half = row_ref.shape[0] // 2
    fold = half + 1
    tiles = slot_of.shape[0]
    owners = out_ref.shape[0]
    data_rows = capacity * SUB
    owned = BLK_DEV * SUB

    pairs = (
        (row_hbm, row_ref),
        (col_hbm, col_ref),
        (mix_hbm, mix_ref),
        (image_hbm, image_ref),
        (frac_hbm, frac_ref),
        (weight_hbm, weight_ref),
        (block_hbm, block_ref),
        (offset_hbm, offset_ref),
    )
    copies = [
        pltpu.make_async_copy(source, target, copied.at[index])
        for index, (source, target) in enumerate(pairs)
    ]
    for copy in copies:
        copy.start()

    @pl.loop(0, owners)
    def _(owner):
        counts[owner] = 0

    if owners * capacity > tiles:
        slots[...] = jnp.zeros(slots.shape, jnp.float32)

        @pl.loop(0, owners * capacity)
        def _(slot):
            starts[slot] = EMPTY

    padded[:fold] = jnp.zeros((fold, cols), jnp.float32)
    padded[fold + rows :] = jnp.zeros((fold, cols), jnp.float32)
    spread[:SUB] = jnp.zeros((SUB, cols), jnp.float32)
    spread[SUB + rows :] = jnp.zeros((SUB, cols), jnp.float32)
    total[...] = jnp.zeros(total.shape, jnp.float32)
    for copy in copies:
        copy.wait()

    combined_taps(row_ref, col_ref, mix_ref, lifted, base)
    padded[fold : fold + rows] = image_ref[0].astype(jnp.float32)
    across, down = lanczos_rows(frac_ref, cols)
    weight = weight_of(visit_ref, weight_ref)

    per_group = moved_a.shape[0]
    steps = fold // (2 * per_group)

    def build(group, band, moved):
        for index in range(per_group):
            r = group * per_group + index
            for part in range(2):
                build_band(base, r + part * fold, half, band, (2 * index + part) * cols)
            moved[index] = padded[pl.ds(r, rows + fold), :].astype(jnp.bfloat16)

    def multiply(band, moved):
        parts = []
        for index in range(per_group):
            parts += [moved[index, :rows, :], moved[index, fold:, :]]
        total[...] += jnp.dot(
            jnp.concatenate(parts, axis=1), band[...], preferred_element_type=jnp.float32
        )

    def assign(tile):
        block = block_ref[tile]
        owner = lax.div(block, BLK_DEV)
        rank = counts[owner]
        counts[owner] = rank + 1
        slot = owner * capacity + rank
        slot_of[tile] = slot
        starts[slot] = (block - owner * BLK_DEV) * SUB + offset_ref[tile]

    build(0, band_a, moved_a)

    @pl.loop(0, steps)
    def _(step):
        build(2 * step + 1, band_b, moved_b)
        multiply(band_a, moved_a)
        build(lax.rem(2 * step + 2, 2 * steps), band_a, moved_a)
        multiply(band_b, moved_b)
        for index in range(tiles // steps):
            assign(step * (tiles // steps) + index)

    lane = iota((1, cols), 1)
    taps_across = [
        jnp.where((lane + m - 2 >= 0) & (lane + m - 2 < cols), across[m : m + 1], 0.0)
        for m in range(TAPS_DOWN)
    ]
    chunk = 64
    for index in range(rows // chunk):
        first = index * chunk
        position = (2 * (iota((chunk, cols), 0) + first) + 1).astype(jnp.float32) / rows - 1.0
        both = total[first : first + chunk, :]
        matched = both[:, :cols] + position * both[:, cols:]
        result = taps_across[2] * matched
        for m in range(TAPS_DOWN):
            if m != 2:
                result = result + taps_across[m] * pltpu.roll(matched, (2 - m) % cols, 1)
        spread[first + SUB : first + SUB + chunk, :] = result

    for tile in range(tiles):
        first = tile * SUB + SUB - 2
        result = down[0:1] * spread[first : first + SUB, :]
        for m in range(1, TAPS_DOWN):
            result = result + down[m : m + 1] * spread[first + m : first + m + SUB, :]
        slots[pl.ds(pl.multiple_of(slot_of[tile] * SUB, SUB), SUB), :] = result

    sub = iota((SUB, cols), 0)
    wide = iota((SUB, cols), 1)
    segment = wide >> (data_rows.bit_length() - 1)
    lane_row = wide & (SUB - 1)
    lane_slot = (wide >> 3) & (capacity - 1)
    spill_slot = wide & (capacity - 1)
    spill_row = wide >> (capacity.bit_length() - 1)
    tile_weight = jnp.broadcast_to(weight, (SUB, cols))

    def message(owner, carry):
        previous = jnp.maximum(owner - 1, 0)
        first = owner * data_rows
        out_ref[owner, :data_rows, :] = slots[
            pl.ds(pl.multiple_of(first, data_rows), data_rows), :
        ].astype(jnp.bfloat16)
        spilled = jnp.zeros((SUB, cols), jnp.float32)
        over = jnp.zeros((SUB, cols), jnp.float32)
        target = jnp.zeros((SUB, cols), jnp.int32)
        for c in range(capacity):
            target = jnp.where(lane_slot == c, starts[owner * capacity + c] + lane_row, target)
            slot = previous * capacity + c
            start = starts[slot]
            past = jnp.where(owner > 0, start + SUB - owned, 0)
            tile = slots[pl.ds(pl.multiple_of(slot * SUB, SUB), SUB), :]
            tile = pltpu.roll(tile, start & (SUB - 1), 0)
            spilled = spilled + jnp.where(sub < past, tile, 0.0)
            over = jnp.where((spill_slot == c) & (spill_row < past), tile_weight, over)
        meta = jnp.where(segment == 1, target.astype(jnp.float32), tile_weight)
        meta = jnp.where(segment == 0, over, meta)
        tail = jnp.where(sub == SUB - 1, meta, spilled * tile_weight)
        out_ref[owner, data_rows:, :] = tail.astype(jnp.bfloat16)
        return carry

    lax.fori_loop(0, owners, message, 0, unroll=min(owners, 16))


def sky_kernel(capacity, got_ref, coadd_ref, map_ref):
    sources, message_rows, cols = got_ref.shape
    data_rows = capacity * SUB
    owned = coadd_ref.shape[0]
    per_chunk = cols // data_rows
    chunks = sources // per_chunk
    place = iota((chunks, cols), 0)
    wide = iota((chunks, cols), 1)
    row = iota((owned, cols), 0)
    spilled = jnp.zeros((SUB, cols), jnp.float32)
    target = jnp.zeros((chunks, cols), jnp.float32)
    weight = jnp.zeros((chunks, cols), jnp.float32)
    for k in range(per_chunk):
        heads = jnp.zeros((chunks, cols), jnp.float32)
        for chunk in range(chunks):
            tail = got_ref[chunk * per_chunk + k, data_rows:, :].astype(jnp.float32)
            spilled = spilled + tail
            heads = jnp.where(place == chunk, tail[SUB - 1 :], heads)
        here = (wide >= k * data_rows) & (wide < (k + 1) * data_rows)
        target = jnp.where(here, pltpu.roll(heads, (k - 1) * data_rows % cols, 1), target)
        weight = jnp.where(here, pltpu.roll(heads, (k - 2) * data_rows % cols, 1), weight)
    target = target.astype(jnp.int32)
    pieces = [
        jnp.where(row == target[chunk : chunk + 1], weight[chunk : chunk + 1], 0.0)
        for chunk in range(chunks)
    ]
    placement = jnp.concatenate(pieces, axis=1).astype(jnp.bfloat16)
    pixels = got_ref[:, :data_rows, :].reshape(sources * data_rows, cols)
    pixels = jnp.concatenate([pixels, jnp.ones(pixels.shape, jnp.bfloat16)], axis=1)
    sums = jnp.dot(placement, pixels, preferred_element_type=jnp.float32)
    sub = iota((SUB, cols), 0)
    wide = iota((SUB, cols), 1)
    last = sub == SUB - 1
    over = jnp.broadcast_to(spilled[SUB - 1 :], (SUB, cols))
    mine = ((wide >> (capacity.bit_length() - 1)) == sub) & ~last
    over = jnp.sum(jnp.where(mine, over, 0.0), axis=1, keepdims=True)
    rest = jnp.zeros((owned - SUB, cols), jnp.float32)
    pixel_sum = sums[:, :cols] + jnp.concatenate([jnp.where(last, 0.0, spilled), rest], axis=0)
    weight_sum = sums[:, cols:] + jnp.concatenate(
        [jnp.broadcast_to(over, (SUB, cols)), rest], axis=0
    )
    coadd_ref[...] = pixel_sum / jnp.maximum(weight_sum, 1.0)
    diagonal = jnp.where(row == iota((owned, cols), 1), weight_sum, 0.0)
    map_ref[...] = jnp.sum(diagonal, axis=0, keepdims=True)


def on_device(
    image,
    row_taps,
    col_taps,
    mix_coeff,
    shift_frac,
    ccd_visit,
    visit_weight,
    tile_block,
    tile_offset,
):
    rows, cols = image.shape[1:]
    tiles = tile_block.shape[0]
    sky = lax.axis_size("sky")
    capacity = max(2, tiles // sky)
    taps, basis = row_taps.shape[1], row_taps.shape[0]
    fold = taps // 2 + 1
    visits = visit_weight.shape[0]
    per_group = 1
    anywhere = pl.BlockSpec(memory_space=pl.ANY)
    vmem = pl.BlockSpec(memory_space=pltpu.VMEM)
    messages = pl.pallas_call(
        functools.partial(window_kernel, capacity),
        out_shape=pltpu.VMEM((sky, capacity * SUB + SUB, cols), jnp.bfloat16),
        in_specs=[anywhere] * 8 + [pl.BlockSpec(memory_space=pltpu.SMEM)],
        out_specs=vmem,
        scratch_shapes=[
            pltpu.VMEM((1, rows, cols), jnp.bfloat16),
            pltpu.VMEM((taps, basis), jnp.bfloat16),
            pltpu.VMEM((taps, basis), jnp.bfloat16),
            pltpu.VMEM((3, 1, basis), jnp.float32),
            pltpu.VMEM((1, visits), jnp.bfloat16),
            pltpu.SMEM((1, 2), jnp.float32),
            pltpu.SMEM((tiles,), jnp.int32),
            pltpu.SMEM((tiles,), jnp.int32),
            pltpu.SemaphoreType.DMA((8,)),
            pltpu.VMEM((rows + 2 * fold, cols), jnp.float32),
            pltpu.VMEM((2 * fold, basis), jnp.float32),
            pltpu.VMEM((3, 2 * fold, cols), jnp.float32),
            pltpu.VMEM((per_group * 2 * cols, 2 * cols), jnp.bfloat16),
            pltpu.VMEM((per_group * 2 * cols, 2 * cols), jnp.bfloat16),
            pltpu.VMEM((per_group, rows + fold, cols), jnp.bfloat16),
            pltpu.VMEM((per_group, rows + fold, cols), jnp.bfloat16),
            pltpu.VMEM((rows, 2 * cols), jnp.float32),
            pltpu.VMEM((rows + 2 * SUB, cols), jnp.float32),
            pltpu.VMEM((sky * capacity * SUB, cols), jnp.float32),
            pltpu.SMEM((tiles,), jnp.int32),
            pltpu.SMEM((sky * capacity,), jnp.int32),
            pltpu.SMEM((sky,), jnp.int32),
        ],
        compiler_params=pltpu.CompilerParams(vmem_limit_bytes=LARGE_VMEM),
        name="match_warp_pack",
    )(
        *[
            pltpu.with_memory_space_constraint(value, pltpu.HBM)
            for value in (
                image,
                row_taps.T,
                col_taps.T,
                mix_coeff.transpose(1, 0, 2),
                visit_weight.reshape(1, -1),
                shift_frac,
                tile_block,
                tile_offset,
            )
        ],
        ccd_visit,
    )
    received = lax.all_to_all(messages, "sky", split_axis=0, concat_axis=0, tiled=True)
    coadd, weight_map = pl.pallas_call(
        functools.partial(sky_kernel, capacity),
        out_shape=(
            jax.ShapeDtypeStruct((BLK_DEV * SUB, cols), jnp.float32),
            jax.ShapeDtypeStruct((1, BLK_DEV * SUB), jnp.float32),
        ),
        in_specs=[vmem],
        out_specs=(vmem, vmem),
        compiler_params=pltpu.CompilerParams(vmem_limit_bytes=SMALL_VMEM),
        name="place_normalise",
    )(received)
    return coadd, weight_map.reshape(-1)


def solution(mesh):
    return jax.shard_map(
        on_device,
        mesh=mesh,
        in_specs=(
            P(("groups", "sky"), None, None),
            P(),
            P(),
            P(("groups", "sky"), None, None),
            P(("groups", "sky"), None),
            P(("groups", "sky")),
            P("groups"),
            P(("groups", "sky")),
            P(("groups", "sky")),
        ),
        out_specs=(P(("groups", "sky"), None), P(("groups", "sky"))),
        check_vma=False,
    )
```

```python
import functools

import jax
import jax.numpy as jnp
from jax import lax
from jax.experimental import pallas as pl
from jax.experimental.pallas import tpu as pltpu
from jax.sharding import PartitionSpec as P

BLK_DEV = 16
SUB = 8
LARGE_VMEM = 32 * 1024 * 1024
SMALL_VMEM = 16 * 1024 * 1024
EMPTY = -64
TAPS_DOWN = 6


def iota(shape, axis):
    return lax.broadcasted_iota(jnp.int32, shape, axis)


def weight_of(visit_ref, weight_ref):
    values = weight_ref[...].astype(jnp.float32)
    chosen = jnp.where(iota(values.shape, 1) == visit_ref[0], values, 0.0)
    return jnp.sum(chosen, axis=1, keepdims=True)


def lanczos_rows(frac_ref, cols):
    row = iota((2 * SUB, cols), 0)
    tap = jnp.where(row < SUB, row, row - SUB)
    fraction = jnp.where(row < SUB, frac_ref[0, 1], frac_ref[0, 0])
    angles = jnp.pi * ((tap - 2).astype(jnp.float32) - fraction)
    third = angles / 3.0
    kernel = jnp.sin(angles) / angles * (jnp.sin(third) / third)
    kernel = jnp.where(tap < TAPS_DOWN, kernel, 0.0)
    across, down = kernel[:SUB], kernel[SUB:]
    across = across / jnp.sum(across, axis=0, keepdims=True)
    down = down / jnp.sum(down, axis=0, keepdims=True)
    return across, down


def combined_taps(row_ref, col_ref, mix_ref, lifted, base):
    taps, basis = row_ref.shape
    count, cols = base.shape[1:]
    half = taps // 2
    l, s = iota((cols, taps), 0), iota((cols, taps), 1)
    turned = ((s + l == half) | (s + l == half + cols)).astype(jnp.float32).astype(jnp.bfloat16)
    across = jnp.dot(turned, row_ref[...], preferred_element_type=jnp.float32)
    across = across.astype(jnp.bfloat16)
    lifted[0:1] = jnp.zeros((1, basis), jnp.float32)
    lifted[1:] = col_ref[...].astype(jnp.float32)
    down = lifted[...]
    scaled = jnp.concatenate([down * mix_ref[term] for term in range(3)], axis=0)
    high = scaled.astype(jnp.bfloat16)
    low = (scaled - high.astype(jnp.float32)).astype(jnp.bfloat16)
    found = lax.dot_general(
        jnp.concatenate([high, low], axis=0),
        across,
        (((1,), (1,)), ((), ())),
        preferred_element_type=jnp.float32,
    )
    found = found[: 3 * count] + found[3 * count :]
    lane = iota((count, cols), 1)
    lane = jnp.where(lane < cols // 2, lane, lane - cols).astype(jnp.float32)
    base[0] = found[:count] + (2.0 / cols) * lane * found[count : 2 * count]
    base[1] = found[count : 2 * count]
    base[2] = found[2 * count :]


def build_band(base, row, half, band, first):
    cols = base.shape[2]
    blocks = cols // SUB
    sub = iota((SUB, cols), 0)
    lane = iota((SUB, cols), 1)
    first_u = (2.0 * sub.astype(jnp.float32) + 1.0) / cols - 1.0

    def spin(term):
        taps = jnp.broadcast_to(base[term, pl.ds(row, 1), :], (SUB, cols))
        return pltpu.roll(taps, 0, 1, stride=1, stride_axis=0)

    def keep(block, value):
        if block * SUB >= half and (block + 1) * SUB - 1 + half < cols:
            return value
        return jnp.where(jnp.abs(lane - sub - block * SUB) <= half, value, 0.0)

    slope = spin(1)
    level = spin(0) + first_u * slope
    rise = spin(2)
    for pair in range(blocks // 2):
        two = []
        for block in (2 * pair, 2 * pair + 1):
            value = level + (2.0 * SUB * block / cols) * slope
            value = keep(block, pltpu.roll(value, SUB * block, 1) if block else value)
            other = keep(block, pltpu.roll(rise, SUB * block, 1) if block else rise)
            two.append(jnp.concatenate([value, other], axis=1))
        at = first + pair * 2 * SUB
        band[at : at + 2 * SUB, :] = jnp.concatenate(two, axis=0).astype(jnp.bfloat16)


def window_kernel(
    capacity,
    image_hbm,
    row_hbm,
    col_hbm,
    mix_hbm,
    weight_hbm,
    frac_hbm,
    block_hbm,
    offset_hbm,
    visit_ref,
    out_ref,
    image_ref,
    row_ref,
    col_ref,
    mix_ref,
    weight_ref,
    frac_ref,
    block_ref,
    offset_ref,
    copied,
    padded,
    lifted,
    base,
    band_a,
    band_b,
    moved_a,
    moved_b,
    total,
    spread,
    slots,
    slot_of,
    starts,
    counts,
):
    rows, cols = image_ref.shape[1:]
    half = row_ref.shape[0] // 2
    fold = half + 1
    tiles = slot_of.shape[0]
    owners = out_ref.shape[0]
    data_rows = capacity * SUB
    owned = BLK_DEV * SUB

    pairs = (
        (row_hbm, row_ref),
        (col_hbm, col_ref),
        (mix_hbm, mix_ref),
        (image_hbm, image_ref),
        (frac_hbm, frac_ref),
        (weight_hbm, weight_ref),
        (block_hbm, block_ref),
        (offset_hbm, offset_ref),
    )
    copies = [
        pltpu.make_async_copy(source, target, copied.at[index])
        for index, (source, target) in enumerate(pairs)
    ]
    for copy in copies:
        copy.start()

    @pl.loop(0, owners)
    def _(owner):
        counts[owner] = 0

    if owners * capacity > tiles:
        slots[...] = jnp.zeros(slots.shape, jnp.float32)

        @pl.loop(0, owners * capacity)
        def _(slot):
            starts[slot] = EMPTY

    padded[:fold] = jnp.zeros((fold, cols), jnp.float32)
    padded[fold + rows :] = jnp.zeros((fold, cols), jnp.float32)
    spread[:SUB] = jnp.zeros((SUB, cols), jnp.float32)
    spread[SUB + rows :] = jnp.zeros((SUB, cols), jnp.float32)
    for copy in copies:
        copy.wait()

    combined_taps(row_ref, col_ref, mix_ref, lifted, base)
    padded[fold : fold + rows] = image_ref[0].astype(jnp.float32)
    across, down = lanczos_rows(frac_ref, cols)
    weight = weight_of(visit_ref, weight_ref)

    per_group = moved_a.shape[0]
    groups = fold // per_group

    def build(group, band, moved):
        for index in range(per_group):
            r = group * per_group + index
            for part in range(2):
                build_band(base, r + part * fold, half, band, (2 * index + part) * cols)
            moved[index] = padded[pl.ds(r, rows + fold), :].astype(jnp.bfloat16)

    def multiply(group, band, moved):
        parts = []
        for index in range(per_group):
            parts += [moved[index, :rows, :], moved[index, fold:, :]]
        product = jnp.dot(
            jnp.concatenate(parts, axis=1), band[...], preferred_element_type=jnp.float32
        )
        total[...] = product if group == 0 else total[...] + product

    def assign(tile):
        block = block_ref[tile]
        owner = lax.div(block, BLK_DEV)
        rank = counts[owner]
        counts[owner] = rank + 1
        slot = owner * capacity + rank
        slot_of[tile] = slot
        starts[slot] = (block - owner * BLK_DEV) * SUB + offset_ref[tile]

    held = ((band_a, moved_a), (band_b, moved_b))
    build(0, *held[0])
    for group in range(groups):
        if group + 1 < groups:
            build(group + 1, *held[(group + 1) % 2])
        multiply(group, *held[group % 2])
        for tile in range(group * tiles // groups, (group + 1) * tiles // groups):
            assign(tile)

    lane = iota((1, cols), 1)
    taps_across = [
        jnp.where((lane + m - 2 >= 0) & (lane + m - 2 < cols), across[m : m + 1], 0.0)
        for m in range(TAPS_DOWN)
    ]
    chunk = 64
    for index in range(rows // chunk):
        first = index * chunk
        position = (2 * (iota((chunk, cols), 0) + first) + 1).astype(jnp.float32) / rows - 1.0
        both = total[first : first + chunk, :]
        matched = both[:, :cols] + position * both[:, cols:]
        result = taps_across[2] * matched
        for m in range(TAPS_DOWN):
            if m != 2:
                result = result + taps_across[m] * pltpu.roll(matched, (2 - m) % cols, 1)
        spread[first + SUB : first + SUB + chunk, :] = result

    for tile in range(tiles):
        first = tile * SUB + SUB - 2
        result = down[0:1] * spread[first : first + SUB, :]
        for m in range(1, TAPS_DOWN):
            result = result + down[m : m + 1] * spread[first + m : first + m + SUB, :]
        slots[pl.ds(pl.multiple_of(slot_of[tile] * SUB, SUB), SUB), :] = result

    sub = iota((SUB, cols), 0)
    wide = iota((SUB, cols), 1)
    segment = wide >> (data_rows.bit_length() - 1)
    lane_row = wide & (SUB - 1)
    lane_slot = (wide >> 3) & (capacity - 1)
    spill_slot = wide & (capacity - 1)
    spill_row = wide >> (capacity.bit_length() - 1)
    tile_weight = jnp.broadcast_to(weight, (SUB, cols))

    def message(owner, carry):
        previous = jnp.maximum(owner - 1, 0)
        first = owner * data_rows
        out_ref[owner, :data_rows, :] = slots[
            pl.ds(pl.multiple_of(first, data_rows), data_rows), :
        ].astype(jnp.bfloat16)
        spilled = jnp.zeros((SUB, cols), jnp.float32)
        over = jnp.zeros((SUB, cols), jnp.float32)
        target = jnp.zeros((SUB, cols), jnp.int32)
        for c in range(capacity):
            target = jnp.where(lane_slot == c, starts[owner * capacity + c] + lane_row, target)
            slot = previous * capacity + c
            start = starts[slot]
            past = jnp.where(owner > 0, start + SUB - owned, 0)
            tile = slots[pl.ds(pl.multiple_of(slot * SUB, SUB), SUB), :]
            tile = pltpu.roll(tile, start & (SUB - 1), 0)
            spilled = spilled + jnp.where(sub < past, tile, 0.0)
            over = jnp.where((spill_slot == c) & (spill_row < past), tile_weight, over)
        meta = jnp.where(segment == 1, target.astype(jnp.float32), tile_weight)
        meta = jnp.where(segment == 0, over, meta)
        tail = jnp.where(sub == SUB - 1, meta, spilled * tile_weight)
        out_ref[owner, data_rows:, :] = tail.astype(jnp.bfloat16)
        return carry

    lax.fori_loop(0, owners, message, 0, unroll=min(owners, 16))


def sky_kernel(capacity, got_ref, coadd_ref, map_ref):
    sources, message_rows, cols = got_ref.shape
    data_rows = capacity * SUB
    owned = coadd_ref.shape[0]
    per_chunk = cols // data_rows
    chunks = sources // per_chunk
    place = iota((chunks, cols), 0)
    wide = iota((chunks, cols), 1)
    row = iota((owned, cols), 0)
    spilled = jnp.zeros((SUB, cols), jnp.float32)
    target = jnp.zeros((chunks, cols), jnp.float32)
    weight = jnp.zeros((chunks, cols), jnp.float32)
    for k in range(per_chunk):
        heads = jnp.zeros((chunks, cols), jnp.float32)
        for chunk in range(chunks):
            tail = got_ref[chunk * per_chunk + k, data_rows:, :].astype(jnp.float32)
            spilled = spilled + tail
            heads = jnp.where(place == chunk, tail[SUB - 1 :], heads)
        here = (wide >= k * data_rows) & (wide < (k + 1) * data_rows)
        target = jnp.where(here, pltpu.roll(heads, (k - 1) * data_rows % cols, 1), target)
        weight = jnp.where(here, pltpu.roll(heads, (k - 2) * data_rows % cols, 1), weight)
    target = target.astype(jnp.int32)
    pieces = [
        jnp.where(row == target[chunk : chunk + 1], weight[chunk : chunk + 1], 0.0)
        for chunk in range(chunks)
    ]
    placement = jnp.concatenate(pieces, axis=1).astype(jnp.bfloat16)
    pixels = got_ref[:, :data_rows, :].reshape(sources * data_rows, cols)
    pixels = jnp.concatenate([pixels, jnp.ones(pixels.shape, jnp.bfloat16)], axis=1)
    sums = jnp.dot(placement, pixels, preferred_element_type=jnp.float32)
    sub = iota((SUB, cols), 0)
    wide = iota((SUB, cols), 1)
    last = sub == SUB - 1
    over = jnp.broadcast_to(spilled[SUB - 1 :], (SUB, cols))
    mine = ((wide >> (capacity.bit_length() - 1)) == sub) & ~last
    over = jnp.sum(jnp.where(mine, over, 0.0), axis=1, keepdims=True)
    rest = jnp.zeros((owned - SUB, cols), jnp.float32)
    pixel_sum = sums[:, :cols] + jnp.concatenate([jnp.where(last, 0.0, spilled), rest], axis=0)
    weight_sum = sums[:, cols:] + jnp.concatenate(
        [jnp.broadcast_to(over, (SUB, cols)), rest], axis=0
    )
    coadd_ref[...] = pixel_sum / jnp.maximum(weight_sum, 1.0)
    diagonal = jnp.where(row == iota((owned, cols), 1), weight_sum, 0.0)
    map_ref[...] = jnp.sum(diagonal, axis=0, keepdims=True)


def on_device(
    image,
    row_taps,
    col_taps,
    mix_coeff,
    shift_frac,
    ccd_visit,
    visit_weight,
    tile_block,
    tile_offset,
):
    rows, cols = image.shape[1:]
    tiles = tile_block.shape[0]
    sky = lax.axis_size("sky")
    capacity = max(2, tiles // sky)
    taps, basis = row_taps.shape[1], row_taps.shape[0]
    fold = taps // 2 + 1
    visits = visit_weight.shape[0]
    per_group = 4
    anywhere = pl.BlockSpec(memory_space=pl.ANY)
    vmem = pl.BlockSpec(memory_space=pltpu.VMEM)
    messages = pl.pallas_call(
        functools.partial(window_kernel, capacity),
        out_shape=pltpu.VMEM((sky, capacity * SUB + SUB, cols), jnp.bfloat16),
        in_specs=[anywhere] * 8 + [pl.BlockSpec(memory_space=pltpu.SMEM)],
        out_specs=vmem,
        scratch_shapes=[
            pltpu.VMEM((1, rows, cols), jnp.bfloat16),
            pltpu.VMEM((taps, basis), jnp.bfloat16),
            pltpu.VMEM((taps, basis), jnp.bfloat16),
            pltpu.VMEM((3, 1, basis), jnp.float32),
            pltpu.VMEM((1, visits), jnp.bfloat16),
            pltpu.SMEM((1, 2), jnp.float32),
            pltpu.SMEM((tiles,), jnp.int32),
            pltpu.SMEM((tiles,), jnp.int32),
            pltpu.SemaphoreType.DMA((8,)),
            pltpu.VMEM((rows + 2 * fold, cols), jnp.float32),
            pltpu.VMEM((2 * fold, basis), jnp.float32),
            pltpu.VMEM((3, 2 * fold, cols), jnp.float32),
            pltpu.VMEM((per_group * 2 * cols, 2 * cols), jnp.bfloat16),
            pltpu.VMEM((per_group * 2 * cols, 2 * cols), jnp.bfloat16),
            pltpu.VMEM((per_group, rows + fold, cols), jnp.bfloat16),
            pltpu.VMEM((per_group, rows + fold, cols), jnp.bfloat16),
            pltpu.VMEM((rows, 2 * cols), jnp.float32),
            pltpu.VMEM((rows + 2 * SUB, cols), jnp.float32),
            pltpu.VMEM((sky * capacity * SUB, cols), jnp.float32),
            pltpu.SMEM((tiles,), jnp.int32),
            pltpu.SMEM((sky * capacity,), jnp.int32),
            pltpu.SMEM((sky,), jnp.int32),
        ],
        compiler_params=pltpu.CompilerParams(vmem_limit_bytes=LARGE_VMEM),
        name="match_warp_pack",
    )(
        *[
            pltpu.with_memory_space_constraint(value, pltpu.HBM)
            for value in (
                image,
                row_taps.T,
                col_taps.T,
                mix_coeff.transpose(1, 0, 2),
                visit_weight.reshape(1, -1),
                shift_frac,
                tile_block,
                tile_offset,
            )
        ],
        ccd_visit,
    )
    received = lax.all_to_all(messages, "sky", split_axis=0, concat_axis=0, tiled=True)
    coadd, weight_map = pl.pallas_call(
        functools.partial(sky_kernel, capacity),
        out_shape=(
            jax.ShapeDtypeStruct((BLK_DEV * SUB, cols), jnp.float32),
            jax.ShapeDtypeStruct((1, BLK_DEV * SUB), jnp.float32),
        ),
        in_specs=[vmem],
        out_specs=(vmem, vmem),
        compiler_params=pltpu.CompilerParams(vmem_limit_bytes=SMALL_VMEM),
        name="place_normalise",
    )(received)
    return coadd, weight_map.reshape(-1)


def solution(mesh):
    return jax.shard_map(
        on_device,
        mesh=mesh,
        in_specs=(
            P(("groups", "sky"), None, None),
            P(),
            P(),
            P(("groups", "sky"), None, None),
            P(("groups", "sky"), None),
            P(("groups", "sky")),
            P("groups"),
            P(("groups", "sky")),
            P(("groups", "sky")),
        ),
        out_specs=(P(("groups", "sky"), None), P(("groups", "sky"))),
        check_vma=False,
    )
```

```python
import functools

import jax
import jax.numpy as jnp
from jax import lax
from jax.experimental import pallas as pl
from jax.experimental.pallas import tpu as pltpu
from jax.sharding import PartitionSpec as P

BLK_DEV = 16
SUB = 8
LARGE_VMEM = 32 * 1024 * 1024
SMALL_VMEM = 16 * 1024 * 1024
EMPTY = -64
TAPS_DOWN = 6


def iota(shape, axis):
    return lax.broadcasted_iota(jnp.int32, shape, axis)


def weight_of(visit_ref, weight_ref):
    values = weight_ref[...].astype(jnp.float32)
    chosen = jnp.where(iota(values.shape, 1) == visit_ref[0], values, 0.0)
    return jnp.sum(chosen, axis=1, keepdims=True)


def lanczos_rows(frac_ref, cols):
    row = iota((2 * SUB, cols), 0)
    tap = jnp.where(row < SUB, row, row - SUB)
    fraction = jnp.where(row < SUB, frac_ref[0, 1], frac_ref[0, 0])
    angles = jnp.pi * ((tap - 2).astype(jnp.float32) - fraction)
    third = angles / 3.0
    kernel = jnp.sin(angles) / angles * (jnp.sin(third) / third)
    kernel = jnp.where(tap < TAPS_DOWN, kernel, 0.0)
    across, down = kernel[:SUB], kernel[SUB:]
    across = across / jnp.sum(across, axis=0, keepdims=True)
    down = down / jnp.sum(down, axis=0, keepdims=True)
    return across, down


def combined_taps(row_ref, col_ref, mix_ref, lifted, base):
    taps, basis = row_ref.shape
    count, cols = base.shape[1:]
    half = taps // 2
    l, s = iota((cols, taps), 0), iota((cols, taps), 1)
    turned = ((s + l == half) | (s + l == half + cols)).astype(jnp.float32).astype(jnp.bfloat16)
    across = jnp.dot(turned, row_ref[...], preferred_element_type=jnp.float32)
    across = across.astype(jnp.bfloat16)
    lifted[0:1] = jnp.zeros((1, basis), jnp.float32)
    lifted[1:] = col_ref[...].astype(jnp.float32)
    down = lifted[...]
    scaled = jnp.concatenate([down * mix_ref[term] for term in range(3)], axis=0)
    high = scaled.astype(jnp.bfloat16)
    low = (scaled - high.astype(jnp.float32)).astype(jnp.bfloat16)
    found = lax.dot_general(
        jnp.concatenate([high, low], axis=0),
        across,
        (((1,), (1,)), ((), ())),
        preferred_element_type=jnp.float32,
    )
    found = found[: 3 * count] + found[3 * count :]
    lane = iota((count, cols), 1)
    lane = jnp.where(lane < cols // 2, lane, lane - cols).astype(jnp.float32)
    base[0] = found[:count] + (2.0 / cols) * lane * found[count : 2 * count]
    base[1] = found[count : 2 * count]
    base[2] = found[2 * count :]


def build_band(base, row, band, first):
    cols = base.shape[2]
    shape = (2 * SUB, cols)
    sub = iota(shape, 0)
    lane = iota(shape, 1)
    lane = jnp.where(lane < cols // 2, lane, lane - cols)
    first_u = (2.0 * sub.astype(jnp.float32) + 1.0) / cols - 1.0

    def spin(term):
        taps = jnp.broadcast_to(base[term, pl.ds(row, 1), :], shape)
        return pltpu.roll(taps, 0, 1, stride=1, stride_axis=0)

    slope = spin(1)
    level = spin(0) + first_u * slope
    rise = spin(2)
    whole = rise.astype(jnp.bfloat16)
    pairs = cols // (2 * SUB)
    for pair in range(pairs):
        shift = 2 * SUB * pair
        value = level + (2.0 * shift / cols) * slope
        other = whole
        if pair == 0 or pair == pairs - 1:
            inside = lane >= 0 if pair == 0 else lane < 2 * SUB
            value = jnp.where(inside, value, 0.0)
            other = jnp.where(inside, rise, 0.0).astype(jnp.bfloat16)
        value = value.astype(jnp.bfloat16)
        if pair:
            value, other = pltpu.roll(value, shift, 1), pltpu.roll(other, shift, 1)
        at = first + shift
        band[at : at + 2 * SUB, :] = jnp.concatenate([value, other], axis=1)


def window_kernel(
    capacity,
    image_hbm,
    row_hbm,
    col_hbm,
    mix_hbm,
    weight_hbm,
    frac_hbm,
    block_hbm,
    offset_hbm,
    visit_ref,
    out_ref,
    image_ref,
    row_ref,
    col_ref,
    mix_ref,
    weight_ref,
    frac_ref,
    block_ref,
    offset_ref,
    copied,
    padded,
    lifted,
    base,
    band_a,
    band_b,
    blocks,
    total,
    spread,
    slots,
    slot_of,
    starts,
    counts,
):
    rows, cols = image_ref.shape[1:]
    fold = row_ref.shape[0] // 2 + 1
    deep = rows // fold
    tiles = slot_of.shape[0]
    owners = out_ref.shape[0]
    data_rows = capacity * SUB
    owned = BLK_DEV * SUB

    pairs = (
        (row_hbm, row_ref),
        (col_hbm, col_ref),
        (mix_hbm, mix_ref),
        (image_hbm, image_ref),
        (frac_hbm, frac_ref),
        (weight_hbm, weight_ref),
        (block_hbm, block_ref),
        (offset_hbm, offset_ref),
    )
    copies = [
        pltpu.make_async_copy(source, target, copied.at[index])
        for index, (source, target) in enumerate(pairs)
    ]
    for copy in copies:
        copy.start()

    @pl.loop(0, owners)
    def _(owner):
        counts[owner] = 0

    if owners * capacity > tiles:
        slots[...] = jnp.zeros(slots.shape, jnp.float32)

        @pl.loop(0, owners * capacity)
        def _(slot):
            starts[slot] = EMPTY

    padded[:fold] = jnp.zeros((fold, cols), jnp.float32)
    padded[fold + rows :] = jnp.zeros((fold, cols), jnp.float32)
    spread[:SUB] = jnp.zeros((SUB, cols), jnp.float32)
    spread[SUB + rows :] = jnp.zeros((SUB, cols), jnp.float32)
    for copy in copies:
        copy.wait()

    combined_taps(row_ref, col_ref, mix_ref, lifted, base)
    padded[fold : fold + rows] = image_ref[0].astype(jnp.float32)
    across, down = lanczos_rows(frac_ref, cols)
    weight = weight_of(visit_ref, weight_ref)

    for index in range(3 * fold - 1):
        blocks[index * deep : (index + 1) * deep, :] = padded[
            pl.ds(index, deep, stride=fold), :
        ].astype(jnp.bfloat16)

    per_group = band_a.shape[0] // (2 * cols)
    groups = fold // per_group

    def build(group, band):
        for index in range(per_group):
            for part in range(2):
                row = group * per_group + index + part * fold
                build_band(base, row, band, (2 * index + part) * cols)

    def multiply(group, band):
        parts = []
        for index in range(per_group):
            for part in range(2):
                first = (group * per_group + index + part * fold) * deep
                parts.append(blocks[first : first + rows, :])
        product = jnp.dot(
            jnp.concatenate(parts, axis=1), band[...], preferred_element_type=jnp.float32
        )
        total[...] = product if group == 0 else total[...] + product

    def assign(tile):
        block = block_ref[tile]
        owner = lax.div(block, BLK_DEV)
        rank = counts[owner]
        counts[owner] = rank + 1
        slot = owner * capacity + rank
        slot_of[tile] = slot
        starts[slot] = (block - owner * BLK_DEV) * SUB + offset_ref[tile]

    held = (band_a, band_b)
    build(0, held[0])
    for group in range(groups):
        if group + 1 < groups:
            build(group + 1, held[(group + 1) % 2])
        multiply(group, held[group % 2])
        for tile in range(group * tiles // groups, (group + 1) * tiles // groups):
            assign(tile)

    lane = iota((1, cols), 1)
    taps_across = [
        jnp.where((lane + m - 2 >= 0) & (lane + m - 2 < cols), across[m : m + 1], 0.0)
        for m in range(TAPS_DOWN)
    ]
    for phase in range(fold):
        first = phase * deep
        position = 2 * (fold * iota((deep, cols), 0) + phase) + 1
        position = position.astype(jnp.float32) / rows - 1.0
        both = total[first : first + deep, :]
        matched = both[:, :cols] + position * both[:, cols:]
        result = taps_across[2] * matched
        for m in range(TAPS_DOWN):
            if m != 2:
                result = result + taps_across[m] * pltpu.roll(matched, (2 - m) % cols, 1)
        spread[pl.ds(SUB + phase, deep, stride=fold), :] = result

    for tile in range(tiles):
        first = tile * SUB + SUB - 2
        result = down[0:1] * spread[first : first + SUB, :]
        for m in range(1, TAPS_DOWN):
            result = result + down[m : m + 1] * spread[first + m : first + m + SUB, :]
        slots[pl.ds(pl.multiple_of(slot_of[tile] * SUB, SUB), SUB), :] = result

    sub = iota((SUB, cols), 0)
    wide = iota((SUB, cols), 1)
    segment = wide >> (data_rows.bit_length() - 1)
    lane_row = wide & (SUB - 1)
    lane_slot = (wide >> 3) & (capacity - 1)
    spill_slot = wide & (capacity - 1)
    spill_row = wide >> (capacity.bit_length() - 1)
    tile_weight = jnp.broadcast_to(weight, (SUB, cols))

    def message(owner, carry):
        previous = jnp.maximum(owner - 1, 0)
        first = owner * data_rows
        out_ref[owner, :data_rows, :] = slots[
            pl.ds(pl.multiple_of(first, data_rows), data_rows), :
        ].astype(jnp.bfloat16)
        spilled = jnp.zeros((SUB, cols), jnp.float32)
        over = jnp.zeros((SUB, cols), jnp.float32)
        target = jnp.zeros((SUB, cols), jnp.int32)
        for c in range(capacity):
            target = jnp.where(lane_slot == c, starts[owner * capacity + c] + lane_row, target)
            slot = previous * capacity + c
            start = starts[slot]
            past = jnp.where(owner > 0, start + SUB - owned, 0)
            tile = slots[pl.ds(pl.multiple_of(slot * SUB, SUB), SUB), :]
            tile = pltpu.roll(tile, start & (SUB - 1), 0)
            spilled = spilled + jnp.where(sub < past, tile, 0.0)
            over = jnp.where((spill_slot == c) & (spill_row < past), tile_weight, over)
        meta = jnp.where(segment == 1, target.astype(jnp.float32), tile_weight)
        meta = jnp.where(segment == 0, over, meta)
        tail = jnp.where(sub == SUB - 1, meta, spilled * tile_weight)
        out_ref[owner, data_rows:, :] = tail.astype(jnp.bfloat16)
        return carry

    lax.fori_loop(0, owners, message, 0, unroll=min(owners, 16))


def sky_kernel(capacity, got_ref, coadd_ref, map_ref):
    sources, message_rows, cols = got_ref.shape
    data_rows = capacity * SUB
    owned = coadd_ref.shape[0]
    per_chunk = cols // data_rows
    chunks = sources // per_chunk
    place = iota((chunks, cols), 0)
    wide = iota((chunks, cols), 1)
    row = iota((owned, cols), 0)
    spilled = jnp.zeros((SUB, cols), jnp.float32)
    target = jnp.zeros((chunks, cols), jnp.float32)
    weight = jnp.zeros((chunks, cols), jnp.float32)
    for k in range(per_chunk):
        heads = jnp.zeros((chunks, cols), jnp.float32)
        for chunk in range(chunks):
            tail = got_ref[chunk * per_chunk + k, data_rows:, :].astype(jnp.float32)
            spilled = spilled + tail
            heads = jnp.where(place == chunk, tail[SUB - 1 :], heads)
        here = (wide >= k * data_rows) & (wide < (k + 1) * data_rows)
        target = jnp.where(here, pltpu.roll(heads, (k - 1) * data_rows % cols, 1), target)
        weight = jnp.where(here, pltpu.roll(heads, (k - 2) * data_rows % cols, 1), weight)
    target = target.astype(jnp.int32)
    pieces = [
        jnp.where(row == target[chunk : chunk + 1], weight[chunk : chunk + 1], 0.0)
        for chunk in range(chunks)
    ]
    placement = jnp.concatenate(pieces, axis=1).astype(jnp.bfloat16)
    pixels = got_ref[:, :data_rows, :].reshape(sources * data_rows, cols)
    pixels = jnp.concatenate([pixels, jnp.ones(pixels.shape, jnp.bfloat16)], axis=1)
    sums = jnp.dot(placement, pixels, preferred_element_type=jnp.float32)
    sub = iota((SUB, cols), 0)
    wide = iota((SUB, cols), 1)
    last = sub == SUB - 1
    over = jnp.broadcast_to(spilled[SUB - 1 :], (SUB, cols))
    mine = ((wide >> (capacity.bit_length() - 1)) == sub) & ~last
    over = jnp.sum(jnp.where(mine, over, 0.0), axis=1, keepdims=True)
    rest = jnp.zeros((owned - SUB, cols), jnp.float32)
    pixel_sum = sums[:, :cols] + jnp.concatenate([jnp.where(last, 0.0, spilled), rest], axis=0)
    weight_sum = sums[:, cols:] + jnp.concatenate(
        [jnp.broadcast_to(over, (SUB, cols)), rest], axis=0
    )
    coadd_ref[...] = pixel_sum / jnp.maximum(weight_sum, 1.0)
    diagonal = jnp.where(row == iota((owned, cols), 1), weight_sum, 0.0)
    map_ref[...] = jnp.sum(diagonal, axis=0, keepdims=True)


def on_device(
    image,
    row_taps,
    col_taps,
    mix_coeff,
    shift_frac,
    ccd_visit,
    visit_weight,
    tile_block,
    tile_offset,
):
    rows, cols = image.shape[1:]
    tiles = tile_block.shape[0]
    sky = lax.axis_size("sky")
    capacity = max(2, tiles // sky)
    taps, basis = row_taps.shape[1], row_taps.shape[0]
    fold = taps // 2 + 1
    visits = visit_weight.shape[0]
    per_group = 4
    anywhere = pl.BlockSpec(memory_space=pl.ANY)
    vmem = pl.BlockSpec(memory_space=pltpu.VMEM)
    messages = pl.pallas_call(
        functools.partial(window_kernel, capacity),
        out_shape=pltpu.VMEM((sky, capacity * SUB + SUB, cols), jnp.bfloat16),
        in_specs=[anywhere] * 8 + [pl.BlockSpec(memory_space=pltpu.SMEM)],
        out_specs=vmem,
        scratch_shapes=[
            pltpu.VMEM((1, rows, cols), jnp.bfloat16),
            pltpu.VMEM((taps, basis), jnp.bfloat16),
            pltpu.VMEM((taps, basis), jnp.bfloat16),
            pltpu.VMEM((3, 1, basis), jnp.float32),
            pltpu.VMEM((1, visits), jnp.bfloat16),
            pltpu.SMEM((1, 2), jnp.float32),
            pltpu.SMEM((tiles,), jnp.int32),
            pltpu.SMEM((tiles,), jnp.int32),
            pltpu.SemaphoreType.DMA((8,)),
            pltpu.VMEM((rows + 2 * fold, cols), jnp.float32),
            pltpu.VMEM((2 * fold, basis), jnp.float32),
            pltpu.VMEM((3, 2 * fold, cols), jnp.float32),
            pltpu.VMEM((per_group * 2 * cols, 2 * cols), jnp.bfloat16),
            pltpu.VMEM((per_group * 2 * cols, 2 * cols), jnp.bfloat16),
            pltpu.VMEM(((3 * fold - 1) * (rows // fold), cols), jnp.bfloat16),
            pltpu.VMEM((rows, 2 * cols), jnp.float32),
            pltpu.VMEM((rows + 2 * SUB, cols), jnp.float32),
            pltpu.VMEM((sky * capacity * SUB, cols), jnp.float32),
            pltpu.SMEM((tiles,), jnp.int32),
            pltpu.SMEM((sky * capacity,), jnp.int32),
            pltpu.SMEM((sky,), jnp.int32),
        ],
        compiler_params=pltpu.CompilerParams(vmem_limit_bytes=LARGE_VMEM),
        name="match_warp_pack",
    )(
        *[
            pltpu.with_memory_space_constraint(value, pltpu.HBM)
            for value in (
                image,
                row_taps.T,
                col_taps.T,
                mix_coeff.transpose(1, 0, 2),
                visit_weight.reshape(1, -1),
                shift_frac,
                tile_block,
                tile_offset,
            )
        ],
        ccd_visit,
    )
    received = lax.all_to_all(messages, "sky", split_axis=0, concat_axis=0, tiled=True)
    coadd, weight_map = pl.pallas_call(
        functools.partial(sky_kernel, capacity),
        out_shape=(
            jax.ShapeDtypeStruct((BLK_DEV * SUB, cols), jnp.float32),
            jax.ShapeDtypeStruct((1, BLK_DEV * SUB), jnp.float32),
        ),
        in_specs=[vmem],
        out_specs=(vmem, vmem),
        compiler_params=pltpu.CompilerParams(vmem_limit_bytes=SMALL_VMEM),
        name="place_normalise",
    )(received)
    return coadd, weight_map.reshape(-1)


def solution(mesh):
    return jax.shard_map(
        on_device,
        mesh=mesh,
        in_specs=(
            P(("groups", "sky"), None, None),
            P(),
            P(),
            P(("groups", "sky"), None, None),
            P(("groups", "sky"), None),
            P(("groups", "sky")),
            P("groups"),
            P(("groups", "sky")),
            P(("groups", "sky")),
        ),
        out_specs=(P(("groups", "sky"), None), P(("groups", "sky"))),
        check_vma=False,
    )
```

```python
import functools
import itertools

import jax
import jax.numpy as jnp
from jax import lax
from jax.experimental import pallas as pl
from jax.experimental.pallas import tpu as pltpu
from jax.sharding import PartitionSpec as P

BLK_DEV = 16
SUB = 8
LARGE_VMEM = 32 * 1024 * 1024
SMALL_VMEM = 16 * 1024 * 1024
EMPTY = -64
TAPS_DOWN = 6


def iota(shape, axis):
    return lax.broadcasted_iota(jnp.int32, shape, axis)


def weight_of(visit_ref, weight_ref):
    values = weight_ref[...].astype(jnp.float32)
    chosen = jnp.where(iota(values.shape, 1) == visit_ref[0], values, 0.0)
    return jnp.sum(chosen, axis=1, keepdims=True)


def lanczos_rows(frac_ref, cols):
    row = iota((2 * SUB, cols), 0)
    tap = jnp.where(row < SUB, row, row - SUB)
    fraction = jnp.where(row < SUB, frac_ref[0, 1], frac_ref[0, 0])
    angles = jnp.pi * ((tap - 2).astype(jnp.float32) - fraction)
    third = angles / 3.0
    kernel = jnp.sin(angles) / angles * (jnp.sin(third) / third)
    kernel = jnp.where(tap < TAPS_DOWN, kernel, 0.0)
    across, down = kernel[:SUB], kernel[SUB:]
    across = across / jnp.sum(across, axis=0, keepdims=True)
    down = down / jnp.sum(down, axis=0, keepdims=True)
    return across, down


def combined_taps(row_ref, col_ref, mix_ref, lifted, base):
    taps, basis = row_ref.shape
    count, cols = base.shape[1:]
    half = taps // 2
    l, s = iota((cols, taps), 0), iota((cols, taps), 1)
    turned = ((s + l == half) | (s + l == half + cols)).astype(jnp.float32).astype(jnp.bfloat16)
    across = jnp.dot(turned, row_ref[...], preferred_element_type=jnp.float32)
    across = across.astype(jnp.bfloat16)
    lifted[0:1] = jnp.zeros((1, basis), jnp.float32)
    lifted[1:] = col_ref[...].astype(jnp.float32)
    down = lifted[...]
    scaled = jnp.concatenate([down * mix_ref[term] for term in range(3)], axis=0)
    high = scaled.astype(jnp.bfloat16)
    low = (scaled - high.astype(jnp.float32)).astype(jnp.bfloat16)
    found = lax.dot_general(
        jnp.concatenate([high, low], axis=0),
        across,
        (((1,), (1,)), ((), ())),
        preferred_element_type=jnp.float32,
    )
    found = found[: 3 * count] + found[3 * count :]
    lane = iota((count, cols), 1)
    lane = jnp.where(lane < cols // 2, lane, lane - cols).astype(jnp.float32)
    base[0] = found[:count] + (2.0 / cols) * lane * found[count : 2 * count]
    base[1] = found[count : 2 * count]
    base[2] = found[2 * count :]


def build_band(base, row, band, first):
    cols = base.shape[2]
    shape = (2 * SUB, cols)
    sub = iota(shape, 0)
    lane = iota(shape, 1)
    lane = jnp.where(lane < cols // 2, lane, lane - cols)
    first_u = (2.0 * sub.astype(jnp.float32) + 1.0) / cols - 1.0

    def spin(term):
        taps = jnp.broadcast_to(base[term, pl.ds(row, 1), :], shape)
        return pltpu.roll(taps, 0, 1, stride=1, stride_axis=0)

    slope = spin(1)
    level = spin(0) + first_u * slope
    rise = spin(2)
    whole = rise.astype(jnp.bfloat16)
    pairs = cols // (2 * SUB)
    for pair in range(pairs):
        shift = 2 * SUB * pair
        value = level + (2.0 * shift / cols) * slope
        other = whole
        if pair == 0 or pair == pairs - 1:
            inside = lane >= 0 if pair == 0 else lane < 2 * SUB
            value = jnp.where(inside, value, 0.0)
            other = jnp.where(inside, rise, 0.0).astype(jnp.bfloat16)
        value = value.astype(jnp.bfloat16)
        if pair:
            value, other = pltpu.roll(value, shift, 1), pltpu.roll(other, shift, 1)
        at = first + shift
        band[at : at + 2 * SUB, :] = jnp.concatenate([value, other], axis=1)


def group_edges(fold):
    return [0, fold // 8, fold // 2, fold]


def window_kernel(
    capacity,
    image_hbm,
    row_hbm,
    col_hbm,
    mix_hbm,
    weight_hbm,
    frac_hbm,
    block_hbm,
    offset_hbm,
    visit_ref,
    out_ref,
    image_ref,
    row_ref,
    col_ref,
    mix_ref,
    weight_ref,
    frac_ref,
    block_ref,
    offset_ref,
    copied,
    padded,
    lifted,
    base,
    band_a,
    band_b,
    blocks,
    total,
    spread,
    slots,
    slot_of,
    starts,
    counts,
):
    rows, cols = image_ref.shape[1:]
    fold = row_ref.shape[0] // 2 + 1
    deep = rows // fold
    tiles = slot_of.shape[0]
    owners = out_ref.shape[0]
    data_rows = capacity * SUB
    owned = BLK_DEV * SUB

    pairs = (
        (row_hbm, row_ref),
        (col_hbm, col_ref),
        (mix_hbm, mix_ref),
        (image_hbm, image_ref),
        (frac_hbm, frac_ref),
        (weight_hbm, weight_ref),
        (block_hbm, block_ref),
        (offset_hbm, offset_ref),
    )
    copies = [
        pltpu.make_async_copy(source, target, copied.at[index])
        for index, (source, target) in enumerate(pairs)
    ]
    for copy in copies:
        copy.start()

    @pl.loop(0, owners)
    def _(owner):
        counts[owner] = 0

    if owners * capacity > tiles:
        slots[...] = jnp.zeros(slots.shape, jnp.float32)

        @pl.loop(0, owners * capacity)
        def _(slot):
            starts[slot] = EMPTY

    padded[:fold] = jnp.zeros((fold, cols), jnp.float32)
    padded[fold + rows :] = jnp.zeros((fold, cols), jnp.float32)
    spread[:SUB] = jnp.zeros((SUB, cols), jnp.float32)
    spread[SUB + rows :] = jnp.zeros((SUB, cols), jnp.float32)
    for copy in copies:
        copy.wait()

    combined_taps(row_ref, col_ref, mix_ref, lifted, base)
    padded[fold : fold + rows] = image_ref[0].astype(jnp.float32)
    across, down = lanczos_rows(frac_ref, cols)
    weight = weight_of(visit_ref, weight_ref)

    for index in range(3 * fold - 1):
        blocks[index * deep : (index + 1) * deep, :] = padded[
            pl.ds(index, deep, stride=fold), :
        ].astype(jnp.bfloat16)

    edges = group_edges(fold)
    groups = len(edges) - 1

    def build(group, band):
        for index, r in enumerate(range(edges[group], edges[group + 1])):
            for part in range(2):
                build_band(base, r + part * fold, band, (2 * index + part) * cols)

    def multiply(group, band):
        parts = []
        for r in range(edges[group], edges[group + 1]):
            for part in range(2):
                first = (r + part * fold) * deep
                parts.append(blocks[first : first + rows, :])
        product = jnp.dot(
            jnp.concatenate(parts, axis=1),
            band[: len(parts) * cols, :],
            preferred_element_type=jnp.float32,
        )
        total[...] = product if group == 0 else total[...] + product

    def assign(tile):
        block = block_ref[tile]
        owner = lax.div(block, BLK_DEV)
        rank = counts[owner]
        counts[owner] = rank + 1
        slot = owner * capacity + rank
        slot_of[tile] = slot
        starts[slot] = (block - owner * BLK_DEV) * SUB + offset_ref[tile]

    held = (band_a, band_b)
    build(0, held[0])
    for group in range(groups):
        if group + 1 < groups:
            build(group + 1, held[(group + 1) % 2])
        multiply(group, held[group % 2])
        for tile in range(group * tiles // groups, (group + 1) * tiles // groups):
            assign(tile)

    lane = iota((1, cols), 1)
    taps_across = [
        jnp.where((lane + m - 2 >= 0) & (lane + m - 2 < cols), across[m : m + 1], 0.0)
        for m in range(TAPS_DOWN)
    ]
    for phase in range(fold):
        first = phase * deep
        position = 2 * (fold * iota((deep, cols), 0) + phase) + 1
        position = position.astype(jnp.float32) / rows - 1.0
        both = total[first : first + deep, :]
        matched = both[:, :cols] + position * both[:, cols:]
        result = taps_across[2] * matched
        for m in range(TAPS_DOWN):
            if m != 2:
                result = result + taps_across[m] * pltpu.roll(matched, (2 - m) % cols, 1)
        spread[pl.ds(SUB + phase, deep, stride=fold), :] = result

    for tile in range(tiles):
        first = tile * SUB + SUB - 2
        result = down[0:1] * spread[first : first + SUB, :]
        for m in range(1, TAPS_DOWN):
            result = result + down[m : m + 1] * spread[first + m : first + m + SUB, :]
        slots[pl.ds(pl.multiple_of(slot_of[tile] * SUB, SUB), SUB), :] = result

    sub = iota((SUB, cols), 0)
    wide = iota((SUB, cols), 1)
    segment = wide >> (data_rows.bit_length() - 1)
    lane_row = wide & (SUB - 1)
    lane_slot = (wide >> 3) & (capacity - 1)
    spill_slot = wide & (capacity - 1)
    spill_row = wide >> (capacity.bit_length() - 1)
    tile_weight = jnp.broadcast_to(weight, (SUB, cols))

    def message(owner, carry):
        previous = jnp.maximum(owner - 1, 0)
        first = owner * data_rows
        out_ref[owner, :data_rows, :] = slots[
            pl.ds(pl.multiple_of(first, data_rows), data_rows), :
        ].astype(jnp.bfloat16)
        spilled = jnp.zeros((SUB, cols), jnp.float32)
        over = jnp.zeros((SUB, cols), jnp.float32)
        target = jnp.zeros((SUB, cols), jnp.int32)
        for c in range(capacity):
            target = jnp.where(lane_slot == c, starts[owner * capacity + c] + lane_row, target)
            slot = previous * capacity + c
            start = starts[slot]
            past = jnp.where(owner > 0, start + SUB - owned, 0)
            tile = slots[pl.ds(pl.multiple_of(slot * SUB, SUB), SUB), :]
            tile = pltpu.roll(tile, start & (SUB - 1), 0)
            spilled = spilled + jnp.where(sub < past, tile, 0.0)
            over = jnp.where((spill_slot == c) & (spill_row < past), tile_weight, over)
        meta = jnp.where(segment == 1, target.astype(jnp.float32), tile_weight)
        meta = jnp.where(segment == 0, over, meta)
        tail = jnp.where(sub == SUB - 1, meta, spilled * tile_weight)
        out_ref[owner, data_rows:, :] = tail.astype(jnp.bfloat16)
        return carry

    lax.fori_loop(0, owners, message, 0, unroll=min(owners, 16))


def sky_kernel(capacity, got_ref, coadd_ref, map_ref):
    sources, message_rows, cols = got_ref.shape
    data_rows = capacity * SUB
    owned = coadd_ref.shape[0]
    per_chunk = cols // data_rows
    chunks = sources // per_chunk
    place = iota((chunks, cols), 0)
    wide = iota((chunks, cols), 1)
    row = iota((owned, cols), 0)
    spilled = jnp.zeros((SUB, cols), jnp.float32)
    target = jnp.zeros((chunks, cols), jnp.float32)
    weight = jnp.zeros((chunks, cols), jnp.float32)
    for k in range(per_chunk):
        heads = jnp.zeros((chunks, cols), jnp.float32)
        for chunk in range(chunks):
            tail = got_ref[chunk * per_chunk + k, data_rows:, :].astype(jnp.float32)
            spilled = spilled + tail
            heads = jnp.where(place == chunk, tail[SUB - 1 :], heads)
        here = (wide >= k * data_rows) & (wide < (k + 1) * data_rows)
        target = jnp.where(here, pltpu.roll(heads, (k - 1) * data_rows % cols, 1), target)
        weight = jnp.where(here, pltpu.roll(heads, (k - 2) * data_rows % cols, 1), weight)
    target = target.astype(jnp.int32)
    pieces = [
        jnp.where(row == target[chunk : chunk + 1], weight[chunk : chunk + 1], 0.0)
        for chunk in range(chunks)
    ]
    placement = jnp.concatenate(pieces, axis=1).astype(jnp.bfloat16)
    pixels = got_ref[:, :data_rows, :].reshape(sources * data_rows, cols)
    pixels = jnp.concatenate([pixels, jnp.ones(pixels.shape, jnp.bfloat16)], axis=1)
    sums = jnp.dot(placement, pixels, preferred_element_type=jnp.float32)
    sub = iota((SUB, cols), 0)
    wide = iota((SUB, cols), 1)
    last = sub == SUB - 1
    over = jnp.broadcast_to(spilled[SUB - 1 :], (SUB, cols))
    mine = ((wide >> (capacity.bit_length() - 1)) == sub) & ~last
    over = jnp.sum(jnp.where(mine, over, 0.0), axis=1, keepdims=True)
    rest = jnp.zeros((owned - SUB, cols), jnp.float32)
    pixel_sum = sums[:, :cols] + jnp.concatenate([jnp.where(last, 0.0, spilled), rest], axis=0)
    weight_sum = sums[:, cols:] + jnp.concatenate(
        [jnp.broadcast_to(over, (SUB, cols)), rest], axis=0
    )
    coadd_ref[...] = pixel_sum / jnp.maximum(weight_sum, 1.0)
    diagonal = jnp.where(row == iota((owned, cols), 1), weight_sum, 0.0)
    map_ref[...] = jnp.sum(diagonal, axis=0, keepdims=True)


def on_device(
    image,
    row_taps,
    col_taps,
    mix_coeff,
    shift_frac,
    ccd_visit,
    visit_weight,
    tile_block,
    tile_offset,
):
    rows, cols = image.shape[1:]
    tiles = tile_block.shape[0]
    sky = lax.axis_size("sky")
    capacity = max(2, tiles // sky)
    taps, basis = row_taps.shape[1], row_taps.shape[0]
    fold = taps // 2 + 1
    visits = visit_weight.shape[0]
    largest = max(b - a for a, b in itertools.pairwise(group_edges(fold)))
    anywhere = pl.BlockSpec(memory_space=pl.ANY)
    vmem = pl.BlockSpec(memory_space=pltpu.VMEM)
    messages = pl.pallas_call(
        functools.partial(window_kernel, capacity),
        out_shape=pltpu.VMEM((sky, capacity * SUB + SUB, cols), jnp.bfloat16),
        in_specs=[anywhere] * 8 + [pl.BlockSpec(memory_space=pltpu.SMEM)],
        out_specs=vmem,
        scratch_shapes=[
            pltpu.VMEM((1, rows, cols), jnp.bfloat16),
            pltpu.VMEM((taps, basis), jnp.bfloat16),
            pltpu.VMEM((taps, basis), jnp.bfloat16),
            pltpu.VMEM((3, 1, basis), jnp.float32),
            pltpu.VMEM((1, visits), jnp.bfloat16),
            pltpu.SMEM((1, 2), jnp.float32),
            pltpu.SMEM((tiles,), jnp.int32),
            pltpu.SMEM((tiles,), jnp.int32),
            pltpu.SemaphoreType.DMA((8,)),
            pltpu.VMEM((rows + 2 * fold, cols), jnp.float32),
            pltpu.VMEM((2 * fold, basis), jnp.float32),
            pltpu.VMEM((3, 2 * fold, cols), jnp.float32),
            pltpu.VMEM((largest * 2 * cols, 2 * cols), jnp.bfloat16),
            pltpu.VMEM((largest * 2 * cols, 2 * cols), jnp.bfloat16),
            pltpu.VMEM(((3 * fold - 1) * (rows // fold), cols), jnp.bfloat16),
            pltpu.VMEM((rows, 2 * cols), jnp.float32),
            pltpu.VMEM((rows + 2 * SUB, cols), jnp.float32),
            pltpu.VMEM((sky * capacity * SUB, cols), jnp.float32),
            pltpu.SMEM((tiles,), jnp.int32),
            pltpu.SMEM((sky * capacity,), jnp.int32),
            pltpu.SMEM((sky,), jnp.int32),
        ],
        compiler_params=pltpu.CompilerParams(vmem_limit_bytes=LARGE_VMEM),
        name="match_warp_pack",
    )(
        *[
            pltpu.with_memory_space_constraint(value, pltpu.HBM)
            for value in (
                image,
                row_taps.T,
                col_taps.T,
                mix_coeff.transpose(1, 0, 2),
                visit_weight.reshape(1, -1),
                shift_frac,
                tile_block,
                tile_offset,
            )
        ],
        ccd_visit,
    )
    received = lax.all_to_all(messages, "sky", split_axis=0, concat_axis=0, tiled=True)
    coadd, weight_map = pl.pallas_call(
        functools.partial(sky_kernel, capacity),
        out_shape=(
            jax.ShapeDtypeStruct((BLK_DEV * SUB, cols), jnp.float32),
            jax.ShapeDtypeStruct((1, BLK_DEV * SUB), jnp.float32),
        ),
        in_specs=[vmem],
        out_specs=(vmem, vmem),
        compiler_params=pltpu.CompilerParams(vmem_limit_bytes=SMALL_VMEM),
        name="place_normalise",
    )(received)
    return coadd, weight_map.reshape(-1)


def solution(mesh):
    return jax.shard_map(
        on_device,
        mesh=mesh,
        in_specs=(
            P(("groups", "sky"), None, None),
            P(),
            P(),
            P(("groups", "sky"), None, None),
            P(("groups", "sky"), None),
            P(("groups", "sky")),
            P("groups"),
            P(("groups", "sky")),
            P(("groups", "sky")),
        ),
        out_specs=(P(("groups", "sky"), None), P(("groups", "sky"))),
        check_vma=False,
    )
```

```python
import functools
import itertools

import jax
import jax.numpy as jnp
from jax import lax
from jax.experimental import pallas as pl
from jax.experimental.pallas import tpu as pltpu
from jax.sharding import PartitionSpec as P

BLK_DEV = 16
SUB = 8
LARGE_VMEM = 32 * 1024 * 1024
SMALL_VMEM = 16 * 1024 * 1024
EMPTY = -64
TAPS_DOWN = 6


def iota(shape, axis):
    return lax.broadcasted_iota(jnp.int32, shape, axis)


def weight_of(visit_ref, weight_ref):
    values = weight_ref[...].astype(jnp.float32)
    chosen = jnp.where(iota(values.shape, 1) == visit_ref[0], values, 0.0)
    return jnp.sum(chosen, axis=1, keepdims=True)


def lanczos_rows(frac_ref, cols):
    row = iota((2 * SUB, cols), 0)
    tap = jnp.where(row < SUB, row, row - SUB)
    fraction = jnp.where(row < SUB, frac_ref[0, 1], frac_ref[0, 0])
    angles = jnp.pi * ((tap - 2).astype(jnp.float32) - fraction)
    third = angles / 3.0
    kernel = jnp.sin(angles) / angles * (jnp.sin(third) / third)
    kernel = jnp.where(tap < TAPS_DOWN, kernel, 0.0)
    across, down = kernel[:SUB], kernel[SUB:]
    across = across / jnp.sum(across, axis=0, keepdims=True)
    down = down / jnp.sum(down, axis=0, keepdims=True)
    return across, down


def combined_taps(row_ref, col_ref, mix_ref, lifted, base):
    taps, basis = row_ref.shape
    count, cols = base.shape[1:]
    half = taps // 2
    l, s = iota((cols, taps), 0), iota((cols, taps), 1)
    turned = ((s + l == half) | (s + l == half + cols)).astype(jnp.float32).astype(jnp.bfloat16)
    across = jnp.dot(turned, row_ref[...], preferred_element_type=jnp.float32)
    across = across.astype(jnp.bfloat16)
    lifted[0:1] = jnp.zeros((1, basis), jnp.float32)
    lifted[1:] = col_ref[...].astype(jnp.float32)
    down = lifted[...]
    scaled = jnp.concatenate([down * mix_ref[term] for term in range(3)], axis=0)
    high = scaled.astype(jnp.bfloat16)
    low = (scaled - high.astype(jnp.float32)).astype(jnp.bfloat16)
    found = lax.dot_general(
        jnp.concatenate([high, low], axis=0),
        across,
        (((1,), (1,)), ((), ())),
        preferred_element_type=jnp.float32,
    )
    found = found[: 3 * count] + found[3 * count :]
    lane = iota((count, cols), 1)
    lane = jnp.where(lane < cols // 2, lane, lane - cols).astype(jnp.float32)
    base[0] = found[:count] + (2.0 / cols) * lane * found[count : 2 * count]
    base[1] = found[count : 2 * count]
    base[2] = found[2 * count :]


def build_band(base, row, band, first):
    cols = base.shape[2]
    shape = (2 * SUB, cols)
    sub = iota(shape, 0)
    lane = iota(shape, 1)
    lane = jnp.where(lane < cols // 2, lane, lane - cols)
    first_u = (2.0 * sub.astype(jnp.float32) + 1.0) / cols - 1.0

    def spin(term):
        taps = jnp.broadcast_to(base[term, pl.ds(row, 1), :], shape)
        return pltpu.roll(taps, 0, 1, stride=1, stride_axis=0)

    slope = spin(1)
    level = spin(0) + first_u * slope
    rise = spin(2)
    whole = rise.astype(jnp.bfloat16)
    pairs = cols // (2 * SUB)
    for pair in range(pairs):
        shift = 2 * SUB * pair
        value = level + (2.0 * shift / cols) * slope
        other = whole
        if pair == 0 or pair == pairs - 1:
            inside = lane >= 0 if pair == 0 else lane < 2 * SUB
            value = jnp.where(inside, value, 0.0)
            other = jnp.where(inside, rise, 0.0).astype(jnp.bfloat16)
        value = value.astype(jnp.bfloat16)
        if pair:
            value, other = pltpu.roll(value, shift, 1), pltpu.roll(other, shift, 1)
        at = first + shift
        band[at : at + 2 * SUB, :] = jnp.concatenate([value, other], axis=1)


def group_edges(fold):
    return [0, fold // 8, fold // 2, fold]


def window_kernel(
    capacity,
    image_hbm,
    row_hbm,
    col_hbm,
    mix_hbm,
    weight_hbm,
    frac_hbm,
    block_hbm,
    offset_hbm,
    visit_ref,
    out_ref,
    image_ref,
    row_ref,
    col_ref,
    mix_ref,
    weight_ref,
    frac_ref,
    block_ref,
    offset_ref,
    copied,
    padded,
    lifted,
    base,
    band_a,
    band_b,
    blocks,
    total,
    spread,
    slots,
    slot_of,
    starts,
    counts,
):
    rows, cols = image_ref.shape[1:]
    fold = row_ref.shape[0] // 2 + 1
    deep = rows // fold
    tiles = slot_of.shape[0]
    owners = out_ref.shape[0]
    data_rows = capacity * SUB
    owned = BLK_DEV * SUB

    pairs = (
        (row_hbm, row_ref),
        (col_hbm, col_ref),
        (mix_hbm, mix_ref),
        (image_hbm, image_ref),
        (frac_hbm, frac_ref),
        (weight_hbm, weight_ref),
        (block_hbm, block_ref),
        (offset_hbm, offset_ref),
    )
    copies = [
        pltpu.make_async_copy(source, target, copied.at[index])
        for index, (source, target) in enumerate(pairs)
    ]
    for copy in copies:
        copy.start()

    @pl.loop(0, owners)
    def _(owner):
        counts[owner] = 0

    if owners * capacity > tiles:
        slots[...] = jnp.zeros(slots.shape, jnp.float32)

        @pl.loop(0, owners * capacity)
        def _(slot):
            starts[slot] = EMPTY

    padded[:fold] = jnp.zeros((fold, cols), jnp.float32)
    padded[fold + rows :] = jnp.zeros((fold, cols), jnp.float32)
    spread[:SUB] = jnp.zeros((SUB, cols), jnp.float32)
    spread[SUB + rows :] = jnp.zeros((SUB, cols), jnp.float32)
    for copy in copies:
        copy.wait()

    combined_taps(row_ref, col_ref, mix_ref, lifted, base)
    padded[fold : fold + rows] = image_ref[0].astype(jnp.float32)
    across, down = lanczos_rows(frac_ref, cols)
    weight = weight_of(visit_ref, weight_ref)

    for index in range(3 * fold - 1):
        blocks[index * deep : (index + 1) * deep, :] = padded[
            pl.ds(index, deep, stride=fold), :
        ].astype(jnp.bfloat16)

    edges = group_edges(fold)
    groups = len(edges) - 1

    def build(group, band):
        for index, r in enumerate(range(edges[group], edges[group + 1])):
            for part in range(2):
                build_band(base, r + part * fold, band, (2 * index + part) * cols)

    def multiply(group, band):
        parts = []
        for r in range(edges[group], edges[group + 1]):
            for part in range(2):
                first = (r + part * fold) * deep
                parts.append(blocks[first : first + rows, :])
        product = jnp.dot(
            jnp.concatenate(parts, axis=1),
            band[: len(parts) * cols, :],
            preferred_element_type=jnp.float32,
        )
        total[...] = product if group == 0 else total[...] + product

    def assign(tile):
        block = block_ref[tile]
        owner = lax.div(block, BLK_DEV)
        rank = counts[owner]
        counts[owner] = rank + 1
        slot = owner * capacity + rank
        slot_of[tile] = slot
        starts[slot] = (block - owner * BLK_DEV) * SUB + offset_ref[tile]

    held = (band_a, band_b)
    build(0, held[0])
    for group in range(groups):
        if group + 1 < groups:
            build(group + 1, held[(group + 1) % 2])
        multiply(group, held[group % 2])
        for tile in range(group * tiles // groups, (group + 1) * tiles // groups):
            assign(tile)

    lane = iota((1, cols), 1)
    taps_across = [
        jnp.where((lane + m - 2 >= 0) & (lane + m - 2 < cols), across[m : m + 1], 0.0)
        for m in range(TAPS_DOWN)
    ]
    def warp_across(phase, carry):
        first = pl.multiple_of(phase * deep, deep)
        position = 2 * (fold * iota((deep, cols), 0) + phase) + 1
        position = position.astype(jnp.float32) / rows - 1.0
        both = total[pl.ds(first, deep), :]
        matched = both[:, :cols] + position * both[:, cols:]
        result = taps_across[2] * matched
        for m in range(TAPS_DOWN):
            if m != 2:
                result = result + taps_across[m] * pltpu.roll(matched, (2 - m) % cols, 1)
        spread[pl.ds(SUB + phase, deep, stride=fold), :] = result
        return carry

    lax.fori_loop(0, fold, warp_across, 0, unroll=4)

    def warp_down(tile, carry):
        first = tile * SUB + SUB - 2
        result = down[0:1] * spread[pl.ds(first, SUB), :]
        for m in range(1, TAPS_DOWN):
            result = result + down[m : m + 1] * spread[pl.ds(first + m, SUB), :]
        slots[pl.ds(pl.multiple_of(slot_of[tile] * SUB, SUB), SUB), :] = result
        return carry

    lax.fori_loop(0, tiles, warp_down, 0, unroll=16)

    sub = iota((SUB, cols), 0)
    wide = iota((SUB, cols), 1)
    segment = wide >> (data_rows.bit_length() - 1)
    lane_row = wide & (SUB - 1)
    lane_slot = (wide >> 3) & (capacity - 1)
    spill_slot = wide & (capacity - 1)
    spill_row = wide >> (capacity.bit_length() - 1)
    tile_weight = jnp.broadcast_to(weight, (SUB, cols))

    def message(owner, carry):
        previous = jnp.maximum(owner - 1, 0)
        first = owner * data_rows
        out_ref[owner, :data_rows, :] = slots[
            pl.ds(pl.multiple_of(first, data_rows), data_rows), :
        ].astype(jnp.bfloat16)
        spilled = jnp.zeros((SUB, cols), jnp.float32)
        over = jnp.zeros((SUB, cols), jnp.float32)
        target = jnp.zeros((SUB, cols), jnp.int32)
        for c in range(capacity):
            target = jnp.where(lane_slot == c, starts[owner * capacity + c] + lane_row, target)
            slot = previous * capacity + c
            start = starts[slot]
            past = jnp.where(owner > 0, start + SUB - owned, 0)
            tile = slots[pl.ds(pl.multiple_of(slot * SUB, SUB), SUB), :]
            tile = pltpu.roll(tile, start & (SUB - 1), 0)
            spilled = spilled + jnp.where(sub < past, tile, 0.0)
            over = jnp.where((spill_slot == c) & (spill_row < past), tile_weight, over)
        meta = jnp.where(segment == 1, target.astype(jnp.float32), tile_weight)
        meta = jnp.where(segment == 0, over, meta)
        tail = jnp.where(sub == SUB - 1, meta, spilled * tile_weight)
        out_ref[owner, data_rows:, :] = tail.astype(jnp.bfloat16)
        return carry

    lax.fori_loop(0, owners, message, 0, unroll=4)


def sky_kernel(capacity, got_ref, coadd_ref, map_ref):
    sources, message_rows, cols = got_ref.shape
    data_rows = capacity * SUB
    owned = coadd_ref.shape[0]
    per_chunk = cols // data_rows
    chunks = sources // per_chunk
    place = iota((chunks, cols), 0)
    wide = iota((chunks, cols), 1)
    row = iota((owned, cols), 0)
    spilled = jnp.zeros((SUB, cols), jnp.float32)
    target = jnp.zeros((chunks, cols), jnp.float32)
    weight = jnp.zeros((chunks, cols), jnp.float32)
    for k in range(per_chunk):
        heads = jnp.zeros((chunks, cols), jnp.float32)
        for chunk in range(chunks):
            tail = got_ref[chunk * per_chunk + k, data_rows:, :].astype(jnp.float32)
            spilled = spilled + tail
            heads = jnp.where(place == chunk, tail[SUB - 1 :], heads)
        here = (wide >= k * data_rows) & (wide < (k + 1) * data_rows)
        target = jnp.where(here, pltpu.roll(heads, (k - 1) * data_rows % cols, 1), target)
        weight = jnp.where(here, pltpu.roll(heads, (k - 2) * data_rows % cols, 1), weight)
    target = target.astype(jnp.int32)
    pieces = [
        jnp.where(row == target[chunk : chunk + 1], weight[chunk : chunk + 1], 0.0)
        for chunk in range(chunks)
    ]
    placement = jnp.concatenate(pieces, axis=1).astype(jnp.bfloat16)
    pixels = got_ref[:, :data_rows, :].reshape(sources * data_rows, cols)
    pixels = jnp.concatenate([pixels, jnp.ones(pixels.shape, jnp.bfloat16)], axis=1)
    sums = jnp.dot(placement, pixels, preferred_element_type=jnp.float32)
    sub = iota((SUB, cols), 0)
    wide = iota((SUB, cols), 1)
    last = sub == SUB - 1
    over = jnp.broadcast_to(spilled[SUB - 1 :], (SUB, cols))
    mine = ((wide >> (capacity.bit_length() - 1)) == sub) & ~last
    over = jnp.sum(jnp.where(mine, over, 0.0), axis=1, keepdims=True)
    rest = jnp.zeros((owned - SUB, cols), jnp.float32)
    pixel_sum = sums[:, :cols] + jnp.concatenate([jnp.where(last, 0.0, spilled), rest], axis=0)
    weight_sum = sums[:, cols:] + jnp.concatenate(
        [jnp.broadcast_to(over, (SUB, cols)), rest], axis=0
    )
    coadd_ref[...] = pixel_sum / jnp.maximum(weight_sum, 1.0)
    diagonal = jnp.where(row == iota((owned, cols), 1), weight_sum, 0.0)
    map_ref[...] = jnp.sum(diagonal, axis=0, keepdims=True)


def on_device(
    image,
    row_taps,
    col_taps,
    mix_coeff,
    shift_frac,
    ccd_visit,
    visit_weight,
    tile_block,
    tile_offset,
):
    rows, cols = image.shape[1:]
    tiles = tile_block.shape[0]
    sky = lax.axis_size("sky")
    capacity = max(2, tiles // sky)
    taps, basis = row_taps.shape[1], row_taps.shape[0]
    fold = taps // 2 + 1
    visits = visit_weight.shape[0]
    largest = max(b - a for a, b in itertools.pairwise(group_edges(fold)))
    anywhere = pl.BlockSpec(memory_space=pl.ANY)
    vmem = pl.BlockSpec(memory_space=pltpu.VMEM)
    messages = pl.pallas_call(
        functools.partial(window_kernel, capacity),
        out_shape=pltpu.VMEM((sky, capacity * SUB + SUB, cols), jnp.bfloat16),
        in_specs=[anywhere] * 8 + [pl.BlockSpec(memory_space=pltpu.SMEM)],
        out_specs=vmem,
        scratch_shapes=[
            pltpu.VMEM((1, rows, cols), jnp.bfloat16),
            pltpu.VMEM((taps, basis), jnp.bfloat16),
            pltpu.VMEM((taps, basis), jnp.bfloat16),
            pltpu.VMEM((3, 1, basis), jnp.float32),
            pltpu.VMEM((1, visits), jnp.bfloat16),
            pltpu.SMEM((1, 2), jnp.float32),
            pltpu.SMEM((tiles,), jnp.int32),
            pltpu.SMEM((tiles,), jnp.int32),
            pltpu.SemaphoreType.DMA((8,)),
            pltpu.VMEM((rows + 2 * fold, cols), jnp.float32),
            pltpu.VMEM((2 * fold, basis), jnp.float32),
            pltpu.VMEM((3, 2 * fold, cols), jnp.float32),
            pltpu.VMEM((largest * 2 * cols, 2 * cols), jnp.bfloat16),
            pltpu.VMEM((largest * 2 * cols, 2 * cols), jnp.bfloat16),
            pltpu.VMEM(((3 * fold - 1) * (rows // fold), cols), jnp.bfloat16),
            pltpu.VMEM((rows, 2 * cols), jnp.float32),
            pltpu.VMEM((rows + 2 * SUB, cols), jnp.float32),
            pltpu.VMEM((sky * capacity * SUB, cols), jnp.float32),
            pltpu.SMEM((tiles,), jnp.int32),
            pltpu.SMEM((sky * capacity,), jnp.int32),
            pltpu.SMEM((sky,), jnp.int32),
        ],
        compiler_params=pltpu.CompilerParams(vmem_limit_bytes=LARGE_VMEM),
        name="match_warp_pack",
    )(
        *[
            pltpu.with_memory_space_constraint(value, pltpu.HBM)
            for value in (
                image,
                row_taps.T,
                col_taps.T,
                mix_coeff.transpose(1, 0, 2),
                visit_weight.reshape(1, -1),
                shift_frac,
                tile_block,
                tile_offset,
            )
        ],
        ccd_visit,
    )
    received = lax.all_to_all(messages, "sky", split_axis=0, concat_axis=0, tiled=True)
    coadd, weight_map = pl.pallas_call(
        functools.partial(sky_kernel, capacity),
        out_shape=(
            jax.ShapeDtypeStruct((BLK_DEV * SUB, cols), jnp.float32),
            jax.ShapeDtypeStruct((1, BLK_DEV * SUB), jnp.float32),
        ),
        in_specs=[vmem],
        out_specs=(vmem, vmem),
        compiler_params=pltpu.CompilerParams(vmem_limit_bytes=SMALL_VMEM),
        name="place_normalise",
    )(received)
    return coadd, weight_map.reshape(-1)


def solution(mesh):
    return jax.shard_map(
        on_device,
        mesh=mesh,
        in_specs=(
            P(("groups", "sky"), None, None),
            P(),
            P(),
            P(("groups", "sky"), None, None),
            P(("groups", "sky"), None),
            P(("groups", "sky")),
            P("groups"),
            P(("groups", "sky")),
            P(("groups", "sky")),
        ),
        out_specs=(P(("groups", "sky"), None), P(("groups", "sky"))),
        check_vma=False,
    )
```

```python
import functools
import itertools

import jax
import jax.numpy as jnp
from jax import lax
from jax.experimental import pallas as pl
from jax.experimental.pallas import tpu as pltpu
from jax.sharding import PartitionSpec as P

BLK_DEV = 16
SUB = 8
LARGE_VMEM = 32 * 1024 * 1024
SMALL_VMEM = 16 * 1024 * 1024
EMPTY = -64
TAPS_DOWN = 6


def iota(shape, axis):
    return lax.broadcasted_iota(jnp.int32, shape, axis)


def weight_of(visit_ref, weight_ref):
    values = weight_ref[...].astype(jnp.float32)
    chosen = jnp.where(iota(values.shape, 1) == visit_ref[0], values, 0.0)
    return jnp.sum(chosen, axis=1, keepdims=True)


def lanczos_rows(frac_ref, cols):
    row = iota((2 * SUB, cols), 0)
    tap = jnp.where(row < SUB, row, row - SUB)
    fraction = jnp.where(row < SUB, frac_ref[0, 1], frac_ref[0, 0])
    angles = jnp.pi * ((tap - 2).astype(jnp.float32) - fraction)
    third = angles / 3.0
    kernel = jnp.sin(angles) / angles * (jnp.sin(third) / third)
    kernel = jnp.where(tap < TAPS_DOWN, kernel, 0.0)
    across, down = kernel[:SUB], kernel[SUB:]
    across = across / jnp.sum(across, axis=0, keepdims=True)
    down = down / jnp.sum(down, axis=0, keepdims=True)
    return across, down


def combined_taps(row_ref, col_ref, mix_ref, lifted, base):
    taps, basis = row_ref.shape
    count, cols = base.shape[1:]
    half = taps // 2
    l, s = iota((cols, taps), 0), iota((cols, taps), 1)
    turned = ((s + l == half) | (s + l == half + cols)).astype(jnp.float32).astype(jnp.bfloat16)
    across = jnp.dot(turned, row_ref[...], preferred_element_type=jnp.float32)
    across = across.astype(jnp.bfloat16)
    lifted[0:1] = jnp.zeros((1, basis), jnp.float32)
    lifted[1:] = col_ref[...].astype(jnp.float32)
    down = lifted[...]
    scaled = jnp.concatenate([down * mix_ref[term] for term in range(3)], axis=0)
    high = scaled.astype(jnp.bfloat16)
    low = (scaled - high.astype(jnp.float32)).astype(jnp.bfloat16)
    found = lax.dot_general(
        jnp.concatenate([high, low], axis=0),
        across,
        (((1,), (1,)), ((), ())),
        preferred_element_type=jnp.float32,
    )
    found = found[: 3 * count] + found[3 * count :]
    lane = iota((count, cols), 1)
    lane = jnp.where(lane < cols // 2, lane, lane - cols).astype(jnp.float32)
    base[0] = found[:count] + (2.0 / cols) * lane * found[count : 2 * count]
    base[1] = found[count : 2 * count]
    base[2] = found[2 * count :]


def build_band(base, row, band, first):
    cols = base.shape[2]
    shape = (2 * SUB, cols)
    sub = iota(shape, 0)
    lane = iota(shape, 1)
    lane = jnp.where(lane < cols // 2, lane, lane - cols)
    first_u = (2.0 * sub.astype(jnp.float32) + 1.0) / cols - 1.0

    def spin(term):
        taps = jnp.broadcast_to(base[term, pl.ds(row, 1), :], shape)
        return pltpu.roll(taps, 0, 1, stride=1, stride_axis=0)

    slope = spin(1)
    level = spin(0) + first_u * slope
    rise = spin(2)
    whole = rise.astype(jnp.bfloat16)
    pairs = cols // (2 * SUB)
    for pair in range(pairs):
        shift = 2 * SUB * pair
        value = level + (2.0 * shift / cols) * slope
        other = whole
        if pair == 0 or pair == pairs - 1:
            inside = lane >= 0 if pair == 0 else lane < 2 * SUB
            value = jnp.where(inside, value, 0.0)
            other = jnp.where(inside, rise, 0.0).astype(jnp.bfloat16)
        value = value.astype(jnp.bfloat16)
        if pair:
            value, other = pltpu.roll(value, shift, 1), pltpu.roll(other, shift, 1)
        at = first + shift
        band[at : at + 2 * SUB, :] = jnp.concatenate([value, other], axis=1)


def group_edges(fold):
    return [0, fold // 8, fold // 2, fold]


def window_kernel(
    capacity,
    image_hbm,
    row_hbm,
    col_hbm,
    mix_hbm,
    weight_hbm,
    frac_hbm,
    block_hbm,
    offset_hbm,
    visit_ref,
    out_ref,
    image_ref,
    row_ref,
    col_ref,
    mix_ref,
    weight_ref,
    frac_ref,
    block_ref,
    offset_ref,
    copied,
    padded,
    lifted,
    base,
    band_a,
    band_b,
    blocks,
    total,
    spread,
    tile_of,
    starts,
    counts,
):
    rows, cols = image_ref.shape[1:]
    fold = row_ref.shape[0] // 2 + 1
    deep = rows // fold
    tiles = block_ref.shape[0]
    owners = out_ref.shape[0]
    data_rows = capacity * SUB
    owned = BLK_DEV * SUB

    pairs = (
        (row_hbm, row_ref),
        (col_hbm, col_ref),
        (mix_hbm, mix_ref),
        (image_hbm, image_ref),
        (frac_hbm, frac_ref),
        (weight_hbm, weight_ref),
        (block_hbm, block_ref),
        (offset_hbm, offset_ref),
    )
    copies = [
        pltpu.make_async_copy(source, target, copied.at[index])
        for index, (source, target) in enumerate(pairs)
    ]
    for copy in copies:
        copy.start()

    @pl.loop(0, owners)
    def _(owner):
        counts[owner] = 0

    if owners * capacity > tiles:

        @pl.loop(0, owners * capacity)
        def _(slot):
            starts[slot] = EMPTY
            tile_of[slot] = 0

    padded[:fold] = jnp.zeros((fold, cols), jnp.float32)
    padded[fold + rows :] = jnp.zeros((fold, cols), jnp.float32)
    spread[:SUB] = jnp.zeros((SUB, cols), jnp.float32)
    spread[SUB + rows :] = jnp.zeros((SUB, cols), jnp.float32)
    for copy in copies:
        copy.wait()

    combined_taps(row_ref, col_ref, mix_ref, lifted, base)
    padded[fold : fold + rows] = image_ref[0].astype(jnp.float32)
    across, down = lanczos_rows(frac_ref, cols)
    weight = weight_of(visit_ref, weight_ref)

    for index in range(3 * fold - 1):
        blocks[index * deep : (index + 1) * deep, :] = padded[
            pl.ds(index, deep, stride=fold), :
        ].astype(jnp.bfloat16)

    edges = group_edges(fold)
    groups = len(edges) - 1

    def build(group, band):
        for index, r in enumerate(range(edges[group], edges[group + 1])):
            for part in range(2):
                build_band(base, r + part * fold, band, (2 * index + part) * cols)

    def multiply(group, band):
        parts = []
        for r in range(edges[group], edges[group + 1]):
            for part in range(2):
                first = (r + part * fold) * deep
                parts.append(blocks[first : first + rows, :])
        product = jnp.dot(
            jnp.concatenate(parts, axis=1),
            band[: len(parts) * cols, :],
            preferred_element_type=jnp.float32,
        )
        total[...] = product if group == 0 else total[...] + product

    def assign(tile):
        block = block_ref[tile]
        owner = lax.div(block, BLK_DEV)
        rank = counts[owner]
        counts[owner] = rank + 1
        slot = owner * capacity + rank
        tile_of[slot] = tile
        starts[slot] = (block - owner * BLK_DEV) * SUB + offset_ref[tile]

    held = (band_a, band_b)
    build(0, held[0])
    for group in range(groups):
        if group + 1 < groups:
            build(group + 1, held[(group + 1) % 2])
        multiply(group, held[group % 2])
        for tile in range(group * tiles // groups, (group + 1) * tiles // groups):
            assign(tile)

    lane = iota((1, cols), 1)
    taps_across = [
        jnp.where((lane + m - 2 >= 0) & (lane + m - 2 < cols), across[m : m + 1], 0.0)
        for m in range(TAPS_DOWN)
    ]
    for phase in range(fold):
        first = phase * deep
        position = 2 * (fold * iota((deep, cols), 0) + phase) + 1
        position = position.astype(jnp.float32) / rows - 1.0
        both = total[first : first + deep, :]
        matched = both[:, :cols] + position * both[:, cols:]
        result = taps_across[2] * matched
        for m in range(TAPS_DOWN):
            if m != 2:
                result = result + taps_across[m] * pltpu.roll(matched, (2 - m) % cols, 1)
        spread[pl.ds(SUB + phase, deep, stride=fold), :] = result

    sub = iota((SUB, cols), 0)
    wide = iota((SUB, cols), 1)
    segment = wide >> (data_rows.bit_length() - 1)
    lane_row = wide & (SUB - 1)
    lane_slot = (wide >> 3) & (capacity - 1)
    spill_slot = wide & (capacity - 1)
    spill_row = wide >> (capacity.bit_length() - 1)
    tile_weight = jnp.broadcast_to(weight, (SUB, cols))

    def warped(slot):
        first = tile_of[slot] * SUB + SUB - 2
        result = down[0:1] * spread[pl.ds(first, SUB), :]
        for m in range(1, TAPS_DOWN):
            result = result + down[m : m + 1] * spread[pl.ds(first + m, SUB), :]
        return result

    def message(owner, carry):
        spilled, over = carry
        target = jnp.zeros((SUB, cols), jnp.int32)
        next_spilled = jnp.zeros((SUB, cols), jnp.float32)
        next_over = jnp.zeros((SUB, cols), jnp.float32)
        tiles_here = []
        for c in range(capacity):
            slot = owner * capacity + c
            start = starts[slot]
            past = start + SUB - owned
            tile = warped(slot)
            tiles_here.append(tile)
            target = jnp.where(lane_slot == c, start + lane_row, target)
            turned = pltpu.roll(tile, start & (SUB - 1), 0)
            next_spilled = next_spilled + jnp.where(sub < past, turned, 0.0)
            next_over = jnp.where((spill_slot == c) & (spill_row < past), tile_weight, next_over)
        meta = jnp.where(segment == 1, target.astype(jnp.float32), tile_weight)
        meta = jnp.where(segment == 0, over, meta)
        tail = jnp.where(sub == SUB - 1, meta, spilled * tile_weight)
        out_ref[owner, :data_rows, :] = jnp.concatenate(tiles_here, axis=0).astype(jnp.bfloat16)
        out_ref[owner, data_rows:, :] = tail.astype(jnp.bfloat16)
        return next_spilled, next_over

    nothing = jnp.zeros((SUB, cols), jnp.float32)
    lax.fori_loop(0, owners, message, (nothing, nothing), unroll=min(owners, 16))


def sky_kernel(capacity, got_ref, coadd_ref, map_ref):
    sources, message_rows, cols = got_ref.shape
    data_rows = capacity * SUB
    owned = coadd_ref.shape[0]
    per_chunk = cols // data_rows
    chunks = sources // per_chunk
    place = iota((chunks, cols), 0)
    wide = iota((chunks, cols), 1)
    row = iota((owned, cols), 0)
    spilled = jnp.zeros((SUB, cols), jnp.float32)
    target = jnp.zeros((chunks, cols), jnp.float32)
    weight = jnp.zeros((chunks, cols), jnp.float32)
    for k in range(per_chunk):
        heads = jnp.zeros((chunks, cols), jnp.float32)
        for chunk in range(chunks):
            tail = got_ref[chunk * per_chunk + k, data_rows:, :].astype(jnp.float32)
            spilled = spilled + tail
            heads = jnp.where(place == chunk, tail[SUB - 1 :], heads)
        here = (wide >= k * data_rows) & (wide < (k + 1) * data_rows)
        target = jnp.where(here, pltpu.roll(heads, (k - 1) * data_rows % cols, 1), target)
        weight = jnp.where(here, pltpu.roll(heads, (k - 2) * data_rows % cols, 1), weight)
    target = target.astype(jnp.int32)
    pieces = [
        jnp.where(row == target[chunk : chunk + 1], weight[chunk : chunk + 1], 0.0)
        for chunk in range(chunks)
    ]
    placement = jnp.concatenate(pieces, axis=1).astype(jnp.bfloat16)
    pixels = got_ref[:, :data_rows, :].reshape(sources * data_rows, cols)
    pixels = jnp.concatenate([pixels, jnp.ones(pixels.shape, jnp.bfloat16)], axis=1)
    sums = jnp.dot(placement, pixels, preferred_element_type=jnp.float32)
    sub = iota((SUB, cols), 0)
    wide = iota((SUB, cols), 1)
    last = sub == SUB - 1
    over = jnp.broadcast_to(spilled[SUB - 1 :], (SUB, cols))
    mine = ((wide >> (capacity.bit_length() - 1)) == sub) & ~last
    over = jnp.sum(jnp.where(mine, over, 0.0), axis=1, keepdims=True)
    rest = jnp.zeros((owned - SUB, cols), jnp.float32)
    pixel_sum = sums[:, :cols] + jnp.concatenate([jnp.where(last, 0.0, spilled), rest], axis=0)
    weight_sum = sums[:, cols:] + jnp.concatenate(
        [jnp.broadcast_to(over, (SUB, cols)), rest], axis=0
    )
    coadd_ref[...] = pixel_sum / jnp.maximum(weight_sum, 1.0)
    diagonal = jnp.where(row == iota((owned, cols), 1), weight_sum, 0.0)
    map_ref[...] = jnp.sum(diagonal, axis=0, keepdims=True)


def on_device(
    image,
    row_taps,
    col_taps,
    mix_coeff,
    shift_frac,
    ccd_visit,
    visit_weight,
    tile_block,
    tile_offset,
):
    rows, cols = image.shape[1:]
    tiles = tile_block.shape[0]
    sky = lax.axis_size("sky")
    capacity = max(2, tiles // sky)
    taps, basis = row_taps.shape[1], row_taps.shape[0]
    fold = taps // 2 + 1
    visits = visit_weight.shape[0]
    largest = max(b - a for a, b in itertools.pairwise(group_edges(fold)))
    anywhere = pl.BlockSpec(memory_space=pl.ANY)
    vmem = pl.BlockSpec(memory_space=pltpu.VMEM)
    messages = pl.pallas_call(
        functools.partial(window_kernel, capacity),
        out_shape=pltpu.VMEM((sky, capacity * SUB + SUB, cols), jnp.bfloat16),
        in_specs=[anywhere] * 8 + [pl.BlockSpec(memory_space=pltpu.SMEM)],
        out_specs=vmem,
        scratch_shapes=[
            pltpu.VMEM((1, rows, cols), jnp.bfloat16),
            pltpu.VMEM((taps, basis), jnp.bfloat16),
            pltpu.VMEM((taps, basis), jnp.bfloat16),
            pltpu.VMEM((3, 1, basis), jnp.float32),
            pltpu.VMEM((1, visits), jnp.bfloat16),
            pltpu.SMEM((1, 2), jnp.float32),
            pltpu.SMEM((tiles,), jnp.int32),
            pltpu.SMEM((tiles,), jnp.int32),
            pltpu.SemaphoreType.DMA((8,)),
            pltpu.VMEM((rows + 2 * fold, cols), jnp.float32),
            pltpu.VMEM((2 * fold, basis), jnp.float32),
            pltpu.VMEM((3, 2 * fold, cols), jnp.float32),
            pltpu.VMEM((largest * 2 * cols, 2 * cols), jnp.bfloat16),
            pltpu.VMEM((largest * 2 * cols, 2 * cols), jnp.bfloat16),
            pltpu.VMEM(((3 * fold - 1) * (rows // fold), cols), jnp.bfloat16),
            pltpu.VMEM((rows, 2 * cols), jnp.float32),
            pltpu.VMEM((rows + 2 * SUB, cols), jnp.float32),
            pltpu.SMEM((sky * capacity,), jnp.int32),
            pltpu.SMEM((sky * capacity,), jnp.int32),
            pltpu.SMEM((sky,), jnp.int32),
        ],
        compiler_params=pltpu.CompilerParams(vmem_limit_bytes=LARGE_VMEM),
        name="match_warp_pack",
    )(
        *[
            pltpu.with_memory_space_constraint(value, pltpu.HBM)
            for value in (
                image,
                row_taps.T,
                col_taps.T,
                mix_coeff.transpose(1, 0, 2),
                visit_weight.reshape(1, -1),
                shift_frac,
                tile_block,
                tile_offset,
            )
        ],
        ccd_visit,
    )
    received = lax.all_to_all(messages, "sky", split_axis=0, concat_axis=0, tiled=True)
    coadd, weight_map = pl.pallas_call(
        functools.partial(sky_kernel, capacity),
        out_shape=(
            jax.ShapeDtypeStruct((BLK_DEV * SUB, cols), jnp.float32),
            jax.ShapeDtypeStruct((1, BLK_DEV * SUB), jnp.float32),
        ),
        in_specs=[vmem],
        out_specs=(vmem, vmem),
        compiler_params=pltpu.CompilerParams(vmem_limit_bytes=SMALL_VMEM),
        name="place_normalise",
    )(received)
    return coadd, weight_map.reshape(-1)


def solution(mesh):
    return jax.shard_map(
        on_device,
        mesh=mesh,
        in_specs=(
            P(("groups", "sky"), None, None),
            P(),
            P(),
            P(("groups", "sky"), None, None),
            P(("groups", "sky"), None),
            P(("groups", "sky")),
            P("groups"),
            P(("groups", "sky")),
            P(("groups", "sky")),
        ),
        out_specs=(P(("groups", "sky"), None), P(("groups", "sky"))),
        check_vma=False,
    )
```

```python
import functools
import itertools

import jax
import jax.numpy as jnp
from jax import lax
from jax.experimental import pallas as pl
from jax.experimental.pallas import tpu as pltpu
from jax.sharding import PartitionSpec as P

BLK_DEV = 16
SUB = 8
LARGE_VMEM = 32 * 1024 * 1024
SMALL_VMEM = 16 * 1024 * 1024
EMPTY = -64
TAPS_DOWN = 6


def iota(shape, axis):
    return lax.broadcasted_iota(jnp.int32, shape, axis)


def weight_of(visit_ref, weight_ref):
    values = weight_ref[...].astype(jnp.float32)
    chosen = jnp.where(iota(values.shape, 1) == visit_ref[0], values, 0.0)
    return jnp.sum(chosen, axis=1, keepdims=True)


def lanczos_rows(frac_ref, cols):
    row = iota((2 * SUB, cols), 0)
    tap = jnp.where(row < SUB, row, row - SUB)
    fraction = jnp.where(row < SUB, frac_ref[0, 1], frac_ref[0, 0])
    angles = jnp.pi * ((tap - 2).astype(jnp.float32) - fraction)
    third = angles / 3.0
    kernel = jnp.sin(angles) / angles * (jnp.sin(third) / third)
    kernel = jnp.where(tap < TAPS_DOWN, kernel, 0.0)
    across, down = kernel[:SUB], kernel[SUB:]
    across = across / jnp.sum(across, axis=0, keepdims=True)
    down = down / jnp.sum(down, axis=0, keepdims=True)
    return across, down


def combined_taps(row_ref, col_ref, mix_ref, lifted, base):
    taps, basis = row_ref.shape
    count, cols = base.shape[1:]
    half = taps // 2
    l, s = iota((cols, taps), 0), iota((cols, taps), 1)
    turned = ((s + l == half) | (s + l == half + cols)).astype(jnp.float32).astype(jnp.bfloat16)
    across = jnp.dot(turned, row_ref[...], preferred_element_type=jnp.float32)
    across = across.astype(jnp.bfloat16)
    lifted[0:1] = jnp.zeros((1, basis), jnp.float32)
    lifted[1:] = col_ref[...].astype(jnp.float32)
    down = lifted[...]
    scaled = jnp.concatenate([down * mix_ref[term] for term in range(3)], axis=0)
    high = scaled.astype(jnp.bfloat16)
    low = (scaled - high.astype(jnp.float32)).astype(jnp.bfloat16)
    found = lax.dot_general(
        jnp.concatenate([high, low], axis=0),
        across,
        (((1,), (1,)), ((), ())),
        preferred_element_type=jnp.float32,
    )
    found = found[: 3 * count] + found[3 * count :]
    lane = iota((count, cols), 1)
    lane = jnp.where(lane < cols // 2, lane, lane - cols).astype(jnp.float32)
    base[0] = found[:count] + (2.0 / cols) * lane * found[count : 2 * count]
    base[1] = found[count : 2 * count]
    base[2] = found[2 * count :]


def build_band(base, row, band, first):
    cols = base.shape[2]
    shape = (2 * SUB, cols)
    sub = iota(shape, 0)
    lane = iota(shape, 1)
    lane = jnp.where(lane < cols // 2, lane, lane - cols)
    first_u = (2.0 * sub.astype(jnp.float32) + 1.0) / cols - 1.0

    def spin(term):
        taps = jnp.broadcast_to(base[term, pl.ds(row, 1), :], shape)
        return pltpu.roll(taps, 0, 1, stride=1, stride_axis=0)

    slope = spin(1)
    level = spin(0) + first_u * slope
    rise = spin(2)
    whole = rise.astype(jnp.bfloat16)
    pairs = cols // (2 * SUB)
    for pair in range(pairs):
        shift = 2 * SUB * pair
        value = level + (2.0 * shift / cols) * slope
        other = whole
        if pair == 0 or pair == pairs - 1:
            inside = lane >= 0 if pair == 0 else lane < 2 * SUB
            value = jnp.where(inside, value, 0.0)
            other = jnp.where(inside, rise, 0.0).astype(jnp.bfloat16)
        value = value.astype(jnp.bfloat16)
        if pair:
            value, other = pltpu.roll(value, shift, 1), pltpu.roll(other, shift, 1)
        at = first + shift
        band[at : at + 2 * SUB, :] = jnp.concatenate([value, other], axis=1)


def first_member(owners):
    return owners // 2


def group_edges(fold):
    return [0, fold // 8, fold // 2, fold]


def window_kernel(
    capacity,
    image_hbm,
    row_hbm,
    col_hbm,
    mix_hbm,
    weight_hbm,
    frac_hbm,
    block_hbm,
    offset_hbm,
    visit_ref,
    out_ref,
    image_ref,
    row_ref,
    col_ref,
    mix_ref,
    weight_ref,
    frac_ref,
    block_ref,
    offset_ref,
    copied,
    padded,
    lifted,
    base,
    band_a,
    band_b,
    blocks,
    total,
    spread,
    tile_of,
    starts,
    counts,
):
    rows, cols = image_ref.shape[1:]
    fold = row_ref.shape[0] // 2 + 1
    deep = rows // fold
    tiles = block_ref.shape[0]
    owners = out_ref.shape[0]
    data_rows = capacity * SUB
    owned = BLK_DEV * SUB

    pairs = (
        (row_hbm, row_ref),
        (col_hbm, col_ref),
        (mix_hbm, mix_ref),
        (image_hbm, image_ref),
        (frac_hbm, frac_ref),
        (weight_hbm, weight_ref),
        (block_hbm, block_ref),
        (offset_hbm, offset_ref),
    )
    copies = [
        pltpu.make_async_copy(source, target, copied.at[index])
        for index, (source, target) in enumerate(pairs)
    ]
    for copy in copies:
        copy.start()

    @pl.loop(0, owners)
    def _(owner):
        counts[owner] = 0

    if owners * capacity > tiles:

        @pl.loop(0, owners * capacity)
        def _(slot):
            starts[slot] = EMPTY
            tile_of[slot] = 0

    padded[:fold] = jnp.zeros((fold, cols), jnp.float32)
    padded[fold + rows :] = jnp.zeros((fold, cols), jnp.float32)
    spread[:SUB] = jnp.zeros((SUB, cols), jnp.float32)
    spread[SUB + rows :] = jnp.zeros((SUB, cols), jnp.float32)
    for copy in copies:
        copy.wait()

    combined_taps(row_ref, col_ref, mix_ref, lifted, base)
    padded[fold : fold + rows] = image_ref[0].astype(jnp.float32)
    across, down = lanczos_rows(frac_ref, cols)
    weight = weight_of(visit_ref, weight_ref)

    for index in range(3 * fold - 1):
        blocks[index * deep : (index + 1) * deep, :] = padded[
            pl.ds(index, deep, stride=fold), :
        ].astype(jnp.bfloat16)

    edges = group_edges(fold)
    groups = len(edges) - 1

    def build(group, band):
        for index, r in enumerate(range(edges[group], edges[group + 1])):
            for part in range(2):
                build_band(base, r + part * fold, band, (2 * index + part) * cols)

    def multiply(group, band):
        parts = []
        for r in range(edges[group], edges[group + 1]):
            for part in range(2):
                first = (r + part * fold) * deep
                parts.append(blocks[first : first + rows, :])
        product = jnp.dot(
            jnp.concatenate(parts, axis=1),
            band[: len(parts) * cols, :],
            preferred_element_type=jnp.float32,
        )
        total[...] = product if group == 0 else total[...] + product

    def assign(tile):
        block = block_ref[tile]
        owner = lax.div(block, BLK_DEV)
        rank = counts[owner]
        counts[owner] = rank + 1
        slot = owner * capacity + rank
        tile_of[slot] = tile
        starts[slot] = (block - owner * BLK_DEV) * SUB + offset_ref[tile]

    held = (band_a, band_b)
    build(0, held[0])
    for group in range(groups):
        if group + 1 < groups:
            build(group + 1, held[(group + 1) % 2])
        multiply(group, held[group % 2])
        for tile in range(group * tiles // groups, (group + 1) * tiles // groups):
            assign(tile)

    lane = iota((1, cols), 1)
    taps_across = [
        jnp.where((lane + m - 2 >= 0) & (lane + m - 2 < cols), across[m : m + 1], 0.0)
        for m in range(TAPS_DOWN)
    ]
    for phase in range(fold):
        first = phase * deep
        position = 2 * (fold * iota((deep, cols), 0) + phase) + 1
        position = position.astype(jnp.float32) / rows - 1.0
        both = total[first : first + deep, :]
        matched = both[:, :cols] + position * both[:, cols:]
        result = taps_across[2] * matched
        for m in range(TAPS_DOWN):
            if m != 2:
                result = result + taps_across[m] * pltpu.roll(matched, (2 - m) % cols, 1)
        spread[pl.ds(SUB + phase, deep, stride=fold), :] = result

    sub = iota((SUB, cols), 0)
    wide = iota((SUB, cols), 1)
    segment = wide >> (data_rows.bit_length() - 1)
    lane_row = wide & (SUB - 1)
    lane_slot = (wide >> 3) & (capacity - 1)
    spill_slot = wide & (capacity - 1)
    spill_row = wide >> (capacity.bit_length() - 1)
    tile_weight = jnp.broadcast_to(weight, (SUB, cols))

    def warped(slot):
        first = tile_of[slot] * SUB + SUB - 2
        result = down[0:1] * spread[pl.ds(first, SUB), :]
        for m in range(1, TAPS_DOWN):
            result = result + down[m : m + 1] * spread[pl.ds(first + m, SUB), :]
        return result

    def message(owner, carry):
        spilled, over = carry
        target = jnp.zeros((SUB, cols), jnp.int32)
        next_spilled = jnp.zeros((SUB, cols), jnp.float32)
        next_over = jnp.zeros((SUB, cols), jnp.float32)
        tiles_here = []
        for c in range(capacity):
            slot = owner * capacity + c
            start = starts[slot]
            past = start + SUB - owned
            tile = warped(slot)
            tiles_here.append(tile)
            target = jnp.where(lane_slot == c, start + lane_row, target)
            turned = pltpu.roll(tile, start & (SUB - 1), 0)
            next_spilled = next_spilled + jnp.where(sub < past, turned, 0.0)
            next_over = jnp.where((spill_slot == c) & (spill_row < past), tile_weight, next_over)
        meta = jnp.where(segment == 1, target.astype(jnp.float32), tile_weight)
        meta = jnp.where(segment == 0, over, meta)
        tail = jnp.where(sub == SUB - 1, meta, spilled * tile_weight)
        place = lax.rem(owner + owners - first_member(owners), owners)
        out_ref[place, :data_rows, :] = jnp.concatenate(tiles_here, axis=0).astype(jnp.bfloat16)
        out_ref[place, data_rows:, :] = tail.astype(jnp.bfloat16)
        return next_spilled, next_over

    nothing = jnp.zeros((SUB, cols), jnp.float32)
    lax.fori_loop(0, owners, message, (nothing, nothing), unroll=min(owners, 16))


def sky_kernel(capacity, got_ref, coadd_ref, map_ref):
    sources, message_rows, cols = got_ref.shape
    data_rows = capacity * SUB
    owned = coadd_ref.shape[0]
    per_chunk = cols // data_rows
    chunks = sources // per_chunk
    place = iota((chunks, cols), 0)
    wide = iota((chunks, cols), 1)
    row = iota((owned, cols), 0)
    spilled = jnp.zeros((SUB, cols), jnp.float32)
    target = jnp.zeros((chunks, cols), jnp.float32)
    weight = jnp.zeros((chunks, cols), jnp.float32)
    for k in range(per_chunk):
        heads = jnp.zeros((chunks, cols), jnp.float32)
        for chunk in range(chunks):
            tail = got_ref[chunk * per_chunk + k, data_rows:, :].astype(jnp.float32)
            spilled = spilled + tail
            heads = jnp.where(place == chunk, tail[SUB - 1 :], heads)
        here = (wide >= k * data_rows) & (wide < (k + 1) * data_rows)
        target = jnp.where(here, pltpu.roll(heads, (k - 1) * data_rows % cols, 1), target)
        weight = jnp.where(here, pltpu.roll(heads, (k - 2) * data_rows % cols, 1), weight)
    target = target.astype(jnp.int32)
    pieces = [
        jnp.where(row == target[chunk : chunk + 1], weight[chunk : chunk + 1], 0.0)
        for chunk in range(chunks)
    ]
    placement = jnp.concatenate(pieces, axis=1).astype(jnp.bfloat16)
    pixels = got_ref[:, :data_rows, :].reshape(sources * data_rows, cols)
    pixels = jnp.concatenate([pixels, jnp.ones(pixels.shape, jnp.bfloat16)], axis=1)
    sums = jnp.dot(placement, pixels, preferred_element_type=jnp.float32)
    sub = iota((SUB, cols), 0)
    wide = iota((SUB, cols), 1)
    last = sub == SUB - 1
    over = jnp.broadcast_to(spilled[SUB - 1 :], (SUB, cols))
    mine = ((wide >> (capacity.bit_length() - 1)) == sub) & ~last
    over = jnp.sum(jnp.where(mine, over, 0.0), axis=1, keepdims=True)
    rest = jnp.zeros((owned - SUB, cols), jnp.float32)
    pixel_sum = sums[:, :cols] + jnp.concatenate([jnp.where(last, 0.0, spilled), rest], axis=0)
    weight_sum = sums[:, cols:] + jnp.concatenate(
        [jnp.broadcast_to(over, (SUB, cols)), rest], axis=0
    )
    coadd_ref[...] = pixel_sum / jnp.maximum(weight_sum, 1.0)
    diagonal = jnp.where(row == iota((owned, cols), 1), weight_sum, 0.0)
    map_ref[...] = jnp.sum(diagonal, axis=0, keepdims=True)


def on_device(
    image,
    row_taps,
    col_taps,
    mix_coeff,
    shift_frac,
    ccd_visit,
    visit_weight,
    tile_block,
    tile_offset,
):
    rows, cols = image.shape[1:]
    tiles = tile_block.shape[0]
    sky = lax.axis_size("sky")
    capacity = max(2, tiles // sky)
    taps, basis = row_taps.shape[1], row_taps.shape[0]
    fold = taps // 2 + 1
    visits = visit_weight.shape[0]
    largest = max(b - a for a, b in itertools.pairwise(group_edges(fold)))
    anywhere = pl.BlockSpec(memory_space=pl.ANY)
    vmem = pl.BlockSpec(memory_space=pltpu.VMEM)
    messages = pl.pallas_call(
        functools.partial(window_kernel, capacity),
        out_shape=pltpu.VMEM((sky, capacity * SUB + SUB, cols), jnp.bfloat16),
        in_specs=[anywhere] * 8 + [pl.BlockSpec(memory_space=pltpu.SMEM)],
        out_specs=vmem,
        scratch_shapes=[
            pltpu.VMEM((1, rows, cols), jnp.bfloat16),
            pltpu.VMEM((taps, basis), jnp.bfloat16),
            pltpu.VMEM((taps, basis), jnp.bfloat16),
            pltpu.VMEM((3, 1, basis), jnp.float32),
            pltpu.VMEM((1, visits), jnp.bfloat16),
            pltpu.SMEM((1, 2), jnp.float32),
            pltpu.SMEM((tiles,), jnp.int32),
            pltpu.SMEM((tiles,), jnp.int32),
            pltpu.SemaphoreType.DMA((8,)),
            pltpu.VMEM((rows + 2 * fold, cols), jnp.float32),
            pltpu.VMEM((2 * fold, basis), jnp.float32),
            pltpu.VMEM((3, 2 * fold, cols), jnp.float32),
            pltpu.VMEM((largest * 2 * cols, 2 * cols), jnp.bfloat16),
            pltpu.VMEM((largest * 2 * cols, 2 * cols), jnp.bfloat16),
            pltpu.VMEM(((3 * fold - 1) * (rows // fold), cols), jnp.bfloat16),
            pltpu.VMEM((rows, 2 * cols), jnp.float32),
            pltpu.VMEM((rows + 2 * SUB, cols), jnp.float32),
            pltpu.SMEM((sky * capacity,), jnp.int32),
            pltpu.SMEM((sky * capacity,), jnp.int32),
            pltpu.SMEM((sky,), jnp.int32),
        ],
        compiler_params=pltpu.CompilerParams(vmem_limit_bytes=LARGE_VMEM),
        name="match_warp_pack",
    )(
        *[
            pltpu.with_memory_space_constraint(value, pltpu.HBM)
            for value in (
                image,
                row_taps.T,
                col_taps.T,
                mix_coeff.transpose(1, 0, 2),
                visit_weight.reshape(1, -1),
                shift_frac,
                tile_block,
                tile_offset,
            )
        ],
        ccd_visit,
    )
    order = [(place + first_member(sky)) % sky for place in range(sky)]
    received = lax.all_to_all(
        messages, "sky", split_axis=0, concat_axis=0, axis_index_groups=[order], tiled=True
    )
    coadd, weight_map = pl.pallas_call(
        functools.partial(sky_kernel, capacity),
        out_shape=(
            jax.ShapeDtypeStruct((BLK_DEV * SUB, cols), jnp.float32),
            jax.ShapeDtypeStruct((1, BLK_DEV * SUB), jnp.float32),
        ),
        in_specs=[vmem],
        out_specs=(vmem, vmem),
        compiler_params=pltpu.CompilerParams(vmem_limit_bytes=SMALL_VMEM),
        name="place_normalise",
    )(received)
    return coadd, weight_map.reshape(-1)


def solution(mesh):
    return jax.shard_map(
        on_device,
        mesh=mesh,
        in_specs=(
            P(("groups", "sky"), None, None),
            P(),
            P(),
            P(("groups", "sky"), None, None),
            P(("groups", "sky"), None),
            P(("groups", "sky")),
            P("groups"),
            P(("groups", "sky")),
            P(("groups", "sky")),
        ),
        out_specs=(P(("groups", "sky"), None), P(("groups", "sky"))),
        check_vma=False,
    )
```

```python
import functools
import itertools

import jax
import jax.numpy as jnp
from jax import lax
from jax.experimental import pallas as pl
from jax.experimental.pallas import tpu as pltpu
from jax.sharding import PartitionSpec as P

BLK_DEV = 16
SUB = 8
LARGE_VMEM = 32 * 1024 * 1024
SMALL_VMEM = 16 * 1024 * 1024
EMPTY = -64
TAPS_DOWN = 6


def iota(shape, axis):
    return lax.broadcasted_iota(jnp.int32, shape, axis)


def weight_of(visit_ref, weight_ref):
    values = weight_ref[...].astype(jnp.float32)
    chosen = jnp.where(iota(values.shape, 1) == visit_ref[0], values, 0.0)
    return jnp.sum(chosen, axis=1, keepdims=True)


def lanczos_rows(frac_ref, cols):
    row = iota((2 * SUB, cols), 0)
    tap = jnp.where(row < SUB, row, row - SUB)
    fraction = jnp.where(row < SUB, frac_ref[0, 1], frac_ref[0, 0])
    angles = jnp.pi * ((tap - 2).astype(jnp.float32) - fraction)
    third = angles / 3.0
    kernel = jnp.sin(angles) / angles * (jnp.sin(third) / third)
    kernel = jnp.where(tap < TAPS_DOWN, kernel, 0.0)
    across, down = kernel[:SUB], kernel[SUB:]
    across = across / jnp.sum(across, axis=0, keepdims=True)
    down = down / jnp.sum(down, axis=0, keepdims=True)
    return across, down


def combined_taps(row_ref, col_ref, mix_ref, lifted, base):
    taps, basis = row_ref.shape
    count, cols = base.shape[1:]
    half = taps // 2
    l, s = iota((cols, taps), 0), iota((cols, taps), 1)
    turned = ((s + l == half) | (s + l == half + cols)).astype(jnp.float32).astype(jnp.bfloat16)
    across = jnp.dot(turned, row_ref[...], preferred_element_type=jnp.float32)
    across = across.astype(jnp.bfloat16)
    lifted[0:1] = jnp.zeros((1, basis), jnp.float32)
    lifted[1:] = col_ref[...].astype(jnp.float32)
    down = lifted[...]
    scaled = jnp.concatenate([down * mix_ref[term] for term in range(3)], axis=0)
    high = scaled.astype(jnp.bfloat16)
    low = (scaled - high.astype(jnp.float32)).astype(jnp.bfloat16)
    found = lax.dot_general(
        jnp.concatenate([high, low], axis=0),
        across,
        (((1,), (1,)), ((), ())),
        preferred_element_type=jnp.float32,
    )
    found = found[: 3 * count] + found[3 * count :]
    lane = iota((count, cols), 1)
    lane = jnp.where(lane < cols // 2, lane, lane - cols).astype(jnp.float32)
    base[0] = found[:count] + (2.0 / cols) * lane * found[count : 2 * count]
    base[1] = found[count : 2 * count]
    base[2] = found[2 * count :]


def build_band(base, row, band, first):
    cols = base.shape[2]
    shape = (2 * SUB, cols)
    sub = iota(shape, 0)
    lane = iota(shape, 1)
    lane = jnp.where(lane < cols // 2, lane, lane - cols)
    first_u = (2.0 * sub.astype(jnp.float32) + 1.0) / cols - 1.0

    def spin(term):
        taps = jnp.broadcast_to(base[term, pl.ds(row, 1), :], shape)
        return pltpu.roll(taps, 0, 1, stride=1, stride_axis=0)

    slope = spin(1)
    level = spin(0) + first_u * slope
    rise = spin(2)
    whole = rise.astype(jnp.bfloat16)
    pairs = cols // (2 * SUB)
    for pair in range(pairs):
        shift = 2 * SUB * pair
        value = level + (2.0 * shift / cols) * slope
        other = whole
        if pair == 0 or pair == pairs - 1:
            inside = lane >= 0 if pair == 0 else lane < 2 * SUB
            value = jnp.where(inside, value, 0.0)
            other = jnp.where(inside, rise, 0.0).astype(jnp.bfloat16)
        value = value.astype(jnp.bfloat16)
        if pair:
            value, other = pltpu.roll(value, shift, 1), pltpu.roll(other, shift, 1)
        at = first + shift
        band[at : at + 2 * SUB, :] = jnp.concatenate([value, other], axis=1)


def place_of(owner, owners):
    slow = 1 << ((owners.bit_length() - 1) // 2)
    fast = owners // slow
    return owner % fast * slow + (owner // fast + slow // 2) % slow


def group_edges(fold):
    return [0, fold // 8, fold // 2, fold]


def window_kernel(
    capacity,
    image_hbm,
    row_hbm,
    col_hbm,
    mix_hbm,
    weight_hbm,
    frac_hbm,
    block_hbm,
    offset_hbm,
    visit_ref,
    out_ref,
    image_ref,
    row_ref,
    col_ref,
    mix_ref,
    weight_ref,
    frac_ref,
    block_ref,
    offset_ref,
    copied,
    padded,
    lifted,
    base,
    band_a,
    band_b,
    blocks,
    total,
    spread,
    tile_of,
    starts,
    counts,
):
    rows, cols = image_ref.shape[1:]
    fold = row_ref.shape[0] // 2 + 1
    deep = rows // fold
    tiles = block_ref.shape[0]
    owners = out_ref.shape[0]
    data_rows = capacity * SUB
    owned = BLK_DEV * SUB

    pairs = (
        (row_hbm, row_ref),
        (col_hbm, col_ref),
        (mix_hbm, mix_ref),
        (image_hbm, image_ref),
        (frac_hbm, frac_ref),
        (weight_hbm, weight_ref),
        (block_hbm, block_ref),
        (offset_hbm, offset_ref),
    )
    copies = [
        pltpu.make_async_copy(source, target, copied.at[index])
        for index, (source, target) in enumerate(pairs)
    ]
    for copy in copies:
        copy.start()

    @pl.loop(0, owners)
    def _(owner):
        counts[owner] = 0

    if owners * capacity > tiles:

        @pl.loop(0, owners * capacity)
        def _(slot):
            starts[slot] = EMPTY
            tile_of[slot] = 0

    padded[:fold] = jnp.zeros((fold, cols), jnp.float32)
    padded[fold + rows :] = jnp.zeros((fold, cols), jnp.float32)
    spread[:SUB] = jnp.zeros((SUB, cols), jnp.float32)
    spread[SUB + rows :] = jnp.zeros((SUB, cols), jnp.float32)
    for copy in copies:
        copy.wait()

    combined_taps(row_ref, col_ref, mix_ref, lifted, base)
    padded[fold : fold + rows] = image_ref[0].astype(jnp.float32)
    across, down = lanczos_rows(frac_ref, cols)
    weight = weight_of(visit_ref, weight_ref)

    for index in range(3 * fold - 1):
        blocks[index * deep : (index + 1) * deep, :] = padded[
            pl.ds(index, deep, stride=fold), :
        ].astype(jnp.bfloat16)

    edges = group_edges(fold)
    groups = len(edges) - 1

    def build(group, band):
        for index, r in enumerate(range(edges[group], edges[group + 1])):
            for part in range(2):
                build_band(base, r + part * fold, band, (2 * index + part) * cols)

    def multiply(group, band):
        parts = []
        for r in range(edges[group], edges[group + 1]):
            for part in range(2):
                first = (r + part * fold) * deep
                parts.append(blocks[first : first + rows, :])
        product = jnp.dot(
            jnp.concatenate(parts, axis=1),
            band[: len(parts) * cols, :],
            preferred_element_type=jnp.float32,
        )
        total[...] = product if group == 0 else total[...] + product

    def assign(tile):
        block = block_ref[tile]
        owner = lax.div(block, BLK_DEV)
        rank = counts[owner]
        counts[owner] = rank + 1
        slot = owner * capacity + rank
        tile_of[slot] = tile
        starts[slot] = (block - owner * BLK_DEV) * SUB + offset_ref[tile]

    held = (band_a, band_b)
    build(0, held[0])
    for group in range(groups):
        if group + 1 < groups:
            build(group + 1, held[(group + 1) % 2])
        multiply(group, held[group % 2])
        for tile in range(group * tiles // groups, (group + 1) * tiles // groups):
            assign(tile)

    lane = iota((1, cols), 1)
    taps_across = [
        jnp.where((lane + m - 2 >= 0) & (lane + m - 2 < cols), across[m : m + 1], 0.0)
        for m in range(TAPS_DOWN)
    ]
    for phase in range(fold):
        first = phase * deep
        position = 2 * (fold * iota((deep, cols), 0) + phase) + 1
        position = position.astype(jnp.float32) / rows - 1.0
        both = total[first : first + deep, :]
        matched = both[:, :cols] + position * both[:, cols:]
        result = taps_across[2] * matched
        for m in range(TAPS_DOWN):
            if m != 2:
                result = result + taps_across[m] * pltpu.roll(matched, (2 - m) % cols, 1)
        spread[pl.ds(SUB + phase, deep, stride=fold), :] = result

    sub = iota((SUB, cols), 0)
    wide = iota((SUB, cols), 1)
    segment = wide >> (data_rows.bit_length() - 1)
    lane_row = wide & (SUB - 1)
    lane_slot = (wide >> 3) & (capacity - 1)
    spill_slot = wide & (capacity - 1)
    spill_row = wide >> (capacity.bit_length() - 1)
    tile_weight = jnp.broadcast_to(weight, (SUB, cols))

    def warped(slot):
        first = tile_of[slot] * SUB + SUB - 2
        result = down[0:1] * spread[pl.ds(first, SUB), :]
        for m in range(1, TAPS_DOWN):
            result = result + down[m : m + 1] * spread[pl.ds(first + m, SUB), :]
        return result

    def message(owner, carry):
        spilled, over = carry
        target = jnp.zeros((SUB, cols), jnp.int32)
        next_spilled = jnp.zeros((SUB, cols), jnp.float32)
        next_over = jnp.zeros((SUB, cols), jnp.float32)
        tiles_here = []
        for c in range(capacity):
            slot = owner * capacity + c
            start = starts[slot]
            past = start + SUB - owned
            tile = warped(slot)
            tiles_here.append(tile)
            target = jnp.where(lane_slot == c, start + lane_row, target)
            turned = pltpu.roll(tile, start & (SUB - 1), 0)
            next_spilled = next_spilled + jnp.where(sub < past, turned, 0.0)
            next_over = jnp.where((spill_slot == c) & (spill_row < past), tile_weight, next_over)
        meta = jnp.where(segment == 1, target.astype(jnp.float32), tile_weight)
        meta = jnp.where(segment == 0, over, meta)
        tail = jnp.where(sub == SUB - 1, meta, spilled * tile_weight)
        place = place_of(owner, owners)
        out_ref[place, :data_rows, :] = jnp.concatenate(tiles_here, axis=0).astype(jnp.bfloat16)
        out_ref[place, data_rows:, :] = tail.astype(jnp.bfloat16)
        return next_spilled, next_over

    nothing = jnp.zeros((SUB, cols), jnp.float32)
    lax.fori_loop(0, owners, message, (nothing, nothing), unroll=min(owners, 16))


def sky_kernel(capacity, got_ref, coadd_ref, map_ref):
    sources, message_rows, cols = got_ref.shape
    data_rows = capacity * SUB
    owned = coadd_ref.shape[0]
    per_chunk = cols // data_rows
    chunks = sources // per_chunk
    place = iota((chunks, cols), 0)
    wide = iota((chunks, cols), 1)
    row = iota((owned, cols), 0)
    spilled = jnp.zeros((SUB, cols), jnp.float32)
    target = jnp.zeros((chunks, cols), jnp.float32)
    weight = jnp.zeros((chunks, cols), jnp.float32)
    for k in range(per_chunk):
        heads = jnp.zeros((chunks, cols), jnp.float32)
        for chunk in range(chunks):
            tail = got_ref[chunk * per_chunk + k, data_rows:, :].astype(jnp.float32)
            spilled = spilled + tail
            heads = jnp.where(place == chunk, tail[SUB - 1 :], heads)
        here = (wide >= k * data_rows) & (wide < (k + 1) * data_rows)
        target = jnp.where(here, pltpu.roll(heads, (k - 1) * data_rows % cols, 1), target)
        weight = jnp.where(here, pltpu.roll(heads, (k - 2) * data_rows % cols, 1), weight)
    target = target.astype(jnp.int32)
    pieces = [
        jnp.where(row == target[chunk : chunk + 1], weight[chunk : chunk + 1], 0.0)
        for chunk in range(chunks)
    ]
    placement = jnp.concatenate(pieces, axis=1).astype(jnp.bfloat16)
    pixels = got_ref[:, :data_rows, :].reshape(sources * data_rows, cols)
    pixels = jnp.concatenate([pixels, jnp.ones(pixels.shape, jnp.bfloat16)], axis=1)
    sums = jnp.dot(placement, pixels, preferred_element_type=jnp.float32)
    sub = iota((SUB, cols), 0)
    wide = iota((SUB, cols), 1)
    last = sub == SUB - 1
    over = jnp.broadcast_to(spilled[SUB - 1 :], (SUB, cols))
    mine = ((wide >> (capacity.bit_length() - 1)) == sub) & ~last
    over = jnp.sum(jnp.where(mine, over, 0.0), axis=1, keepdims=True)
    rest = jnp.zeros((owned - SUB, cols), jnp.float32)
    pixel_sum = sums[:, :cols] + jnp.concatenate([jnp.where(last, 0.0, spilled), rest], axis=0)
    weight_sum = sums[:, cols:] + jnp.concatenate(
        [jnp.broadcast_to(over, (SUB, cols)), rest], axis=0
    )
    coadd_ref[...] = pixel_sum / jnp.maximum(weight_sum, 1.0)
    diagonal = jnp.where(row == iota((owned, cols), 1), weight_sum, 0.0)
    map_ref[...] = jnp.sum(diagonal, axis=0, keepdims=True)


def on_device(
    image,
    row_taps,
    col_taps,
    mix_coeff,
    shift_frac,
    ccd_visit,
    visit_weight,
    tile_block,
    tile_offset,
):
    rows, cols = image.shape[1:]
    tiles = tile_block.shape[0]
    sky = lax.axis_size("sky")
    capacity = max(2, tiles // sky)
    taps, basis = row_taps.shape[1], row_taps.shape[0]
    fold = taps // 2 + 1
    visits = visit_weight.shape[0]
    largest = max(b - a for a, b in itertools.pairwise(group_edges(fold)))
    anywhere = pl.BlockSpec(memory_space=pl.ANY)
    vmem = pl.BlockSpec(memory_space=pltpu.VMEM)
    messages = pl.pallas_call(
        functools.partial(window_kernel, capacity),
        out_shape=pltpu.VMEM((sky, capacity * SUB + SUB, cols), jnp.bfloat16),
        in_specs=[anywhere] * 8 + [pl.BlockSpec(memory_space=pltpu.SMEM)],
        out_specs=vmem,
        scratch_shapes=[
            pltpu.VMEM((1, rows, cols), jnp.bfloat16),
            pltpu.VMEM((taps, basis), jnp.bfloat16),
            pltpu.VMEM((taps, basis), jnp.bfloat16),
            pltpu.VMEM((3, 1, basis), jnp.float32),
            pltpu.VMEM((1, visits), jnp.bfloat16),
            pltpu.SMEM((1, 2), jnp.float32),
            pltpu.SMEM((tiles,), jnp.int32),
            pltpu.SMEM((tiles,), jnp.int32),
            pltpu.SemaphoreType.DMA((8,)),
            pltpu.VMEM((rows + 2 * fold, cols), jnp.float32),
            pltpu.VMEM((2 * fold, basis), jnp.float32),
            pltpu.VMEM((3, 2 * fold, cols), jnp.float32),
            pltpu.VMEM((largest * 2 * cols, 2 * cols), jnp.bfloat16),
            pltpu.VMEM((largest * 2 * cols, 2 * cols), jnp.bfloat16),
            pltpu.VMEM(((3 * fold - 1) * (rows // fold), cols), jnp.bfloat16),
            pltpu.VMEM((rows, 2 * cols), jnp.float32),
            pltpu.VMEM((rows + 2 * SUB, cols), jnp.float32),
            pltpu.SMEM((sky * capacity,), jnp.int32),
            pltpu.SMEM((sky * capacity,), jnp.int32),
            pltpu.SMEM((sky,), jnp.int32),
        ],
        compiler_params=pltpu.CompilerParams(vmem_limit_bytes=LARGE_VMEM),
        name="match_warp_pack",
    )(
        *[
            pltpu.with_memory_space_constraint(value, pltpu.HBM)
            for value in (
                image,
                row_taps.T,
                col_taps.T,
                mix_coeff.transpose(1, 0, 2),
                visit_weight.reshape(1, -1),
                shift_frac,
                tile_block,
                tile_offset,
            )
        ],
        ccd_visit,
    )
    order = sorted(range(sky), key=lambda owner: place_of(owner, sky))
    received = lax.all_to_all(
        messages, "sky", split_axis=0, concat_axis=0, axis_index_groups=[order], tiled=True
    )
    coadd, weight_map = pl.pallas_call(
        functools.partial(sky_kernel, capacity),
        out_shape=(
            jax.ShapeDtypeStruct((BLK_DEV * SUB, cols), jnp.float32),
            jax.ShapeDtypeStruct((1, BLK_DEV * SUB), jnp.float32),
        ),
        in_specs=[vmem],
        out_specs=(vmem, vmem),
        compiler_params=pltpu.CompilerParams(vmem_limit_bytes=SMALL_VMEM),
        name="place_normalise",
    )(received)
    return coadd, weight_map.reshape(-1)


def solution(mesh):
    return jax.shard_map(
        on_device,
        mesh=mesh,
        in_specs=(
            P(("groups", "sky"), None, None),
            P(),
            P(),
            P(("groups", "sky"), None, None),
            P(("groups", "sky"), None),
            P(("groups", "sky")),
            P("groups"),
            P(("groups", "sky")),
            P(("groups", "sky")),
        ),
        out_specs=(P(("groups", "sky"), None), P(("groups", "sky"))),
        check_vma=False,
    )
```

```python
import functools
import itertools

import jax
import jax.numpy as jnp
from jax import lax
from jax.experimental import pallas as pl
from jax.experimental.pallas import tpu as pltpu
from jax.sharding import PartitionSpec as P

BLK_DEV = 16
SUB = 8
LARGE_VMEM = 32 * 1024 * 1024
SMALL_VMEM = 16 * 1024 * 1024
EMPTY = -64
TAPS_DOWN = 6


def iota(shape, axis):
    return lax.broadcasted_iota(jnp.int32, shape, axis)


def weight_of(visit_ref, weight_ref):
    values = weight_ref[...].astype(jnp.float32)
    chosen = jnp.where(iota(values.shape, 1) == visit_ref[0], values, 0.0)
    return jnp.sum(chosen, axis=1, keepdims=True)


def lanczos_rows(frac_ref, cols):
    row = iota((2 * SUB, cols), 0)
    tap = jnp.where(row < SUB, row, row - SUB)
    fraction = jnp.where(row < SUB, frac_ref[0, 1], frac_ref[0, 0])
    angles = jnp.pi * ((tap - 2).astype(jnp.float32) - fraction)
    third = angles / 3.0
    kernel = jnp.sin(angles) / angles * (jnp.sin(third) / third)
    kernel = jnp.where(tap < TAPS_DOWN, kernel, 0.0)
    across, down = kernel[:SUB], kernel[SUB:]
    across = across / jnp.sum(across, axis=0, keepdims=True)
    down = down / jnp.sum(down, axis=0, keepdims=True)
    return across, down


def combined_taps(row_ref, col_ref, mix_ref, lifted, base):
    taps, basis = row_ref.shape
    count, cols = base.shape[1:]
    half = taps // 2
    l, s = iota((cols, taps), 0), iota((cols, taps), 1)
    turned = ((s + l == half) | (s + l == half + cols)).astype(jnp.float32).astype(jnp.bfloat16)
    across = jnp.dot(turned, row_ref[...], preferred_element_type=jnp.float32)
    across = across.astype(jnp.bfloat16)
    lifted[0:1] = jnp.zeros((1, basis), jnp.float32)
    lifted[1:] = col_ref[...].astype(jnp.float32)
    down = lifted[...]
    scaled = jnp.concatenate([down * mix_ref[term] for term in range(3)], axis=0)
    high = scaled.astype(jnp.bfloat16)
    low = (scaled - high.astype(jnp.float32)).astype(jnp.bfloat16)
    found = lax.dot_general(
        jnp.concatenate([high, low], axis=0),
        across,
        (((1,), (1,)), ((), ())),
        preferred_element_type=jnp.float32,
    )
    found = found[: 3 * count] + found[3 * count :]
    lane = iota((count, cols), 1)
    lane = jnp.where(lane < cols // 2, lane, lane - cols).astype(jnp.float32)
    base[0] = found[:count] + (2.0 / cols) * lane * found[count : 2 * count]
    base[1] = found[count : 2 * count]
    base[2] = found[2 * count :]


def build_band(base, row, band, first):
    cols = base.shape[2]
    shape = (2 * SUB, cols)
    sub = iota(shape, 0)
    lane = iota(shape, 1)
    lane = jnp.where(lane < cols // 2, lane, lane - cols)
    first_u = (2.0 * sub.astype(jnp.float32) + 1.0) / cols - 1.0

    def spin(term):
        taps = jnp.broadcast_to(base[term, pl.ds(row, 1), :], shape)
        return pltpu.roll(taps, 0, 1, stride=1, stride_axis=0)

    slope = spin(1)
    level = spin(0) + first_u * slope
    rise = spin(2)
    whole = rise.astype(jnp.bfloat16)
    pairs = cols // (2 * SUB)
    for pair in range(pairs):
        shift = 2 * SUB * pair
        value = level + (2.0 * shift / cols) * slope
        other = whole
        if pair == 0 or pair == pairs - 1:
            inside = lane >= 0 if pair == 0 else lane < 2 * SUB
            value = jnp.where(inside, value, 0.0)
            other = jnp.where(inside, rise, 0.0).astype(jnp.bfloat16)
        value = value.astype(jnp.bfloat16)
        if pair:
            value, other = pltpu.roll(value, shift, 1), pltpu.roll(other, shift, 1)
        at = first + shift
        band[at : at + 2 * SUB, :] = jnp.concatenate([value, other], axis=1)


def place_of(owner, owners):
    slow = 1 << ((owners.bit_length() - 1) // 2)
    fast = owners // slow
    return (owner + fast // 2) % fast * slow + (owner // fast + 1) % slow


def group_edges(fold):
    return [0, fold // 8, fold // 2, fold]


def window_kernel(
    capacity,
    image_hbm,
    row_hbm,
    col_hbm,
    mix_hbm,
    weight_hbm,
    frac_hbm,
    block_hbm,
    offset_hbm,
    visit_ref,
    out_ref,
    image_ref,
    row_ref,
    col_ref,
    mix_ref,
    weight_ref,
    frac_ref,
    block_ref,
    offset_ref,
    copied,
    padded,
    lifted,
    base,
    band_a,
    band_b,
    blocks,
    total,
    spread,
    tile_of,
    starts,
    counts,
):
    rows, cols = image_ref.shape[1:]
    fold = row_ref.shape[0] // 2 + 1
    deep = rows // fold
    tiles = block_ref.shape[0]
    owners = out_ref.shape[0]
    data_rows = capacity * SUB
    owned = BLK_DEV * SUB

    pairs = (
        (row_hbm, row_ref),
        (col_hbm, col_ref),
        (mix_hbm, mix_ref),
        (image_hbm, image_ref),
        (frac_hbm, frac_ref),
        (weight_hbm, weight_ref),
        (block_hbm, block_ref),
        (offset_hbm, offset_ref),
    )
    copies = [
        pltpu.make_async_copy(source, target, copied.at[index])
        for index, (source, target) in enumerate(pairs)
    ]
    for copy in copies:
        copy.start()

    @pl.loop(0, owners)
    def _(owner):
        counts[owner] = 0

    if owners * capacity > tiles:

        @pl.loop(0, owners * capacity)
        def _(slot):
            starts[slot] = EMPTY
            tile_of[slot] = 0

    padded[:fold] = jnp.zeros((fold, cols), jnp.float32)
    padded[fold + rows :] = jnp.zeros((fold, cols), jnp.float32)
    spread[:SUB] = jnp.zeros((SUB, cols), jnp.float32)
    spread[SUB + rows :] = jnp.zeros((SUB, cols), jnp.float32)
    for copy in copies:
        copy.wait()

    combined_taps(row_ref, col_ref, mix_ref, lifted, base)
    padded[fold : fold + rows] = image_ref[0].astype(jnp.float32)
    across, down = lanczos_rows(frac_ref, cols)
    weight = weight_of(visit_ref, weight_ref)

    for index in range(3 * fold - 1):
        blocks[index * deep : (index + 1) * deep, :] = padded[
            pl.ds(index, deep, stride=fold), :
        ].astype(jnp.bfloat16)

    edges = group_edges(fold)
    groups = len(edges) - 1

    def build(group, band):
        for index, r in enumerate(range(edges[group], edges[group + 1])):
            for part in range(2):
                build_band(base, r + part * fold, band, (2 * index + part) * cols)

    def multiply(group, band):
        parts = []
        for r in range(edges[group], edges[group + 1]):
            for part in range(2):
                first = (r + part * fold) * deep
                parts.append(blocks[first : first + rows, :])
        product = jnp.dot(
            jnp.concatenate(parts, axis=1),
            band[: len(parts) * cols, :],
            preferred_element_type=jnp.float32,
        )
        total[...] = product if group == 0 else total[...] + product

    def assign(tile):
        block = block_ref[tile]
        owner = lax.div(block, BLK_DEV)
        rank = counts[owner]
        counts[owner] = rank + 1
        slot = owner * capacity + rank
        tile_of[slot] = tile
        starts[slot] = (block - owner * BLK_DEV) * SUB + offset_ref[tile]

    held = (band_a, band_b)
    build(0, held[0])
    for group in range(groups):
        if group + 1 < groups:
            build(group + 1, held[(group + 1) % 2])
        multiply(group, held[group % 2])
        for tile in range(group * tiles // groups, (group + 1) * tiles // groups):
            assign(tile)

    lane = iota((1, cols), 1)
    taps_across = [
        jnp.where((lane + m - 2 >= 0) & (lane + m - 2 < cols), across[m : m + 1], 0.0)
        for m in range(TAPS_DOWN)
    ]
    for phase in range(fold):
        first = phase * deep
        position = 2 * (fold * iota((deep, cols), 0) + phase) + 1
        position = position.astype(jnp.float32) / rows - 1.0
        both = total[first : first + deep, :]
        matched = both[:, :cols] + position * both[:, cols:]
        result = taps_across[2] * matched
        for m in range(TAPS_DOWN):
            if m != 2:
                result = result + taps_across[m] * pltpu.roll(matched, (2 - m) % cols, 1)
        spread[pl.ds(SUB + phase, deep, stride=fold), :] = result

    sub = iota((SUB, cols), 0)
    wide = iota((SUB, cols), 1)
    segment = wide >> (data_rows.bit_length() - 1)
    lane_row = wide & (SUB - 1)
    lane_slot = (wide >> 3) & (capacity - 1)
    spill_slot = wide & (capacity - 1)
    spill_row = wide >> (capacity.bit_length() - 1)
    tile_weight = jnp.broadcast_to(weight, (SUB, cols))

    def warped(slot):
        first = tile_of[slot] * SUB + SUB - 2
        result = down[0:1] * spread[pl.ds(first, SUB), :]
        for m in range(1, TAPS_DOWN):
            result = result + down[m : m + 1] * spread[pl.ds(first + m, SUB), :]
        return result

    def message(owner, carry):
        spilled, over = carry
        target = jnp.zeros((SUB, cols), jnp.int32)
        next_spilled = jnp.zeros((SUB, cols), jnp.float32)
        next_over = jnp.zeros((SUB, cols), jnp.float32)
        tiles_here = []
        for c in range(capacity):
            slot = owner * capacity + c
            start = starts[slot]
            past = start + SUB - owned
            tile = warped(slot)
            tiles_here.append(tile)
            target = jnp.where(lane_slot == c, start + lane_row, target)
            turned = pltpu.roll(tile, start & (SUB - 1), 0)
            next_spilled = next_spilled + jnp.where(sub < past, turned, 0.0)
            next_over = jnp.where((spill_slot == c) & (spill_row < past), tile_weight, next_over)
        meta = jnp.where(segment == 1, target.astype(jnp.float32), tile_weight)
        meta = jnp.where(segment == 0, over, meta)
        tail = jnp.where(sub == SUB - 1, meta, spilled * tile_weight)
        place = place_of(owner, owners)
        out_ref[place, :data_rows, :] = jnp.concatenate(tiles_here, axis=0).astype(jnp.bfloat16)
        out_ref[place, data_rows:, :] = tail.astype(jnp.bfloat16)
        return next_spilled, next_over

    nothing = jnp.zeros((SUB, cols), jnp.float32)
    lax.fori_loop(0, owners, message, (nothing, nothing), unroll=min(owners, 16))


def sky_kernel(capacity, got_ref, coadd_ref, map_ref):
    sources, message_rows, cols = got_ref.shape
    data_rows = capacity * SUB
    owned = coadd_ref.shape[0]
    per_chunk = cols // data_rows
    chunks = sources // per_chunk
    place = iota((chunks, cols), 0)
    wide = iota((chunks, cols), 1)
    row = iota((owned, cols), 0)
    spilled = jnp.zeros((SUB, cols), jnp.float32)
    target = jnp.zeros((chunks, cols), jnp.float32)
    weight = jnp.zeros((chunks, cols), jnp.float32)
    for k in range(per_chunk):
        heads = jnp.zeros((chunks, cols), jnp.float32)
        for chunk in range(chunks):
            tail = got_ref[chunk * per_chunk + k, data_rows:, :].astype(jnp.float32)
            spilled = spilled + tail
            heads = jnp.where(place == chunk, tail[SUB - 1 :], heads)
        here = (wide >= k * data_rows) & (wide < (k + 1) * data_rows)
        target = jnp.where(here, pltpu.roll(heads, (k - 1) * data_rows % cols, 1), target)
        weight = jnp.where(here, pltpu.roll(heads, (k - 2) * data_rows % cols, 1), weight)
    target = target.astype(jnp.int32)
    pieces = [
        jnp.where(row == target[chunk : chunk + 1], weight[chunk : chunk + 1], 0.0)
        for chunk in range(chunks)
    ]
    placement = jnp.concatenate(pieces, axis=1).astype(jnp.bfloat16)
    pixels = got_ref[:, :data_rows, :].reshape(sources * data_rows, cols)
    pixels = jnp.concatenate([pixels, jnp.ones(pixels.shape, jnp.bfloat16)], axis=1)
    sums = jnp.dot(placement, pixels, preferred_element_type=jnp.float32)
    sub = iota((SUB, cols), 0)
    wide = iota((SUB, cols), 1)
    last = sub == SUB - 1
    over = jnp.broadcast_to(spilled[SUB - 1 :], (SUB, cols))
    mine = ((wide >> (capacity.bit_length() - 1)) == sub) & ~last
    over = jnp.sum(jnp.where(mine, over, 0.0), axis=1, keepdims=True)
    rest = jnp.zeros((owned - SUB, cols), jnp.float32)
    pixel_sum = sums[:, :cols] + jnp.concatenate([jnp.where(last, 0.0, spilled), rest], axis=0)
    weight_sum = sums[:, cols:] + jnp.concatenate(
        [jnp.broadcast_to(over, (SUB, cols)), rest], axis=0
    )
    coadd_ref[...] = pixel_sum / jnp.maximum(weight_sum, 1.0)
    diagonal = jnp.where(row == iota((owned, cols), 1), weight_sum, 0.0)
    map_ref[...] = jnp.sum(diagonal, axis=0, keepdims=True)


def on_device(
    image,
    row_taps,
    col_taps,
    mix_coeff,
    shift_frac,
    ccd_visit,
    visit_weight,
    tile_block,
    tile_offset,
):
    rows, cols = image.shape[1:]
    tiles = tile_block.shape[0]
    sky = lax.axis_size("sky")
    capacity = max(2, tiles // sky)
    taps, basis = row_taps.shape[1], row_taps.shape[0]
    fold = taps // 2 + 1
    visits = visit_weight.shape[0]
    largest = max(b - a for a, b in itertools.pairwise(group_edges(fold)))
    anywhere = pl.BlockSpec(memory_space=pl.ANY)
    vmem = pl.BlockSpec(memory_space=pltpu.VMEM)
    messages = pl.pallas_call(
        functools.partial(window_kernel, capacity),
        out_shape=pltpu.VMEM((sky, capacity * SUB + SUB, cols), jnp.bfloat16),
        in_specs=[anywhere] * 8 + [pl.BlockSpec(memory_space=pltpu.SMEM)],
        out_specs=vmem,
        scratch_shapes=[
            pltpu.VMEM((1, rows, cols), jnp.bfloat16),
            pltpu.VMEM((taps, basis), jnp.bfloat16),
            pltpu.VMEM((taps, basis), jnp.bfloat16),
            pltpu.VMEM((3, 1, basis), jnp.float32),
            pltpu.VMEM((1, visits), jnp.bfloat16),
            pltpu.SMEM((1, 2), jnp.float32),
            pltpu.SMEM((tiles,), jnp.int32),
            pltpu.SMEM((tiles,), jnp.int32),
            pltpu.SemaphoreType.DMA((8,)),
            pltpu.VMEM((rows + 2 * fold, cols), jnp.float32),
            pltpu.VMEM((2 * fold, basis), jnp.float32),
            pltpu.VMEM((3, 2 * fold, cols), jnp.float32),
            pltpu.VMEM((largest * 2 * cols, 2 * cols), jnp.bfloat16),
            pltpu.VMEM((largest * 2 * cols, 2 * cols), jnp.bfloat16),
            pltpu.VMEM(((3 * fold - 1) * (rows // fold), cols), jnp.bfloat16),
            pltpu.VMEM((rows, 2 * cols), jnp.float32),
            pltpu.VMEM((rows + 2 * SUB, cols), jnp.float32),
            pltpu.SMEM((sky * capacity,), jnp.int32),
            pltpu.SMEM((sky * capacity,), jnp.int32),
            pltpu.SMEM((sky,), jnp.int32),
        ],
        compiler_params=pltpu.CompilerParams(vmem_limit_bytes=LARGE_VMEM),
        name="match_warp_pack",
    )(
        *[
            pltpu.with_memory_space_constraint(value, pltpu.HBM)
            for value in (
                image,
                row_taps.T,
                col_taps.T,
                mix_coeff.transpose(1, 0, 2),
                visit_weight.reshape(1, -1),
                shift_frac,
                tile_block,
                tile_offset,
            )
        ],
        ccd_visit,
    )
    order = sorted(range(sky), key=lambda owner: place_of(owner, sky))
    received = lax.all_to_all(
        messages, "sky", split_axis=0, concat_axis=0, axis_index_groups=[order], tiled=True
    )
    coadd, weight_map = pl.pallas_call(
        functools.partial(sky_kernel, capacity),
        out_shape=(
            jax.ShapeDtypeStruct((BLK_DEV * SUB, cols), jnp.float32),
            jax.ShapeDtypeStruct((1, BLK_DEV * SUB), jnp.float32),
        ),
        in_specs=[vmem],
        out_specs=(vmem, vmem),
        compiler_params=pltpu.CompilerParams(vmem_limit_bytes=SMALL_VMEM),
        name="place_normalise",
    )(received)
    return coadd, weight_map.reshape(-1)


def solution(mesh):
    return jax.shard_map(
        on_device,
        mesh=mesh,
        in_specs=(
            P(("groups", "sky"), None, None),
            P(),
            P(),
            P(("groups", "sky"), None, None),
            P(("groups", "sky"), None),
            P(("groups", "sky")),
            P("groups"),
            P(("groups", "sky")),
            P(("groups", "sky")),
        ),
        out_specs=(P(("groups", "sky"), None), P(("groups", "sky"))),
        check_vma=False,
    )
```

```python
import functools
import itertools

import jax
import jax.numpy as jnp
from jax import lax
from jax.experimental import pallas as pl
from jax.experimental.pallas import tpu as pltpu
from jax.sharding import PartitionSpec as P

BLK_DEV = 16
SUB = 8
LARGE_VMEM = 32 * 1024 * 1024
SMALL_VMEM = 16 * 1024 * 1024
EMPTY = -64
TAPS_DOWN = 6


def iota(shape, axis):
    return lax.broadcasted_iota(jnp.int32, shape, axis)


def weight_of(visit_ref, weight_ref):
    values = weight_ref[...].astype(jnp.float32)
    chosen = jnp.where(iota(values.shape, 1) == visit_ref[0], values, 0.0)
    return jnp.sum(chosen, axis=1, keepdims=True)


def lanczos_rows(frac_ref, cols):
    row = iota((2 * SUB, cols), 0)
    tap = jnp.where(row < SUB, row, row - SUB)
    fraction = jnp.where(row < SUB, frac_ref[0, 1], frac_ref[0, 0])
    angles = jnp.pi * ((tap - 2).astype(jnp.float32) - fraction)
    third = angles / 3.0
    kernel = jnp.sin(angles) / angles * (jnp.sin(third) / third)
    kernel = jnp.where(tap < TAPS_DOWN, kernel, 0.0)
    across, down = kernel[:SUB], kernel[SUB:]
    across = across / jnp.sum(across, axis=0, keepdims=True)
    down = down / jnp.sum(down, axis=0, keepdims=True)
    return across, down


def combined_taps(row_ref, col_ref, mix_ref, lifted, base):
    taps, basis = row_ref.shape
    count, cols = base.shape[1:]
    half = taps // 2
    l, s = iota((cols, taps), 0), iota((cols, taps), 1)
    turned = ((s + l == half) | (s + l == half + cols)).astype(jnp.float32).astype(jnp.bfloat16)
    across = jnp.dot(turned, row_ref[...], preferred_element_type=jnp.float32)
    across = across.astype(jnp.bfloat16)
    lifted[0:1] = jnp.zeros((1, basis), jnp.float32)
    lifted[1:] = col_ref[...].astype(jnp.float32)
    down = lifted[...]
    scaled = jnp.concatenate([down * mix_ref[term] for term in range(3)], axis=0)
    high = scaled.astype(jnp.bfloat16)
    low = (scaled - high.astype(jnp.float32)).astype(jnp.bfloat16)
    found = lax.dot_general(
        jnp.concatenate([high, low], axis=0),
        across,
        (((1,), (1,)), ((), ())),
        preferred_element_type=jnp.float32,
    )
    found = found[: 3 * count] + found[3 * count :]
    lane = iota((count, cols), 1)
    lane = jnp.where(lane < cols // 2, lane, lane - cols).astype(jnp.float32)
    base[0] = found[:count] + (2.0 / cols) * lane * found[count : 2 * count]
    base[1] = found[count : 2 * count]
    base[2] = found[2 * count :]


def build_band(base, row, band, first):
    cols = base.shape[2]
    shape = (2 * SUB, cols)
    sub = iota(shape, 0)
    lane = iota(shape, 1)
    lane = jnp.where(lane < cols // 2, lane, lane - cols)
    first_u = (2.0 * sub.astype(jnp.float32) + 1.0) / cols - 1.0

    def spin(term):
        taps = jnp.broadcast_to(base[term, pl.ds(row, 1), :], shape)
        return pltpu.roll(taps, 0, 1, stride=1, stride_axis=0)

    slope = spin(1)
    level = spin(0) + first_u * slope
    rise = spin(2)
    whole = rise.astype(jnp.bfloat16)
    pairs = cols // (2 * SUB)
    for pair in range(pairs):
        shift = 2 * SUB * pair
        value = level + (2.0 * shift / cols) * slope
        other = whole
        if pair == 0 or pair == pairs - 1:
            inside = lane >= 0 if pair == 0 else lane < 2 * SUB
            value = jnp.where(inside, value, 0.0)
            other = jnp.where(inside, rise, 0.0).astype(jnp.bfloat16)
        value = value.astype(jnp.bfloat16)
        if pair:
            value, other = pltpu.roll(value, shift, 1), pltpu.roll(other, shift, 1)
        at = first + shift
        band[at : at + 2 * SUB, :] = jnp.concatenate([value, other], axis=1)


def place_of(owner, owners):
    slow = 1 << ((owners.bit_length() - 1) // 2)
    fast = owners // slow
    return (owner + fast // 2) % fast * slow + (owner // fast + slow // 2) % slow


def group_edges(fold):
    return [0, fold // 8, fold // 2, fold]


def window_kernel(
    capacity,
    image_hbm,
    row_hbm,
    col_hbm,
    mix_hbm,
    weight_hbm,
    frac_hbm,
    block_hbm,
    offset_hbm,
    visit_ref,
    out_ref,
    image_ref,
    row_ref,
    col_ref,
    mix_ref,
    weight_ref,
    frac_ref,
    block_ref,
    offset_ref,
    copied,
    padded,
    lifted,
    base,
    band_a,
    band_b,
    blocks,
    total,
    spread,
    tile_of,
    starts,
    counts,
):
    rows, cols = image_ref.shape[1:]
    fold = row_ref.shape[0] // 2 + 1
    deep = rows // fold
    tiles = block_ref.shape[0]
    owners = out_ref.shape[0]
    data_rows = capacity * SUB
    owned = BLK_DEV * SUB

    pairs = (
        (row_hbm, row_ref),
        (col_hbm, col_ref),
        (mix_hbm, mix_ref),
        (image_hbm, image_ref),
        (frac_hbm, frac_ref),
        (weight_hbm, weight_ref),
        (block_hbm, block_ref),
        (offset_hbm, offset_ref),
    )
    copies = [
        pltpu.make_async_copy(source, target, copied.at[index])
        for index, (source, target) in enumerate(pairs)
    ]
    for copy in copies:
        copy.start()

    @pl.loop(0, owners)
    def _(owner):
        counts[owner] = 0

    if owners * capacity > tiles:

        @pl.loop(0, owners * capacity)
        def _(slot):
            starts[slot] = EMPTY
            tile_of[slot] = 0

    padded[:fold] = jnp.zeros((fold, cols), jnp.float32)
    padded[fold + rows :] = jnp.zeros((fold, cols), jnp.float32)
    spread[:SUB] = jnp.zeros((SUB, cols), jnp.float32)
    spread[SUB + rows :] = jnp.zeros((SUB, cols), jnp.float32)
    for copy in copies:
        copy.wait()

    combined_taps(row_ref, col_ref, mix_ref, lifted, base)
    padded[fold : fold + rows] = image_ref[0].astype(jnp.float32)
    across, down = lanczos_rows(frac_ref, cols)
    weight = weight_of(visit_ref, weight_ref)

    for index in range(3 * fold - 1):
        blocks[index * deep : (index + 1) * deep, :] = padded[
            pl.ds(index, deep, stride=fold), :
        ].astype(jnp.bfloat16)

    edges = group_edges(fold)
    groups = len(edges) - 1

    def build(group, band):
        for index, r in enumerate(range(edges[group], edges[group + 1])):
            for part in range(2):
                build_band(base, r + part * fold, band, (2 * index + part) * cols)

    def multiply(group, band):
        parts = []
        for r in range(edges[group], edges[group + 1]):
            for part in range(2):
                first = (r + part * fold) * deep
                parts.append(blocks[first : first + rows, :])
        product = jnp.dot(
            jnp.concatenate(parts, axis=1),
            band[: len(parts) * cols, :],
            preferred_element_type=jnp.float32,
        )
        total[...] = product if group == 0 else total[...] + product

    def assign(tile):
        block = block_ref[tile]
        owner = lax.div(block, BLK_DEV)
        rank = counts[owner]
        counts[owner] = rank + 1
        slot = owner * capacity + rank
        tile_of[slot] = tile
        starts[slot] = (block - owner * BLK_DEV) * SUB + offset_ref[tile]

    held = (band_a, band_b)
    build(0, held[0])
    for group in range(groups):
        if group + 1 < groups:
            build(group + 1, held[(group + 1) % 2])
        multiply(group, held[group % 2])
        for tile in range(group * tiles // groups, (group + 1) * tiles // groups):
            assign(tile)

    lane = iota((1, cols), 1)
    taps_across = [
        jnp.where((lane + m - 2 >= 0) & (lane + m - 2 < cols), across[m : m + 1], 0.0)
        for m in range(TAPS_DOWN)
    ]
    for phase in range(fold):
        first = phase * deep
        position = 2 * (fold * iota((deep, cols), 0) + phase) + 1
        position = position.astype(jnp.float32) / rows - 1.0
        both = total[first : first + deep, :]
        matched = both[:, :cols] + position * both[:, cols:]
        result = taps_across[2] * matched
        for m in range(TAPS_DOWN):
            if m != 2:
                result = result + taps_across[m] * pltpu.roll(matched, (2 - m) % cols, 1)
        spread[pl.ds(SUB + phase, deep, stride=fold), :] = result

    sub = iota((SUB, cols), 0)
    wide = iota((SUB, cols), 1)
    segment = wide >> (data_rows.bit_length() - 1)
    lane_row = wide & (SUB - 1)
    lane_slot = (wide >> 3) & (capacity - 1)
    spill_slot = wide & (capacity - 1)
    spill_row = wide >> (capacity.bit_length() - 1)
    tile_weight = jnp.broadcast_to(weight, (SUB, cols))

    def warped(slot):
        first = tile_of[slot] * SUB + SUB - 2
        result = down[0:1] * spread[pl.ds(first, SUB), :]
        for m in range(1, TAPS_DOWN):
            result = result + down[m : m + 1] * spread[pl.ds(first + m, SUB), :]
        return result

    def message(owner, carry):
        spilled, over = carry
        target = jnp.zeros((SUB, cols), jnp.int32)
        next_spilled = jnp.zeros((SUB, cols), jnp.float32)
        next_over = jnp.zeros((SUB, cols), jnp.float32)
        tiles_here = []
        for c in range(capacity):
            slot = owner * capacity + c
            start = starts[slot]
            past = start + SUB - owned
            tile = warped(slot)
            tiles_here.append(tile)
            target = jnp.where(lane_slot == c, start + lane_row, target)
            turned = pltpu.roll(tile, start & (SUB - 1), 0)
            next_spilled = next_spilled + jnp.where(sub < past, turned, 0.0)
            next_over = jnp.where((spill_slot == c) & (spill_row < past), tile_weight, next_over)
        meta = jnp.where(segment == 1, target.astype(jnp.float32), tile_weight)
        meta = jnp.where(segment == 0, over, meta)
        tail = jnp.where(sub == SUB - 1, meta, spilled * tile_weight)
        place = place_of(owner, owners)
        out_ref[place, :data_rows, :] = jnp.concatenate(tiles_here, axis=0).astype(jnp.bfloat16)
        out_ref[place, data_rows:, :] = tail.astype(jnp.bfloat16)
        return next_spilled, next_over

    nothing = jnp.zeros((SUB, cols), jnp.float32)
    lax.fori_loop(0, owners, message, (nothing, nothing), unroll=min(owners, 16))


def sky_kernel(capacity, got_ref, coadd_ref, map_ref):
    sources, message_rows, cols = got_ref.shape
    data_rows = capacity * SUB
    owned = coadd_ref.shape[0]
    per_chunk = cols // data_rows
    chunks = sources // per_chunk
    place = iota((chunks, cols), 0)
    wide = iota((chunks, cols), 1)
    row = iota((owned, cols), 0)
    spilled = jnp.zeros((SUB, cols), jnp.float32)
    target = jnp.zeros((chunks, cols), jnp.float32)
    weight = jnp.zeros((chunks, cols), jnp.float32)
    for k in range(per_chunk):
        heads = jnp.zeros((chunks, cols), jnp.float32)
        for chunk in range(chunks):
            tail = got_ref[chunk * per_chunk + k, data_rows:, :].astype(jnp.float32)
            spilled = spilled + tail
            heads = jnp.where(place == chunk, tail[SUB - 1 :], heads)
        here = (wide >= k * data_rows) & (wide < (k + 1) * data_rows)
        target = jnp.where(here, pltpu.roll(heads, (k - 1) * data_rows % cols, 1), target)
        weight = jnp.where(here, pltpu.roll(heads, (k - 2) * data_rows % cols, 1), weight)
    target = target.astype(jnp.int32)
    pieces = [
        jnp.where(row == target[chunk : chunk + 1], weight[chunk : chunk + 1], 0.0)
        for chunk in range(chunks)
    ]
    placement = jnp.concatenate(pieces, axis=1).astype(jnp.bfloat16)
    pixels = got_ref[:, :data_rows, :].reshape(sources * data_rows, cols)
    pixels = jnp.concatenate([pixels, jnp.ones(pixels.shape, jnp.bfloat16)], axis=1)
    sums = jnp.dot(placement, pixels, preferred_element_type=jnp.float32)
    sub = iota((SUB, cols), 0)
    wide = iota((SUB, cols), 1)
    last = sub == SUB - 1
    over = jnp.broadcast_to(spilled[SUB - 1 :], (SUB, cols))
    mine = ((wide >> (capacity.bit_length() - 1)) == sub) & ~last
    over = jnp.sum(jnp.where(mine, over, 0.0), axis=1, keepdims=True)
    rest = jnp.zeros((owned - SUB, cols), jnp.float32)
    pixel_sum = sums[:, :cols] + jnp.concatenate([jnp.where(last, 0.0, spilled), rest], axis=0)
    weight_sum = sums[:, cols:] + jnp.concatenate(
        [jnp.broadcast_to(over, (SUB, cols)), rest], axis=0
    )
    coadd_ref[...] = pixel_sum / jnp.maximum(weight_sum, 1.0)
    diagonal = jnp.where(row == iota((owned, cols), 1), weight_sum, 0.0)
    map_ref[...] = jnp.sum(diagonal, axis=0, keepdims=True)


def on_device(
    image,
    row_taps,
    col_taps,
    mix_coeff,
    shift_frac,
    ccd_visit,
    visit_weight,
    tile_block,
    tile_offset,
):
    rows, cols = image.shape[1:]
    tiles = tile_block.shape[0]
    sky = lax.axis_size("sky")
    capacity = max(2, tiles // sky)
    taps, basis = row_taps.shape[1], row_taps.shape[0]
    fold = taps // 2 + 1
    visits = visit_weight.shape[0]
    largest = max(b - a for a, b in itertools.pairwise(group_edges(fold)))
    anywhere = pl.BlockSpec(memory_space=pl.ANY)
    vmem = pl.BlockSpec(memory_space=pltpu.VMEM)
    messages = pl.pallas_call(
        functools.partial(window_kernel, capacity),
        out_shape=pltpu.VMEM((sky, capacity * SUB + SUB, cols), jnp.bfloat16),
        in_specs=[anywhere] * 8 + [pl.BlockSpec(memory_space=pltpu.SMEM)],
        out_specs=vmem,
        scratch_shapes=[
            pltpu.VMEM((1, rows, cols), jnp.bfloat16),
            pltpu.VMEM((taps, basis), jnp.bfloat16),
            pltpu.VMEM((taps, basis), jnp.bfloat16),
            pltpu.VMEM((3, 1, basis), jnp.float32),
            pltpu.VMEM((1, visits), jnp.bfloat16),
            pltpu.SMEM((1, 2), jnp.float32),
            pltpu.SMEM((tiles,), jnp.int32),
            pltpu.SMEM((tiles,), jnp.int32),
            pltpu.SemaphoreType.DMA((8,)),
            pltpu.VMEM((rows + 2 * fold, cols), jnp.float32),
            pltpu.VMEM((2 * fold, basis), jnp.float32),
            pltpu.VMEM((3, 2 * fold, cols), jnp.float32),
            pltpu.VMEM((largest * 2 * cols, 2 * cols), jnp.bfloat16),
            pltpu.VMEM((largest * 2 * cols, 2 * cols), jnp.bfloat16),
            pltpu.VMEM(((3 * fold - 1) * (rows // fold), cols), jnp.bfloat16),
            pltpu.VMEM((rows, 2 * cols), jnp.float32),
            pltpu.VMEM((rows + 2 * SUB, cols), jnp.float32),
            pltpu.SMEM((sky * capacity,), jnp.int32),
            pltpu.SMEM((sky * capacity,), jnp.int32),
            pltpu.SMEM((sky,), jnp.int32),
        ],
        compiler_params=pltpu.CompilerParams(vmem_limit_bytes=LARGE_VMEM),
        name="match_warp_pack",
    )(
        *[
            pltpu.with_memory_space_constraint(value, pltpu.HBM)
            for value in (
                image,
                row_taps.T,
                col_taps.T,
                mix_coeff.transpose(1, 0, 2),
                visit_weight.reshape(1, -1),
                shift_frac,
                tile_block,
                tile_offset,
            )
        ],
        ccd_visit,
    )
    order = sorted(range(sky), key=lambda owner: place_of(owner, sky))
    received = lax.all_to_all(
        messages, "sky", split_axis=0, concat_axis=0, axis_index_groups=[order], tiled=True
    )
    coadd, weight_map = pl.pallas_call(
        functools.partial(sky_kernel, capacity),
        out_shape=(
            jax.ShapeDtypeStruct((BLK_DEV * SUB, cols), jnp.float32),
            jax.ShapeDtypeStruct((1, BLK_DEV * SUB), jnp.float32),
        ),
        in_specs=[vmem],
        out_specs=(vmem, vmem),
        compiler_params=pltpu.CompilerParams(vmem_limit_bytes=SMALL_VMEM),
        name="place_normalise",
    )(received)
    return coadd, weight_map.reshape(-1)


def solution(mesh):
    return jax.shard_map(
        on_device,
        mesh=mesh,
        in_specs=(
            P(("groups", "sky"), None, None),
            P(),
            P(),
            P(("groups", "sky"), None, None),
            P(("groups", "sky"), None),
            P(("groups", "sky")),
            P("groups"),
            P(("groups", "sky")),
            P(("groups", "sky")),
        ),
        out_specs=(P(("groups", "sky"), None), P(("groups", "sky"))),
        check_vma=False,
    )
```

```python
import functools
import itertools

import jax
import jax.numpy as jnp
from jax import lax
from jax.experimental import pallas as pl
from jax.experimental.pallas import tpu as pltpu
from jax.sharding import PartitionSpec as P

BLK_DEV = 16
SUB = 8
LARGE_VMEM = 32 * 1024 * 1024
SMALL_VMEM = 16 * 1024 * 1024
EMPTY = -64
TAPS_DOWN = 6


def iota(shape, axis):
    return lax.broadcasted_iota(jnp.int32, shape, axis)


def weight_of(visit_ref, weight_ref):
    values = weight_ref[...].astype(jnp.float32)
    chosen = jnp.where(iota(values.shape, 1) == visit_ref[0], values, 0.0)
    return jnp.sum(chosen, axis=1, keepdims=True)


def lanczos_rows(frac_ref, cols):
    row = iota((2 * SUB, cols), 0)
    tap = jnp.where(row < SUB, row, row - SUB)
    fraction = jnp.where(row < SUB, frac_ref[0, 1], frac_ref[0, 0])
    angles = jnp.pi * ((tap - 2).astype(jnp.float32) - fraction)
    third = angles / 3.0
    kernel = jnp.sin(angles) / angles * (jnp.sin(third) / third)
    kernel = jnp.where(tap < TAPS_DOWN, kernel, 0.0)
    across, down = kernel[:SUB], kernel[SUB:]
    across = across / jnp.sum(across, axis=0, keepdims=True)
    down = down / jnp.sum(down, axis=0, keepdims=True)
    return across, down


def combined_taps(row_ref, col_ref, mix_ref, turned, lifted, base):
    taps, basis = row_ref.shape
    count, cols = base.shape[1:]
    half = taps // 2
    rows = row_ref[...].astype(jnp.float32)
    for tap in range(taps):
        turned[(half - tap) % cols, :] = rows[tap]
    across = turned[...].astype(jnp.bfloat16)
    lifted[0:1] = jnp.zeros((1, basis), jnp.float32)
    lifted[1:] = col_ref[...].astype(jnp.float32)
    down = lifted[...]
    scaled = jnp.concatenate([down * mix_ref[term] for term in range(3)], axis=0)
    high = scaled.astype(jnp.bfloat16)
    low = (scaled - high.astype(jnp.float32)).astype(jnp.bfloat16)
    found = lax.dot_general(
        jnp.concatenate([high, low], axis=0),
        across,
        (((1,), (1,)), ((), ())),
        preferred_element_type=jnp.float32,
    )
    found = found[: 3 * count] + found[3 * count :]
    lane = iota((count, cols), 1)
    lane = jnp.where(lane < cols // 2, lane, lane - cols).astype(jnp.float32)
    base[0] = found[:count] + (2.0 / cols) * lane * found[count : 2 * count]
    base[1] = found[count : 2 * count]
    base[2] = found[2 * count :]


def build_band(base, row, band, first):
    cols = base.shape[2]
    shape = (2 * SUB, cols)
    sub = iota(shape, 0)
    lane = iota(shape, 1)
    lane = jnp.where(lane < cols // 2, lane, lane - cols)
    first_u = (2.0 * sub.astype(jnp.float32) + 1.0) / cols - 1.0

    def spin(term):
        taps = jnp.broadcast_to(base[term, pl.ds(row, 1), :], shape)
        return pltpu.roll(taps, 0, 1, stride=1, stride_axis=0)

    slope = spin(1)
    level = spin(0) + first_u * slope
    rise = spin(2)
    whole = rise.astype(jnp.bfloat16)
    pairs = cols // (2 * SUB)
    for pair in range(pairs):
        shift = 2 * SUB * pair
        value = level + (2.0 * shift / cols) * slope
        other = whole
        if pair == 0 or pair == pairs - 1:
            inside = lane >= 0 if pair == 0 else lane < 2 * SUB
            value = jnp.where(inside, value, 0.0)
            other = jnp.where(inside, rise, 0.0).astype(jnp.bfloat16)
        value = value.astype(jnp.bfloat16)
        if pair:
            value, other = pltpu.roll(value, shift, 1), pltpu.roll(other, shift, 1)
        at = first + shift
        band[at : at + 2 * SUB, :] = jnp.concatenate([value, other], axis=1)


def place_of(owner, owners):
    slow = 1 << ((owners.bit_length() - 1) // 2)
    fast = owners // slow
    return (owner + fast // 2) % fast * slow + (owner // fast + slow // 2) % slow


def group_edges(fold):
    return [0, fold // 8, fold // 2, fold]


def window_kernel(
    capacity,
    image_hbm,
    row_hbm,
    col_hbm,
    mix_hbm,
    weight_hbm,
    frac_hbm,
    block_hbm,
    offset_hbm,
    visit_ref,
    out_ref,
    image_ref,
    row_ref,
    col_ref,
    mix_ref,
    weight_ref,
    frac_ref,
    block_ref,
    offset_ref,
    copied,
    padded,
    turned,
    lifted,
    base,
    band_a,
    band_b,
    blocks,
    total,
    spread,
    tile_of,
    starts,
    counts,
):
    rows, cols = image_ref.shape[1:]
    fold = row_ref.shape[0] // 2 + 1
    deep = rows // fold
    tiles = block_ref.shape[0]
    owners = out_ref.shape[0]
    data_rows = capacity * SUB
    owned = BLK_DEV * SUB

    pairs = (
        (row_hbm, row_ref),
        (col_hbm, col_ref),
        (mix_hbm, mix_ref),
        (image_hbm, image_ref),
        (frac_hbm, frac_ref),
        (weight_hbm, weight_ref),
        (block_hbm, block_ref),
        (offset_hbm, offset_ref),
    )
    copies = [
        pltpu.make_async_copy(source, target, copied.at[index])
        for index, (source, target) in enumerate(pairs)
    ]
    for copy in copies:
        copy.start()

    @pl.loop(0, owners)
    def _(owner):
        counts[owner] = 0

    if owners * capacity > tiles:

        @pl.loop(0, owners * capacity)
        def _(slot):
            starts[slot] = EMPTY
            tile_of[slot] = 0

    padded[:fold] = jnp.zeros((fold, cols), jnp.float32)
    padded[fold + rows :] = jnp.zeros((fold, cols), jnp.float32)
    spread[:SUB] = jnp.zeros((SUB, cols), jnp.float32)
    spread[SUB + rows :] = jnp.zeros((SUB, cols), jnp.float32)
    turned[...] = jnp.zeros(turned.shape, jnp.float32)
    for copy in copies[:4]:
        copy.wait()

    combined_taps(row_ref, col_ref, mix_ref, turned, lifted, base)
    padded[fold : fold + rows] = image_ref[0].astype(jnp.float32)

    for index in range(3 * fold - 1):
        blocks[index * deep : (index + 1) * deep, :] = padded[
            pl.ds(index, deep, stride=fold), :
        ].astype(jnp.bfloat16)

    for copy in copies[4:]:
        copy.wait()
    across, down = lanczos_rows(frac_ref, cols)
    weight = weight_of(visit_ref, weight_ref)

    edges = group_edges(fold)
    groups = len(edges) - 1

    def build(group, band):
        for index, r in enumerate(range(edges[group], edges[group + 1])):
            for part in range(2):
                build_band(base, r + part * fold, band, (2 * index + part) * cols)

    def multiply(group, band):
        parts = []
        for r in range(edges[group], edges[group + 1]):
            for part in range(2):
                first = (r + part * fold) * deep
                parts.append(blocks[first : first + rows, :])
        product = jnp.dot(
            jnp.concatenate(parts, axis=1),
            band[: len(parts) * cols, :],
            preferred_element_type=jnp.float32,
        )
        total[...] = product if group == 0 else total[...] + product

    def assign(tile):
        block = block_ref[tile]
        owner = lax.div(block, BLK_DEV)
        rank = counts[owner]
        counts[owner] = rank + 1
        slot = owner * capacity + rank
        tile_of[slot] = tile
        starts[slot] = (block - owner * BLK_DEV) * SUB + offset_ref[tile]

    held = (band_a, band_b)
    build(0, held[0])
    for group in range(groups):
        if group + 1 < groups:
            build(group + 1, held[(group + 1) % 2])
        multiply(group, held[group % 2])
        for tile in range(group * tiles // groups, (group + 1) * tiles // groups):
            assign(tile)

    lane = iota((1, cols), 1)
    taps_across = [
        jnp.where((lane + m - 2 >= 0) & (lane + m - 2 < cols), across[m : m + 1], 0.0)
        for m in range(TAPS_DOWN)
    ]
    for phase in range(fold):
        first = phase * deep
        position = 2 * (fold * iota((deep, cols), 0) + phase) + 1
        position = position.astype(jnp.float32) / rows - 1.0
        both = total[first : first + deep, :]
        matched = both[:, :cols] + position * both[:, cols:]
        result = taps_across[2] * matched
        for m in range(TAPS_DOWN):
            if m != 2:
                result = result + taps_across[m] * pltpu.roll(matched, (2 - m) % cols, 1)
        spread[pl.ds(SUB + phase, deep, stride=fold), :] = result

    sub = iota((SUB, cols), 0)
    wide = iota((SUB, cols), 1)
    segment = wide >> (data_rows.bit_length() - 1)
    lane_row = wide & (SUB - 1)
    lane_slot = (wide >> 3) & (capacity - 1)
    spill_slot = wide & (capacity - 1)
    spill_row = wide >> (capacity.bit_length() - 1)
    tile_weight = jnp.broadcast_to(weight, (SUB, cols))

    def warped(slot):
        first = tile_of[slot] * SUB + SUB - 2
        result = down[0:1] * spread[pl.ds(first, SUB), :]
        for m in range(1, TAPS_DOWN):
            result = result + down[m : m + 1] * spread[pl.ds(first + m, SUB), :]
        return result

    def message(owner, carry):
        spilled, over = carry
        target = jnp.zeros((SUB, cols), jnp.int32)
        next_spilled = jnp.zeros((SUB, cols), jnp.float32)
        next_over = jnp.zeros((SUB, cols), jnp.float32)
        tiles_here = []
        for c in range(capacity):
            slot = owner * capacity + c
            start = starts[slot]
            past = start + SUB - owned
            tile = warped(slot)
            tiles_here.append(tile)
            target = jnp.where(lane_slot == c, start + lane_row, target)
            turned = pltpu.roll(tile, start & (SUB - 1), 0)
            next_spilled = next_spilled + jnp.where(sub < past, turned, 0.0)
            next_over = jnp.where((spill_slot == c) & (spill_row < past), tile_weight, next_over)
        meta = jnp.where(segment == 1, target.astype(jnp.float32), tile_weight)
        meta = jnp.where(segment == 0, over, meta)
        tail = jnp.where(sub == SUB - 1, meta, spilled * tile_weight)
        place = place_of(owner, owners)
        out_ref[place, :data_rows, :] = jnp.concatenate(tiles_here, axis=0).astype(jnp.bfloat16)
        out_ref[place, data_rows:, :] = tail.astype(jnp.bfloat16)
        return next_spilled, next_over

    nothing = jnp.zeros((SUB, cols), jnp.float32)
    lax.fori_loop(0, owners, message, (nothing, nothing), unroll=min(owners, 16))


def sky_kernel(capacity, got_ref, coadd_ref, map_ref):
    sources, message_rows, cols = got_ref.shape
    data_rows = capacity * SUB
    owned = coadd_ref.shape[0]
    per_chunk = cols // data_rows
    chunks = sources // per_chunk
    place = iota((chunks, cols), 0)
    wide = iota((chunks, cols), 1)
    row = iota((owned, cols), 0)
    spilled = jnp.zeros((SUB, cols), jnp.float32)
    target = jnp.zeros((chunks, cols), jnp.float32)
    weight = jnp.zeros((chunks, cols), jnp.float32)
    for k in range(per_chunk):
        heads = jnp.zeros((chunks, cols), jnp.float32)
        for chunk in range(chunks):
            tail = got_ref[chunk * per_chunk + k, data_rows:, :].astype(jnp.float32)
            spilled = spilled + tail
            heads = jnp.where(place == chunk, tail[SUB - 1 :], heads)
        here = (wide >= k * data_rows) & (wide < (k + 1) * data_rows)
        target = jnp.where(here, pltpu.roll(heads, (k - 1) * data_rows % cols, 1), target)
        weight = jnp.where(here, pltpu.roll(heads, (k - 2) * data_rows % cols, 1), weight)
    target = target.astype(jnp.int32)
    pieces = [
        jnp.where(row == target[chunk : chunk + 1], weight[chunk : chunk + 1], 0.0)
        for chunk in range(chunks)
    ]
    placement = jnp.concatenate(pieces, axis=1).astype(jnp.bfloat16)
    pixels = got_ref[:, :data_rows, :].reshape(sources * data_rows, cols)
    pixels = jnp.concatenate([pixels, jnp.ones(pixels.shape, jnp.bfloat16)], axis=1)
    sums = jnp.dot(placement, pixels, preferred_element_type=jnp.float32)
    sub = iota((SUB, cols), 0)
    wide = iota((SUB, cols), 1)
    last = sub == SUB - 1
    over = jnp.broadcast_to(spilled[SUB - 1 :], (SUB, cols))
    mine = ((wide >> (capacity.bit_length() - 1)) == sub) & ~last
    over = jnp.sum(jnp.where(mine, over, 0.0), axis=1, keepdims=True)
    rest = jnp.zeros((owned - SUB, cols), jnp.float32)
    pixel_sum = sums[:, :cols] + jnp.concatenate([jnp.where(last, 0.0, spilled), rest], axis=0)
    weight_sum = sums[:, cols:] + jnp.concatenate(
        [jnp.broadcast_to(over, (SUB, cols)), rest], axis=0
    )
    coadd_ref[...] = pixel_sum / jnp.maximum(weight_sum, 1.0)
    diagonal = jnp.where(row == iota((owned, cols), 1), weight_sum, 0.0)
    map_ref[...] = jnp.sum(diagonal, axis=0, keepdims=True)


def on_device(
    image,
    row_taps,
    col_taps,
    mix_coeff,
    shift_frac,
    ccd_visit,
    visit_weight,
    tile_block,
    tile_offset,
):
    rows, cols = image.shape[1:]
    tiles = tile_block.shape[0]
    sky = lax.axis_size("sky")
    capacity = max(2, tiles // sky)
    taps, basis = row_taps.shape[1], row_taps.shape[0]
    fold = taps // 2 + 1
    visits = visit_weight.shape[0]
    largest = max(b - a for a, b in itertools.pairwise(group_edges(fold)))
    anywhere = pl.BlockSpec(memory_space=pl.ANY)
    vmem = pl.BlockSpec(memory_space=pltpu.VMEM)
    messages = pl.pallas_call(
        functools.partial(window_kernel, capacity),
        out_shape=pltpu.VMEM((sky, capacity * SUB + SUB, cols), jnp.bfloat16),
        in_specs=[anywhere] * 8 + [pl.BlockSpec(memory_space=pltpu.SMEM)],
        out_specs=vmem,
        scratch_shapes=[
            pltpu.VMEM((1, rows, cols), jnp.bfloat16),
            pltpu.VMEM((taps, basis), jnp.bfloat16),
            pltpu.VMEM((taps, basis), jnp.bfloat16),
            pltpu.VMEM((3, 1, basis), jnp.float32),
            pltpu.VMEM((1, visits), jnp.bfloat16),
            pltpu.SMEM((1, 2), jnp.float32),
            pltpu.SMEM((tiles,), jnp.int32),
            pltpu.SMEM((tiles,), jnp.int32),
            pltpu.SemaphoreType.DMA((8,)),
            pltpu.VMEM((rows + 2 * fold, cols), jnp.float32),
            pltpu.VMEM((cols, basis), jnp.float32),
            pltpu.VMEM((2 * fold, basis), jnp.float32),
            pltpu.VMEM((3, 2 * fold, cols), jnp.float32),
            pltpu.VMEM((largest * 2 * cols, 2 * cols), jnp.bfloat16),
            pltpu.VMEM((largest * 2 * cols, 2 * cols), jnp.bfloat16),
            pltpu.VMEM(((3 * fold - 1) * (rows // fold), cols), jnp.bfloat16),
            pltpu.VMEM((rows, 2 * cols), jnp.float32),
            pltpu.VMEM((rows + 2 * SUB, cols), jnp.float32),
            pltpu.SMEM((sky * capacity,), jnp.int32),
            pltpu.SMEM((sky * capacity,), jnp.int32),
            pltpu.SMEM((sky,), jnp.int32),
        ],
        compiler_params=pltpu.CompilerParams(vmem_limit_bytes=LARGE_VMEM),
        name="match_warp_pack",
    )(
        *[
            pltpu.with_memory_space_constraint(value, pltpu.HBM)
            for value in (
                image,
                row_taps.T,
                col_taps.T,
                mix_coeff.transpose(1, 0, 2),
                visit_weight.reshape(1, -1),
                shift_frac,
                tile_block,
                tile_offset,
            )
        ],
        ccd_visit,
    )
    order = sorted(range(sky), key=lambda owner: place_of(owner, sky))
    received = lax.all_to_all(
        messages, "sky", split_axis=0, concat_axis=0, axis_index_groups=[order], tiled=True
    )
    coadd, weight_map = pl.pallas_call(
        functools.partial(sky_kernel, capacity),
        out_shape=(
            jax.ShapeDtypeStruct((BLK_DEV * SUB, cols), jnp.float32),
            jax.ShapeDtypeStruct((1, BLK_DEV * SUB), jnp.float32),
        ),
        in_specs=[vmem],
        out_specs=(vmem, vmem),
        compiler_params=pltpu.CompilerParams(vmem_limit_bytes=SMALL_VMEM),
        name="place_normalise",
    )(received)
    return coadd, weight_map.reshape(-1)


def solution(mesh):
    return jax.shard_map(
        on_device,
        mesh=mesh,
        in_specs=(
            P(("groups", "sky"), None, None),
            P(),
            P(),
            P(("groups", "sky"), None, None),
            P(("groups", "sky"), None),
            P(("groups", "sky")),
            P("groups"),
            P(("groups", "sky")),
            P(("groups", "sky")),
        ),
        out_specs=(P(("groups", "sky"), None), P(("groups", "sky"))),
        check_vma=False,
    )
```

```python
import functools
import itertools

import jax
import jax.numpy as jnp
from jax import lax
from jax.experimental import pallas as pl
from jax.experimental.pallas import tpu as pltpu
from jax.sharding import PartitionSpec as P

BLK_DEV = 16
SUB = 8
LARGE_VMEM = 32 * 1024 * 1024
SMALL_VMEM = 16 * 1024 * 1024
EMPTY = -64
TAPS_DOWN = 6


def iota(shape, axis):
    return lax.broadcasted_iota(jnp.int32, shape, axis)


def weight_of(visit_ref, weight_ref):
    values = weight_ref[...].astype(jnp.float32)
    chosen = jnp.where(iota(values.shape, 1) == visit_ref[0], values, 0.0)
    return jnp.sum(chosen, axis=1, keepdims=True)


def lanczos_rows(frac_ref, cols):
    row = iota((2 * SUB, cols), 0)
    tap = jnp.where(row < SUB, row, row - SUB)
    fraction = jnp.where(row < SUB, frac_ref[0, 1], frac_ref[0, 0])
    angles = jnp.pi * ((tap - 2).astype(jnp.float32) - fraction)
    third = angles / 3.0
    kernel = jnp.sin(angles) / angles * (jnp.sin(third) / third)
    kernel = jnp.where(tap < TAPS_DOWN, kernel, 0.0)
    across, down = kernel[:SUB], kernel[SUB:]
    across = across / jnp.sum(across, axis=0, keepdims=True)
    down = down / jnp.sum(down, axis=0, keepdims=True)
    return across, down


def combined_taps(row_ref, col_ref, mix_ref, lifted, base):
    taps, basis = row_ref.shape
    count, cols = base.shape[1:]
    half = taps // 2
    l, s = iota((cols, taps), 0), iota((cols, taps), 1)
    turned = ((s + l == half) | (s + l == half + cols)).astype(jnp.float32).astype(jnp.bfloat16)
    across = jnp.dot(turned, row_ref[...], preferred_element_type=jnp.float32)
    across = across.astype(jnp.bfloat16)
    lifted[0:1] = jnp.zeros((1, basis), jnp.float32)
    lifted[1:] = col_ref[...].astype(jnp.float32)
    down = lifted[...]
    scaled = jnp.concatenate([down * mix_ref[term] for term in range(3)], axis=0)
    high = scaled.astype(jnp.bfloat16)
    low = (scaled - high.astype(jnp.float32)).astype(jnp.bfloat16)
    found = lax.dot_general(
        jnp.concatenate([high, low], axis=0),
        across,
        (((1,), (1,)), ((), ())),
        preferred_element_type=jnp.float32,
    )
    found = found[: 3 * count] + found[3 * count :]
    lane = iota((count, cols), 1)
    lane = jnp.where(lane < cols // 2, lane, lane - cols).astype(jnp.float32)
    base[0] = found[:count] + (2.0 / cols) * lane * found[count : 2 * count]
    base[1] = found[count : 2 * count]
    base[2] = found[2 * count :]


def build_band(base, row, band, first):
    cols = base.shape[2]
    shape = (2 * SUB, cols)
    sub = iota(shape, 0)
    lane = iota(shape, 1)
    lane = jnp.where(lane < cols // 2, lane, lane - cols)
    first_u = (2.0 * sub.astype(jnp.float32) + 1.0) / cols - 1.0

    def spin(term):
        taps = jnp.broadcast_to(base[term, pl.ds(row, 1), :], shape)
        return pltpu.roll(taps, 0, 1, stride=1, stride_axis=0)

    slope = spin(1)
    level = spin(0) + first_u * slope
    rise = spin(2)
    whole = rise.astype(jnp.bfloat16)
    pairs = cols // (2 * SUB)
    for pair in range(pairs):
        shift = 2 * SUB * pair
        value = level + (2.0 * shift / cols) * slope
        other = whole
        if pair == 0 or pair == pairs - 1:
            inside = lane >= 0 if pair == 0 else lane < 2 * SUB
            value = jnp.where(inside, value, 0.0)
            other = jnp.where(inside, rise, 0.0).astype(jnp.bfloat16)
        value = value.astype(jnp.bfloat16)
        if pair:
            value, other = pltpu.roll(value, shift, 1), pltpu.roll(other, shift, 1)
        at = first + shift
        band[at : at + 2 * SUB, :] = jnp.concatenate([value, other], axis=1)


def place_of(owner, owners):
    slow = 1 << ((owners.bit_length() - 1) // 2)
    fast = owners // slow
    return (owner // fast + slow // 2) % slow * fast + (owner + fast // 2) % fast


def group_edges(fold):
    return [0, fold // 8, fold // 2, fold]


def window_kernel(
    capacity,
    image_hbm,
    row_hbm,
    col_hbm,
    mix_hbm,
    weight_hbm,
    frac_hbm,
    block_hbm,
    offset_hbm,
    visit_ref,
    out_ref,
    image_ref,
    row_ref,
    col_ref,
    mix_ref,
    weight_ref,
    frac_ref,
    block_ref,
    offset_ref,
    copied,
    padded,
    lifted,
    base,
    band_a,
    band_b,
    blocks,
    total,
    spread,
    tile_of,
    starts,
    counts,
):
    rows, cols = image_ref.shape[1:]
    fold = row_ref.shape[0] // 2 + 1
    deep = rows // fold
    tiles = block_ref.shape[0]
    owners = out_ref.shape[0]
    data_rows = capacity * SUB
    owned = BLK_DEV * SUB

    pairs = (
        (row_hbm, row_ref),
        (col_hbm, col_ref),
        (mix_hbm, mix_ref),
        (image_hbm, image_ref),
        (frac_hbm, frac_ref),
        (weight_hbm, weight_ref),
        (block_hbm, block_ref),
        (offset_hbm, offset_ref),
    )
    copies = [
        pltpu.make_async_copy(source, target, copied.at[index])
        for index, (source, target) in enumerate(pairs)
    ]
    for copy in copies:
        copy.start()

    @pl.loop(0, owners)
    def _(owner):
        counts[owner] = 0

    if owners * capacity > tiles:

        @pl.loop(0, owners * capacity)
        def _(slot):
            starts[slot] = EMPTY
            tile_of[slot] = 0

    padded[:fold] = jnp.zeros((fold, cols), jnp.float32)
    padded[fold + rows :] = jnp.zeros((fold, cols), jnp.float32)
    spread[:SUB] = jnp.zeros((SUB, cols), jnp.float32)
    spread[SUB + rows :] = jnp.zeros((SUB, cols), jnp.float32)
    for copy in copies:
        copy.wait()

    combined_taps(row_ref, col_ref, mix_ref, lifted, base)
    padded[fold : fold + rows] = image_ref[0].astype(jnp.float32)
    across, down = lanczos_rows(frac_ref, cols)
    weight = weight_of(visit_ref, weight_ref)

    for index in range(3 * fold - 1):
        blocks[index * deep : (index + 1) * deep, :] = padded[
            pl.ds(index, deep, stride=fold), :
        ].astype(jnp.bfloat16)

    edges = group_edges(fold)
    groups = len(edges) - 1

    def build(group, band):
        for index, r in enumerate(range(edges[group], edges[group + 1])):
            for part in range(2):
                build_band(base, r + part * fold, band, (2 * index + part) * cols)

    def multiply(group, band):
        parts = []
        for r in range(edges[group], edges[group + 1]):
            for part in range(2):
                first = (r + part * fold) * deep
                parts.append(blocks[first : first + rows, :])
        product = jnp.dot(
            jnp.concatenate(parts, axis=1),
            band[: len(parts) * cols, :],
            preferred_element_type=jnp.float32,
        )
        total[...] = product if group == 0 else total[...] + product

    def assign(tile):
        block = block_ref[tile]
        owner = lax.div(block, BLK_DEV)
        rank = counts[owner]
        counts[owner] = rank + 1
        slot = owner * capacity + rank
        tile_of[slot] = tile
        starts[slot] = (block - owner * BLK_DEV) * SUB + offset_ref[tile]

    held = (band_a, band_b)
    build(0, held[0])
    for group in range(groups):
        if group + 1 < groups:
            build(group + 1, held[(group + 1) % 2])
        multiply(group, held[group % 2])
        for tile in range(group * tiles // groups, (group + 1) * tiles // groups):
            assign(tile)

    lane = iota((1, cols), 1)
    taps_across = [
        jnp.where((lane + m - 2 >= 0) & (lane + m - 2 < cols), across[m : m + 1], 0.0)
        for m in range(TAPS_DOWN)
    ]
    for phase in range(fold):
        first = phase * deep
        position = 2 * (fold * iota((deep, cols), 0) + phase) + 1
        position = position.astype(jnp.float32) / rows - 1.0
        both = total[first : first + deep, :]
        matched = both[:, :cols] + position * both[:, cols:]
        result = taps_across[2] * matched
        for m in range(TAPS_DOWN):
            if m != 2:
                result = result + taps_across[m] * pltpu.roll(matched, (2 - m) % cols, 1)
        spread[pl.ds(SUB + phase, deep, stride=fold), :] = result

    sub = iota((SUB, cols), 0)
    wide = iota((SUB, cols), 1)
    segment = wide >> (data_rows.bit_length() - 1)
    lane_row = wide & (SUB - 1)
    lane_slot = (wide >> 3) & (capacity - 1)
    spill_slot = wide & (capacity - 1)
    spill_row = wide >> (capacity.bit_length() - 1)
    tile_weight = jnp.broadcast_to(weight, (SUB, cols))

    def warped(slot):
        first = tile_of[slot] * SUB + SUB - 2
        result = down[0:1] * spread[pl.ds(first, SUB), :]
        for m in range(1, TAPS_DOWN):
            result = result + down[m : m + 1] * spread[pl.ds(first + m, SUB), :]
        return result

    def message(owner, carry):
        spilled, over = carry
        target = jnp.zeros((SUB, cols), jnp.int32)
        next_spilled = jnp.zeros((SUB, cols), jnp.float32)
        next_over = jnp.zeros((SUB, cols), jnp.float32)
        tiles_here = []
        for c in range(capacity):
            slot = owner * capacity + c
            start = starts[slot]
            past = start + SUB - owned
            tile = warped(slot)
            tiles_here.append(tile)
            target = jnp.where(lane_slot == c, start + lane_row, target)
            turned = pltpu.roll(tile, start & (SUB - 1), 0)
            next_spilled = next_spilled + jnp.where(sub < past, turned, 0.0)
            next_over = jnp.where((spill_slot == c) & (spill_row < past), tile_weight, next_over)
        meta = jnp.where(segment == 1, target.astype(jnp.float32), tile_weight)
        meta = jnp.where(segment == 0, over, meta)
        tail = jnp.where(sub == SUB - 1, meta, spilled * tile_weight)
        place = place_of(owner, owners)
        out_ref[place, :data_rows, :] = jnp.concatenate(tiles_here, axis=0).astype(jnp.bfloat16)
        out_ref[place, data_rows:, :] = tail.astype(jnp.bfloat16)
        return next_spilled, next_over

    nothing = jnp.zeros((SUB, cols), jnp.float32)
    lax.fori_loop(0, owners, message, (nothing, nothing), unroll=min(owners, 16))


def sky_kernel(capacity, got_ref, coadd_ref, map_ref):
    sources, message_rows, cols = got_ref.shape
    data_rows = capacity * SUB
    owned = coadd_ref.shape[0]
    per_chunk = cols // data_rows
    chunks = sources // per_chunk
    place = iota((chunks, cols), 0)
    wide = iota((chunks, cols), 1)
    row = iota((owned, cols), 0)
    spilled = jnp.zeros((SUB, cols), jnp.float32)
    target = jnp.zeros((chunks, cols), jnp.float32)
    weight = jnp.zeros((chunks, cols), jnp.float32)
    for k in range(per_chunk):
        heads = jnp.zeros((chunks, cols), jnp.float32)
        for chunk in range(chunks):
            tail = got_ref[chunk * per_chunk + k, data_rows:, :].astype(jnp.float32)
            spilled = spilled + tail
            heads = jnp.where(place == chunk, tail[SUB - 1 :], heads)
        here = (wide >= k * data_rows) & (wide < (k + 1) * data_rows)
        target = jnp.where(here, pltpu.roll(heads, (k - 1) * data_rows % cols, 1), target)
        weight = jnp.where(here, pltpu.roll(heads, (k - 2) * data_rows % cols, 1), weight)
    target = target.astype(jnp.int32)
    pieces = [
        jnp.where(row == target[chunk : chunk + 1], weight[chunk : chunk + 1], 0.0)
        for chunk in range(chunks)
    ]
    placement = jnp.concatenate(pieces, axis=1).astype(jnp.bfloat16)
    pixels = got_ref[:, :data_rows, :].reshape(sources * data_rows, cols)
    pixels = jnp.concatenate([pixels, jnp.ones(pixels.shape, jnp.bfloat16)], axis=1)
    sums = jnp.dot(placement, pixels, preferred_element_type=jnp.float32)
    sub = iota((SUB, cols), 0)
    wide = iota((SUB, cols), 1)
    last = sub == SUB - 1
    over = jnp.broadcast_to(spilled[SUB - 1 :], (SUB, cols))
    mine = ((wide >> (capacity.bit_length() - 1)) == sub) & ~last
    over = jnp.sum(jnp.where(mine, over, 0.0), axis=1, keepdims=True)
    rest = jnp.zeros((owned - SUB, cols), jnp.float32)
    pixel_sum = sums[:, :cols] + jnp.concatenate([jnp.where(last, 0.0, spilled), rest], axis=0)
    weight_sum = sums[:, cols:] + jnp.concatenate(
        [jnp.broadcast_to(over, (SUB, cols)), rest], axis=0
    )
    coadd_ref[...] = pixel_sum / jnp.maximum(weight_sum, 1.0)
    diagonal = jnp.where(row == iota((owned, cols), 1), weight_sum, 0.0)
    map_ref[...] = jnp.sum(diagonal, axis=0, keepdims=True)


def on_device(
    image,
    row_taps,
    col_taps,
    mix_coeff,
    shift_frac,
    ccd_visit,
    visit_weight,
    tile_block,
    tile_offset,
):
    rows, cols = image.shape[1:]
    tiles = tile_block.shape[0]
    sky = lax.axis_size("sky")
    capacity = max(2, tiles // sky)
    taps, basis = row_taps.shape[1], row_taps.shape[0]
    fold = taps // 2 + 1
    visits = visit_weight.shape[0]
    largest = max(b - a for a, b in itertools.pairwise(group_edges(fold)))
    anywhere = pl.BlockSpec(memory_space=pl.ANY)
    vmem = pl.BlockSpec(memory_space=pltpu.VMEM)
    messages = pl.pallas_call(
        functools.partial(window_kernel, capacity),
        out_shape=pltpu.VMEM((sky, capacity * SUB + SUB, cols), jnp.bfloat16),
        in_specs=[anywhere] * 8 + [pl.BlockSpec(memory_space=pltpu.SMEM)],
        out_specs=vmem,
        scratch_shapes=[
            pltpu.VMEM((1, rows, cols), jnp.bfloat16),
            pltpu.VMEM((taps, basis), jnp.bfloat16),
            pltpu.VMEM((taps, basis), jnp.bfloat16),
            pltpu.VMEM((3, 1, basis), jnp.float32),
            pltpu.VMEM((1, visits), jnp.bfloat16),
            pltpu.SMEM((1, 2), jnp.float32),
            pltpu.SMEM((tiles,), jnp.int32),
            pltpu.SMEM((tiles,), jnp.int32),
            pltpu.SemaphoreType.DMA((8,)),
            pltpu.VMEM((rows + 2 * fold, cols), jnp.float32),
            pltpu.VMEM((2 * fold, basis), jnp.float32),
            pltpu.VMEM((3, 2 * fold, cols), jnp.float32),
            pltpu.VMEM((largest * 2 * cols, 2 * cols), jnp.bfloat16),
            pltpu.VMEM((largest * 2 * cols, 2 * cols), jnp.bfloat16),
            pltpu.VMEM(((3 * fold - 1) * (rows // fold), cols), jnp.bfloat16),
            pltpu.VMEM((rows, 2 * cols), jnp.float32),
            pltpu.VMEM((rows + 2 * SUB, cols), jnp.float32),
            pltpu.SMEM((sky * capacity,), jnp.int32),
            pltpu.SMEM((sky * capacity,), jnp.int32),
            pltpu.SMEM((sky,), jnp.int32),
        ],
        compiler_params=pltpu.CompilerParams(vmem_limit_bytes=LARGE_VMEM),
        name="match_warp_pack",
    )(
        *[
            pltpu.with_memory_space_constraint(value, pltpu.HBM)
            for value in (
                image,
                row_taps.T,
                col_taps.T,
                mix_coeff.transpose(1, 0, 2),
                visit_weight.reshape(1, -1),
                shift_frac,
                tile_block,
                tile_offset,
            )
        ],
        ccd_visit,
    )
    order = sorted(range(sky), key=lambda owner: place_of(owner, sky))
    received = lax.all_to_all(
        messages, "sky", split_axis=0, concat_axis=0, axis_index_groups=[order], tiled=True
    )
    coadd, weight_map = pl.pallas_call(
        functools.partial(sky_kernel, capacity),
        out_shape=(
            jax.ShapeDtypeStruct((BLK_DEV * SUB, cols), jnp.float32),
            jax.ShapeDtypeStruct((1, BLK_DEV * SUB), jnp.float32),
        ),
        in_specs=[vmem],
        out_specs=(vmem, vmem),
        compiler_params=pltpu.CompilerParams(vmem_limit_bytes=SMALL_VMEM),
        name="place_normalise",
    )(received)
    return coadd, weight_map.reshape(-1)


def solution(mesh):
    return jax.shard_map(
        on_device,
        mesh=mesh,
        in_specs=(
            P(("groups", "sky"), None, None),
            P(),
            P(),
            P(("groups", "sky"), None, None),
            P(("groups", "sky"), None),
            P(("groups", "sky")),
            P("groups"),
            P(("groups", "sky")),
            P(("groups", "sky")),
        ),
        out_specs=(P(("groups", "sky"), None), P(("groups", "sky"))),
        check_vma=False,
    )
```

```python
import functools
import itertools

import jax
import jax.numpy as jnp
from jax import lax
from jax.experimental import pallas as pl
from jax.experimental.pallas import tpu as pltpu
from jax.sharding import PartitionSpec as P

BLK_DEV = 16
SUB = 8
LARGE_VMEM = 32 * 1024 * 1024
SMALL_VMEM = 16 * 1024 * 1024
EMPTY = -64
TAPS_DOWN = 6


def iota(shape, axis):
    return lax.broadcasted_iota(jnp.int32, shape, axis)


def weight_of(visit_ref, weight_ref):
    values = weight_ref[...].astype(jnp.float32)
    chosen = jnp.where(iota(values.shape, 1) == visit_ref[0], values, 0.0)
    return jnp.sum(chosen, axis=1, keepdims=True)


def lanczos_rows(frac_ref, cols):
    row = iota((2 * SUB, cols), 0)
    tap = jnp.where(row < SUB, row, row - SUB)
    fraction = jnp.where(row < SUB, frac_ref[0, 1], frac_ref[0, 0])
    angles = jnp.pi * ((tap - 2).astype(jnp.float32) - fraction)
    third = angles / 3.0
    kernel = jnp.sin(angles) / angles * (jnp.sin(third) / third)
    kernel = jnp.where(tap < TAPS_DOWN, kernel, 0.0)
    across, down = kernel[:SUB], kernel[SUB:]
    across = across / jnp.sum(across, axis=0, keepdims=True)
    down = down / jnp.sum(down, axis=0, keepdims=True)
    return across, down


def combined_taps(row_ref, col_ref, mix_ref, lifted, base):
    taps, basis = row_ref.shape
    count, cols = base.shape[1:]
    half = taps // 2
    l, s = iota((cols, taps), 0), iota((cols, taps), 1)
    turned = ((s + l == half) | (s + l == half + cols)).astype(jnp.float32).astype(jnp.bfloat16)
    across = jnp.dot(turned, row_ref[...], preferred_element_type=jnp.float32)
    across = across.astype(jnp.bfloat16)
    lifted[0:1] = jnp.zeros((1, basis), jnp.float32)
    lifted[1:] = col_ref[...].astype(jnp.float32)
    down = lifted[...]
    scaled = jnp.concatenate([down * mix_ref[term] for term in range(3)], axis=0)
    high = scaled.astype(jnp.bfloat16)
    low = (scaled - high.astype(jnp.float32)).astype(jnp.bfloat16)
    found = lax.dot_general(
        jnp.concatenate([high, low], axis=0),
        across,
        (((1,), (1,)), ((), ())),
        preferred_element_type=jnp.float32,
    )
    found = found[: 3 * count] + found[3 * count :]
    lane = iota((count, cols), 1)
    lane = jnp.where(lane < cols // 2, lane, lane - cols).astype(jnp.float32)
    base[0] = found[:count] + (2.0 / cols) * lane * found[count : 2 * count]
    base[1] = found[count : 2 * count]
    base[2] = found[2 * count :]


def build_band(base, row, band, first):
    cols = base.shape[2]
    shape = (2 * SUB, cols)
    sub = iota(shape, 0)
    lane = iota(shape, 1)
    lane = jnp.where(lane < cols // 2, lane, lane - cols)
    first_u = (2.0 * sub.astype(jnp.float32) + 1.0) / cols - 1.0

    def spin(term):
        taps = jnp.broadcast_to(base[term, pl.ds(row, 1), :], shape)
        return pltpu.roll(taps, 0, 1, stride=1, stride_axis=0)

    slope = spin(1)
    level = spin(0) + first_u * slope
    rise = spin(2)
    whole = rise.astype(jnp.bfloat16)
    pairs = cols // (2 * SUB)
    for pair in range(pairs):
        shift = 2 * SUB * pair
        value = level + (2.0 * shift / cols) * slope
        other = whole
        if pair == 0 or pair == pairs - 1:
            inside = lane >= 0 if pair == 0 else lane < 2 * SUB
            value = jnp.where(inside, value, 0.0)
            other = jnp.where(inside, rise, 0.0).astype(jnp.bfloat16)
        value = value.astype(jnp.bfloat16)
        if pair:
            value, other = pltpu.roll(value, shift, 1), pltpu.roll(other, shift, 1)
        at = first + shift
        band[at : at + 2 * SUB, :] = jnp.concatenate([value, other], axis=1)


def place_of(owner, owners):
    slow = 1 << ((owners.bit_length() - 1) // 2)
    fast = owners // slow
    return (slow // 2 + slow - owner // fast) % slow * fast + (owner + fast // 2) % fast


def group_edges(fold):
    return [0, fold // 8, fold // 2, fold]


def window_kernel(
    capacity,
    image_hbm,
    row_hbm,
    col_hbm,
    mix_hbm,
    weight_hbm,
    frac_hbm,
    block_hbm,
    offset_hbm,
    visit_ref,
    out_ref,
    image_ref,
    row_ref,
    col_ref,
    mix_ref,
    weight_ref,
    frac_ref,
    block_ref,
    offset_ref,
    copied,
    padded,
    lifted,
    base,
    band_a,
    band_b,
    blocks,
    total,
    spread,
    tile_of,
    starts,
    counts,
):
    rows, cols = image_ref.shape[1:]
    fold = row_ref.shape[0] // 2 + 1
    deep = rows // fold
    tiles = block_ref.shape[0]
    owners = out_ref.shape[0]
    data_rows = capacity * SUB
    owned = BLK_DEV * SUB

    pairs = (
        (row_hbm, row_ref),
        (col_hbm, col_ref),
        (mix_hbm, mix_ref),
        (image_hbm, image_ref),
        (frac_hbm, frac_ref),
        (weight_hbm, weight_ref),
        (block_hbm, block_ref),
        (offset_hbm, offset_ref),
    )
    copies = [
        pltpu.make_async_copy(source, target, copied.at[index])
        for index, (source, target) in enumerate(pairs)
    ]
    for copy in copies:
        copy.start()

    @pl.loop(0, owners)
    def _(owner):
        counts[owner] = 0

    if owners * capacity > tiles:

        @pl.loop(0, owners * capacity)
        def _(slot):
            starts[slot] = EMPTY
            tile_of[slot] = 0

    padded[:fold] = jnp.zeros((fold, cols), jnp.float32)
    padded[fold + rows :] = jnp.zeros((fold, cols), jnp.float32)
    spread[:SUB] = jnp.zeros((SUB, cols), jnp.float32)
    spread[SUB + rows :] = jnp.zeros((SUB, cols), jnp.float32)
    for copy in copies:
        copy.wait()

    combined_taps(row_ref, col_ref, mix_ref, lifted, base)
    padded[fold : fold + rows] = image_ref[0].astype(jnp.float32)
    across, down = lanczos_rows(frac_ref, cols)
    weight = weight_of(visit_ref, weight_ref)

    for index in range(3 * fold - 1):
        blocks[index * deep : (index + 1) * deep, :] = padded[
            pl.ds(index, deep, stride=fold), :
        ].astype(jnp.bfloat16)

    edges = group_edges(fold)
    groups = len(edges) - 1

    def build(group, band):
        for index, r in enumerate(range(edges[group], edges[group + 1])):
            for part in range(2):
                build_band(base, r + part * fold, band, (2 * index + part) * cols)

    def multiply(group, band):
        parts = []
        for r in range(edges[group], edges[group + 1]):
            for part in range(2):
                first = (r + part * fold) * deep
                parts.append(blocks[first : first + rows, :])
        product = jnp.dot(
            jnp.concatenate(parts, axis=1),
            band[: len(parts) * cols, :],
            preferred_element_type=jnp.float32,
        )
        total[...] = product if group == 0 else total[...] + product

    def assign(tile):
        block = block_ref[tile]
        owner = lax.div(block, BLK_DEV)
        rank = counts[owner]
        counts[owner] = rank + 1
        slot = owner * capacity + rank
        tile_of[slot] = tile
        starts[slot] = (block - owner * BLK_DEV) * SUB + offset_ref[tile]

    held = (band_a, band_b)
    build(0, held[0])
    for group in range(groups):
        if group + 1 < groups:
            build(group + 1, held[(group + 1) % 2])
        multiply(group, held[group % 2])
        for tile in range(group * tiles // groups, (group + 1) * tiles // groups):
            assign(tile)

    lane = iota((1, cols), 1)
    taps_across = [
        jnp.where((lane + m - 2 >= 0) & (lane + m - 2 < cols), across[m : m + 1], 0.0)
        for m in range(TAPS_DOWN)
    ]
    for phase in range(fold):
        first = phase * deep
        position = 2 * (fold * iota((deep, cols), 0) + phase) + 1
        position = position.astype(jnp.float32) / rows - 1.0
        both = total[first : first + deep, :]
        matched = both[:, :cols] + position * both[:, cols:]
        result = taps_across[2] * matched
        for m in range(TAPS_DOWN):
            if m != 2:
                result = result + taps_across[m] * pltpu.roll(matched, (2 - m) % cols, 1)
        spread[pl.ds(SUB + phase, deep, stride=fold), :] = result

    sub = iota((SUB, cols), 0)
    wide = iota((SUB, cols), 1)
    segment = wide >> (data_rows.bit_length() - 1)
    lane_row = wide & (SUB - 1)
    lane_slot = (wide >> 3) & (capacity - 1)
    spill_slot = wide & (capacity - 1)
    spill_row = wide >> (capacity.bit_length() - 1)
    tile_weight = jnp.broadcast_to(weight, (SUB, cols))

    def warped(slot):
        first = tile_of[slot] * SUB + SUB - 2
        result = down[0:1] * spread[pl.ds(first, SUB), :]
        for m in range(1, TAPS_DOWN):
            result = result + down[m : m + 1] * spread[pl.ds(first + m, SUB), :]
        return result

    def message(owner, carry):
        spilled, over = carry
        target = jnp.zeros((SUB, cols), jnp.int32)
        next_spilled = jnp.zeros((SUB, cols), jnp.float32)
        next_over = jnp.zeros((SUB, cols), jnp.float32)
        tiles_here = []
        for c in range(capacity):
            slot = owner * capacity + c
            start = starts[slot]
            past = start + SUB - owned
            tile = warped(slot)
            tiles_here.append(tile)
            target = jnp.where(lane_slot == c, start + lane_row, target)
            turned = pltpu.roll(tile, start & (SUB - 1), 0)
            next_spilled = next_spilled + jnp.where(sub < past, turned, 0.0)
            next_over = jnp.where((spill_slot == c) & (spill_row < past), tile_weight, next_over)
        meta = jnp.where(segment == 1, target.astype(jnp.float32), tile_weight)
        meta = jnp.where(segment == 0, over, meta)
        tail = jnp.where(sub == SUB - 1, meta, spilled * tile_weight)
        place = place_of(owner, owners)
        out_ref[place, :data_rows, :] = jnp.concatenate(tiles_here, axis=0).astype(jnp.bfloat16)
        out_ref[place, data_rows:, :] = tail.astype(jnp.bfloat16)
        return next_spilled, next_over

    nothing = jnp.zeros((SUB, cols), jnp.float32)
    lax.fori_loop(0, owners, message, (nothing, nothing), unroll=min(owners, 16))


def sky_kernel(capacity, got_ref, coadd_ref, map_ref):
    sources, message_rows, cols = got_ref.shape
    data_rows = capacity * SUB
    owned = coadd_ref.shape[0]
    per_chunk = cols // data_rows
    chunks = sources // per_chunk
    place = iota((chunks, cols), 0)
    wide = iota((chunks, cols), 1)
    row = iota((owned, cols), 0)
    spilled = jnp.zeros((SUB, cols), jnp.float32)
    target = jnp.zeros((chunks, cols), jnp.float32)
    weight = jnp.zeros((chunks, cols), jnp.float32)
    for k in range(per_chunk):
        heads = jnp.zeros((chunks, cols), jnp.float32)
        for chunk in range(chunks):
            tail = got_ref[chunk * per_chunk + k, data_rows:, :].astype(jnp.float32)
            spilled = spilled + tail
            heads = jnp.where(place == chunk, tail[SUB - 1 :], heads)
        here = (wide >= k * data_rows) & (wide < (k + 1) * data_rows)
        target = jnp.where(here, pltpu.roll(heads, (k - 1) * data_rows % cols, 1), target)
        weight = jnp.where(here, pltpu.roll(heads, (k - 2) * data_rows % cols, 1), weight)
    target = target.astype(jnp.int32)
    pieces = [
        jnp.where(row == target[chunk : chunk + 1], weight[chunk : chunk + 1], 0.0)
        for chunk in range(chunks)
    ]
    placement = jnp.concatenate(pieces, axis=1).astype(jnp.bfloat16)
    pixels = got_ref[:, :data_rows, :].reshape(sources * data_rows, cols)
    pixels = jnp.concatenate([pixels, jnp.ones(pixels.shape, jnp.bfloat16)], axis=1)
    sums = jnp.dot(placement, pixels, preferred_element_type=jnp.float32)
    sub = iota((SUB, cols), 0)
    wide = iota((SUB, cols), 1)
    last = sub == SUB - 1
    over = jnp.broadcast_to(spilled[SUB - 1 :], (SUB, cols))
    mine = ((wide >> (capacity.bit_length() - 1)) == sub) & ~last
    over = jnp.sum(jnp.where(mine, over, 0.0), axis=1, keepdims=True)
    rest = jnp.zeros((owned - SUB, cols), jnp.float32)
    pixel_sum = sums[:, :cols] + jnp.concatenate([jnp.where(last, 0.0, spilled), rest], axis=0)
    weight_sum = sums[:, cols:] + jnp.concatenate(
        [jnp.broadcast_to(over, (SUB, cols)), rest], axis=0
    )
    coadd_ref[...] = pixel_sum / jnp.maximum(weight_sum, 1.0)
    diagonal = jnp.where(row == iota((owned, cols), 1), weight_sum, 0.0)
    map_ref[...] = jnp.sum(diagonal, axis=0, keepdims=True)


def on_device(
    image,
    row_taps,
    col_taps,
    mix_coeff,
    shift_frac,
    ccd_visit,
    visit_weight,
    tile_block,
    tile_offset,
):
    rows, cols = image.shape[1:]
    tiles = tile_block.shape[0]
    sky = lax.axis_size("sky")
    capacity = max(2, tiles // sky)
    taps, basis = row_taps.shape[1], row_taps.shape[0]
    fold = taps // 2 + 1
    visits = visit_weight.shape[0]
    largest = max(b - a for a, b in itertools.pairwise(group_edges(fold)))
    anywhere = pl.BlockSpec(memory_space=pl.ANY)
    vmem = pl.BlockSpec(memory_space=pltpu.VMEM)
    messages = pl.pallas_call(
        functools.partial(window_kernel, capacity),
        out_shape=pltpu.VMEM((sky, capacity * SUB + SUB, cols), jnp.bfloat16),
        in_specs=[anywhere] * 8 + [pl.BlockSpec(memory_space=pltpu.SMEM)],
        out_specs=vmem,
        scratch_shapes=[
            pltpu.VMEM((1, rows, cols), jnp.bfloat16),
            pltpu.VMEM((taps, basis), jnp.bfloat16),
            pltpu.VMEM((taps, basis), jnp.bfloat16),
            pltpu.VMEM((3, 1, basis), jnp.float32),
            pltpu.VMEM((1, visits), jnp.bfloat16),
            pltpu.SMEM((1, 2), jnp.float32),
            pltpu.SMEM((tiles,), jnp.int32),
            pltpu.SMEM((tiles,), jnp.int32),
            pltpu.SemaphoreType.DMA((8,)),
            pltpu.VMEM((rows + 2 * fold, cols), jnp.float32),
            pltpu.VMEM((2 * fold, basis), jnp.float32),
            pltpu.VMEM((3, 2 * fold, cols), jnp.float32),
            pltpu.VMEM((largest * 2 * cols, 2 * cols), jnp.bfloat16),
            pltpu.VMEM((largest * 2 * cols, 2 * cols), jnp.bfloat16),
            pltpu.VMEM(((3 * fold - 1) * (rows // fold), cols), jnp.bfloat16),
            pltpu.VMEM((rows, 2 * cols), jnp.float32),
            pltpu.VMEM((rows + 2 * SUB, cols), jnp.float32),
            pltpu.SMEM((sky * capacity,), jnp.int32),
            pltpu.SMEM((sky * capacity,), jnp.int32),
            pltpu.SMEM((sky,), jnp.int32),
        ],
        compiler_params=pltpu.CompilerParams(vmem_limit_bytes=LARGE_VMEM),
        name="match_warp_pack",
    )(
        *[
            pltpu.with_memory_space_constraint(value, pltpu.HBM)
            for value in (
                image,
                row_taps.T,
                col_taps.T,
                mix_coeff.transpose(1, 0, 2),
                visit_weight.reshape(1, -1),
                shift_frac,
                tile_block,
                tile_offset,
            )
        ],
        ccd_visit,
    )
    order = sorted(range(sky), key=lambda owner: place_of(owner, sky))
    received = lax.all_to_all(
        messages, "sky", split_axis=0, concat_axis=0, axis_index_groups=[order], tiled=True
    )
    coadd, weight_map = pl.pallas_call(
        functools.partial(sky_kernel, capacity),
        out_shape=(
            jax.ShapeDtypeStruct((BLK_DEV * SUB, cols), jnp.float32),
            jax.ShapeDtypeStruct((1, BLK_DEV * SUB), jnp.float32),
        ),
        in_specs=[vmem],
        out_specs=(vmem, vmem),
        compiler_params=pltpu.CompilerParams(vmem_limit_bytes=SMALL_VMEM),
        name="place_normalise",
    )(received)
    return coadd, weight_map.reshape(-1)


def solution(mesh):
    return jax.shard_map(
        on_device,
        mesh=mesh,
        in_specs=(
            P(("groups", "sky"), None, None),
            P(),
            P(),
            P(("groups", "sky"), None, None),
            P(("groups", "sky"), None),
            P(("groups", "sky")),
            P("groups"),
            P(("groups", "sky")),
            P(("groups", "sky")),
        ),
        out_specs=(P(("groups", "sky"), None), P(("groups", "sky"))),
        check_vma=False,
    )
```

```python
import functools
import itertools

import jax
import jax.numpy as jnp
from jax import lax
from jax.experimental import pallas as pl
from jax.experimental.pallas import tpu as pltpu
from jax.sharding import PartitionSpec as P

BLK_DEV = 16
SUB = 8
LARGE_VMEM = 32 * 1024 * 1024
SMALL_VMEM = 16 * 1024 * 1024
EMPTY = -64
TAPS_DOWN = 6


def iota(shape, axis):
    return lax.broadcasted_iota(jnp.int32, shape, axis)


def weight_of(visit_ref, weight_ref):
    values = weight_ref[...].astype(jnp.float32)
    chosen = jnp.where(iota(values.shape, 1) == visit_ref[0], values, 0.0)
    return jnp.sum(chosen, axis=1, keepdims=True)


def lanczos_rows(frac_ref, cols):
    row = iota((2 * SUB, cols), 0)
    tap = jnp.where(row < SUB, row, row - SUB)
    fraction = jnp.where(row < SUB, frac_ref[0, 1], frac_ref[0, 0])
    angles = jnp.pi * ((tap - 2).astype(jnp.float32) - fraction)
    third = angles / 3.0
    kernel = jnp.sin(angles) / angles * (jnp.sin(third) / third)
    kernel = jnp.where(tap < TAPS_DOWN, kernel, 0.0)
    across, down = kernel[:SUB], kernel[SUB:]
    across = across / jnp.sum(across, axis=0, keepdims=True)
    down = down / jnp.sum(down, axis=0, keepdims=True)
    return across, down


def combined_taps(row_ref, col_ref, mix_ref, lifted, base):
    taps, basis = row_ref.shape
    count, cols = base.shape[1:]
    half = taps // 2
    l, s = iota((cols, taps), 0), iota((cols, taps), 1)
    turned = ((s + l == half) | (s + l == half + cols)).astype(jnp.float32).astype(jnp.bfloat16)
    across = jnp.dot(turned, row_ref[...], preferred_element_type=jnp.float32)
    across = across.astype(jnp.bfloat16)
    lifted[0:1] = jnp.zeros((1, basis), jnp.float32)
    lifted[1:] = col_ref[...].astype(jnp.float32)
    down = lifted[...]
    scaled = jnp.concatenate([down * mix_ref[term] for term in range(3)], axis=0)
    high = scaled.astype(jnp.bfloat16)
    low = (scaled - high.astype(jnp.float32)).astype(jnp.bfloat16)
    found = lax.dot_general(
        jnp.concatenate([high, low], axis=0),
        across,
        (((1,), (1,)), ((), ())),
        preferred_element_type=jnp.float32,
    )
    found = found[: 3 * count] + found[3 * count :]
    lane = iota((count, cols), 1)
    lane = jnp.where(lane < cols // 2, lane, lane - cols).astype(jnp.float32)
    base[0] = found[:count] + (2.0 / cols) * lane * found[count : 2 * count]
    base[1] = found[count : 2 * count]
    base[2] = found[2 * count :]


def build_band(base, row, band, first):
    cols = base.shape[2]
    shape = (2 * SUB, cols)
    sub = iota(shape, 0)
    lane = iota(shape, 1)
    lane = jnp.where(lane < cols // 2, lane, lane - cols)
    first_u = (2.0 * sub.astype(jnp.float32) + 1.0) / cols - 1.0

    def spin(term):
        taps = jnp.broadcast_to(base[term, pl.ds(row, 1), :], shape)
        return pltpu.roll(taps, 0, 1, stride=1, stride_axis=0)

    slope = spin(1)
    level = spin(0) + first_u * slope
    rise = spin(2)
    whole = rise.astype(jnp.bfloat16)
    pairs = cols // (2 * SUB)
    for pair in range(pairs):
        shift = 2 * SUB * pair
        value = level + (2.0 * shift / cols) * slope
        other = whole
        if pair == 0 or pair == pairs - 1:
            inside = lane >= 0 if pair == 0 else lane < 2 * SUB
            value = jnp.where(inside, value, 0.0)
            other = jnp.where(inside, rise, 0.0).astype(jnp.bfloat16)
        value = value.astype(jnp.bfloat16)
        if pair:
            value, other = pltpu.roll(value, shift, 1), pltpu.roll(other, shift, 1)
        at = first + shift
        band[at : at + 2 * SUB, :] = jnp.concatenate([value, other], axis=1)


def place_of(owner, owners):
    slow = 1 << ((owners.bit_length() - 1) // 2)
    fast = owners // slow
    return (owner // fast + slow // 2) % slow * fast + (owner + fast // 2) % fast


def group_edges(fold):
    return [0, fold // 8, fold // 2, fold]


def window_kernel(
    capacity,
    image_hbm,
    row_hbm,
    col_hbm,
    mix_hbm,
    weight_hbm,
    frac_hbm,
    block_hbm,
    offset_hbm,
    visit_ref,
    out_ref,
    image_ref,
    row_ref,
    col_ref,
    mix_ref,
    weight_ref,
    frac_ref,
    block_ref,
    offset_ref,
    copied,
    padded,
    lifted,
    base,
    band_a,
    band_b,
    blocks,
    total,
    spread,
    tile_of,
    starts,
    counts,
):
    rows, cols = image_ref.shape[1:]
    fold = row_ref.shape[0] // 2 + 1
    deep = rows // fold
    tiles = block_ref.shape[0]
    owners = out_ref.shape[0]
    data_rows = capacity * SUB
    owned = BLK_DEV * SUB

    pairs = (
        (row_hbm, row_ref),
        (col_hbm, col_ref),
        (mix_hbm, mix_ref),
        (image_hbm, image_ref),
        (frac_hbm, frac_ref),
        (weight_hbm, weight_ref),
        (block_hbm, block_ref),
        (offset_hbm, offset_ref),
    )
    copies = [
        pltpu.make_async_copy(source, target, copied.at[index])
        for index, (source, target) in enumerate(pairs)
    ]
    for copy in copies:
        copy.start()

    @pl.loop(0, owners)
    def _(owner):
        counts[owner] = 0

    if owners * capacity > tiles:

        @pl.loop(0, owners * capacity)
        def _(slot):
            starts[slot] = EMPTY
            tile_of[slot] = 0

    padded[:fold] = jnp.zeros((fold, cols), jnp.float32)
    padded[fold + rows :] = jnp.zeros((fold, cols), jnp.float32)
    spread[:SUB] = jnp.zeros((SUB, cols), jnp.float32)
    spread[SUB + rows :] = jnp.zeros((SUB, cols), jnp.float32)
    for copy in copies:
        copy.wait()

    combined_taps(row_ref, col_ref, mix_ref, lifted, base)
    padded[fold : fold + rows] = image_ref[0].astype(jnp.float32)
    across, down = lanczos_rows(frac_ref, cols)
    weight = weight_of(visit_ref, weight_ref)

    for index in range(3 * fold - 1):
        blocks[index * deep : (index + 1) * deep, :] = padded[
            pl.ds(index, deep, stride=fold), :
        ].astype(jnp.bfloat16)

    edges = group_edges(fold)
    groups = len(edges) - 1
    pieces = 2

    def build(group, band):
        for index, r in enumerate(range(edges[group], edges[group + 1])):
            for part in range(2):
                build_band(base, r + part * fold, band, (2 * index + part) * cols)

    def multiply(group, band):
        for piece in range(pieces):
            height = rows // pieces
            parts = []
            for r in range(edges[group], edges[group + 1]):
                for part in range(2):
                    first = (r + part * fold) * deep + piece * height
                    parts.append(blocks[first : first + height, :])
            product = jnp.dot(
                jnp.concatenate(parts, axis=1),
                band[: len(parts) * cols, :],
                preferred_element_type=jnp.float32,
            )
            here = slice(piece * height, (piece + 1) * height)
            total[here, :] = product if group == 0 else total[here, :] + product

    def assign(tile):
        block = block_ref[tile]
        owner = lax.div(block, BLK_DEV)
        rank = counts[owner]
        counts[owner] = rank + 1
        slot = owner * capacity + rank
        tile_of[slot] = tile
        starts[slot] = (block - owner * BLK_DEV) * SUB + offset_ref[tile]

    held = (band_a, band_b)
    build(0, held[0])
    for group in range(groups):
        if group + 1 < groups:
            build(group + 1, held[(group + 1) % 2])
        multiply(group, held[group % 2])
        for tile in range(group * tiles // groups, (group + 1) * tiles // groups):
            assign(tile)

    lane = iota((1, cols), 1)
    taps_across = [
        jnp.where((lane + m - 2 >= 0) & (lane + m - 2 < cols), across[m : m + 1], 0.0)
        for m in range(TAPS_DOWN)
    ]
    for phase in range(fold):
        first = phase * deep
        position = 2 * (fold * iota((deep, cols), 0) + phase) + 1
        position = position.astype(jnp.float32) / rows - 1.0
        both = total[first : first + deep, :]
        matched = both[:, :cols] + position * both[:, cols:]
        result = taps_across[2] * matched
        for m in range(TAPS_DOWN):
            if m != 2:
                result = result + taps_across[m] * pltpu.roll(matched, (2 - m) % cols, 1)
        spread[pl.ds(SUB + phase, deep, stride=fold), :] = result

    sub = iota((SUB, cols), 0)
    wide = iota((SUB, cols), 1)
    segment = wide >> (data_rows.bit_length() - 1)
    lane_row = wide & (SUB - 1)
    lane_slot = (wide >> 3) & (capacity - 1)
    spill_slot = wide & (capacity - 1)
    spill_row = wide >> (capacity.bit_length() - 1)
    tile_weight = jnp.broadcast_to(weight, (SUB, cols))

    def warped(slot):
        first = tile_of[slot] * SUB + SUB - 2
        result = down[0:1] * spread[pl.ds(first, SUB), :]
        for m in range(1, TAPS_DOWN):
            result = result + down[m : m + 1] * spread[pl.ds(first + m, SUB), :]
        return result

    def message(owner, carry):
        spilled, over = carry
        target = jnp.zeros((SUB, cols), jnp.int32)
        next_spilled = jnp.zeros((SUB, cols), jnp.float32)
        next_over = jnp.zeros((SUB, cols), jnp.float32)
        tiles_here = []
        for c in range(capacity):
            slot = owner * capacity + c
            start = starts[slot]
            past = start + SUB - owned
            tile = warped(slot)
            tiles_here.append(tile)
            target = jnp.where(lane_slot == c, start + lane_row, target)
            turned = pltpu.roll(tile, start & (SUB - 1), 0)
            next_spilled = next_spilled + jnp.where(sub < past, turned, 0.0)
            next_over = jnp.where((spill_slot == c) & (spill_row < past), tile_weight, next_over)
        meta = jnp.where(segment == 1, target.astype(jnp.float32), tile_weight)
        meta = jnp.where(segment == 0, over, meta)
        tail = jnp.where(sub == SUB - 1, meta, spilled * tile_weight)
        place = place_of(owner, owners)
        out_ref[place, :data_rows, :] = jnp.concatenate(tiles_here, axis=0).astype(jnp.bfloat16)
        out_ref[place, data_rows:, :] = tail.astype(jnp.bfloat16)
        return next_spilled, next_over

    nothing = jnp.zeros((SUB, cols), jnp.float32)
    lax.fori_loop(0, owners, message, (nothing, nothing), unroll=min(owners, 16))


def sky_kernel(capacity, got_ref, coadd_ref, map_ref):
    sources, message_rows, cols = got_ref.shape
    data_rows = capacity * SUB
    owned = coadd_ref.shape[0]
    per_chunk = cols // data_rows
    chunks = sources // per_chunk
    place = iota((chunks, cols), 0)
    wide = iota((chunks, cols), 1)
    row = iota((owned, cols), 0)
    spilled = jnp.zeros((SUB, cols), jnp.float32)
    target = jnp.zeros((chunks, cols), jnp.float32)
    weight = jnp.zeros((chunks, cols), jnp.float32)
    for k in range(per_chunk):
        heads = jnp.zeros((chunks, cols), jnp.float32)
        for chunk in range(chunks):
            tail = got_ref[chunk * per_chunk + k, data_rows:, :].astype(jnp.float32)
            spilled = spilled + tail
            heads = jnp.where(place == chunk, tail[SUB - 1 :], heads)
        here = (wide >= k * data_rows) & (wide < (k + 1) * data_rows)
        target = jnp.where(here, pltpu.roll(heads, (k - 1) * data_rows % cols, 1), target)
        weight = jnp.where(here, pltpu.roll(heads, (k - 2) * data_rows % cols, 1), weight)
    target = target.astype(jnp.int32)
    pieces = [
        jnp.where(row == target[chunk : chunk + 1], weight[chunk : chunk + 1], 0.0)
        for chunk in range(chunks)
    ]
    placement = jnp.concatenate(pieces, axis=1).astype(jnp.bfloat16)
    pixels = got_ref[:, :data_rows, :].reshape(sources * data_rows, cols)
    pixels = jnp.concatenate([pixels, jnp.ones(pixels.shape, jnp.bfloat16)], axis=1)
    sums = jnp.dot(placement, pixels, preferred_element_type=jnp.float32)
    sub = iota((SUB, cols), 0)
    wide = iota((SUB, cols), 1)
    last = sub == SUB - 1
    over = jnp.broadcast_to(spilled[SUB - 1 :], (SUB, cols))
    mine = ((wide >> (capacity.bit_length() - 1)) == sub) & ~last
    over = jnp.sum(jnp.where(mine, over, 0.0), axis=1, keepdims=True)
    rest = jnp.zeros((owned - SUB, cols), jnp.float32)
    pixel_sum = sums[:, :cols] + jnp.concatenate([jnp.where(last, 0.0, spilled), rest], axis=0)
    weight_sum = sums[:, cols:] + jnp.concatenate(
        [jnp.broadcast_to(over, (SUB, cols)), rest], axis=0
    )
    coadd_ref[...] = pixel_sum / jnp.maximum(weight_sum, 1.0)
    diagonal = jnp.where(row == iota((owned, cols), 1), weight_sum, 0.0)
    map_ref[...] = jnp.sum(diagonal, axis=0, keepdims=True)


def on_device(
    image,
    row_taps,
    col_taps,
    mix_coeff,
    shift_frac,
    ccd_visit,
    visit_weight,
    tile_block,
    tile_offset,
):
    rows, cols = image.shape[1:]
    tiles = tile_block.shape[0]
    sky = lax.axis_size("sky")
    capacity = max(2, tiles // sky)
    taps, basis = row_taps.shape[1], row_taps.shape[0]
    fold = taps // 2 + 1
    visits = visit_weight.shape[0]
    largest = max(b - a for a, b in itertools.pairwise(group_edges(fold)))
    anywhere = pl.BlockSpec(memory_space=pl.ANY)
    vmem = pl.BlockSpec(memory_space=pltpu.VMEM)
    messages = pl.pallas_call(
        functools.partial(window_kernel, capacity),
        out_shape=pltpu.VMEM((sky, capacity * SUB + SUB, cols), jnp.bfloat16),
        in_specs=[anywhere] * 8 + [pl.BlockSpec(memory_space=pltpu.SMEM)],
        out_specs=vmem,
        scratch_shapes=[
            pltpu.VMEM((1, rows, cols), jnp.bfloat16),
            pltpu.VMEM((taps, basis), jnp.bfloat16),
            pltpu.VMEM((taps, basis), jnp.bfloat16),
            pltpu.VMEM((3, 1, basis), jnp.float32),
            pltpu.VMEM((1, visits), jnp.bfloat16),
            pltpu.SMEM((1, 2), jnp.float32),
            pltpu.SMEM((tiles,), jnp.int32),
            pltpu.SMEM((tiles,), jnp.int32),
            pltpu.SemaphoreType.DMA((8,)),
            pltpu.VMEM((rows + 2 * fold, cols), jnp.float32),
            pltpu.VMEM((2 * fold, basis), jnp.float32),
            pltpu.VMEM((3, 2 * fold, cols), jnp.float32),
            pltpu.VMEM((largest * 2 * cols, 2 * cols), jnp.bfloat16),
            pltpu.VMEM((largest * 2 * cols, 2 * cols), jnp.bfloat16),
            pltpu.VMEM(((3 * fold - 1) * (rows // fold), cols), jnp.bfloat16),
            pltpu.VMEM((rows, 2 * cols), jnp.float32),
            pltpu.VMEM((rows + 2 * SUB, cols), jnp.float32),
            pltpu.SMEM((sky * capacity,), jnp.int32),
            pltpu.SMEM((sky * capacity,), jnp.int32),
            pltpu.SMEM((sky,), jnp.int32),
        ],
        compiler_params=pltpu.CompilerParams(vmem_limit_bytes=LARGE_VMEM),
        name="match_warp_pack",
    )(
        *[
            pltpu.with_memory_space_constraint(value, pltpu.HBM)
            for value in (
                image,
                row_taps.T,
                col_taps.T,
                mix_coeff.transpose(1, 0, 2),
                visit_weight.reshape(1, -1),
                shift_frac,
                tile_block,
                tile_offset,
            )
        ],
        ccd_visit,
    )
    order = sorted(range(sky), key=lambda owner: place_of(owner, sky))
    received = lax.all_to_all(
        messages, "sky", split_axis=0, concat_axis=0, axis_index_groups=[order], tiled=True
    )
    coadd, weight_map = pl.pallas_call(
        functools.partial(sky_kernel, capacity),
        out_shape=(
            jax.ShapeDtypeStruct((BLK_DEV * SUB, cols), jnp.float32),
            jax.ShapeDtypeStruct((1, BLK_DEV * SUB), jnp.float32),
        ),
        in_specs=[vmem],
        out_specs=(vmem, vmem),
        compiler_params=pltpu.CompilerParams(vmem_limit_bytes=SMALL_VMEM),
        name="place_normalise",
    )(received)
    return coadd, weight_map.reshape(-1)


def solution(mesh):
    return jax.shard_map(
        on_device,
        mesh=mesh,
        in_specs=(
            P(("groups", "sky"), None, None),
            P(),
            P(),
            P(("groups", "sky"), None, None),
            P(("groups", "sky"), None),
            P(("groups", "sky")),
            P("groups"),
            P(("groups", "sky")),
            P(("groups", "sky")),
        ),
        out_specs=(P(("groups", "sky"), None), P(("groups", "sky"))),
        check_vma=False,
    )
```

```python
import functools
import itertools

import jax
import jax.numpy as jnp
from jax import lax
from jax.experimental import pallas as pl
from jax.experimental.pallas import tpu as pltpu
from jax.sharding import PartitionSpec as P

BLK_DEV = 16
SUB = 8
LARGE_VMEM = 32 * 1024 * 1024
SMALL_VMEM = 16 * 1024 * 1024
EMPTY = -64
IMAGE_PIECES = 8
TAPS_DOWN = 6


def iota(shape, axis):
    return lax.broadcasted_iota(jnp.int32, shape, axis)


def weight_of(visit_ref, weight_ref):
    values = weight_ref[...].astype(jnp.float32)
    chosen = jnp.where(iota(values.shape, 1) == visit_ref[0], values, 0.0)
    return jnp.sum(chosen, axis=1, keepdims=True)


def lanczos_rows(frac_ref, cols):
    row = iota((2 * SUB, cols), 0)
    tap = jnp.where(row < SUB, row, row - SUB)
    fraction = jnp.where(row < SUB, frac_ref[0, 1], frac_ref[0, 0])
    angles = jnp.pi * ((tap - 2).astype(jnp.float32) - fraction)
    third = angles / 3.0
    kernel = jnp.sin(angles) / angles * (jnp.sin(third) / third)
    kernel = jnp.where(tap < TAPS_DOWN, kernel, 0.0)
    across, down = kernel[:SUB], kernel[SUB:]
    across = across / jnp.sum(across, axis=0, keepdims=True)
    down = down / jnp.sum(down, axis=0, keepdims=True)
    return across, down


def combined_taps(row_ref, col_ref, mix_ref, lifted, base):
    taps, basis = row_ref.shape
    count, cols = base.shape[1:]
    half = taps // 2
    l, s = iota((cols, taps), 0), iota((cols, taps), 1)
    turned = ((s + l == half) | (s + l == half + cols)).astype(jnp.float32).astype(jnp.bfloat16)
    across = jnp.dot(turned, row_ref[...], preferred_element_type=jnp.float32)
    across = across.astype(jnp.bfloat16)
    lifted[0:1] = jnp.zeros((1, basis), jnp.float32)
    lifted[1:] = col_ref[...].astype(jnp.float32)
    down = lifted[...]
    scaled = jnp.concatenate([down * mix_ref[term] for term in range(3)], axis=0)
    high = scaled.astype(jnp.bfloat16)
    low = (scaled - high.astype(jnp.float32)).astype(jnp.bfloat16)
    found = lax.dot_general(
        jnp.concatenate([high, low], axis=0),
        across,
        (((1,), (1,)), ((), ())),
        preferred_element_type=jnp.float32,
    )
    found = found[: 3 * count] + found[3 * count :]
    lane = iota((count, cols), 1)
    lane = jnp.where(lane < cols // 2, lane, lane - cols).astype(jnp.float32)
    base[0] = found[:count] + (2.0 / cols) * lane * found[count : 2 * count]
    base[1] = found[count : 2 * count]
    base[2] = found[2 * count :]


def build_band(base, row, band, first):
    cols = base.shape[2]
    shape = (2 * SUB, cols)
    sub = iota(shape, 0)
    lane = iota(shape, 1)
    lane = jnp.where(lane < cols // 2, lane, lane - cols)
    first_u = (2.0 * sub.astype(jnp.float32) + 1.0) / cols - 1.0

    def spin(term):
        taps = jnp.broadcast_to(base[term, pl.ds(row, 1), :], shape)
        return pltpu.roll(taps, 0, 1, stride=1, stride_axis=0)

    slope = spin(1)
    level = spin(0) + first_u * slope
    rise = spin(2)
    whole = rise.astype(jnp.bfloat16)
    pairs = cols // (2 * SUB)
    for pair in range(pairs):
        shift = 2 * SUB * pair
        value = level + (2.0 * shift / cols) * slope
        other = whole
        if pair == 0 or pair == pairs - 1:
            inside = lane >= 0 if pair == 0 else lane < 2 * SUB
            value = jnp.where(inside, value, 0.0)
            other = jnp.where(inside, rise, 0.0).astype(jnp.bfloat16)
        value = value.astype(jnp.bfloat16)
        if pair:
            value, other = pltpu.roll(value, shift, 1), pltpu.roll(other, shift, 1)
        at = first + shift
        band[at : at + 2 * SUB, :] = jnp.concatenate([value, other], axis=1)


def place_of(owner, owners):
    slow = 1 << ((owners.bit_length() - 1) // 2)
    fast = owners // slow
    return (owner // fast + slow // 2) % slow * fast + (owner + fast // 2) % fast


def group_edges(fold):
    return [0, fold // 8, fold // 2, fold]


def window_kernel(
    capacity,
    image_hbm,
    row_hbm,
    col_hbm,
    mix_hbm,
    weight_hbm,
    frac_hbm,
    block_hbm,
    offset_hbm,
    visit_ref,
    out_ref,
    image_ref,
    row_ref,
    col_ref,
    mix_ref,
    weight_ref,
    frac_ref,
    block_ref,
    offset_ref,
    copied,
    padded,
    lifted,
    base,
    band_a,
    band_b,
    blocks,
    total,
    spread,
    tile_of,
    starts,
    counts,
):
    rows, cols = image_ref.shape[1:]
    fold = row_ref.shape[0] // 2 + 1
    deep = rows // fold
    tiles = block_ref.shape[0]
    owners = out_ref.shape[0]
    data_rows = capacity * SUB
    owned = BLK_DEV * SUB

    piece = rows // IMAGE_PIECES
    parts = [pl.ds(index * piece, piece) for index in range(IMAGE_PIECES)]
    small = [
        (row_hbm, row_ref),
        (col_hbm, col_ref),
        (mix_hbm, mix_ref),
        (block_hbm, block_ref),
        (offset_hbm, offset_ref),
        (frac_hbm, frac_ref),
        (weight_hbm, weight_ref),
    ]
    large = [(image_hbm.at[:, part, :], image_ref.at[:, part, :]) for part in parts]
    copies = [
        pltpu.make_async_copy(source, target, copied.at[index])
        for index, (source, target) in enumerate(small[:3] + large + small[3:])
    ]
    for copy in copies:
        copy.start()

    @pl.loop(0, owners)
    def _(owner):
        counts[owner] = 0

    if owners * capacity > tiles:

        @pl.loop(0, owners * capacity)
        def _(slot):
            starts[slot] = EMPTY
            tile_of[slot] = 0

    padded[:fold] = jnp.zeros((fold, cols), jnp.float32)
    padded[fold + rows :] = jnp.zeros((fold, cols), jnp.float32)
    spread[:SUB] = jnp.zeros((SUB, cols), jnp.float32)
    spread[SUB + rows :] = jnp.zeros((SUB, cols), jnp.float32)
    for copy in copies[:3]:
        copy.wait()
    combined_taps(row_ref, col_ref, mix_ref, lifted, base)
    for copy in copies[3:]:
        copy.wait()
    padded[fold : fold + rows] = image_ref[0].astype(jnp.float32)
    across, down = lanczos_rows(frac_ref, cols)
    weight = weight_of(visit_ref, weight_ref)

    for index in range(3 * fold - 1):
        blocks[index * deep : (index + 1) * deep, :] = padded[
            pl.ds(index, deep, stride=fold), :
        ].astype(jnp.bfloat16)

    edges = group_edges(fold)
    groups = len(edges) - 1

    def build(group, band):
        for index, r in enumerate(range(edges[group], edges[group + 1])):
            for part in range(2):
                build_band(base, r + part * fold, band, (2 * index + part) * cols)

    def multiply(group, band):
        parts = []
        for r in range(edges[group], edges[group + 1]):
            for part in range(2):
                first = (r + part * fold) * deep
                parts.append(blocks[first : first + rows, :])
        product = jnp.dot(
            jnp.concatenate(parts, axis=1),
            band[: len(parts) * cols, :],
            preferred_element_type=jnp.float32,
        )
        total[...] = product if group == 0 else total[...] + product

    def assign(tile):
        block = block_ref[tile]
        owner = lax.div(block, BLK_DEV)
        rank = counts[owner]
        counts[owner] = rank + 1
        slot = owner * capacity + rank
        tile_of[slot] = tile
        starts[slot] = (block - owner * BLK_DEV) * SUB + offset_ref[tile]

    held = (band_a, band_b)
    build(0, held[0])
    for group in range(groups):
        if group + 1 < groups:
            build(group + 1, held[(group + 1) % 2])
        multiply(group, held[group % 2])
        for tile in range(group * tiles // groups, (group + 1) * tiles // groups):
            assign(tile)

    lane = iota((1, cols), 1)
    taps_across = [
        jnp.where((lane + m - 2 >= 0) & (lane + m - 2 < cols), across[m : m + 1], 0.0)
        for m in range(TAPS_DOWN)
    ]
    for phase in range(fold):
        first = phase * deep
        position = 2 * (fold * iota((deep, cols), 0) + phase) + 1
        position = position.astype(jnp.float32) / rows - 1.0
        both = total[first : first + deep, :]
        matched = both[:, :cols] + position * both[:, cols:]
        result = taps_across[2] * matched
        for m in range(TAPS_DOWN):
            if m != 2:
                result = result + taps_across[m] * pltpu.roll(matched, (2 - m) % cols, 1)
        spread[pl.ds(SUB + phase, deep, stride=fold), :] = result

    sub = iota((SUB, cols), 0)
    wide = iota((SUB, cols), 1)
    segment = wide >> (data_rows.bit_length() - 1)
    lane_row = wide & (SUB - 1)
    lane_slot = (wide >> 3) & (capacity - 1)
    spill_slot = wide & (capacity - 1)
    spill_row = wide >> (capacity.bit_length() - 1)
    tile_weight = jnp.broadcast_to(weight, (SUB, cols))

    def warped(slot):
        first = tile_of[slot] * SUB + SUB - 2
        result = down[0:1] * spread[pl.ds(first, SUB), :]
        for m in range(1, TAPS_DOWN):
            result = result + down[m : m + 1] * spread[pl.ds(first + m, SUB), :]
        return result

    def message(owner, carry):
        spilled, over = carry
        target = jnp.zeros((SUB, cols), jnp.int32)
        next_spilled = jnp.zeros((SUB, cols), jnp.float32)
        next_over = jnp.zeros((SUB, cols), jnp.float32)
        tiles_here = []
        for c in range(capacity):
            slot = owner * capacity + c
            start = starts[slot]
            past = start + SUB - owned
            tile = warped(slot)
            tiles_here.append(tile)
            target = jnp.where(lane_slot == c, start + lane_row, target)
            turned = pltpu.roll(tile, start & (SUB - 1), 0)
            next_spilled = next_spilled + jnp.where(sub < past, turned, 0.0)
            next_over = jnp.where((spill_slot == c) & (spill_row < past), tile_weight, next_over)
        meta = jnp.where(segment == 1, target.astype(jnp.float32), tile_weight)
        meta = jnp.where(segment == 0, over, meta)
        tail = jnp.where(sub == SUB - 1, meta, spilled * tile_weight)
        place = place_of(owner, owners)
        out_ref[place, :data_rows, :] = jnp.concatenate(tiles_here, axis=0).astype(jnp.bfloat16)
        out_ref[place, data_rows:, :] = tail.astype(jnp.bfloat16)
        return next_spilled, next_over

    nothing = jnp.zeros((SUB, cols), jnp.float32)
    lax.fori_loop(0, owners, message, (nothing, nothing), unroll=min(owners, 16))


def sky_kernel(capacity, got_ref, coadd_ref, map_ref):
    sources, message_rows, cols = got_ref.shape
    data_rows = capacity * SUB
    owned = coadd_ref.shape[0]
    per_chunk = cols // data_rows
    chunks = sources // per_chunk
    place = iota((chunks, cols), 0)
    wide = iota((chunks, cols), 1)
    row = iota((owned, cols), 0)
    spilled = jnp.zeros((SUB, cols), jnp.float32)
    target = jnp.zeros((chunks, cols), jnp.float32)
    weight = jnp.zeros((chunks, cols), jnp.float32)
    for k in range(per_chunk):
        heads = jnp.zeros((chunks, cols), jnp.float32)
        for chunk in range(chunks):
            tail = got_ref[chunk * per_chunk + k, data_rows:, :].astype(jnp.float32)
            spilled = spilled + tail
            heads = jnp.where(place == chunk, tail[SUB - 1 :], heads)
        here = (wide >= k * data_rows) & (wide < (k + 1) * data_rows)
        target = jnp.where(here, pltpu.roll(heads, (k - 1) * data_rows % cols, 1), target)
        weight = jnp.where(here, pltpu.roll(heads, (k - 2) * data_rows % cols, 1), weight)
    target = target.astype(jnp.int32)
    pieces = [
        jnp.where(row == target[chunk : chunk + 1], weight[chunk : chunk + 1], 0.0)
        for chunk in range(chunks)
    ]
    placement = jnp.concatenate(pieces, axis=1).astype(jnp.bfloat16)
    pixels = got_ref[:, :data_rows, :].reshape(sources * data_rows, cols)
    pixels = jnp.concatenate([pixels, jnp.ones(pixels.shape, jnp.bfloat16)], axis=1)
    sums = jnp.dot(placement, pixels, preferred_element_type=jnp.float32)
    sub = iota((SUB, cols), 0)
    wide = iota((SUB, cols), 1)
    last = sub == SUB - 1
    over = jnp.broadcast_to(spilled[SUB - 1 :], (SUB, cols))
    mine = ((wide >> (capacity.bit_length() - 1)) == sub) & ~last
    over = jnp.sum(jnp.where(mine, over, 0.0), axis=1, keepdims=True)
    rest = jnp.zeros((owned - SUB, cols), jnp.float32)
    pixel_sum = sums[:, :cols] + jnp.concatenate([jnp.where(last, 0.0, spilled), rest], axis=0)
    weight_sum = sums[:, cols:] + jnp.concatenate(
        [jnp.broadcast_to(over, (SUB, cols)), rest], axis=0
    )
    coadd_ref[...] = pixel_sum / jnp.maximum(weight_sum, 1.0)
    diagonal = jnp.where(row == iota((owned, cols), 1), weight_sum, 0.0)
    map_ref[...] = jnp.sum(diagonal, axis=0, keepdims=True)


def on_device(
    image,
    row_taps,
    col_taps,
    mix_coeff,
    shift_frac,
    ccd_visit,
    visit_weight,
    tile_block,
    tile_offset,
):
    rows, cols = image.shape[1:]
    tiles = tile_block.shape[0]
    sky = lax.axis_size("sky")
    capacity = max(2, tiles // sky)
    taps, basis = row_taps.shape[1], row_taps.shape[0]
    fold = taps // 2 + 1
    visits = visit_weight.shape[0]
    largest = max(b - a for a, b in itertools.pairwise(group_edges(fold)))
    anywhere = pl.BlockSpec(memory_space=pl.ANY)
    vmem = pl.BlockSpec(memory_space=pltpu.VMEM)
    messages = pl.pallas_call(
        functools.partial(window_kernel, capacity),
        out_shape=pltpu.VMEM((sky, capacity * SUB + SUB, cols), jnp.bfloat16),
        in_specs=[anywhere] * 8 + [pl.BlockSpec(memory_space=pltpu.SMEM)],
        out_specs=vmem,
        scratch_shapes=[
            pltpu.VMEM((1, rows, cols), jnp.bfloat16),
            pltpu.VMEM((taps, basis), jnp.bfloat16),
            pltpu.VMEM((taps, basis), jnp.bfloat16),
            pltpu.VMEM((3, 1, basis), jnp.float32),
            pltpu.VMEM((1, visits), jnp.bfloat16),
            pltpu.SMEM((1, 2), jnp.float32),
            pltpu.SMEM((tiles,), jnp.int32),
            pltpu.SMEM((tiles,), jnp.int32),
            pltpu.SemaphoreType.DMA((7 + IMAGE_PIECES,)),
            pltpu.VMEM((rows + 2 * fold, cols), jnp.float32),
            pltpu.VMEM((2 * fold, basis), jnp.float32),
            pltpu.VMEM((3, 2 * fold, cols), jnp.float32),
            pltpu.VMEM((largest * 2 * cols, 2 * cols), jnp.bfloat16),
            pltpu.VMEM((largest * 2 * cols, 2 * cols), jnp.bfloat16),
            pltpu.VMEM(((3 * fold - 1) * (rows // fold), cols), jnp.bfloat16),
            pltpu.VMEM((rows, 2 * cols), jnp.float32),
            pltpu.VMEM((rows + 2 * SUB, cols), jnp.float32),
            pltpu.SMEM((sky * capacity,), jnp.int32),
            pltpu.SMEM((sky * capacity,), jnp.int32),
            pltpu.SMEM((sky,), jnp.int32),
        ],
        compiler_params=pltpu.CompilerParams(vmem_limit_bytes=LARGE_VMEM),
        name="match_warp_pack",
    )(
        *[
            pltpu.with_memory_space_constraint(value, pltpu.HBM)
            for value in (
                image,
                row_taps.T,
                col_taps.T,
                mix_coeff.transpose(1, 0, 2),
                visit_weight.reshape(1, -1),
                shift_frac,
                tile_block,
                tile_offset,
            )
        ],
        ccd_visit,
    )
    order = sorted(range(sky), key=lambda owner: place_of(owner, sky))
    received = lax.all_to_all(
        messages, "sky", split_axis=0, concat_axis=0, axis_index_groups=[order], tiled=True
    )
    coadd, weight_map = pl.pallas_call(
        functools.partial(sky_kernel, capacity),
        out_shape=(
            jax.ShapeDtypeStruct((BLK_DEV * SUB, cols), jnp.float32),
            jax.ShapeDtypeStruct((1, BLK_DEV * SUB), jnp.float32),
        ),
        in_specs=[vmem],
        out_specs=(vmem, vmem),
        compiler_params=pltpu.CompilerParams(vmem_limit_bytes=SMALL_VMEM),
        name="place_normalise",
    )(received)
    return coadd, weight_map.reshape(-1)


def solution(mesh):
    return jax.shard_map(
        on_device,
        mesh=mesh,
        in_specs=(
            P(("groups", "sky"), None, None),
            P(),
            P(),
            P(("groups", "sky"), None, None),
            P(("groups", "sky"), None),
            P(("groups", "sky")),
            P("groups"),
            P(("groups", "sky")),
            P(("groups", "sky")),
        ),
        out_specs=(P(("groups", "sky"), None), P(("groups", "sky"))),
        check_vma=False,
    )
```

```python
import functools
import itertools

import jax
import jax.numpy as jnp
from jax import lax
from jax.experimental import pallas as pl
from jax.experimental.pallas import tpu as pltpu
from jax.sharding import PartitionSpec as P

BLK_DEV = 16
SUB = 8
LARGE_VMEM = 32 * 1024 * 1024
SMALL_VMEM = 16 * 1024 * 1024
EMPTY = -64
TAPS_DOWN = 6


def iota(shape, axis):
    return lax.broadcasted_iota(jnp.int32, shape, axis)


def weight_of(visit_ref, weight_ref):
    values = weight_ref[...].astype(jnp.float32)
    chosen = jnp.where(iota(values.shape, 1) == visit_ref[0], values, 0.0)
    return jnp.sum(chosen, axis=1, keepdims=True)


def lanczos_rows(frac_ref, cols):
    row = iota((2 * SUB, cols), 0)
    tap = jnp.where(row < SUB, row, row - SUB)
    fraction = jnp.where(row < SUB, frac_ref[0, 1], frac_ref[0, 0])
    angles = jnp.pi * ((tap - 2).astype(jnp.float32) - fraction)
    third = angles / 3.0
    kernel = jnp.sin(angles) / angles * (jnp.sin(third) / third)
    kernel = jnp.where(tap < TAPS_DOWN, kernel, 0.0)
    across, down = kernel[:SUB], kernel[SUB:]
    across = across / jnp.sum(across, axis=0, keepdims=True)
    down = down / jnp.sum(down, axis=0, keepdims=True)
    return across, down


def combined_taps(row_ref, col_ref, mix_ref, lifted, base):
    taps, basis = row_ref.shape
    count, cols = base.shape[1:]
    half = taps // 2
    l, s = iota((cols, taps), 0), iota((cols, taps), 1)
    turned = ((s + l == half) | (s + l == half + cols)).astype(jnp.float32).astype(jnp.bfloat16)
    across = jnp.dot(turned, row_ref[...], preferred_element_type=jnp.float32)
    across = across.astype(jnp.bfloat16)
    lifted[0:1] = jnp.zeros((1, basis), jnp.float32)
    lifted[1:] = col_ref[...].astype(jnp.float32)
    down = lifted[...]
    scaled = jnp.concatenate([down * mix_ref[term] for term in range(3)], axis=0)
    high = scaled.astype(jnp.bfloat16)
    low = (scaled - high.astype(jnp.float32)).astype(jnp.bfloat16)
    found = lax.dot_general(
        jnp.concatenate([high, low], axis=0),
        across,
        (((1,), (1,)), ((), ())),
        preferred_element_type=jnp.float32,
    )
    found = found[: 3 * count] + found[3 * count :]
    lane = iota((count, cols), 1)
    lane = jnp.where(lane < cols // 2, lane, lane - cols).astype(jnp.float32)
    base[0] = found[:count] + (2.0 / cols) * lane * found[count : 2 * count]
    base[1] = found[count : 2 * count]
    base[2] = found[2 * count :]


def build_band(base, row, band, first):
    cols = base.shape[2]
    shape = (2 * SUB, cols)
    sub = iota(shape, 0)
    lane = iota(shape, 1)
    lane = jnp.where(lane < cols // 2, lane, lane - cols)
    first_u = (2.0 * sub.astype(jnp.float32) + 1.0) / cols - 1.0

    def spin(term):
        taps = jnp.broadcast_to(base[term, pl.ds(row, 1), :], shape)
        return pltpu.roll(taps, 0, 1, stride=1, stride_axis=0)

    slope = spin(1)
    level = spin(0) + first_u * slope
    rise = spin(2)
    whole = rise.astype(jnp.bfloat16)
    pairs = cols // (2 * SUB)
    for pair in range(pairs):
        shift = 2 * SUB * pair
        value = level + (2.0 * shift / cols) * slope
        other = whole
        if pair == 0 or pair == pairs - 1:
            inside = lane >= 0 if pair == 0 else lane < 2 * SUB
            value = jnp.where(inside, value, 0.0)
            other = jnp.where(inside, rise, 0.0).astype(jnp.bfloat16)
        value = value.astype(jnp.bfloat16)
        if pair:
            value, other = pltpu.roll(value, shift, 1), pltpu.roll(other, shift, 1)
        at = first + shift
        band[at : at + 2 * SUB, :] = jnp.concatenate([value, other], axis=1)


def place_of(owner, owners):
    slow = 1 << ((owners.bit_length() - 1) // 2)
    fast = owners // slow
    return (owner // fast + slow // 2) % slow * fast + (owner + fast // 2) % fast


def group_edges(fold):
    return [0, fold // 8, fold // 2, fold]


def window_kernel(
    capacity,
    image_hbm,
    row_hbm,
    col_hbm,
    mix_hbm,
    weight_hbm,
    frac_hbm,
    block_hbm,
    offset_hbm,
    visit_ref,
    out_ref,
    image_ref,
    row_ref,
    col_ref,
    mix_ref,
    weight_ref,
    frac_ref,
    block_ref,
    offset_ref,
    copied,
    padded,
    lifted,
    base,
    band_a,
    band_b,
    blocks,
    total,
    spread,
    tile_of,
    starts,
    counts,
):
    rows, cols = image_ref.shape[1:]
    fold = row_ref.shape[0] // 2 + 1
    deep = rows // fold
    tiles = block_ref.shape[0]
    owners = out_ref.shape[0]
    data_rows = capacity * SUB
    owned = BLK_DEV * SUB

    pairs = (
        (image_hbm, image_ref),
        (row_hbm, row_ref),
        (col_hbm, col_ref),
        (mix_hbm, mix_ref),
        (frac_hbm, frac_ref),
        (weight_hbm, weight_ref),
        (block_hbm, block_ref),
        (offset_hbm, offset_ref),
    )
    copies = [
        pltpu.make_async_copy(source, target, copied.at[index])
        for index, (source, target) in enumerate(pairs)
    ]
    for copy in copies:
        copy.start()

    @pl.loop(0, owners)
    def _(owner):
        counts[owner] = 0

    if owners * capacity > tiles:

        @pl.loop(0, owners * capacity)
        def _(slot):
            starts[slot] = EMPTY
            tile_of[slot] = 0

    padded[:fold] = jnp.zeros((fold, cols), jnp.float32)
    padded[fold + rows :] = jnp.zeros((fold, cols), jnp.float32)
    spread[:SUB] = jnp.zeros((SUB, cols), jnp.float32)
    spread[SUB + rows :] = jnp.zeros((SUB, cols), jnp.float32)
    for copy in copies:
        copy.wait()

    combined_taps(row_ref, col_ref, mix_ref, lifted, base)
    padded[fold : fold + rows] = image_ref[0].astype(jnp.float32)
    across, down = lanczos_rows(frac_ref, cols)
    weight = weight_of(visit_ref, weight_ref)

    for index in range(3 * fold - 1):
        blocks[index * deep : (index + 1) * deep, :] = padded[
            pl.ds(index, deep, stride=fold), :
        ].astype(jnp.bfloat16)

    edges = group_edges(fold)
    groups = len(edges) - 1

    def build(group, band):
        for index, r in enumerate(range(edges[group], edges[group + 1])):
            for part in range(2):
                build_band(base, r + part * fold, band, (2 * index + part) * cols)

    def multiply(group, band):
        parts = []
        for r in range(edges[group], edges[group + 1]):
            for part in range(2):
                first = (r + part * fold) * deep
                parts.append(blocks[first : first + rows, :])
        product = jnp.dot(
            jnp.concatenate(parts, axis=1),
            band[: len(parts) * cols, :],
            preferred_element_type=jnp.float32,
        )
        total[...] = product if group == 0 else total[...] + product

    def assign(tile):
        block = block_ref[tile]
        owner = lax.div(block, BLK_DEV)
        rank = counts[owner]
        counts[owner] = rank + 1
        slot = owner * capacity + rank
        tile_of[slot] = tile
        starts[slot] = (block - owner * BLK_DEV) * SUB + offset_ref[tile]

    held = (band_a, band_b)
    build(0, held[0])
    for group in range(groups):
        if group + 1 < groups:
            build(group + 1, held[(group + 1) % 2])
        multiply(group, held[group % 2])
        for tile in range(group * tiles // groups, (group + 1) * tiles // groups):
            assign(tile)

    lane = iota((1, cols), 1)
    taps_across = [
        jnp.where((lane + m - 2 >= 0) & (lane + m - 2 < cols), across[m : m + 1], 0.0)
        for m in range(TAPS_DOWN)
    ]
    for phase in range(fold):
        first = phase * deep
        position = 2 * (fold * iota((deep, cols), 0) + phase) + 1
        position = position.astype(jnp.float32) / rows - 1.0
        both = total[first : first + deep, :]
        matched = both[:, :cols] + position * both[:, cols:]
        result = taps_across[2] * matched
        for m in range(TAPS_DOWN):
            if m != 2:
                result = result + taps_across[m] * pltpu.roll(matched, (2 - m) % cols, 1)
        spread[pl.ds(SUB + phase, deep, stride=fold), :] = result

    sub = iota((SUB, cols), 0)
    wide = iota((SUB, cols), 1)
    segment = wide >> (data_rows.bit_length() - 1)
    lane_row = wide & (SUB - 1)
    lane_slot = (wide >> 3) & (capacity - 1)
    spill_slot = wide & (capacity - 1)
    spill_row = wide >> (capacity.bit_length() - 1)
    tile_weight = jnp.broadcast_to(weight, (SUB, cols))

    def warped(slot):
        first = tile_of[slot] * SUB + SUB - 2
        result = down[0:1] * spread[pl.ds(first, SUB), :]
        for m in range(1, TAPS_DOWN):
            result = result + down[m : m + 1] * spread[pl.ds(first + m, SUB), :]
        return result

    def message(owner, carry):
        spilled, over = carry
        target = jnp.zeros((SUB, cols), jnp.int32)
        next_spilled = jnp.zeros((SUB, cols), jnp.float32)
        next_over = jnp.zeros((SUB, cols), jnp.float32)
        tiles_here = []
        for c in range(capacity):
            slot = owner * capacity + c
            start = starts[slot]
            past = start + SUB - owned
            tile = warped(slot)
            tiles_here.append(tile)
            target = jnp.where(lane_slot == c, start + lane_row, target)
            turned = pltpu.roll(tile, start & (SUB - 1), 0)
            next_spilled = next_spilled + jnp.where(sub < past, turned, 0.0)
            next_over = jnp.where((spill_slot == c) & (spill_row < past), tile_weight, next_over)
        meta = jnp.where(segment == 1, target.astype(jnp.float32), tile_weight)
        meta = jnp.where(segment == 0, over, meta)
        tail = jnp.where(sub == SUB - 1, meta, spilled * tile_weight)
        place = place_of(owner, owners)
        out_ref[place, :data_rows, :] = jnp.concatenate(tiles_here, axis=0).astype(jnp.bfloat16)
        out_ref[place, data_rows:, :] = tail.astype(jnp.bfloat16)
        return next_spilled, next_over

    nothing = jnp.zeros((SUB, cols), jnp.float32)
    lax.fori_loop(0, owners, message, (nothing, nothing), unroll=min(owners, 16))


def sky_kernel(capacity, got_ref, coadd_ref, map_ref):
    sources, message_rows, cols = got_ref.shape
    data_rows = capacity * SUB
    owned = coadd_ref.shape[0]
    per_chunk = cols // data_rows
    chunks = sources // per_chunk
    place = iota((chunks, cols), 0)
    wide = iota((chunks, cols), 1)
    row = iota((owned, cols), 0)
    spilled = jnp.zeros((SUB, cols), jnp.float32)
    target = jnp.zeros((chunks, cols), jnp.float32)
    weight = jnp.zeros((chunks, cols), jnp.float32)
    for k in range(per_chunk):
        heads = jnp.zeros((chunks, cols), jnp.float32)
        for chunk in range(chunks):
            tail = got_ref[chunk * per_chunk + k, data_rows:, :].astype(jnp.float32)
            spilled = spilled + tail
            heads = jnp.where(place == chunk, tail[SUB - 1 :], heads)
        here = (wide >= k * data_rows) & (wide < (k + 1) * data_rows)
        target = jnp.where(here, pltpu.roll(heads, (k - 1) * data_rows % cols, 1), target)
        weight = jnp.where(here, pltpu.roll(heads, (k - 2) * data_rows % cols, 1), weight)
    target = target.astype(jnp.int32)
    pieces = [
        jnp.where(row == target[chunk : chunk + 1], weight[chunk : chunk + 1], 0.0)
        for chunk in range(chunks)
    ]
    placement = jnp.concatenate(pieces, axis=1).astype(jnp.bfloat16)
    pixels = got_ref[:, :data_rows, :].reshape(sources * data_rows, cols)
    pixels = jnp.concatenate([pixels, jnp.ones(pixels.shape, jnp.bfloat16)], axis=1)
    sums = jnp.dot(placement, pixels, preferred_element_type=jnp.float32)
    sub = iota((SUB, cols), 0)
    wide = iota((SUB, cols), 1)
    last = sub == SUB - 1
    over = jnp.broadcast_to(spilled[SUB - 1 :], (SUB, cols))
    mine = ((wide >> (capacity.bit_length() - 1)) == sub) & ~last
    over = jnp.sum(jnp.where(mine, over, 0.0), axis=1, keepdims=True)
    rest = jnp.zeros((owned - SUB, cols), jnp.float32)
    pixel_sum = sums[:, :cols] + jnp.concatenate([jnp.where(last, 0.0, spilled), rest], axis=0)
    weight_sum = sums[:, cols:] + jnp.concatenate(
        [jnp.broadcast_to(over, (SUB, cols)), rest], axis=0
    )
    coadd_ref[...] = pixel_sum / jnp.maximum(weight_sum, 1.0)
    diagonal = jnp.where(row == iota((owned, cols), 1), weight_sum, 0.0)
    map_ref[...] = jnp.sum(diagonal, axis=0, keepdims=True)


def on_device(
    image,
    row_taps,
    col_taps,
    mix_coeff,
    shift_frac,
    ccd_visit,
    visit_weight,
    tile_block,
    tile_offset,
):
    rows, cols = image.shape[1:]
    tiles = tile_block.shape[0]
    sky = lax.axis_size("sky")
    capacity = max(2, tiles // sky)
    taps, basis = row_taps.shape[1], row_taps.shape[0]
    fold = taps // 2 + 1
    visits = visit_weight.shape[0]
    largest = max(b - a for a, b in itertools.pairwise(group_edges(fold)))
    anywhere = pl.BlockSpec(memory_space=pl.ANY)
    vmem = pl.BlockSpec(memory_space=pltpu.VMEM)
    messages = pl.pallas_call(
        functools.partial(window_kernel, capacity),
        out_shape=pltpu.VMEM((sky, capacity * SUB + SUB, cols), jnp.bfloat16),
        in_specs=[anywhere] * 8 + [pl.BlockSpec(memory_space=pltpu.SMEM)],
        out_specs=vmem,
        scratch_shapes=[
            pltpu.VMEM((1, rows, cols), jnp.bfloat16),
            pltpu.VMEM((taps, basis), jnp.bfloat16),
            pltpu.VMEM((taps, basis), jnp.bfloat16),
            pltpu.VMEM((3, 1, basis), jnp.float32),
            pltpu.VMEM((1, visits), jnp.bfloat16),
            pltpu.SMEM((1, 2), jnp.float32),
            pltpu.SMEM((tiles,), jnp.int32),
            pltpu.SMEM((tiles,), jnp.int32),
            pltpu.SemaphoreType.DMA((8,)),
            pltpu.VMEM((rows + 2 * fold, cols), jnp.float32),
            pltpu.VMEM((2 * fold, basis), jnp.float32),
            pltpu.VMEM((3, 2 * fold, cols), jnp.float32),
            pltpu.VMEM((largest * 2 * cols, 2 * cols), jnp.bfloat16),
            pltpu.VMEM((largest * 2 * cols, 2 * cols), jnp.bfloat16),
            pltpu.VMEM(((3 * fold - 1) * (rows // fold), cols), jnp.bfloat16),
            pltpu.VMEM((rows, 2 * cols), jnp.float32),
            pltpu.VMEM((rows + 2 * SUB, cols), jnp.float32),
            pltpu.SMEM((sky * capacity,), jnp.int32),
            pltpu.SMEM((sky * capacity,), jnp.int32),
            pltpu.SMEM((sky,), jnp.int32),
        ],
        compiler_params=pltpu.CompilerParams(vmem_limit_bytes=LARGE_VMEM),
        name="match_warp_pack",
    )(
        *[
            pltpu.with_memory_space_constraint(value, pltpu.HBM)
            for value in (
                image,
                row_taps.T,
                col_taps.T,
                mix_coeff.transpose(1, 0, 2),
                visit_weight.reshape(1, -1),
                shift_frac,
                tile_block,
                tile_offset,
            )
        ],
        ccd_visit,
    )
    order = sorted(range(sky), key=lambda owner: place_of(owner, sky))
    received = lax.all_to_all(
        messages, "sky", split_axis=0, concat_axis=0, axis_index_groups=[order], tiled=True
    )
    coadd, weight_map = pl.pallas_call(
        functools.partial(sky_kernel, capacity),
        out_shape=(
            jax.ShapeDtypeStruct((BLK_DEV * SUB, cols), jnp.float32),
            jax.ShapeDtypeStruct((1, BLK_DEV * SUB), jnp.float32),
        ),
        in_specs=[vmem],
        out_specs=(vmem, vmem),
        compiler_params=pltpu.CompilerParams(vmem_limit_bytes=SMALL_VMEM),
        name="place_normalise",
    )(received)
    return coadd, weight_map.reshape(-1)


def solution(mesh):
    return jax.shard_map(
        on_device,
        mesh=mesh,
        in_specs=(
            P(("groups", "sky"), None, None),
            P(),
            P(),
            P(("groups", "sky"), None, None),
            P(("groups", "sky"), None),
            P(("groups", "sky")),
            P("groups"),
            P(("groups", "sky")),
            P(("groups", "sky")),
        ),
        out_specs=(P(("groups", "sky"), None), P(("groups", "sky"))),
        check_vma=False,
    )
```

```python
import functools
import itertools

import jax
import jax.numpy as jnp
from jax import lax
from jax.experimental import pallas as pl
from jax.experimental.pallas import tpu as pltpu
from jax.sharding import PartitionSpec as P

BLK_DEV = 16
SUB = 8
LARGE_VMEM = 32 * 1024 * 1024
SMALL_VMEM = 16 * 1024 * 1024
EMPTY = -64
TAPS_DOWN = 6


def iota(shape, axis):
    return lax.broadcasted_iota(jnp.int32, shape, axis)


def weight_of(visit_ref, weight_ref):
    values = weight_ref[...].astype(jnp.float32)
    chosen = jnp.where(iota(values.shape, 1) == visit_ref[0], values, 0.0)
    return jnp.sum(chosen, axis=1, keepdims=True)


def lanczos_rows(frac_ref, cols):
    row = iota((2 * SUB, cols), 0)
    tap = jnp.where(row < SUB, row, row - SUB)
    fraction = jnp.where(row < SUB, frac_ref[0, 1], frac_ref[0, 0])
    angles = jnp.pi * ((tap - 2).astype(jnp.float32) - fraction)
    third = angles / 3.0
    kernel = jnp.sin(angles) / angles * (jnp.sin(third) / third)
    kernel = jnp.where(tap < TAPS_DOWN, kernel, 0.0)
    across, down = kernel[:SUB], kernel[SUB:]
    across = across / jnp.sum(across, axis=0, keepdims=True)
    down = down / jnp.sum(down, axis=0, keepdims=True)
    return across, down


def combined_taps(row_ref, col_ref, mix_ref, lifted, base):
    taps, basis = row_ref.shape
    count, cols = base.shape[1:]
    half = taps // 2
    l, s = iota((cols, taps), 0), iota((cols, taps), 1)
    turned = ((s + l == half) | (s + l == half + cols)).astype(jnp.float32).astype(jnp.bfloat16)
    across = jnp.dot(turned, row_ref[...], preferred_element_type=jnp.float32)
    across = across.astype(jnp.bfloat16)
    lifted[0:1] = jnp.zeros((1, basis), jnp.float32)
    lifted[1:] = col_ref[...].astype(jnp.float32)
    down = lifted[...]
    scaled = jnp.concatenate([down * mix_ref[term] for term in range(3)], axis=0)
    high = scaled.astype(jnp.bfloat16)
    low = (scaled - high.astype(jnp.float32)).astype(jnp.bfloat16)
    found = lax.dot_general(
        jnp.concatenate([high, low], axis=0),
        across,
        (((1,), (1,)), ((), ())),
        preferred_element_type=jnp.float32,
    )
    found = found[: 3 * count] + found[3 * count :]
    lane = iota((count, cols), 1)
    lane = jnp.where(lane < cols // 2, lane, lane - cols).astype(jnp.float32)
    base[0] = found[:count] + (2.0 / cols) * lane * found[count : 2 * count]
    base[1] = found[count : 2 * count]
    base[2] = found[2 * count :]


def build_band(base, row, band, first):
    cols = base.shape[2]
    shape = (2 * SUB, cols)
    sub = iota(shape, 0)
    lane = iota(shape, 1)
    lane = jnp.where(lane < cols // 2, lane, lane - cols)
    first_u = (2.0 * sub.astype(jnp.float32) + 1.0) / cols - 1.0

    def spin(term):
        taps = jnp.broadcast_to(base[term, pl.ds(row, 1), :], shape)
        return pltpu.roll(taps, 0, 1, stride=1, stride_axis=0)

    slope = spin(1)
    level = spin(0) + first_u * slope
    rise = spin(2)
    whole = rise.astype(jnp.bfloat16)
    pairs = cols // (2 * SUB)
    for pair in range(pairs):
        shift = 2 * SUB * pair
        value = level + (2.0 * shift / cols) * slope
        other = whole
        if pair == 0 or pair == pairs - 1:
            inside = lane >= 0 if pair == 0 else lane < 2 * SUB
            value = jnp.where(inside, value, 0.0)
            other = jnp.where(inside, rise, 0.0).astype(jnp.bfloat16)
        value = value.astype(jnp.bfloat16)
        if pair:
            value, other = pltpu.roll(value, shift, 1), pltpu.roll(other, shift, 1)
        at = first + shift
        band[at : at + 2 * SUB, :] = jnp.concatenate([value, other], axis=1)


def place_of(owner, owners):
    slow = 1 << ((owners.bit_length() - 1) // 2)
    fast = owners // slow
    return (owner // fast + slow // 2) % slow * fast + (owner + fast // 2) % fast


def group_edges(fold):
    return [0, fold // 8, fold // 2, fold]


def window_kernel(
    capacity,
    image_hbm,
    row_hbm,
    col_hbm,
    mix_hbm,
    weight_hbm,
    frac_hbm,
    block_hbm,
    offset_hbm,
    visit_ref,
    out_ref,
    image_ref,
    row_ref,
    col_ref,
    mix_ref,
    weight_ref,
    frac_ref,
    block_ref,
    offset_ref,
    copied,
    padded,
    lifted,
    base,
    band_a,
    band_b,
    blocks,
    total,
    spread,
    tile_of,
    starts,
    counts,
):
    rows, cols = image_ref.shape[1:]
    fold = row_ref.shape[0] // 2 + 1
    deep = rows // fold
    tiles = block_ref.shape[0]
    owners = out_ref.shape[0]
    data_rows = capacity * SUB
    owned = BLK_DEV * SUB

    pairs = (
        (image_hbm, image_ref),
        (row_hbm, row_ref),
        (col_hbm, col_ref),
        (mix_hbm, mix_ref),
        (frac_hbm, frac_ref),
        (weight_hbm, weight_ref),
        (block_hbm, block_ref),
        (offset_hbm, offset_ref),
    )
    copies = [
        pltpu.make_async_copy(source, target, copied.at[index])
        for index, (source, target) in enumerate(pairs)
    ]
    for copy in copies:
        copy.start()

    @pl.loop(0, owners)
    def _(owner):
        counts[owner] = 0

    if owners * capacity > tiles:

        @pl.loop(0, owners * capacity)
        def _(slot):
            starts[slot] = EMPTY
            tile_of[slot] = 0

    padded[:fold] = jnp.zeros((fold, cols), jnp.float32)
    padded[fold + rows :] = jnp.zeros((fold, cols), jnp.float32)
    spread[:SUB] = jnp.zeros((SUB, cols), jnp.float32)
    spread[SUB + rows :] = jnp.zeros((SUB, cols), jnp.float32)
    for copy in copies:
        copy.wait()

    combined_taps(row_ref, col_ref, mix_ref, lifted, base)
    padded[fold : fold + rows] = image_ref[0].astype(jnp.float32)
    across, down = lanczos_rows(frac_ref, cols)
    weight = weight_of(visit_ref, weight_ref)

    for index in range(3 * fold - 1):
        blocks[index * deep : (index + 1) * deep, :] = padded[
            pl.ds(index, deep, stride=fold), :
        ].astype(jnp.bfloat16)

    edges = group_edges(fold)
    groups = len(edges) - 1

    def build(group, band):
        for index, r in enumerate(range(edges[group], edges[group + 1])):
            for part in range(2):
                build_band(base, r + part * fold, band, (2 * index + part) * cols)

    def multiply(group, band):
        parts = []
        for r in range(edges[group], edges[group + 1]):
            for part in range(2):
                first = (r + part * fold) * deep
                parts.append(blocks[first : first + rows, :])
        product = jnp.dot(
            jnp.concatenate(parts, axis=1),
            band[: len(parts) * cols, :],
            preferred_element_type=jnp.float32,
        )
        total[...] = product if group == 0 else total[...] + product

    def assign(tile):
        block = block_ref[tile]
        owner = lax.div(block, BLK_DEV)
        rank = counts[owner]
        counts[owner] = rank + 1
        slot = owner * capacity + rank
        tile_of[slot] = tile
        starts[slot] = (block - owner * BLK_DEV) * SUB + offset_ref[tile]

    held = (band_a, band_b)
    build(0, held[0])
    for group in range(groups):
        multiply(group, held[group % 2])
        if group + 1 < groups:
            build(group + 1, held[(group + 1) % 2])
        for tile in range(group * tiles // groups, (group + 1) * tiles // groups):
            assign(tile)

    lane = iota((1, cols), 1)
    taps_across = [
        jnp.where((lane + m - 2 >= 0) & (lane + m - 2 < cols), across[m : m + 1], 0.0)
        for m in range(TAPS_DOWN)
    ]
    for phase in range(fold):
        first = phase * deep
        position = 2 * (fold * iota((deep, cols), 0) + phase) + 1
        position = position.astype(jnp.float32) / rows - 1.0
        both = total[first : first + deep, :]
        matched = both[:, :cols] + position * both[:, cols:]
        result = taps_across[2] * matched
        for m in range(TAPS_DOWN):
            if m != 2:
                result = result + taps_across[m] * pltpu.roll(matched, (2 - m) % cols, 1)
        spread[pl.ds(SUB + phase, deep, stride=fold), :] = result

    sub = iota((SUB, cols), 0)
    wide = iota((SUB, cols), 1)
    segment = wide >> (data_rows.bit_length() - 1)
    lane_row = wide & (SUB - 1)
    lane_slot = (wide >> 3) & (capacity - 1)
    spill_slot = wide & (capacity - 1)
    spill_row = wide >> (capacity.bit_length() - 1)
    tile_weight = jnp.broadcast_to(weight, (SUB, cols))

    def warped(slot):
        first = tile_of[slot] * SUB + SUB - 2
        result = down[0:1] * spread[pl.ds(first, SUB), :]
        for m in range(1, TAPS_DOWN):
            result = result + down[m : m + 1] * spread[pl.ds(first + m, SUB), :]
        return result

    def message(owner, carry):
        spilled, over = carry
        target = jnp.zeros((SUB, cols), jnp.int32)
        next_spilled = jnp.zeros((SUB, cols), jnp.float32)
        next_over = jnp.zeros((SUB, cols), jnp.float32)
        tiles_here = []
        for c in range(capacity):
            slot = owner * capacity + c
            start = starts[slot]
            past = start + SUB - owned
            tile = warped(slot)
            tiles_here.append(tile)
            target = jnp.where(lane_slot == c, start + lane_row, target)
            turned = pltpu.roll(tile, start & (SUB - 1), 0)
            next_spilled = next_spilled + jnp.where(sub < past, turned, 0.0)
            next_over = jnp.where((spill_slot == c) & (spill_row < past), tile_weight, next_over)
        meta = jnp.where(segment == 1, target.astype(jnp.float32), tile_weight)
        meta = jnp.where(segment == 0, over, meta)
        tail = jnp.where(sub == SUB - 1, meta, spilled * tile_weight)
        place = place_of(owner, owners)
        out_ref[place, :data_rows, :] = jnp.concatenate(tiles_here, axis=0).astype(jnp.bfloat16)
        out_ref[place, data_rows:, :] = tail.astype(jnp.bfloat16)
        return next_spilled, next_over

    nothing = jnp.zeros((SUB, cols), jnp.float32)
    lax.fori_loop(0, owners, message, (nothing, nothing), unroll=min(owners, 16))


def sky_kernel(capacity, got_ref, coadd_ref, map_ref):
    sources, message_rows, cols = got_ref.shape
    data_rows = capacity * SUB
    owned = coadd_ref.shape[0]
    per_chunk = cols // data_rows
    chunks = sources // per_chunk
    place = iota((chunks, cols), 0)
    wide = iota((chunks, cols), 1)
    row = iota((owned, cols), 0)
    spilled = jnp.zeros((SUB, cols), jnp.float32)
    target = jnp.zeros((chunks, cols), jnp.float32)
    weight = jnp.zeros((chunks, cols), jnp.float32)
    for k in range(per_chunk):
        heads = jnp.zeros((chunks, cols), jnp.float32)
        for chunk in range(chunks):
            tail = got_ref[chunk * per_chunk + k, data_rows:, :].astype(jnp.float32)
            spilled = spilled + tail
            heads = jnp.where(place == chunk, tail[SUB - 1 :], heads)
        here = (wide >= k * data_rows) & (wide < (k + 1) * data_rows)
        target = jnp.where(here, pltpu.roll(heads, (k - 1) * data_rows % cols, 1), target)
        weight = jnp.where(here, pltpu.roll(heads, (k - 2) * data_rows % cols, 1), weight)
    target = target.astype(jnp.int32)
    pieces = [
        jnp.where(row == target[chunk : chunk + 1], weight[chunk : chunk + 1], 0.0)
        for chunk in range(chunks)
    ]
    placement = jnp.concatenate(pieces, axis=1).astype(jnp.bfloat16)
    pixels = got_ref[:, :data_rows, :].reshape(sources * data_rows, cols)
    pixels = jnp.concatenate([pixels, jnp.ones(pixels.shape, jnp.bfloat16)], axis=1)
    sums = jnp.dot(placement, pixels, preferred_element_type=jnp.float32)
    sub = iota((SUB, cols), 0)
    wide = iota((SUB, cols), 1)
    last = sub == SUB - 1
    over = jnp.broadcast_to(spilled[SUB - 1 :], (SUB, cols))
    mine = ((wide >> (capacity.bit_length() - 1)) == sub) & ~last
    over = jnp.sum(jnp.where(mine, over, 0.0), axis=1, keepdims=True)
    rest = jnp.zeros((owned - SUB, cols), jnp.float32)
    pixel_sum = sums[:, :cols] + jnp.concatenate([jnp.where(last, 0.0, spilled), rest], axis=0)
    weight_sum = sums[:, cols:] + jnp.concatenate(
        [jnp.broadcast_to(over, (SUB, cols)), rest], axis=0
    )
    coadd_ref[...] = pixel_sum / jnp.maximum(weight_sum, 1.0)
    diagonal = jnp.where(row == iota((owned, cols), 1), weight_sum, 0.0)
    map_ref[...] = jnp.sum(diagonal, axis=0, keepdims=True)


def on_device(
    image,
    row_taps,
    col_taps,
    mix_coeff,
    shift_frac,
    ccd_visit,
    visit_weight,
    tile_block,
    tile_offset,
):
    rows, cols = image.shape[1:]
    tiles = tile_block.shape[0]
    sky = lax.axis_size("sky")
    capacity = max(2, tiles // sky)
    taps, basis = row_taps.shape[1], row_taps.shape[0]
    fold = taps // 2 + 1
    visits = visit_weight.shape[0]
    largest = max(b - a for a, b in itertools.pairwise(group_edges(fold)))
    anywhere = pl.BlockSpec(memory_space=pl.ANY)
    vmem = pl.BlockSpec(memory_space=pltpu.VMEM)
    messages = pl.pallas_call(
        functools.partial(window_kernel, capacity),
        out_shape=pltpu.VMEM((sky, capacity * SUB + SUB, cols), jnp.bfloat16),
        in_specs=[anywhere] * 8 + [pl.BlockSpec(memory_space=pltpu.SMEM)],
        out_specs=vmem,
        scratch_shapes=[
            pltpu.VMEM((1, rows, cols), jnp.bfloat16),
            pltpu.VMEM((taps, basis), jnp.bfloat16),
            pltpu.VMEM((taps, basis), jnp.bfloat16),
            pltpu.VMEM((3, 1, basis), jnp.float32),
            pltpu.VMEM((1, visits), jnp.bfloat16),
            pltpu.SMEM((1, 2), jnp.float32),
            pltpu.SMEM((tiles,), jnp.int32),
            pltpu.SMEM((tiles,), jnp.int32),
            pltpu.SemaphoreType.DMA((8,)),
            pltpu.VMEM((rows + 2 * fold, cols), jnp.float32),
            pltpu.VMEM((2 * fold, basis), jnp.float32),
            pltpu.VMEM((3, 2 * fold, cols), jnp.float32),
            pltpu.VMEM((largest * 2 * cols, 2 * cols), jnp.bfloat16),
            pltpu.VMEM((largest * 2 * cols, 2 * cols), jnp.bfloat16),
            pltpu.VMEM(((3 * fold - 1) * (rows // fold), cols), jnp.bfloat16),
            pltpu.VMEM((rows, 2 * cols), jnp.float32),
            pltpu.VMEM((rows + 2 * SUB, cols), jnp.float32),
            pltpu.SMEM((sky * capacity,), jnp.int32),
            pltpu.SMEM((sky * capacity,), jnp.int32),
            pltpu.SMEM((sky,), jnp.int32),
        ],
        compiler_params=pltpu.CompilerParams(vmem_limit_bytes=LARGE_VMEM),
        name="match_warp_pack",
    )(
        *[
            pltpu.with_memory_space_constraint(value, pltpu.HBM)
            for value in (
                image,
                row_taps.T,
                col_taps.T,
                mix_coeff.transpose(1, 0, 2),
                visit_weight.reshape(1, -1),
                shift_frac,
                tile_block,
                tile_offset,
            )
        ],
        ccd_visit,
    )
    order = sorted(range(sky), key=lambda owner: place_of(owner, sky))
    received = lax.all_to_all(
        messages, "sky", split_axis=0, concat_axis=0, axis_index_groups=[order], tiled=True
    )
    coadd, weight_map = pl.pallas_call(
        functools.partial(sky_kernel, capacity),
        out_shape=(
            jax.ShapeDtypeStruct((BLK_DEV * SUB, cols), jnp.float32),
            jax.ShapeDtypeStruct((1, BLK_DEV * SUB), jnp.float32),
        ),
        in_specs=[vmem],
        out_specs=(vmem, vmem),
        compiler_params=pltpu.CompilerParams(vmem_limit_bytes=SMALL_VMEM),
        name="place_normalise",
    )(received)
    return coadd, weight_map.reshape(-1)


def solution(mesh):
    return jax.shard_map(
        on_device,
        mesh=mesh,
        in_specs=(
            P(("groups", "sky"), None, None),
            P(),
            P(),
            P(("groups", "sky"), None, None),
            P(("groups", "sky"), None),
            P(("groups", "sky")),
            P("groups"),
            P(("groups", "sky")),
            P(("groups", "sky")),
        ),
        out_specs=(P(("groups", "sky"), None), P(("groups", "sky"))),
        check_vma=False,
    )
```

```python
import functools
import itertools

import jax
import jax.numpy as jnp
from jax import lax
from jax.experimental import pallas as pl
from jax.experimental.pallas import tpu as pltpu
from jax.sharding import PartitionSpec as P

BLK_DEV = 16
SUB = 8
LARGE_VMEM = 32 * 1024 * 1024
SMALL_VMEM = 16 * 1024 * 1024
EMPTY = -64
TAPS_DOWN = 6


def iota(shape, axis):
    return lax.broadcasted_iota(jnp.int32, shape, axis)


def weight_of(visit_ref, weight_ref):
    values = weight_ref[...].astype(jnp.float32)
    chosen = jnp.where(iota(values.shape, 1) == visit_ref[0], values, 0.0)
    return jnp.sum(chosen, axis=1, keepdims=True)


def lanczos_rows(frac_ref, cols):
    row = iota((2 * SUB, cols), 0)
    tap = jnp.where(row < SUB, row, row - SUB)
    fraction = jnp.where(row < SUB, frac_ref[0, 1], frac_ref[0, 0])
    angles = jnp.pi * ((tap - 2).astype(jnp.float32) - fraction)
    third = angles / 3.0
    kernel = jnp.sin(angles) / angles * (jnp.sin(third) / third)
    kernel = jnp.where(tap < TAPS_DOWN, kernel, 0.0)
    across, down = kernel[:SUB], kernel[SUB:]
    across = across / jnp.sum(across, axis=0, keepdims=True)
    down = down / jnp.sum(down, axis=0, keepdims=True)
    return across, down


def combined_taps(row_ref, col_ref, mix_ref, lifted, base):
    taps, basis = row_ref.shape
    count, cols = base.shape[1:]
    half = taps // 2
    l, s = iota((cols, taps), 0), iota((cols, taps), 1)
    turned = ((s + l == half) | (s + l == half + cols)).astype(jnp.float32).astype(jnp.bfloat16)
    across = jnp.dot(turned, row_ref[...], preferred_element_type=jnp.float32)
    across = across.astype(jnp.bfloat16)
    lifted[0:1] = jnp.zeros((1, basis), jnp.float32)
    lifted[1:] = col_ref[...].astype(jnp.float32)
    down = lifted[...]
    scaled = jnp.concatenate([down * mix_ref[term] for term in range(3)], axis=0)
    high = scaled.astype(jnp.bfloat16)
    low = (scaled - high.astype(jnp.float32)).astype(jnp.bfloat16)
    found = lax.dot_general(
        jnp.concatenate([high, low], axis=0),
        across,
        (((1,), (1,)), ((), ())),
        preferred_element_type=jnp.float32,
    )
    found = found[: 3 * count] + found[3 * count :]
    lane = iota((count, cols), 1)
    lane = jnp.where(lane < cols // 2, lane, lane - cols).astype(jnp.float32)
    base[0] = found[:count] + (2.0 / cols) * lane * found[count : 2 * count]
    base[1] = found[count : 2 * count]
    base[2] = found[2 * count :]


def build_band(base, row, band, first):
    cols = base.shape[2]
    shape = (2 * SUB, cols)
    sub = iota(shape, 0)
    lane = iota(shape, 1)
    lane = jnp.where(lane < cols // 2, lane, lane - cols)
    first_u = (2.0 * sub.astype(jnp.float32) + 1.0) / cols - 1.0

    def spin(term):
        taps = jnp.broadcast_to(base[term, pl.ds(row, 1), :], shape)
        return pltpu.roll(taps, 0, 1, stride=1, stride_axis=0)

    slope = spin(1)
    level = spin(0) + first_u * slope
    rise = spin(2)
    whole = rise.astype(jnp.bfloat16)
    pairs = cols // (2 * SUB)
    for pair in range(pairs):
        shift = 2 * SUB * pair
        value = level + (2.0 * shift / cols) * slope
        other = whole
        if pair == 0 or pair == pairs - 1:
            inside = lane >= 0 if pair == 0 else lane < 2 * SUB
            value = jnp.where(inside, value, 0.0)
            other = jnp.where(inside, rise, 0.0).astype(jnp.bfloat16)
        value = value.astype(jnp.bfloat16)
        if pair:
            value, other = pltpu.roll(value, shift, 1), pltpu.roll(other, shift, 1)
        at = first + shift
        band[at : at + 2 * SUB, :] = jnp.concatenate([value, other], axis=1)


def place_of(owner, owners):
    slow = 1 << ((owners.bit_length() - 1) // 2)
    fast = owners // slow
    half = slow // 2
    far = owner // fast // half
    block = far * (owner // fast - half) + (1 - far) * (slow - 1 - owner // fast)
    return block * fast + (owner + fast // 2) % fast


def group_edges(fold):
    return [0, fold // 8, fold // 2, fold]


def window_kernel(
    capacity,
    image_hbm,
    row_hbm,
    col_hbm,
    mix_hbm,
    weight_hbm,
    frac_hbm,
    block_hbm,
    offset_hbm,
    visit_ref,
    out_ref,
    image_ref,
    row_ref,
    col_ref,
    mix_ref,
    weight_ref,
    frac_ref,
    block_ref,
    offset_ref,
    copied,
    padded,
    lifted,
    base,
    band_a,
    band_b,
    blocks,
    total,
    spread,
    tile_of,
    starts,
    counts,
):
    rows, cols = image_ref.shape[1:]
    fold = row_ref.shape[0] // 2 + 1
    deep = rows // fold
    tiles = block_ref.shape[0]
    owners = out_ref.shape[0]
    data_rows = capacity * SUB
    owned = BLK_DEV * SUB

    pairs = (
        (image_hbm, image_ref),
        (row_hbm, row_ref),
        (col_hbm, col_ref),
        (mix_hbm, mix_ref),
        (frac_hbm, frac_ref),
        (weight_hbm, weight_ref),
        (block_hbm, block_ref),
        (offset_hbm, offset_ref),
    )
    copies = [
        pltpu.make_async_copy(source, target, copied.at[index])
        for index, (source, target) in enumerate(pairs)
    ]
    for copy in copies:
        copy.start()

    @pl.loop(0, owners)
    def _(owner):
        counts[owner] = 0

    if owners * capacity > tiles:

        @pl.loop(0, owners * capacity)
        def _(slot):
            starts[slot] = EMPTY
            tile_of[slot] = 0

    padded[:fold] = jnp.zeros((fold, cols), jnp.float32)
    padded[fold + rows :] = jnp.zeros((fold, cols), jnp.float32)
    spread[:SUB] = jnp.zeros((SUB, cols), jnp.float32)
    spread[SUB + rows :] = jnp.zeros((SUB, cols), jnp.float32)
    for copy in copies:
        copy.wait()

    combined_taps(row_ref, col_ref, mix_ref, lifted, base)
    padded[fold : fold + rows] = image_ref[0].astype(jnp.float32)
    across, down = lanczos_rows(frac_ref, cols)
    weight = weight_of(visit_ref, weight_ref)

    for index in range(3 * fold - 1):
        blocks[index * deep : (index + 1) * deep, :] = padded[
            pl.ds(index, deep, stride=fold), :
        ].astype(jnp.bfloat16)

    edges = group_edges(fold)
    groups = len(edges) - 1

    def build(group, band):
        for index, r in enumerate(range(edges[group], edges[group + 1])):
            for part in range(2):
                build_band(base, r + part * fold, band, (2 * index + part) * cols)

    def multiply(group, band):
        parts = []
        for r in range(edges[group], edges[group + 1]):
            for part in range(2):
                first = (r + part * fold) * deep
                parts.append(blocks[first : first + rows, :])
        product = jnp.dot(
            jnp.concatenate(parts, axis=1),
            band[: len(parts) * cols, :],
            preferred_element_type=jnp.float32,
        )
        total[...] = product if group == 0 else total[...] + product

    def assign(tile):
        block = block_ref[tile]
        owner = lax.div(block, BLK_DEV)
        rank = counts[owner]
        counts[owner] = rank + 1
        slot = owner * capacity + rank
        tile_of[slot] = tile
        starts[slot] = (block - owner * BLK_DEV) * SUB + offset_ref[tile]

    held = (band_a, band_b)
    build(0, held[0])
    for group in range(groups):
        if group + 1 < groups:
            build(group + 1, held[(group + 1) % 2])
        multiply(group, held[group % 2])
        for tile in range(group * tiles // groups, (group + 1) * tiles // groups):
            assign(tile)

    lane = iota((1, cols), 1)
    taps_across = [
        jnp.where((lane + m - 2 >= 0) & (lane + m - 2 < cols), across[m : m + 1], 0.0)
        for m in range(TAPS_DOWN)
    ]
    for phase in range(fold):
        first = phase * deep
        position = 2 * (fold * iota((deep, cols), 0) + phase) + 1
        position = position.astype(jnp.float32) / rows - 1.0
        both = total[first : first + deep, :]
        matched = both[:, :cols] + position * both[:, cols:]
        result = taps_across[2] * matched
        for m in range(TAPS_DOWN):
            if m != 2:
                result = result + taps_across[m] * pltpu.roll(matched, (2 - m) % cols, 1)
        spread[pl.ds(SUB + phase, deep, stride=fold), :] = result

    sub = iota((SUB, cols), 0)
    wide = iota((SUB, cols), 1)
    segment = wide >> (data_rows.bit_length() - 1)
    lane_row = wide & (SUB - 1)
    lane_slot = (wide >> 3) & (capacity - 1)
    spill_slot = wide & (capacity - 1)
    spill_row = wide >> (capacity.bit_length() - 1)
    tile_weight = jnp.broadcast_to(weight, (SUB, cols))

    def warped(slot):
        first = tile_of[slot] * SUB + SUB - 2
        result = down[0:1] * spread[pl.ds(first, SUB), :]
        for m in range(1, TAPS_DOWN):
            result = result + down[m : m + 1] * spread[pl.ds(first + m, SUB), :]
        return result

    def message(owner, carry):
        spilled, over = carry
        target = jnp.zeros((SUB, cols), jnp.int32)
        next_spilled = jnp.zeros((SUB, cols), jnp.float32)
        next_over = jnp.zeros((SUB, cols), jnp.float32)
        tiles_here = []
        for c in range(capacity):
            slot = owner * capacity + c
            start = starts[slot]
            past = start + SUB - owned
            tile = warped(slot)
            tiles_here.append(tile)
            target = jnp.where(lane_slot == c, start + lane_row, target)
            turned = pltpu.roll(tile, start & (SUB - 1), 0)
            next_spilled = next_spilled + jnp.where(sub < past, turned, 0.0)
            next_over = jnp.where((spill_slot == c) & (spill_row < past), tile_weight, next_over)
        meta = jnp.where(segment == 1, target.astype(jnp.float32), tile_weight)
        meta = jnp.where(segment == 0, over, meta)
        tail = jnp.where(sub == SUB - 1, meta, spilled * tile_weight)
        place = place_of(owner, owners)
        out_ref[place, :data_rows, :] = jnp.concatenate(tiles_here, axis=0).astype(jnp.bfloat16)
        out_ref[place, data_rows:, :] = tail.astype(jnp.bfloat16)
        return next_spilled, next_over

    nothing = jnp.zeros((SUB, cols), jnp.float32)
    lax.fori_loop(0, owners, message, (nothing, nothing), unroll=min(owners, 16))


def sky_kernel(capacity, got_ref, coadd_ref, map_ref):
    sources, message_rows, cols = got_ref.shape
    data_rows = capacity * SUB
    owned = coadd_ref.shape[0]
    per_chunk = cols // data_rows
    chunks = sources // per_chunk
    place = iota((chunks, cols), 0)
    wide = iota((chunks, cols), 1)
    row = iota((owned, cols), 0)
    spilled = jnp.zeros((SUB, cols), jnp.float32)
    target = jnp.zeros((chunks, cols), jnp.float32)
    weight = jnp.zeros((chunks, cols), jnp.float32)
    for k in range(per_chunk):
        heads = jnp.zeros((chunks, cols), jnp.float32)
        for chunk in range(chunks):
            tail = got_ref[chunk * per_chunk + k, data_rows:, :].astype(jnp.float32)
            spilled = spilled + tail
            heads = jnp.where(place == chunk, tail[SUB - 1 :], heads)
        here = (wide >= k * data_rows) & (wide < (k + 1) * data_rows)
        target = jnp.where(here, pltpu.roll(heads, (k - 1) * data_rows % cols, 1), target)
        weight = jnp.where(here, pltpu.roll(heads, (k - 2) * data_rows % cols, 1), weight)
    target = target.astype(jnp.int32)
    pieces = [
        jnp.where(row == target[chunk : chunk + 1], weight[chunk : chunk + 1], 0.0)
        for chunk in range(chunks)
    ]
    placement = jnp.concatenate(pieces, axis=1).astype(jnp.bfloat16)
    pixels = got_ref[:, :data_rows, :].reshape(sources * data_rows, cols)
    pixels = jnp.concatenate([pixels, jnp.ones(pixels.shape, jnp.bfloat16)], axis=1)
    sums = jnp.dot(placement, pixels, preferred_element_type=jnp.float32)
    sub = iota((SUB, cols), 0)
    wide = iota((SUB, cols), 1)
    last = sub == SUB - 1
    over = jnp.broadcast_to(spilled[SUB - 1 :], (SUB, cols))
    mine = ((wide >> (capacity.bit_length() - 1)) == sub) & ~last
    over = jnp.sum(jnp.where(mine, over, 0.0), axis=1, keepdims=True)
    rest = jnp.zeros((owned - SUB, cols), jnp.float32)
    pixel_sum = sums[:, :cols] + jnp.concatenate([jnp.where(last, 0.0, spilled), rest], axis=0)
    weight_sum = sums[:, cols:] + jnp.concatenate(
        [jnp.broadcast_to(over, (SUB, cols)), rest], axis=0
    )
    coadd_ref[...] = pixel_sum / jnp.maximum(weight_sum, 1.0)
    diagonal = jnp.where(row == iota((owned, cols), 1), weight_sum, 0.0)
    map_ref[...] = jnp.sum(diagonal, axis=0, keepdims=True)


def on_device(
    image,
    row_taps,
    col_taps,
    mix_coeff,
    shift_frac,
    ccd_visit,
    visit_weight,
    tile_block,
    tile_offset,
):
    rows, cols = image.shape[1:]
    tiles = tile_block.shape[0]
    sky = lax.axis_size("sky")
    capacity = max(2, tiles // sky)
    taps, basis = row_taps.shape[1], row_taps.shape[0]
    fold = taps // 2 + 1
    visits = visit_weight.shape[0]
    largest = max(b - a for a, b in itertools.pairwise(group_edges(fold)))
    anywhere = pl.BlockSpec(memory_space=pl.ANY)
    vmem = pl.BlockSpec(memory_space=pltpu.VMEM)
    messages = pl.pallas_call(
        functools.partial(window_kernel, capacity),
        out_shape=pltpu.VMEM((sky, capacity * SUB + SUB, cols), jnp.bfloat16),
        in_specs=[anywhere] * 8 + [pl.BlockSpec(memory_space=pltpu.SMEM)],
        out_specs=vmem,
        scratch_shapes=[
            pltpu.VMEM((1, rows, cols), jnp.bfloat16),
            pltpu.VMEM((taps, basis), jnp.bfloat16),
            pltpu.VMEM((taps, basis), jnp.bfloat16),
            pltpu.VMEM((3, 1, basis), jnp.float32),
            pltpu.VMEM((1, visits), jnp.bfloat16),
            pltpu.SMEM((1, 2), jnp.float32),
            pltpu.SMEM((tiles,), jnp.int32),
            pltpu.SMEM((tiles,), jnp.int32),
            pltpu.SemaphoreType.DMA((8,)),
            pltpu.VMEM((rows + 2 * fold, cols), jnp.float32),
            pltpu.VMEM((2 * fold, basis), jnp.float32),
            pltpu.VMEM((3, 2 * fold, cols), jnp.float32),
            pltpu.VMEM((largest * 2 * cols, 2 * cols), jnp.bfloat16),
            pltpu.VMEM((largest * 2 * cols, 2 * cols), jnp.bfloat16),
            pltpu.VMEM(((3 * fold - 1) * (rows // fold), cols), jnp.bfloat16),
            pltpu.VMEM((rows, 2 * cols), jnp.float32),
            pltpu.VMEM((rows + 2 * SUB, cols), jnp.float32),
            pltpu.SMEM((sky * capacity,), jnp.int32),
            pltpu.SMEM((sky * capacity,), jnp.int32),
            pltpu.SMEM((sky,), jnp.int32),
        ],
        compiler_params=pltpu.CompilerParams(vmem_limit_bytes=LARGE_VMEM),
        name="match_warp_pack",
    )(
        *[
            pltpu.with_memory_space_constraint(value, pltpu.HBM)
            for value in (
                image,
                row_taps.T,
                col_taps.T,
                mix_coeff.transpose(1, 0, 2),
                visit_weight.reshape(1, -1),
                shift_frac,
                tile_block,
                tile_offset,
            )
        ],
        ccd_visit,
    )
    order = sorted(range(sky), key=lambda owner: place_of(owner, sky))
    received = lax.all_to_all(
        messages, "sky", split_axis=0, concat_axis=0, axis_index_groups=[order], tiled=True
    )
    coadd, weight_map = pl.pallas_call(
        functools.partial(sky_kernel, capacity),
        out_shape=(
            jax.ShapeDtypeStruct((BLK_DEV * SUB, cols), jnp.float32),
            jax.ShapeDtypeStruct((1, BLK_DEV * SUB), jnp.float32),
        ),
        in_specs=[vmem],
        out_specs=(vmem, vmem),
        compiler_params=pltpu.CompilerParams(vmem_limit_bytes=SMALL_VMEM),
        name="place_normalise",
    )(received)
    return coadd, weight_map.reshape(-1)


def solution(mesh):
    return jax.shard_map(
        on_device,
        mesh=mesh,
        in_specs=(
            P(("groups", "sky"), None, None),
            P(),
            P(),
            P(("groups", "sky"), None, None),
            P(("groups", "sky"), None),
            P(("groups", "sky")),
            P("groups"),
            P(("groups", "sky")),
            P(("groups", "sky")),
        ),
        out_specs=(P(("groups", "sky"), None), P(("groups", "sky"))),
        check_vma=False,
    )
```

```python
import functools
import itertools

import jax
import jax.numpy as jnp
from jax import lax
from jax.experimental import pallas as pl
from jax.experimental.pallas import tpu as pltpu
from jax.sharding import PartitionSpec as P

BLK_DEV = 16
SUB = 8
LARGE_VMEM = 32 * 1024 * 1024
SMALL_VMEM = 16 * 1024 * 1024
EMPTY = -64
TAPS_DOWN = 6


def iota(shape, axis):
    return lax.broadcasted_iota(jnp.int32, shape, axis)


def weight_of(visit_ref, weight_ref):
    values = weight_ref[...].astype(jnp.float32)
    chosen = jnp.where(iota(values.shape, 1) == visit_ref[0], values, 0.0)
    return jnp.sum(chosen, axis=1, keepdims=True)


def lanczos_rows(frac_ref, cols):
    row = iota((2 * SUB, cols), 0)
    tap = jnp.where(row < SUB, row, row - SUB)
    fraction = jnp.where(row < SUB, frac_ref[0, 1], frac_ref[0, 0])
    angles = jnp.pi * ((tap - 2).astype(jnp.float32) - fraction)
    third = angles / 3.0
    kernel = jnp.sin(angles) / angles * (jnp.sin(third) / third)
    kernel = jnp.where(tap < TAPS_DOWN, kernel, 0.0)
    across, down = kernel[:SUB], kernel[SUB:]
    across = across / jnp.sum(across, axis=0, keepdims=True)
    down = down / jnp.sum(down, axis=0, keepdims=True)
    return across, down


def combined_taps(row_ref, col_ref, mix_ref, lifted, base):
    taps, basis = row_ref.shape
    count, cols = base.shape[1:]
    half = taps // 2
    l, s = iota((cols, taps), 0), iota((cols, taps), 1)
    turned = ((s + l == half) | (s + l == half + cols)).astype(jnp.float32).astype(jnp.bfloat16)
    across = jnp.dot(turned, row_ref[...], preferred_element_type=jnp.float32)
    across = across.astype(jnp.bfloat16)
    lifted[0:1] = jnp.zeros((1, basis), jnp.float32)
    lifted[1:] = col_ref[...].astype(jnp.float32)
    down = lifted[...]
    scaled = jnp.concatenate([down * mix_ref[term] for term in range(3)], axis=0)
    high = scaled.astype(jnp.bfloat16)
    low = (scaled - high.astype(jnp.float32)).astype(jnp.bfloat16)
    found = lax.dot_general(
        jnp.concatenate([high, low], axis=0),
        across,
        (((1,), (1,)), ((), ())),
        preferred_element_type=jnp.float32,
    )
    found = found[: 3 * count] + found[3 * count :]
    lane = iota((count, cols), 1)
    lane = jnp.where(lane < cols // 2, lane, lane - cols).astype(jnp.float32)
    base[0] = found[:count] + (2.0 / cols) * lane * found[count : 2 * count]
    base[1] = found[count : 2 * count]
    base[2] = found[2 * count :]


def build_band(base, row, band, first):
    cols = base.shape[2]
    shape = (2 * SUB, cols)
    sub = iota(shape, 0)
    lane = iota(shape, 1)
    lane = jnp.where(lane < cols // 2, lane, lane - cols)
    first_u = (2.0 * sub.astype(jnp.float32) + 1.0) / cols - 1.0

    def spin(term):
        taps = jnp.broadcast_to(base[term, pl.ds(row, 1), :], shape)
        return pltpu.roll(taps, 0, 1, stride=1, stride_axis=0)

    slope = spin(1)
    level = spin(0) + first_u * slope
    rise = spin(2)
    whole = rise.astype(jnp.bfloat16)
    pairs = cols // (2 * SUB)
    for pair in range(pairs):
        shift = 2 * SUB * pair
        value = level + (2.0 * shift / cols) * slope
        other = whole
        if pair == 0 or pair == pairs - 1:
            inside = lane >= 0 if pair == 0 else lane < 2 * SUB
            value = jnp.where(inside, value, 0.0)
            other = jnp.where(inside, rise, 0.0).astype(jnp.bfloat16)
        value = value.astype(jnp.bfloat16)
        if pair:
            value, other = pltpu.roll(value, shift, 1), pltpu.roll(other, shift, 1)
        at = first + shift
        band[at : at + 2 * SUB, :] = jnp.concatenate([value, other], axis=1)


def place_of(owner, owners):
    slow = 1 << ((owners.bit_length() - 1) // 2)
    fast = owners // slow
    return (owner // fast + slow // 2) % slow * fast + (owner + fast // 2) % fast


def group_edges(fold):
    return [0, fold // 8, fold // 2, fold]


def window_kernel(
    capacity,
    image_hbm,
    row_hbm,
    col_hbm,
    mix_hbm,
    weight_hbm,
    frac_hbm,
    block_hbm,
    offset_hbm,
    visit_ref,
    out_ref,
    image_ref,
    row_ref,
    col_ref,
    mix_ref,
    weight_ref,
    frac_ref,
    block_ref,
    offset_ref,
    copied,
    padded,
    lifted,
    base,
    band_a,
    band_b,
    blocks,
    total,
    spread,
    tile_of,
    starts,
    counts,
):
    rows, cols = image_ref.shape[1:]
    fold = row_ref.shape[0] // 2 + 1
    deep = rows // fold
    tiles = block_ref.shape[0]
    owners = out_ref.shape[0]
    data_rows = capacity * SUB
    owned = BLK_DEV * SUB

    pairs = (
        (image_hbm, image_ref),
        (row_hbm, row_ref),
        (col_hbm, col_ref),
        (mix_hbm, mix_ref),
        (frac_hbm, frac_ref),
        (weight_hbm, weight_ref),
        (block_hbm, block_ref),
        (offset_hbm, offset_ref),
    )
    copies = [
        pltpu.make_async_copy(source, target, copied.at[index])
        for index, (source, target) in enumerate(pairs)
    ]
    for copy in copies:
        copy.start()

    @pl.loop(0, owners)
    def _(owner):
        counts[owner] = 0

    if owners * capacity > tiles:

        @pl.loop(0, owners * capacity)
        def _(slot):
            starts[slot] = EMPTY
            tile_of[slot] = 0

    padded[:fold] = jnp.zeros((fold, cols), jnp.float32)
    padded[fold + rows :] = jnp.zeros((fold, cols), jnp.float32)
    spread[:SUB] = jnp.zeros((SUB, cols), jnp.float32)
    spread[SUB + rows :] = jnp.zeros((SUB, cols), jnp.float32)
    for copy in copies[1:4]:
        copy.wait()
    combined_taps(row_ref, col_ref, mix_ref, lifted, base)
    for copy in copies[:1] + copies[4:]:
        copy.wait()
    padded[fold : fold + rows] = image_ref[0].astype(jnp.float32)
    across, down = lanczos_rows(frac_ref, cols)
    weight = weight_of(visit_ref, weight_ref)

    for index in range(3 * fold - 1):
        blocks[index * deep : (index + 1) * deep, :] = padded[
            pl.ds(index, deep, stride=fold), :
        ].astype(jnp.bfloat16)

    edges = group_edges(fold)
    groups = len(edges) - 1

    def build(group, band):
        for index, r in enumerate(range(edges[group], edges[group + 1])):
            for part in range(2):
                build_band(base, r + part * fold, band, (2 * index + part) * cols)

    def multiply(group, band):
        parts = []
        for r in range(edges[group], edges[group + 1]):
            for part in range(2):
                first = (r + part * fold) * deep
                parts.append(blocks[first : first + rows, :])
        product = jnp.dot(
            jnp.concatenate(parts, axis=1),
            band[: len(parts) * cols, :],
            preferred_element_type=jnp.float32,
        )
        total[...] = product if group == 0 else total[...] + product

    def assign(tile):
        block = block_ref[tile]
        owner = lax.div(block, BLK_DEV)
        rank = counts[owner]
        counts[owner] = rank + 1
        slot = owner * capacity + rank
        tile_of[slot] = tile
        starts[slot] = (block - owner * BLK_DEV) * SUB + offset_ref[tile]

    held = (band_a, band_b)
    build(0, held[0])
    for group in range(groups):
        if group + 1 < groups:
            build(group + 1, held[(group + 1) % 2])
        multiply(group, held[group % 2])
        for tile in range(group * tiles // groups, (group + 1) * tiles // groups):
            assign(tile)

    lane = iota((1, cols), 1)
    taps_across = [
        jnp.where((lane + m - 2 >= 0) & (lane + m - 2 < cols), across[m : m + 1], 0.0)
        for m in range(TAPS_DOWN)
    ]
    for phase in range(fold):
        first = phase * deep
        position = 2 * (fold * iota((deep, cols), 0) + phase) + 1
        position = position.astype(jnp.float32) / rows - 1.0
        both = total[first : first + deep, :]
        matched = both[:, :cols] + position * both[:, cols:]
        result = taps_across[2] * matched
        for m in range(TAPS_DOWN):
            if m != 2:
                result = result + taps_across[m] * pltpu.roll(matched, (2 - m) % cols, 1)
        spread[pl.ds(SUB + phase, deep, stride=fold), :] = result

    sub = iota((SUB, cols), 0)
    wide = iota((SUB, cols), 1)
    segment = wide >> (data_rows.bit_length() - 1)
    lane_row = wide & (SUB - 1)
    lane_slot = (wide >> 3) & (capacity - 1)
    spill_slot = wide & (capacity - 1)
    spill_row = wide >> (capacity.bit_length() - 1)
    tile_weight = jnp.broadcast_to(weight, (SUB, cols))

    def warped(slot):
        first = tile_of[slot] * SUB + SUB - 2
        result = down[0:1] * spread[pl.ds(first, SUB), :]
        for m in range(1, TAPS_DOWN):
            result = result + down[m : m + 1] * spread[pl.ds(first + m, SUB), :]
        return result

    def message(owner, carry):
        spilled, over = carry
        target = jnp.zeros((SUB, cols), jnp.int32)
        next_spilled = jnp.zeros((SUB, cols), jnp.float32)
        next_over = jnp.zeros((SUB, cols), jnp.float32)
        tiles_here = []
        for c in range(capacity):
            slot = owner * capacity + c
            start = starts[slot]
            past = start + SUB - owned
            tile = warped(slot)
            tiles_here.append(tile)
            target = jnp.where(lane_slot == c, start + lane_row, target)
            turned = pltpu.roll(tile, start & (SUB - 1), 0)
            next_spilled = next_spilled + jnp.where(sub < past, turned, 0.0)
            next_over = jnp.where((spill_slot == c) & (spill_row < past), tile_weight, next_over)
        meta = jnp.where(segment == 1, target.astype(jnp.float32), tile_weight)
        meta = jnp.where(segment == 0, over, meta)
        tail = jnp.where(sub == SUB - 1, meta, spilled * tile_weight)
        place = place_of(owner, owners)
        out_ref[place, :data_rows, :] = jnp.concatenate(tiles_here, axis=0).astype(jnp.bfloat16)
        out_ref[place, data_rows:, :] = tail.astype(jnp.bfloat16)
        return next_spilled, next_over

    nothing = jnp.zeros((SUB, cols), jnp.float32)
    lax.fori_loop(0, owners, message, (nothing, nothing), unroll=min(owners, 16))


def sky_kernel(capacity, got_ref, coadd_ref, map_ref):
    sources, message_rows, cols = got_ref.shape
    data_rows = capacity * SUB
    owned = coadd_ref.shape[0]
    per_chunk = cols // data_rows
    chunks = sources // per_chunk
    place = iota((chunks, cols), 0)
    wide = iota((chunks, cols), 1)
    row = iota((owned, cols), 0)
    spilled = jnp.zeros((SUB, cols), jnp.float32)
    target = jnp.zeros((chunks, cols), jnp.float32)
    weight = jnp.zeros((chunks, cols), jnp.float32)
    for k in range(per_chunk):
        heads = jnp.zeros((chunks, cols), jnp.float32)
        for chunk in range(chunks):
            tail = got_ref[chunk * per_chunk + k, data_rows:, :].astype(jnp.float32)
            spilled = spilled + tail
            heads = jnp.where(place == chunk, tail[SUB - 1 :], heads)
        here = (wide >= k * data_rows) & (wide < (k + 1) * data_rows)
        target = jnp.where(here, pltpu.roll(heads, (k - 1) * data_rows % cols, 1), target)
        weight = jnp.where(here, pltpu.roll(heads, (k - 2) * data_rows % cols, 1), weight)
    target = target.astype(jnp.int32)
    pieces = [
        jnp.where(row == target[chunk : chunk + 1], weight[chunk : chunk + 1], 0.0)
        for chunk in range(chunks)
    ]
    placement = jnp.concatenate(pieces, axis=1).astype(jnp.bfloat16)
    pixels = got_ref[:, :data_rows, :].reshape(sources * data_rows, cols)
    pixels = jnp.concatenate([pixels, jnp.ones(pixels.shape, jnp.bfloat16)], axis=1)
    sums = jnp.dot(placement, pixels, preferred_element_type=jnp.float32)
    sub = iota((SUB, cols), 0)
    wide = iota((SUB, cols), 1)
    last = sub == SUB - 1
    over = jnp.broadcast_to(spilled[SUB - 1 :], (SUB, cols))
    mine = ((wide >> (capacity.bit_length() - 1)) == sub) & ~last
    over = jnp.sum(jnp.where(mine, over, 0.0), axis=1, keepdims=True)
    rest = jnp.zeros((owned - SUB, cols), jnp.float32)
    pixel_sum = sums[:, :cols] + jnp.concatenate([jnp.where(last, 0.0, spilled), rest], axis=0)
    weight_sum = sums[:, cols:] + jnp.concatenate(
        [jnp.broadcast_to(over, (SUB, cols)), rest], axis=0
    )
    coadd_ref[...] = pixel_sum / jnp.maximum(weight_sum, 1.0)
    diagonal = jnp.where(row == iota((owned, cols), 1), weight_sum, 0.0)
    map_ref[...] = jnp.sum(diagonal, axis=0, keepdims=True)


def on_device(
    image,
    row_taps,
    col_taps,
    mix_coeff,
    shift_frac,
    ccd_visit,
    visit_weight,
    tile_block,
    tile_offset,
):
    rows, cols = image.shape[1:]
    tiles = tile_block.shape[0]
    sky = lax.axis_size("sky")
    capacity = max(2, tiles // sky)
    taps, basis = row_taps.shape[1], row_taps.shape[0]
    fold = taps // 2 + 1
    visits = visit_weight.shape[0]
    largest = max(b - a for a, b in itertools.pairwise(group_edges(fold)))
    anywhere = pl.BlockSpec(memory_space=pl.ANY)
    vmem = pl.BlockSpec(memory_space=pltpu.VMEM)
    messages = pl.pallas_call(
        functools.partial(window_kernel, capacity),
        out_shape=pltpu.VMEM((sky, capacity * SUB + SUB, cols), jnp.bfloat16),
        in_specs=[anywhere] * 8 + [pl.BlockSpec(memory_space=pltpu.SMEM)],
        out_specs=vmem,
        scratch_shapes=[
            pltpu.VMEM((1, rows, cols), jnp.bfloat16),
            pltpu.VMEM((taps, basis), jnp.bfloat16),
            pltpu.VMEM((taps, basis), jnp.bfloat16),
            pltpu.VMEM((3, 1, basis), jnp.float32),
            pltpu.VMEM((1, visits), jnp.bfloat16),
            pltpu.SMEM((1, 2), jnp.float32),
            pltpu.SMEM((tiles,), jnp.int32),
            pltpu.SMEM((tiles,), jnp.int32),
            pltpu.SemaphoreType.DMA((8,)),
            pltpu.VMEM((rows + 2 * fold, cols), jnp.float32),
            pltpu.VMEM((2 * fold, basis), jnp.float32),
            pltpu.VMEM((3, 2 * fold, cols), jnp.float32),
            pltpu.VMEM((largest * 2 * cols, 2 * cols), jnp.bfloat16),
            pltpu.VMEM((largest * 2 * cols, 2 * cols), jnp.bfloat16),
            pltpu.VMEM(((3 * fold - 1) * (rows // fold), cols), jnp.bfloat16),
            pltpu.VMEM((rows, 2 * cols), jnp.float32),
            pltpu.VMEM((rows + 2 * SUB, cols), jnp.float32),
            pltpu.SMEM((sky * capacity,), jnp.int32),
            pltpu.SMEM((sky * capacity,), jnp.int32),
            pltpu.SMEM((sky,), jnp.int32),
        ],
        compiler_params=pltpu.CompilerParams(vmem_limit_bytes=LARGE_VMEM),
        name="match_warp_pack",
    )(
        *[
            pltpu.with_memory_space_constraint(value, pltpu.HBM)
            for value in (
                image,
                row_taps.T,
                col_taps.T,
                mix_coeff.transpose(1, 0, 2),
                visit_weight.reshape(1, -1),
                shift_frac,
                tile_block,
                tile_offset,
            )
        ],
        ccd_visit,
    )
    order = sorted(range(sky), key=lambda owner: place_of(owner, sky))
    received = lax.all_to_all(
        messages, "sky", split_axis=0, concat_axis=0, axis_index_groups=[order], tiled=True
    )
    coadd, weight_map = pl.pallas_call(
        functools.partial(sky_kernel, capacity),
        out_shape=(
            jax.ShapeDtypeStruct((BLK_DEV * SUB, cols), jnp.float32),
            jax.ShapeDtypeStruct((1, BLK_DEV * SUB), jnp.float32),
        ),
        in_specs=[vmem],
        out_specs=(vmem, vmem),
        compiler_params=pltpu.CompilerParams(vmem_limit_bytes=SMALL_VMEM),
        name="place_normalise",
    )(received)
    return coadd, weight_map.reshape(-1)


def solution(mesh):
    return jax.shard_map(
        on_device,
        mesh=mesh,
        in_specs=(
            P(("groups", "sky"), None, None),
            P(),
            P(),
            P(("groups", "sky"), None, None),
            P(("groups", "sky"), None),
            P(("groups", "sky")),
            P("groups"),
            P(("groups", "sky")),
            P(("groups", "sky")),
        ),
        out_specs=(P(("groups", "sky"), None), P(("groups", "sky"))),
        check_vma=False,
    )
```

```python
import functools
import itertools

import jax
import jax.numpy as jnp
from jax import lax
from jax.experimental import pallas as pl
from jax.experimental.pallas import tpu as pltpu
from jax.sharding import PartitionSpec as P

BLK_DEV = 16
SUB = 8
LARGE_VMEM = 32 * 1024 * 1024
SMALL_VMEM = 16 * 1024 * 1024
EMPTY = -64
TAPS_DOWN = 6


def iota(shape, axis):
    return lax.broadcasted_iota(jnp.int32, shape, axis)


def weight_of(visit_ref, weight_ref):
    values = weight_ref[...].astype(jnp.float32)
    chosen = jnp.where(iota(values.shape, 1) == visit_ref[0], values, 0.0)
    return jnp.sum(chosen, axis=1, keepdims=True)


def lanczos_rows(frac_ref, cols):
    row = iota((2 * SUB, cols), 0)
    tap = jnp.where(row < SUB, row, row - SUB)
    fraction = jnp.where(row < SUB, frac_ref[0, 1], frac_ref[0, 0])
    angles = jnp.pi * ((tap - 2).astype(jnp.float32) - fraction)
    third = angles / 3.0
    kernel = jnp.sin(angles) / angles * (jnp.sin(third) / third)
    kernel = jnp.where(tap < TAPS_DOWN, kernel, 0.0)
    across, down = kernel[:SUB], kernel[SUB:]
    across = across / jnp.sum(across, axis=0, keepdims=True)
    down = down / jnp.sum(down, axis=0, keepdims=True)
    return across, down


def combined_taps(row_ref, col_ref, mix_ref, lifted, base):
    taps, basis = row_ref.shape
    count, cols = base.shape[1:]
    half = taps // 2
    l, s = iota((cols, taps), 0), iota((cols, taps), 1)
    turned = ((s + l == half) | (s + l == half + cols)).astype(jnp.float32).astype(jnp.bfloat16)
    across = jnp.dot(turned, row_ref[...], preferred_element_type=jnp.float32)
    across = across.astype(jnp.bfloat16)
    lifted[0:1] = jnp.zeros((1, basis), jnp.float32)
    lifted[1:] = col_ref[...].astype(jnp.float32)
    down = lifted[...]
    scaled = jnp.concatenate([down * mix_ref[term] for term in range(3)], axis=0)
    high = scaled.astype(jnp.bfloat16)
    low = (scaled - high.astype(jnp.float32)).astype(jnp.bfloat16)
    found = lax.dot_general(
        jnp.concatenate([high, low], axis=0),
        across,
        (((1,), (1,)), ((), ())),
        preferred_element_type=jnp.float32,
    )
    found = found[: 3 * count] + found[3 * count :]
    lane = iota((count, cols), 1)
    lane = jnp.where(lane < cols // 2, lane, lane - cols).astype(jnp.float32)
    base[0] = found[:count] + (2.0 / cols) * lane * found[count : 2 * count]
    base[1] = found[count : 2 * count]
    base[2] = found[2 * count :]


def build_band(base, row, band, first):
    cols = base.shape[2]
    shape = (2 * SUB, cols)
    sub = iota(shape, 0)
    lane = iota(shape, 1)
    lane = jnp.where(lane < cols // 2, lane, lane - cols)
    first_u = (2.0 * sub.astype(jnp.float32) + 1.0) / cols - 1.0

    def spin(term):
        taps = jnp.broadcast_to(base[term, pl.ds(row, 1), :], shape)
        return pltpu.roll(taps, 0, 1, stride=1, stride_axis=0)

    slope = spin(1)
    level = spin(0) + first_u * slope
    rise = spin(2)
    whole = rise.astype(jnp.bfloat16)
    pairs = cols // (2 * SUB)
    for pair in range(pairs):
        shift = 2 * SUB * pair
        value = level + (2.0 * shift / cols) * slope
        other = whole
        if pair == 0 or pair == pairs - 1:
            inside = lane >= 0 if pair == 0 else lane < 2 * SUB
            value = jnp.where(inside, value, 0.0)
            other = jnp.where(inside, rise, 0.0).astype(jnp.bfloat16)
        value = value.astype(jnp.bfloat16)
        if pair:
            value, other = pltpu.roll(value, shift, 1), pltpu.roll(other, shift, 1)
        at = first + shift
        band[at : at + 2 * SUB, :] = jnp.concatenate([value, other], axis=1)


def place_of(owner, owners):
    slow = 1 << ((owners.bit_length() - 1) // 2)
    fast = owners // slow
    return (owner // fast + slow // 2) % slow * fast + (owner + fast // 2) % fast


def group_edges(fold):
    return [0, fold // 8, fold // 2, fold]


def window_kernel(
    capacity,
    image_hbm,
    row_hbm,
    col_hbm,
    mix_hbm,
    weight_hbm,
    frac_hbm,
    block_hbm,
    offset_hbm,
    visit_ref,
    out_ref,
    image_ref,
    row_ref,
    col_ref,
    mix_ref,
    weight_ref,
    frac_ref,
    block_ref,
    offset_ref,
    copied,
    padded,
    lifted,
    base,
    band_a,
    band_b,
    blocks,
    total,
    spread,
    tile_of,
    starts,
    counts,
):
    rows, cols = image_ref.shape[1:]
    fold = row_ref.shape[0] // 2 + 1
    deep = rows // fold
    tiles = block_ref.shape[0]
    owners = out_ref.shape[0]
    data_rows = capacity * SUB
    owned = BLK_DEV * SUB

    pairs = (
        (image_hbm, image_ref),
        (row_hbm, row_ref),
        (col_hbm, col_ref),
        (mix_hbm, mix_ref),
        (frac_hbm, frac_ref),
        (weight_hbm, weight_ref),
        (block_hbm, block_ref),
        (offset_hbm, offset_ref),
    )
    copies = [
        pltpu.make_async_copy(source, target, copied.at[index])
        for index, (source, target) in enumerate(pairs)
    ]
    for copy in copies:
        copy.start()

    @pl.loop(0, owners)
    def _(owner):
        counts[owner] = 0

    if owners * capacity > tiles:

        @pl.loop(0, owners * capacity)
        def _(slot):
            starts[slot] = EMPTY
            tile_of[slot] = 0

    padded[:fold] = jnp.zeros((fold, cols), jnp.float32)
    padded[fold + rows :] = jnp.zeros((fold, cols), jnp.float32)
    spread[:SUB] = jnp.zeros((SUB, cols), jnp.float32)
    spread[SUB + rows :] = jnp.zeros((SUB, cols), jnp.float32)
    for copy in copies[1:4]:
        copy.wait()
    combined_taps(row_ref, col_ref, mix_ref, lifted, base)
    for copy in copies[:1] + copies[4:]:
        copy.wait()
    padded[fold : fold + rows] = image_ref[0].astype(jnp.float32)
    across, down = lanczos_rows(frac_ref, cols)
    weight = weight_of(visit_ref, weight_ref)

    for index in range(3 * fold - 1):
        blocks[index * deep : (index + 1) * deep, :] = padded[
            pl.ds(index, deep, stride=fold), :
        ].astype(jnp.bfloat16)

    edges = group_edges(fold)
    groups = len(edges) - 1

    def build(group, band):
        for index, r in enumerate(range(edges[group], edges[group + 1])):
            for part in range(2):
                build_band(base, r + part * fold, band, (2 * index + part) * cols)

    def multiply(group, band):
        parts = []
        for r in range(edges[group], edges[group + 1]):
            for part in range(2):
                first = (r + part * fold) * deep
                parts.append(blocks[first : first + rows, :])
        product = jnp.dot(
            jnp.concatenate(parts, axis=1),
            band[: len(parts) * cols, :],
            preferred_element_type=jnp.float32,
        )
        total[...] = product if group == 0 else total[...] + product

    def assign(tile):
        block = block_ref[tile]
        owner = lax.div(block, BLK_DEV)
        rank = counts[owner]
        counts[owner] = rank + 1
        slot = owner * capacity + rank
        tile_of[slot] = tile
        starts[slot] = (block - owner * BLK_DEV) * SUB + offset_ref[tile]

    held = (band_a, band_b)
    build(0, held[0])
    for group in range(groups):
        if group + 1 < groups:
            build(group + 1, held[(group + 1) % 2])
        multiply(group, held[group % 2])
        for tile in range(group * tiles // groups, (group + 1) * tiles // groups):
            assign(tile)

    lane = iota((1, cols), 1)
    taps_across = [
        jnp.where((lane + m - 2 >= 0) & (lane + m - 2 < cols), across[m : m + 1], 0.0)
        for m in range(TAPS_DOWN)
    ]
    position = (2 * fold * iota((deep, cols), 0) + 1).astype(jnp.float32) / rows - 1.0
    for phase in range(fold):
        first = phase * deep
        both = total[first : first + deep, :]
        matched = both[:, :cols] + (position + 2.0 * phase / rows) * both[:, cols:]
        result = taps_across[2] * matched
        for m in range(TAPS_DOWN):
            if m != 2:
                result = result + taps_across[m] * pltpu.roll(matched, (2 - m) % cols, 1)
        spread[pl.ds(SUB + phase, deep, stride=fold), :] = result

    sub = iota((SUB, cols), 0)
    wide = iota((SUB, cols), 1)
    segment = wide >> (data_rows.bit_length() - 1)
    lane_row = wide & (SUB - 1)
    lane_slot = (wide >> 3) & (capacity - 1)
    spill_row = wide >> (capacity.bit_length() - 1)
    spill_rows = [jnp.where(wide & (capacity - 1) == c, spill_row, owned) for c in range(capacity)]
    tile_weight = jnp.broadcast_to(weight, (SUB, cols))

    def warped(slot):
        first = tile_of[slot] * SUB + SUB - 2
        result = down[0:1] * spread[pl.ds(first, SUB), :]
        for m in range(1, TAPS_DOWN):
            result = result + down[m : m + 1] * spread[pl.ds(first + m, SUB), :]
        return result

    def message(owner, carry):
        spilled, over = carry
        target = jnp.zeros((SUB, cols), jnp.int32)
        next_spilled = jnp.zeros((SUB, cols), jnp.float32)
        next_over = jnp.zeros((SUB, cols), jnp.float32)
        tiles_here = []
        for c in range(capacity):
            slot = owner * capacity + c
            start = starts[slot]
            past = start + SUB - owned
            tile = warped(slot)
            tiles_here.append(tile)
            target = jnp.where(lane_slot == c, start, target)
            turned = pltpu.roll(tile, start & (SUB - 1), 0)
            next_spilled = next_spilled + jnp.where(sub < past, turned, 0.0)
            next_over = jnp.where(spill_rows[c] < past, tile_weight, next_over)
        meta = jnp.where(segment == 1, (target + lane_row).astype(jnp.float32), tile_weight)
        meta = jnp.where(segment == 0, over, meta)
        tail = jnp.where(sub == SUB - 1, meta, spilled * tile_weight)
        place = place_of(owner, owners)
        out_ref[place, :data_rows, :] = jnp.concatenate(tiles_here, axis=0).astype(jnp.bfloat16)
        out_ref[place, data_rows:, :] = tail.astype(jnp.bfloat16)
        return next_spilled, next_over

    nothing = jnp.zeros((SUB, cols), jnp.float32)
    lax.fori_loop(0, owners, message, (nothing, nothing), unroll=min(owners, 16))


def sky_kernel(capacity, got_ref, coadd_ref, map_ref):
    sources, message_rows, cols = got_ref.shape
    data_rows = capacity * SUB
    owned = coadd_ref.shape[0]
    per_chunk = cols // data_rows
    chunks = sources // per_chunk
    place = iota((chunks, cols), 0)
    wide = iota((chunks, cols), 1)
    row = iota((owned, cols), 0)
    spilled = jnp.zeros((SUB, cols), jnp.float32)
    target = jnp.zeros((chunks, cols), jnp.float32)
    weight = jnp.zeros((chunks, cols), jnp.float32)
    for k in range(per_chunk):
        heads = jnp.zeros((chunks, cols), jnp.float32)
        for chunk in range(chunks):
            tail = got_ref[chunk * per_chunk + k, data_rows:, :].astype(jnp.float32)
            spilled = spilled + tail
            heads = jnp.where(place == chunk, tail[SUB - 1 :], heads)
        here = (wide >= k * data_rows) & (wide < (k + 1) * data_rows)
        target = jnp.where(here, pltpu.roll(heads, (k - 1) * data_rows % cols, 1), target)
        weight = jnp.where(here, pltpu.roll(heads, (k - 2) * data_rows % cols, 1), weight)
    target = target.astype(jnp.int32)
    pieces = [
        jnp.where(row == target[chunk : chunk + 1], weight[chunk : chunk + 1], 0.0)
        for chunk in range(chunks)
    ]
    placement = jnp.concatenate(pieces, axis=1).astype(jnp.bfloat16)
    pixels = got_ref[:, :data_rows, :].reshape(sources * data_rows, cols)
    pixels = jnp.concatenate([pixels, jnp.ones(pixels.shape, jnp.bfloat16)], axis=1)
    sums = jnp.dot(placement, pixels, preferred_element_type=jnp.float32)
    sub = iota((SUB, cols), 0)
    wide = iota((SUB, cols), 1)
    last = sub == SUB - 1
    over = jnp.broadcast_to(spilled[SUB - 1 :], (SUB, cols))
    mine = ((wide >> (capacity.bit_length() - 1)) == sub) & ~last
    over = jnp.sum(jnp.where(mine, over, 0.0), axis=1, keepdims=True)
    rest = jnp.zeros((owned - SUB, cols), jnp.float32)
    pixel_sum = sums[:, :cols] + jnp.concatenate([jnp.where(last, 0.0, spilled), rest], axis=0)
    weight_sum = sums[:, cols:] + jnp.concatenate(
        [jnp.broadcast_to(over, (SUB, cols)), rest], axis=0
    )
    coadd_ref[...] = pixel_sum / jnp.maximum(weight_sum, 1.0)
    diagonal = jnp.where(row == iota((owned, cols), 1), weight_sum, 0.0)
    map_ref[...] = jnp.sum(diagonal, axis=0, keepdims=True)


def on_device(
    image,
    row_taps,
    col_taps,
    mix_coeff,
    shift_frac,
    ccd_visit,
    visit_weight,
    tile_block,
    tile_offset,
):
    rows, cols = image.shape[1:]
    tiles = tile_block.shape[0]
    sky = lax.axis_size("sky")
    capacity = max(2, tiles // sky)
    taps, basis = row_taps.shape[1], row_taps.shape[0]
    fold = taps // 2 + 1
    visits = visit_weight.shape[0]
    largest = max(b - a for a, b in itertools.pairwise(group_edges(fold)))
    anywhere = pl.BlockSpec(memory_space=pl.ANY)
    vmem = pl.BlockSpec(memory_space=pltpu.VMEM)
    messages = pl.pallas_call(
        functools.partial(window_kernel, capacity),
        out_shape=pltpu.VMEM((sky, capacity * SUB + SUB, cols), jnp.bfloat16),
        in_specs=[anywhere] * 8 + [pl.BlockSpec(memory_space=pltpu.SMEM)],
        out_specs=vmem,
        scratch_shapes=[
            pltpu.VMEM((1, rows, cols), jnp.bfloat16),
            pltpu.VMEM((taps, basis), jnp.bfloat16),
            pltpu.VMEM((taps, basis), jnp.bfloat16),
            pltpu.VMEM((3, 1, basis), jnp.float32),
            pltpu.VMEM((1, visits), jnp.bfloat16),
            pltpu.SMEM((1, 2), jnp.float32),
            pltpu.SMEM((tiles,), jnp.int32),
            pltpu.SMEM((tiles,), jnp.int32),
            pltpu.SemaphoreType.DMA((8,)),
            pltpu.VMEM((rows + 2 * fold, cols), jnp.float32),
            pltpu.VMEM((2 * fold, basis), jnp.float32),
            pltpu.VMEM((3, 2 * fold, cols), jnp.float32),
            pltpu.VMEM((largest * 2 * cols, 2 * cols), jnp.bfloat16),
            pltpu.VMEM((largest * 2 * cols, 2 * cols), jnp.bfloat16),
            pltpu.VMEM(((3 * fold - 1) * (rows // fold), cols), jnp.bfloat16),
            pltpu.VMEM((rows, 2 * cols), jnp.float32),
            pltpu.VMEM((rows + 2 * SUB, cols), jnp.float32),
            pltpu.SMEM((sky * capacity,), jnp.int32),
            pltpu.SMEM((sky * capacity,), jnp.int32),
            pltpu.SMEM((sky,), jnp.int32),
        ],
        compiler_params=pltpu.CompilerParams(vmem_limit_bytes=LARGE_VMEM),
        name="match_warp_pack",
    )(
        *[
            pltpu.with_memory_space_constraint(value, pltpu.HBM)
            for value in (
                image,
                row_taps.T,
                col_taps.T,
                mix_coeff.transpose(1, 0, 2),
                visit_weight.reshape(1, -1),
                shift_frac,
                tile_block,
                tile_offset,
            )
        ],
        ccd_visit,
    )
    order = sorted(range(sky), key=lambda owner: place_of(owner, sky))
    received = lax.all_to_all(
        messages, "sky", split_axis=0, concat_axis=0, axis_index_groups=[order], tiled=True
    )
    coadd, weight_map = pl.pallas_call(
        functools.partial(sky_kernel, capacity),
        out_shape=(
            jax.ShapeDtypeStruct((BLK_DEV * SUB, cols), jnp.float32),
            jax.ShapeDtypeStruct((1, BLK_DEV * SUB), jnp.float32),
        ),
        in_specs=[vmem],
        out_specs=(vmem, vmem),
        compiler_params=pltpu.CompilerParams(vmem_limit_bytes=SMALL_VMEM),
        name="place_normalise",
    )(received)
    return coadd, weight_map.reshape(-1)


def solution(mesh):
    return jax.shard_map(
        on_device,
        mesh=mesh,
        in_specs=(
            P(("groups", "sky"), None, None),
            P(),
            P(),
            P(("groups", "sky"), None, None),
            P(("groups", "sky"), None),
            P(("groups", "sky")),
            P("groups"),
            P(("groups", "sky")),
            P(("groups", "sky")),
        ),
        out_specs=(P(("groups", "sky"), None), P(("groups", "sky"))),
        check_vma=False,
    )
```

```python
import functools
import itertools

import jax
import jax.numpy as jnp
from jax import lax
from jax.experimental import pallas as pl
from jax.experimental.pallas import tpu as pltpu
from jax.sharding import PartitionSpec as P

BLK_DEV = 16
SUB = 8
LARGE_VMEM = 32 * 1024 * 1024
SMALL_VMEM = 16 * 1024 * 1024
EMPTY = -64
TAPS_DOWN = 6


def iota(shape, axis):
    return lax.broadcasted_iota(jnp.int32, shape, axis)


def weight_of(visit_ref, weight_ref):
    values = weight_ref[...].astype(jnp.float32)
    chosen = jnp.where(iota(values.shape, 1) == visit_ref[0], values, 0.0)
    return jnp.sum(chosen, axis=1, keepdims=True)


def lanczos_rows(frac_ref, cols):
    row = iota((2 * SUB, cols), 0)
    tap = jnp.where(row < SUB, row, row - SUB)
    fraction = jnp.where(row < SUB, frac_ref[0, 1], frac_ref[0, 0])
    angles = jnp.pi * ((tap - 2).astype(jnp.float32) - fraction)
    third = angles / 3.0
    kernel = jnp.sin(angles) / angles * (jnp.sin(third) / third)
    kernel = jnp.where(tap < TAPS_DOWN, kernel, 0.0)
    across, down = kernel[:SUB], kernel[SUB:]
    across = across / jnp.sum(across, axis=0, keepdims=True)
    down = down / jnp.sum(down, axis=0, keepdims=True)
    return across, down


def combined_taps(row_ref, col_ref, mix_ref, lifted, base):
    taps, basis = row_ref.shape
    count, cols = base.shape[1:]
    half = taps // 2
    l, s = iota((cols, taps), 0), iota((cols, taps), 1)
    turned = ((s + l == half) | (s + l == half + cols)).astype(jnp.float32).astype(jnp.bfloat16)
    across = jnp.dot(turned, row_ref[...], preferred_element_type=jnp.float32)
    across = across.astype(jnp.bfloat16)
    lifted[0:1] = jnp.zeros((1, basis), jnp.float32)
    lifted[1:] = col_ref[...].astype(jnp.float32)
    down = lifted[...]
    scaled = jnp.concatenate([down * mix_ref[term] for term in range(3)], axis=0)
    high = scaled.astype(jnp.bfloat16)
    low = (scaled - high.astype(jnp.float32)).astype(jnp.bfloat16)
    found = lax.dot_general(
        jnp.concatenate([high, low], axis=0),
        across,
        (((1,), (1,)), ((), ())),
        preferred_element_type=jnp.float32,
    )
    found = found[: 3 * count] + found[3 * count :]
    lane = iota((count, cols), 1)
    lane = jnp.where(lane < cols // 2, lane, lane - cols).astype(jnp.float32)
    base[0] = found[:count] + (2.0 / cols) * lane * found[count : 2 * count]
    base[1] = found[count : 2 * count]
    base[2] = found[2 * count :]


def build_band(base, row, band, first):
    cols = base.shape[2]
    shape = (2 * SUB, cols)
    sub = iota(shape, 0)
    lane = iota(shape, 1)
    lane = jnp.where(lane < cols // 2, lane, lane - cols)
    first_u = (2.0 * sub.astype(jnp.float32) + 1.0) / cols - 1.0

    def spin(term):
        taps = jnp.broadcast_to(base[term, pl.ds(row, 1), :], shape)
        return pltpu.roll(taps, 0, 1, stride=1, stride_axis=0)

    slope = spin(1)
    level = spin(0) + first_u * slope
    rise = spin(2)
    whole = rise.astype(jnp.bfloat16)
    pairs = cols // (2 * SUB)
    for pair in range(pairs):
        shift = 2 * SUB * pair
        value = level + (2.0 * shift / cols) * slope
        other = whole
        if pair == 0 or pair == pairs - 1:
            inside = lane >= 0 if pair == 0 else lane < 2 * SUB
            value = jnp.where(inside, value, 0.0)
            other = jnp.where(inside, rise, 0.0).astype(jnp.bfloat16)
        value = value.astype(jnp.bfloat16)
        if pair:
            value, other = pltpu.roll(value, shift, 1), pltpu.roll(other, shift, 1)
        at = first + shift
        band[at : at + 2 * SUB, :] = jnp.concatenate([value, other], axis=1)


def place_of(owner, owners):
    slow = 1 << ((owners.bit_length() - 1) // 2)
    fast = owners // slow
    return (owner // fast + slow // 2 + 1) % slow * fast + (owner + fast // 2) % fast


def group_edges(fold):
    return [0, fold // 8, fold // 2, fold]


def window_kernel(
    capacity,
    image_hbm,
    row_hbm,
    col_hbm,
    mix_hbm,
    weight_hbm,
    frac_hbm,
    block_hbm,
    offset_hbm,
    visit_ref,
    out_ref,
    image_ref,
    row_ref,
    col_ref,
    mix_ref,
    weight_ref,
    frac_ref,
    block_ref,
    offset_ref,
    copied,
    padded,
    lifted,
    base,
    band_a,
    band_b,
    blocks,
    total,
    spread,
    tile_of,
    starts,
    counts,
):
    rows, cols = image_ref.shape[1:]
    fold = row_ref.shape[0] // 2 + 1
    deep = rows // fold
    tiles = block_ref.shape[0]
    owners = out_ref.shape[0]
    data_rows = capacity * SUB
    owned = BLK_DEV * SUB

    pairs = (
        (image_hbm, image_ref),
        (row_hbm, row_ref),
        (col_hbm, col_ref),
        (mix_hbm, mix_ref),
        (frac_hbm, frac_ref),
        (weight_hbm, weight_ref),
        (block_hbm, block_ref),
        (offset_hbm, offset_ref),
    )
    copies = [
        pltpu.make_async_copy(source, target, copied.at[index])
        for index, (source, target) in enumerate(pairs)
    ]
    for copy in copies:
        copy.start()

    @pl.loop(0, owners)
    def _(owner):
        counts[owner] = 0

    if owners * capacity > tiles:

        @pl.loop(0, owners * capacity)
        def _(slot):
            starts[slot] = EMPTY
            tile_of[slot] = 0

    padded[:fold] = jnp.zeros((fold, cols), jnp.float32)
    padded[fold + rows :] = jnp.zeros((fold, cols), jnp.float32)
    spread[:SUB] = jnp.zeros((SUB, cols), jnp.float32)
    spread[SUB + rows :] = jnp.zeros((SUB, cols), jnp.float32)
    for copy in copies[1:4]:
        copy.wait()
    combined_taps(row_ref, col_ref, mix_ref, lifted, base)
    for copy in copies[:1] + copies[4:]:
        copy.wait()
    padded[fold : fold + rows] = image_ref[0].astype(jnp.float32)
    across, down = lanczos_rows(frac_ref, cols)
    weight = weight_of(visit_ref, weight_ref)

    for index in range(3 * fold - 1):
        blocks[index * deep : (index + 1) * deep, :] = padded[
            pl.ds(index, deep, stride=fold), :
        ].astype(jnp.bfloat16)

    edges = group_edges(fold)
    groups = len(edges) - 1

    def build(group, band):
        for index, r in enumerate(range(edges[group], edges[group + 1])):
            for part in range(2):
                build_band(base, r + part * fold, band, (2 * index + part) * cols)

    def multiply(group, band):
        parts = []
        for r in range(edges[group], edges[group + 1]):
            for part in range(2):
                first = (r + part * fold) * deep
                parts.append(blocks[first : first + rows, :])
        product = jnp.dot(
            jnp.concatenate(parts, axis=1),
            band[: len(parts) * cols, :],
            preferred_element_type=jnp.float32,
        )
        total[...] = product if group == 0 else total[...] + product

    def assign(tile):
        block = block_ref[tile]
        owner = lax.div(block, BLK_DEV)
        rank = counts[owner]
        counts[owner] = rank + 1
        slot = owner * capacity + rank
        tile_of[slot] = tile
        starts[slot] = (block - owner * BLK_DEV) * SUB + offset_ref[tile]

    held = (band_a, band_b)
    build(0, held[0])
    for group in range(groups):
        if group + 1 < groups:
            build(group + 1, held[(group + 1) % 2])
        multiply(group, held[group % 2])
        for tile in range(group * tiles // groups, (group + 1) * tiles // groups):
            assign(tile)

    lane = iota((1, cols), 1)
    taps_across = [
        jnp.where((lane + m - 2 >= 0) & (lane + m - 2 < cols), across[m : m + 1], 0.0)
        for m in range(TAPS_DOWN)
    ]
    position = (2 * fold * iota((deep, cols), 0) + 1).astype(jnp.float32) / rows - 1.0
    for phase in range(fold):
        first = phase * deep
        both = total[first : first + deep, :]
        matched = both[:, :cols] + (position + 2.0 * phase / rows) * both[:, cols:]
        result = taps_across[2] * matched
        for m in range(TAPS_DOWN):
            if m != 2:
                result = result + taps_across[m] * pltpu.roll(matched, (2 - m) % cols, 1)
        spread[pl.ds(SUB + phase, deep, stride=fold), :] = result

    sub = iota((SUB, cols), 0)
    wide = iota((SUB, cols), 1)
    segment = wide >> (data_rows.bit_length() - 1)
    lane_row = wide & (SUB - 1)
    lane_slot = (wide >> 3) & (capacity - 1)
    spill_row = wide >> (capacity.bit_length() - 1)
    spill_rows = [jnp.where(wide & (capacity - 1) == c, spill_row, owned) for c in range(capacity)]
    tile_weight = jnp.broadcast_to(weight, (SUB, cols))

    def warped(slot):
        first = tile_of[slot] * SUB + SUB - 2
        result = down[0:1] * spread[pl.ds(first, SUB), :]
        for m in range(1, TAPS_DOWN):
            result = result + down[m : m + 1] * spread[pl.ds(first + m, SUB), :]
        return result

    def message(owner, carry):
        spilled, over = carry
        target = jnp.zeros((SUB, cols), jnp.int32)
        next_spilled = jnp.zeros((SUB, cols), jnp.float32)
        next_over = jnp.zeros((SUB, cols), jnp.float32)
        tiles_here = []
        for c in range(capacity):
            slot = owner * capacity + c
            start = starts[slot]
            past = start + SUB - owned
            tile = warped(slot)
            tiles_here.append(tile)
            target = jnp.where(lane_slot == c, start, target)
            turned = pltpu.roll(tile, start & (SUB - 1), 0)
            next_spilled = next_spilled + jnp.where(sub < past, turned, 0.0)
            next_over = jnp.where(spill_rows[c] < past, tile_weight, next_over)
        meta = jnp.where(segment == 1, (target + lane_row).astype(jnp.float32), tile_weight)
        meta = jnp.where(segment == 0, over, meta)
        tail = jnp.where(sub == SUB - 1, meta, spilled * tile_weight)
        place = place_of(owner, owners)
        out_ref[place, :data_rows, :] = jnp.concatenate(tiles_here, axis=0).astype(jnp.bfloat16)
        out_ref[place, data_rows:, :] = tail.astype(jnp.bfloat16)
        return next_spilled, next_over

    nothing = jnp.zeros((SUB, cols), jnp.float32)
    lax.fori_loop(0, owners, message, (nothing, nothing), unroll=min(owners, 16))


def sky_kernel(capacity, got_ref, coadd_ref, map_ref):
    sources, message_rows, cols = got_ref.shape
    data_rows = capacity * SUB
    owned = coadd_ref.shape[0]
    per_chunk = cols // data_rows
    chunks = sources // per_chunk
    place = iota((chunks, cols), 0)
    wide = iota((chunks, cols), 1)
    row = iota((owned, cols), 0)
    spilled = jnp.zeros((SUB, cols), jnp.float32)
    target = jnp.zeros((chunks, cols), jnp.float32)
    weight = jnp.zeros((chunks, cols), jnp.float32)
    for k in range(per_chunk):
        heads = jnp.zeros((chunks, cols), jnp.float32)
        for chunk in range(chunks):
            tail = got_ref[chunk * per_chunk + k, data_rows:, :].astype(jnp.float32)
            spilled = spilled + tail
            heads = jnp.where(place == chunk, tail[SUB - 1 :], heads)
        here = (wide >= k * data_rows) & (wide < (k + 1) * data_rows)
        target = jnp.where(here, pltpu.roll(heads, (k - 1) * data_rows % cols, 1), target)
        weight = jnp.where(here, pltpu.roll(heads, (k - 2) * data_rows % cols, 1), weight)
    target = target.astype(jnp.int32)
    pieces = [
        jnp.where(row == target[chunk : chunk + 1], weight[chunk : chunk + 1], 0.0)
        for chunk in range(chunks)
    ]
    placement = jnp.concatenate(pieces, axis=1).astype(jnp.bfloat16)
    pixels = got_ref[:, :data_rows, :].reshape(sources * data_rows, cols)
    pixels = jnp.concatenate([pixels, jnp.ones(pixels.shape, jnp.bfloat16)], axis=1)
    sums = jnp.dot(placement, pixels, preferred_element_type=jnp.float32)
    sub = iota((SUB, cols), 0)
    wide = iota((SUB, cols), 1)
    last = sub == SUB - 1
    over = jnp.broadcast_to(spilled[SUB - 1 :], (SUB, cols))
    mine = ((wide >> (capacity.bit_length() - 1)) == sub) & ~last
    over = jnp.sum(jnp.where(mine, over, 0.0), axis=1, keepdims=True)
    rest = jnp.zeros((owned - SUB, cols), jnp.float32)
    pixel_sum = sums[:, :cols] + jnp.concatenate([jnp.where(last, 0.0, spilled), rest], axis=0)
    weight_sum = sums[:, cols:] + jnp.concatenate(
        [jnp.broadcast_to(over, (SUB, cols)), rest], axis=0
    )
    coadd_ref[...] = pixel_sum / jnp.maximum(weight_sum, 1.0)
    diagonal = jnp.where(row == iota((owned, cols), 1), weight_sum, 0.0)
    map_ref[...] = jnp.sum(diagonal, axis=0, keepdims=True)


def on_device(
    image,
    row_taps,
    col_taps,
    mix_coeff,
    shift_frac,
    ccd_visit,
    visit_weight,
    tile_block,
    tile_offset,
):
    rows, cols = image.shape[1:]
    tiles = tile_block.shape[0]
    sky = lax.axis_size("sky")
    capacity = max(2, tiles // sky)
    taps, basis = row_taps.shape[1], row_taps.shape[0]
    fold = taps // 2 + 1
    visits = visit_weight.shape[0]
    largest = max(b - a for a, b in itertools.pairwise(group_edges(fold)))
    anywhere = pl.BlockSpec(memory_space=pl.ANY)
    vmem = pl.BlockSpec(memory_space=pltpu.VMEM)
    messages = pl.pallas_call(
        functools.partial(window_kernel, capacity),
        out_shape=pltpu.VMEM((sky, capacity * SUB + SUB, cols), jnp.bfloat16),
        in_specs=[anywhere] * 8 + [pl.BlockSpec(memory_space=pltpu.SMEM)],
        out_specs=vmem,
        scratch_shapes=[
            pltpu.VMEM((1, rows, cols), jnp.bfloat16),
            pltpu.VMEM((taps, basis), jnp.bfloat16),
            pltpu.VMEM((taps, basis), jnp.bfloat16),
            pltpu.VMEM((3, 1, basis), jnp.float32),
            pltpu.VMEM((1, visits), jnp.bfloat16),
            pltpu.SMEM((1, 2), jnp.float32),
            pltpu.SMEM((tiles,), jnp.int32),
            pltpu.SMEM((tiles,), jnp.int32),
            pltpu.SemaphoreType.DMA((8,)),
            pltpu.VMEM((rows + 2 * fold, cols), jnp.float32),
            pltpu.VMEM((2 * fold, basis), jnp.float32),
            pltpu.VMEM((3, 2 * fold, cols), jnp.float32),
            pltpu.VMEM((largest * 2 * cols, 2 * cols), jnp.bfloat16),
            pltpu.VMEM((largest * 2 * cols, 2 * cols), jnp.bfloat16),
            pltpu.VMEM(((3 * fold - 1) * (rows // fold), cols), jnp.bfloat16),
            pltpu.VMEM((rows, 2 * cols), jnp.float32),
            pltpu.VMEM((rows + 2 * SUB, cols), jnp.float32),
            pltpu.SMEM((sky * capacity,), jnp.int32),
            pltpu.SMEM((sky * capacity,), jnp.int32),
            pltpu.SMEM((sky,), jnp.int32),
        ],
        compiler_params=pltpu.CompilerParams(vmem_limit_bytes=LARGE_VMEM),
        name="match_warp_pack",
    )(
        *[
            pltpu.with_memory_space_constraint(value, pltpu.HBM)
            for value in (
                image,
                row_taps.T,
                col_taps.T,
                mix_coeff.transpose(1, 0, 2),
                visit_weight.reshape(1, -1),
                shift_frac,
                tile_block,
                tile_offset,
            )
        ],
        ccd_visit,
    )
    order = sorted(range(sky), key=lambda owner: place_of(owner, sky))
    received = lax.all_to_all(
        messages, "sky", split_axis=0, concat_axis=0, axis_index_groups=[order], tiled=True
    )
    coadd, weight_map = pl.pallas_call(
        functools.partial(sky_kernel, capacity),
        out_shape=(
            jax.ShapeDtypeStruct((BLK_DEV * SUB, cols), jnp.float32),
            jax.ShapeDtypeStruct((1, BLK_DEV * SUB), jnp.float32),
        ),
        in_specs=[vmem],
        out_specs=(vmem, vmem),
        compiler_params=pltpu.CompilerParams(vmem_limit_bytes=SMALL_VMEM),
        name="place_normalise",
    )(received)
    return coadd, weight_map.reshape(-1)


def solution(mesh):
    return jax.shard_map(
        on_device,
        mesh=mesh,
        in_specs=(
            P(("groups", "sky"), None, None),
            P(),
            P(),
            P(("groups", "sky"), None, None),
            P(("groups", "sky"), None),
            P(("groups", "sky")),
            P("groups"),
            P(("groups", "sky")),
            P(("groups", "sky")),
        ),
        out_specs=(P(("groups", "sky"), None), P(("groups", "sky"))),
        check_vma=False,
    )
```

```python
import functools
import itertools

import jax
import jax.numpy as jnp
from jax import lax
from jax.experimental import pallas as pl
from jax.experimental.pallas import tpu as pltpu
from jax.sharding import PartitionSpec as P

BLK_DEV = 16
SUB = 8
LARGE_VMEM = 32 * 1024 * 1024
SMALL_VMEM = 16 * 1024 * 1024
EMPTY = -64
TAPS_DOWN = 6


def iota(shape, axis):
    return lax.broadcasted_iota(jnp.int32, shape, axis)


def weight_of(visit_ref, weight_ref):
    values = weight_ref[...].astype(jnp.float32)
    chosen = jnp.where(iota(values.shape, 1) == visit_ref[0], values, 0.0)
    return jnp.sum(chosen, axis=1, keepdims=True)


def lanczos_rows(frac_ref, cols):
    row = iota((2 * SUB, cols), 0)
    tap = jnp.where(row < SUB, row, row - SUB)
    fraction = jnp.where(row < SUB, frac_ref[0, 1], frac_ref[0, 0])
    angles = jnp.pi * ((tap - 2).astype(jnp.float32) - fraction)
    third = angles / 3.0
    kernel = jnp.sin(angles) / angles * (jnp.sin(third) / third)
    kernel = jnp.where(tap < TAPS_DOWN, kernel, 0.0)
    across, down = kernel[:SUB], kernel[SUB:]
    across = across / jnp.sum(across, axis=0, keepdims=True)
    down = down / jnp.sum(down, axis=0, keepdims=True)
    return across, down


def combined_taps(row_ref, col_ref, mix_ref, lifted, base):
    taps, basis = row_ref.shape
    count, cols = base.shape[1:]
    half = taps // 2
    l, s = iota((cols, taps), 0), iota((cols, taps), 1)
    turned = ((s + l == half) | (s + l == half + cols)).astype(jnp.float32).astype(jnp.bfloat16)
    across = jnp.dot(turned, row_ref[...], preferred_element_type=jnp.float32)
    across = across.astype(jnp.bfloat16)
    lifted[0:1] = jnp.zeros((1, basis), jnp.float32)
    lifted[1:] = col_ref[...].astype(jnp.float32)
    down = lifted[...]
    scaled = jnp.concatenate([down * mix_ref[term] for term in range(3)], axis=0)
    high = scaled.astype(jnp.bfloat16)
    low = (scaled - high.astype(jnp.float32)).astype(jnp.bfloat16)
    found = lax.dot_general(
        jnp.concatenate([high, low], axis=0),
        across,
        (((1,), (1,)), ((), ())),
        preferred_element_type=jnp.float32,
    )
    found = found[: 3 * count] + found[3 * count :]
    lane = iota((count, cols), 1)
    lane = jnp.where(lane < cols // 2, lane, lane - cols).astype(jnp.float32)
    base[0] = found[:count] + (2.0 / cols) * lane * found[count : 2 * count]
    base[1] = found[count : 2 * count]
    base[2] = found[2 * count :]


def build_band(base, row, band, first):
    cols = base.shape[2]
    shape = (2 * SUB, cols)
    sub = iota(shape, 0)
    lane = iota(shape, 1)
    lane = jnp.where(lane < cols // 2, lane, lane - cols)
    first_u = (2.0 * sub.astype(jnp.float32) + 1.0) / cols - 1.0

    def spin(term):
        taps = jnp.broadcast_to(base[term, pl.ds(row, 1), :], shape)
        return pltpu.roll(taps, 0, 1, stride=1, stride_axis=0)

    slope = spin(1)
    level = spin(0) + first_u * slope
    rise = spin(2)
    whole = rise.astype(jnp.bfloat16)
    pairs = cols // (2 * SUB)
    for pair in range(pairs):
        shift = 2 * SUB * pair
        value = level + (2.0 * shift / cols) * slope
        other = whole
        if pair == 0 or pair == pairs - 1:
            inside = lane >= 0 if pair == 0 else lane < 2 * SUB
            value = jnp.where(inside, value, 0.0)
            other = jnp.where(inside, rise, 0.0).astype(jnp.bfloat16)
        value = value.astype(jnp.bfloat16)
        if pair:
            value, other = pltpu.roll(value, shift, 1), pltpu.roll(other, shift, 1)
        at = first + shift
        band[at : at + 2 * SUB, :] = jnp.concatenate([value, other], axis=1)


def place_of(owner, owners):
    slow = 1 << ((owners.bit_length() - 1) // 2)
    fast = owners // slow
    block = (owner // fast + slow // 2) % slow
    pair = (owner % fast // 2 + fast // 4) % (fast // 2)
    return (pair * slow + block) * 2 + owner % 2


def group_edges(fold):
    return [0, fold // 8, fold // 2, fold]


def window_kernel(
    capacity,
    image_hbm,
    row_hbm,
    col_hbm,
    mix_hbm,
    weight_hbm,
    frac_hbm,
    block_hbm,
    offset_hbm,
    visit_ref,
    out_ref,
    image_ref,
    row_ref,
    col_ref,
    mix_ref,
    weight_ref,
    frac_ref,
    block_ref,
    offset_ref,
    copied,
    padded,
    lifted,
    base,
    band_a,
    band_b,
    blocks,
    total,
    spread,
    tile_of,
    starts,
    counts,
):
    rows, cols = image_ref.shape[1:]
    fold = row_ref.shape[0] // 2 + 1
    deep = rows // fold
    tiles = block_ref.shape[0]
    owners = out_ref.shape[0]
    data_rows = capacity * SUB
    owned = BLK_DEV * SUB

    pairs = (
        (image_hbm, image_ref),
        (row_hbm, row_ref),
        (col_hbm, col_ref),
        (mix_hbm, mix_ref),
        (frac_hbm, frac_ref),
        (weight_hbm, weight_ref),
        (block_hbm, block_ref),
        (offset_hbm, offset_ref),
    )
    copies = [
        pltpu.make_async_copy(source, target, copied.at[index])
        for index, (source, target) in enumerate(pairs)
    ]
    for copy in copies:
        copy.start()

    @pl.loop(0, owners)
    def _(owner):
        counts[owner] = 0

    if owners * capacity > tiles:

        @pl.loop(0, owners * capacity)
        def _(slot):
            starts[slot] = EMPTY
            tile_of[slot] = 0

    padded[:fold] = jnp.zeros((fold, cols), jnp.float32)
    padded[fold + rows :] = jnp.zeros((fold, cols), jnp.float32)
    spread[:SUB] = jnp.zeros((SUB, cols), jnp.float32)
    spread[SUB + rows :] = jnp.zeros((SUB, cols), jnp.float32)
    for copy in copies[1:4]:
        copy.wait()
    combined_taps(row_ref, col_ref, mix_ref, lifted, base)
    for copy in copies[:1] + copies[4:]:
        copy.wait()
    padded[fold : fold + rows] = image_ref[0].astype(jnp.float32)
    across, down = lanczos_rows(frac_ref, cols)
    weight = weight_of(visit_ref, weight_ref)

    for index in range(3 * fold - 1):
        blocks[index * deep : (index + 1) * deep, :] = padded[
            pl.ds(index, deep, stride=fold), :
        ].astype(jnp.bfloat16)

    edges = group_edges(fold)
    groups = len(edges) - 1

    def build(group, band):
        for index, r in enumerate(range(edges[group], edges[group + 1])):
            for part in range(2):
                build_band(base, r + part * fold, band, (2 * index + part) * cols)

    def multiply(group, band):
        parts = []
        for r in range(edges[group], edges[group + 1]):
            for part in range(2):
                first = (r + part * fold) * deep
                parts.append(blocks[first : first + rows, :])
        product = jnp.dot(
            jnp.concatenate(parts, axis=1),
            band[: len(parts) * cols, :],
            preferred_element_type=jnp.float32,
        )
        total[...] = product if group == 0 else total[...] + product

    def assign(tile):
        block = block_ref[tile]
        owner = lax.div(block, BLK_DEV)
        rank = counts[owner]
        counts[owner] = rank + 1
        slot = owner * capacity + rank
        tile_of[slot] = tile
        starts[slot] = (block - owner * BLK_DEV) * SUB + offset_ref[tile]

    held = (band_a, band_b)
    build(0, held[0])
    for group in range(groups):
        if group + 1 < groups:
            build(group + 1, held[(group + 1) % 2])
        multiply(group, held[group % 2])
        for tile in range(group * tiles // groups, (group + 1) * tiles // groups):
            assign(tile)

    lane = iota((1, cols), 1)
    taps_across = [
        jnp.where((lane + m - 2 >= 0) & (lane + m - 2 < cols), across[m : m + 1], 0.0)
        for m in range(TAPS_DOWN)
    ]
    position = (2 * fold * iota((deep, cols), 0) + 1).astype(jnp.float32) / rows - 1.0
    for phase in range(fold):
        first = phase * deep
        both = total[first : first + deep, :]
        matched = both[:, :cols] + (position + 2.0 * phase / rows) * both[:, cols:]
        result = taps_across[2] * matched
        for m in range(TAPS_DOWN):
            if m != 2:
                result = result + taps_across[m] * pltpu.roll(matched, (2 - m) % cols, 1)
        spread[pl.ds(SUB + phase, deep, stride=fold), :] = result

    sub = iota((SUB, cols), 0)
    wide = iota((SUB, cols), 1)
    segment = wide >> (data_rows.bit_length() - 1)
    lane_row = wide & (SUB - 1)
    lane_slot = (wide >> 3) & (capacity - 1)
    spill_row = wide >> (capacity.bit_length() - 1)
    spill_rows = [jnp.where(wide & (capacity - 1) == c, spill_row, owned) for c in range(capacity)]
    tile_weight = jnp.broadcast_to(weight, (SUB, cols))

    def warped(slot):
        first = tile_of[slot] * SUB + SUB - 2
        result = down[0:1] * spread[pl.ds(first, SUB), :]
        for m in range(1, TAPS_DOWN):
            result = result + down[m : m + 1] * spread[pl.ds(first + m, SUB), :]
        return result

    def message(owner, carry):
        spilled, over = carry
        target = jnp.zeros((SUB, cols), jnp.int32)
        next_spilled = jnp.zeros((SUB, cols), jnp.float32)
        next_over = jnp.zeros((SUB, cols), jnp.float32)
        tiles_here = []
        for c in range(capacity):
            slot = owner * capacity + c
            start = starts[slot]
            past = start + SUB - owned
            tile = warped(slot)
            tiles_here.append(tile)
            target = jnp.where(lane_slot == c, start, target)
            turned = pltpu.roll(tile, start & (SUB - 1), 0)
            next_spilled = next_spilled + jnp.where(sub < past, turned, 0.0)
            next_over = jnp.where(spill_rows[c] < past, tile_weight, next_over)
        meta = jnp.where(segment == 1, (target + lane_row).astype(jnp.float32), tile_weight)
        meta = jnp.where(segment == 0, over, meta)
        tail = jnp.where(sub == SUB - 1, meta, spilled * tile_weight)
        place = place_of(owner, owners)
        out_ref[place, :data_rows, :] = jnp.concatenate(tiles_here, axis=0).astype(jnp.bfloat16)
        out_ref[place, data_rows:, :] = tail.astype(jnp.bfloat16)
        return next_spilled, next_over

    nothing = jnp.zeros((SUB, cols), jnp.float32)
    lax.fori_loop(0, owners, message, (nothing, nothing), unroll=min(owners, 16))


def sky_kernel(capacity, got_ref, coadd_ref, map_ref):
    sources, message_rows, cols = got_ref.shape
    data_rows = capacity * SUB
    owned = coadd_ref.shape[0]
    per_chunk = cols // data_rows
    chunks = sources // per_chunk
    place = iota((chunks, cols), 0)
    wide = iota((chunks, cols), 1)
    row = iota((owned, cols), 0)
    spilled = jnp.zeros((SUB, cols), jnp.float32)
    target = jnp.zeros((chunks, cols), jnp.float32)
    weight = jnp.zeros((chunks, cols), jnp.float32)
    for k in range(per_chunk):
        heads = jnp.zeros((chunks, cols), jnp.float32)
        for chunk in range(chunks):
            tail = got_ref[chunk * per_chunk + k, data_rows:, :].astype(jnp.float32)
            spilled = spilled + tail
            heads = jnp.where(place == chunk, tail[SUB - 1 :], heads)
        here = (wide >= k * data_rows) & (wide < (k + 1) * data_rows)
        target = jnp.where(here, pltpu.roll(heads, (k - 1) * data_rows % cols, 1), target)
        weight = jnp.where(here, pltpu.roll(heads, (k - 2) * data_rows % cols, 1), weight)
    target = target.astype(jnp.int32)
    pieces = [
        jnp.where(row == target[chunk : chunk + 1], weight[chunk : chunk + 1], 0.0)
        for chunk in range(chunks)
    ]
    placement = jnp.concatenate(pieces, axis=1).astype(jnp.bfloat16)
    pixels = got_ref[:, :data_rows, :].reshape(sources * data_rows, cols)
    pixels = jnp.concatenate([pixels, jnp.ones(pixels.shape, jnp.bfloat16)], axis=1)
    sums = jnp.dot(placement, pixels, preferred_element_type=jnp.float32)
    sub = iota((SUB, cols), 0)
    wide = iota((SUB, cols), 1)
    last = sub == SUB - 1
    over = jnp.broadcast_to(spilled[SUB - 1 :], (SUB, cols))
    mine = ((wide >> (capacity.bit_length() - 1)) == sub) & ~last
    over = jnp.sum(jnp.where(mine, over, 0.0), axis=1, keepdims=True)
    rest = jnp.zeros((owned - SUB, cols), jnp.float32)
    pixel_sum = sums[:, :cols] + jnp.concatenate([jnp.where(last, 0.0, spilled), rest], axis=0)
    weight_sum = sums[:, cols:] + jnp.concatenate(
        [jnp.broadcast_to(over, (SUB, cols)), rest], axis=0
    )
    coadd_ref[...] = pixel_sum / jnp.maximum(weight_sum, 1.0)
    diagonal = jnp.where(row == iota((owned, cols), 1), weight_sum, 0.0)
    map_ref[...] = jnp.sum(diagonal, axis=0, keepdims=True)


def on_device(
    image,
    row_taps,
    col_taps,
    mix_coeff,
    shift_frac,
    ccd_visit,
    visit_weight,
    tile_block,
    tile_offset,
):
    rows, cols = image.shape[1:]
    tiles = tile_block.shape[0]
    sky = lax.axis_size("sky")
    capacity = max(2, tiles // sky)
    taps, basis = row_taps.shape[1], row_taps.shape[0]
    fold = taps // 2 + 1
    visits = visit_weight.shape[0]
    largest = max(b - a for a, b in itertools.pairwise(group_edges(fold)))
    anywhere = pl.BlockSpec(memory_space=pl.ANY)
    vmem = pl.BlockSpec(memory_space=pltpu.VMEM)
    messages = pl.pallas_call(
        functools.partial(window_kernel, capacity),
        out_shape=pltpu.VMEM((sky, capacity * SUB + SUB, cols), jnp.bfloat16),
        in_specs=[anywhere] * 8 + [pl.BlockSpec(memory_space=pltpu.SMEM)],
        out_specs=vmem,
        scratch_shapes=[
            pltpu.VMEM((1, rows, cols), jnp.bfloat16),
            pltpu.VMEM((taps, basis), jnp.bfloat16),
            pltpu.VMEM((taps, basis), jnp.bfloat16),
            pltpu.VMEM((3, 1, basis), jnp.float32),
            pltpu.VMEM((1, visits), jnp.bfloat16),
            pltpu.SMEM((1, 2), jnp.float32),
            pltpu.SMEM((tiles,), jnp.int32),
            pltpu.SMEM((tiles,), jnp.int32),
            pltpu.SemaphoreType.DMA((8,)),
            pltpu.VMEM((rows + 2 * fold, cols), jnp.float32),
            pltpu.VMEM((2 * fold, basis), jnp.float32),
            pltpu.VMEM((3, 2 * fold, cols), jnp.float32),
            pltpu.VMEM((largest * 2 * cols, 2 * cols), jnp.bfloat16),
            pltpu.VMEM((largest * 2 * cols, 2 * cols), jnp.bfloat16),
            pltpu.VMEM(((3 * fold - 1) * (rows // fold), cols), jnp.bfloat16),
            pltpu.VMEM((rows, 2 * cols), jnp.float32),
            pltpu.VMEM((rows + 2 * SUB, cols), jnp.float32),
            pltpu.SMEM((sky * capacity,), jnp.int32),
            pltpu.SMEM((sky * capacity,), jnp.int32),
            pltpu.SMEM((sky,), jnp.int32),
        ],
        compiler_params=pltpu.CompilerParams(vmem_limit_bytes=LARGE_VMEM),
        name="match_warp_pack",
    )(
        *[
            pltpu.with_memory_space_constraint(value, pltpu.HBM)
            for value in (
                image,
                row_taps.T,
                col_taps.T,
                mix_coeff.transpose(1, 0, 2),
                visit_weight.reshape(1, -1),
                shift_frac,
                tile_block,
                tile_offset,
            )
        ],
        ccd_visit,
    )
    order = sorted(range(sky), key=lambda owner: place_of(owner, sky))
    received = lax.all_to_all(
        messages, "sky", split_axis=0, concat_axis=0, axis_index_groups=[order], tiled=True
    )
    coadd, weight_map = pl.pallas_call(
        functools.partial(sky_kernel, capacity),
        out_shape=(
            jax.ShapeDtypeStruct((BLK_DEV * SUB, cols), jnp.float32),
            jax.ShapeDtypeStruct((1, BLK_DEV * SUB), jnp.float32),
        ),
        in_specs=[vmem],
        out_specs=(vmem, vmem),
        compiler_params=pltpu.CompilerParams(vmem_limit_bytes=SMALL_VMEM),
        name="place_normalise",
    )(received)
    return coadd, weight_map.reshape(-1)


def solution(mesh):
    return jax.shard_map(
        on_device,
        mesh=mesh,
        in_specs=(
            P(("groups", "sky"), None, None),
            P(),
            P(),
            P(("groups", "sky"), None, None),
            P(("groups", "sky"), None),
            P(("groups", "sky")),
            P("groups"),
            P(("groups", "sky")),
            P(("groups", "sky")),
        ),
        out_specs=(P(("groups", "sky"), None), P(("groups", "sky"))),
        check_vma=False,
    )
```

```python
import functools
import itertools

import jax
import jax.numpy as jnp
from jax import lax
from jax.experimental import pallas as pl
from jax.experimental.pallas import tpu as pltpu
from jax.sharding import PartitionSpec as P

BLK_DEV = 16
SUB = 8
LARGE_VMEM = 32 * 1024 * 1024
SMALL_VMEM = 16 * 1024 * 1024
EMPTY = -64
TAPS_DOWN = 6


def iota(shape, axis):
    return lax.broadcasted_iota(jnp.int32, shape, axis)


def weight_of(visit_ref, weight_ref):
    values = weight_ref[...].astype(jnp.float32)
    chosen = jnp.where(iota(values.shape, 1) == visit_ref[0], values, 0.0)
    return jnp.sum(chosen, axis=1, keepdims=True)


def lanczos_rows(frac_ref, cols):
    row = iota((2 * SUB, cols), 0)
    tap = jnp.where(row < SUB, row, row - SUB)
    fraction = jnp.where(row < SUB, frac_ref[0, 1], frac_ref[0, 0])
    angles = jnp.pi * ((tap - 2).astype(jnp.float32) - fraction)
    third = angles / 3.0
    kernel = jnp.sin(angles) / angles * (jnp.sin(third) / third)
    kernel = jnp.where(tap < TAPS_DOWN, kernel, 0.0)
    across, down = kernel[:SUB], kernel[SUB:]
    across = across / jnp.sum(across, axis=0, keepdims=True)
    down = down / jnp.sum(down, axis=0, keepdims=True)
    return across, down


def combined_taps(row_ref, col_ref, mix_ref, lifted, base):
    taps, basis = row_ref.shape
    count, cols = base.shape[1:]
    half = taps // 2
    l, s = iota((cols, taps), 0), iota((cols, taps), 1)
    turned = ((s + l == half) | (s + l == half + cols)).astype(jnp.float32).astype(jnp.bfloat16)
    across = jnp.dot(turned, row_ref[...], preferred_element_type=jnp.float32)
    across = across.astype(jnp.bfloat16)
    lifted[0:1] = jnp.zeros((1, basis), jnp.float32)
    lifted[1:] = col_ref[...].astype(jnp.float32)
    down = lifted[...]
    scaled = jnp.concatenate([down * mix_ref[term] for term in range(3)], axis=0)
    high = scaled.astype(jnp.bfloat16)
    low = (scaled - high.astype(jnp.float32)).astype(jnp.bfloat16)
    found = lax.dot_general(
        jnp.concatenate([high, low], axis=0),
        across,
        (((1,), (1,)), ((), ())),
        preferred_element_type=jnp.float32,
    )
    found = found[: 3 * count] + found[3 * count :]
    lane = iota((count, cols), 1)
    lane = jnp.where(lane < cols // 2, lane, lane - cols).astype(jnp.float32)
    base[0] = found[:count] + (2.0 / cols) * lane * found[count : 2 * count]
    base[1] = found[count : 2 * count]
    base[2] = found[2 * count :]


def build_band(base, row, band, first):
    cols = base.shape[2]
    shape = (2 * SUB, cols)
    sub = iota(shape, 0)
    lane = iota(shape, 1)
    lane = jnp.where(lane < cols // 2, lane, lane - cols)
    first_u = (2.0 * sub.astype(jnp.float32) + 1.0) / cols - 1.0

    def spin(term):
        taps = jnp.broadcast_to(base[term, pl.ds(row, 1), :], shape)
        return pltpu.roll(taps, 0, 1, stride=1, stride_axis=0)

    slope = spin(1)
    level = spin(0) + first_u * slope
    rise = spin(2)
    whole = rise.astype(jnp.bfloat16)
    pairs = cols // (2 * SUB)
    for pair in range(pairs):
        shift = 2 * SUB * pair
        value = level + (2.0 * shift / cols) * slope
        other = whole
        if pair == 0 or pair == pairs - 1:
            inside = lane >= 0 if pair == 0 else lane < 2 * SUB
            value = jnp.where(inside, value, 0.0)
            other = jnp.where(inside, rise, 0.0).astype(jnp.bfloat16)
        value = value.astype(jnp.bfloat16)
        if pair:
            value, other = pltpu.roll(value, shift, 1), pltpu.roll(other, shift, 1)
        at = first + shift
        band[at : at + 2 * SUB, :] = jnp.concatenate([value, other], axis=1)


def place_of(owner, owners):
    slow = 1 << ((owners.bit_length() - 1) // 2)
    fast = owners // slow
    return (owner // fast + slow // 2) % slow * fast + (owner + fast // 2) % fast


def group_edges(fold):
    return [0, fold // 2, fold]


def window_kernel(
    capacity,
    image_hbm,
    row_hbm,
    col_hbm,
    mix_hbm,
    weight_hbm,
    frac_hbm,
    block_hbm,
    offset_hbm,
    visit_ref,
    out_ref,
    image_ref,
    row_ref,
    col_ref,
    mix_ref,
    weight_ref,
    frac_ref,
    block_ref,
    offset_ref,
    copied,
    padded,
    lifted,
    base,
    band_a,
    band_b,
    blocks,
    total,
    spread,
    tile_of,
    starts,
    counts,
):
    rows, cols = image_ref.shape[1:]
    fold = row_ref.shape[0] // 2 + 1
    deep = rows // fold
    tiles = block_ref.shape[0]
    owners = out_ref.shape[0]
    data_rows = capacity * SUB
    owned = BLK_DEV * SUB

    pairs = (
        (image_hbm, image_ref),
        (row_hbm, row_ref),
        (col_hbm, col_ref),
        (mix_hbm, mix_ref),
        (frac_hbm, frac_ref),
        (weight_hbm, weight_ref),
        (block_hbm, block_ref),
        (offset_hbm, offset_ref),
    )
    copies = [
        pltpu.make_async_copy(source, target, copied.at[index])
        for index, (source, target) in enumerate(pairs)
    ]
    for copy in copies:
        copy.start()

    @pl.loop(0, owners)
    def _(owner):
        counts[owner] = 0

    if owners * capacity > tiles:

        @pl.loop(0, owners * capacity)
        def _(slot):
            starts[slot] = EMPTY
            tile_of[slot] = 0

    padded[:fold] = jnp.zeros((fold, cols), jnp.float32)
    padded[fold + rows :] = jnp.zeros((fold, cols), jnp.float32)
    spread[:SUB] = jnp.zeros((SUB, cols), jnp.float32)
    spread[SUB + rows :] = jnp.zeros((SUB, cols), jnp.float32)
    for copy in copies[1:4]:
        copy.wait()
    combined_taps(row_ref, col_ref, mix_ref, lifted, base)

    edges = group_edges(fold)
    groups = len(edges) - 1

    def build(group, band):
        for index, r in enumerate(range(edges[group], edges[group + 1])):
            for part in range(2):
                build_band(base, r + part * fold, band, (2 * index + part) * cols)

    held = (band_a, band_b)
    build(0, held[0])
    for copy in copies[:1] + copies[4:]:
        copy.wait()
    padded[fold : fold + rows] = image_ref[0].astype(jnp.float32)
    across, down = lanczos_rows(frac_ref, cols)
    weight = weight_of(visit_ref, weight_ref)

    for index in range(3 * fold - 1):
        blocks[index * deep : (index + 1) * deep, :] = padded[
            pl.ds(index, deep, stride=fold), :
        ].astype(jnp.bfloat16)

    def multiply(group, band):
        parts = []
        for r in range(edges[group], edges[group + 1]):
            for part in range(2):
                first = (r + part * fold) * deep
                parts.append(blocks[first : first + rows, :])
        product = jnp.dot(
            jnp.concatenate(parts, axis=1),
            band[: len(parts) * cols, :],
            preferred_element_type=jnp.float32,
        )
        total[...] = product if group == 0 else total[...] + product

    def assign(tile):
        block = block_ref[tile]
        owner = lax.div(block, BLK_DEV)
        rank = counts[owner]
        counts[owner] = rank + 1
        slot = owner * capacity + rank
        tile_of[slot] = tile
        starts[slot] = (block - owner * BLK_DEV) * SUB + offset_ref[tile]

    for group in range(groups):
        if group + 1 < groups:
            build(group + 1, held[(group + 1) % 2])
        multiply(group, held[group % 2])
        for tile in range(group * tiles // groups, (group + 1) * tiles // groups):
            assign(tile)

    lane = iota((1, cols), 1)
    taps_across = [
        jnp.where((lane + m - 2 >= 0) & (lane + m - 2 < cols), across[m : m + 1], 0.0)
        for m in range(TAPS_DOWN)
    ]
    position = (2 * fold * iota((deep, cols), 0) + 1).astype(jnp.float32) / rows - 1.0
    for phase in range(fold):
        first = phase * deep
        both = total[first : first + deep, :]
        matched = both[:, :cols] + (position + 2.0 * phase / rows) * both[:, cols:]
        result = taps_across[2] * matched
        for m in range(TAPS_DOWN):
            if m != 2:
                result = result + taps_across[m] * pltpu.roll(matched, (2 - m) % cols, 1)
        spread[pl.ds(SUB + phase, deep, stride=fold), :] = result

    sub = iota((SUB, cols), 0)
    wide = iota((SUB, cols), 1)
    segment = wide >> (data_rows.bit_length() - 1)
    lane_row = wide & (SUB - 1)
    lane_slot = (wide >> 3) & (capacity - 1)
    spill_row = wide >> (capacity.bit_length() - 1)
    spill_rows = [jnp.where(wide & (capacity - 1) == c, spill_row, owned) for c in range(capacity)]
    tile_weight = jnp.broadcast_to(weight, (SUB, cols))

    def warped(slot):
        first = tile_of[slot] * SUB + SUB - 2
        result = down[0:1] * spread[pl.ds(first, SUB), :]
        for m in range(1, TAPS_DOWN):
            result = result + down[m : m + 1] * spread[pl.ds(first + m, SUB), :]
        return result

    def message(owner, carry):
        spilled, over = carry
        target = jnp.zeros((SUB, cols), jnp.int32)
        next_spilled = jnp.zeros((SUB, cols), jnp.float32)
        next_over = jnp.zeros((SUB, cols), jnp.float32)
        tiles_here = []
        for c in range(capacity):
            slot = owner * capacity + c
            start = starts[slot]
            past = start + SUB - owned
            tile = warped(slot)
            tiles_here.append(tile)
            target = jnp.where(lane_slot == c, start, target)
            turned = pltpu.roll(tile, start & (SUB - 1), 0)
            next_spilled = next_spilled + jnp.where(sub < past, turned, 0.0)
            next_over = jnp.where(spill_rows[c] < past, tile_weight, next_over)
        meta = jnp.where(segment == 1, (target + lane_row).astype(jnp.float32), tile_weight)
        meta = jnp.where(segment == 0, over, meta)
        tail = jnp.where(sub == SUB - 1, meta, spilled * tile_weight)
        place = place_of(owner, owners)
        out_ref[place, :data_rows, :] = jnp.concatenate(tiles_here, axis=0).astype(jnp.bfloat16)
        out_ref[place, data_rows:, :] = tail.astype(jnp.bfloat16)
        return next_spilled, next_over

    nothing = jnp.zeros((SUB, cols), jnp.float32)
    lax.fori_loop(0, owners, message, (nothing, nothing), unroll=min(owners, 16))


def sky_kernel(capacity, got_ref, coadd_ref, map_ref):
    sources, message_rows, cols = got_ref.shape
    data_rows = capacity * SUB
    owned = coadd_ref.shape[0]
    per_chunk = cols // data_rows
    chunks = sources // per_chunk
    place = iota((chunks, cols), 0)
    wide = iota((chunks, cols), 1)
    row = iota((owned, cols), 0)
    spilled = jnp.zeros((SUB, cols), jnp.float32)
    target = jnp.zeros((chunks, cols), jnp.float32)
    weight = jnp.zeros((chunks, cols), jnp.float32)
    for k in range(per_chunk):
        heads = jnp.zeros((chunks, cols), jnp.float32)
        for chunk in range(chunks):
            tail = got_ref[chunk * per_chunk + k, data_rows:, :].astype(jnp.float32)
            spilled = spilled + tail
            heads = jnp.where(place == chunk, tail[SUB - 1 :], heads)
        here = (wide >= k * data_rows) & (wide < (k + 1) * data_rows)
        target = jnp.where(here, pltpu.roll(heads, (k - 1) * data_rows % cols, 1), target)
        weight = jnp.where(here, pltpu.roll(heads, (k - 2) * data_rows % cols, 1), weight)
    target = target.astype(jnp.int32)
    pieces = [
        jnp.where(row == target[chunk : chunk + 1], weight[chunk : chunk + 1], 0.0)
        for chunk in range(chunks)
    ]
    placement = jnp.concatenate(pieces, axis=1).astype(jnp.bfloat16)
    pixels = got_ref[:, :data_rows, :].reshape(sources * data_rows, cols)
    pixels = jnp.concatenate([pixels, jnp.ones(pixels.shape, jnp.bfloat16)], axis=1)
    sums = jnp.dot(placement, pixels, preferred_element_type=jnp.float32)
    sub = iota((SUB, cols), 0)
    wide = iota((SUB, cols), 1)
    last = sub == SUB - 1
    over = jnp.broadcast_to(spilled[SUB - 1 :], (SUB, cols))
    mine = ((wide >> (capacity.bit_length() - 1)) == sub) & ~last
    over = jnp.sum(jnp.where(mine, over, 0.0), axis=1, keepdims=True)
    rest = jnp.zeros((owned - SUB, cols), jnp.float32)
    pixel_sum = sums[:, :cols] + jnp.concatenate([jnp.where(last, 0.0, spilled), rest], axis=0)
    weight_sum = sums[:, cols:] + jnp.concatenate(
        [jnp.broadcast_to(over, (SUB, cols)), rest], axis=0
    )
    coadd_ref[...] = pixel_sum / jnp.maximum(weight_sum, 1.0)
    diagonal = jnp.where(row == iota((owned, cols), 1), weight_sum, 0.0)
    map_ref[...] = jnp.sum(diagonal, axis=0, keepdims=True)


def on_device(
    image,
    row_taps,
    col_taps,
    mix_coeff,
    shift_frac,
    ccd_visit,
    visit_weight,
    tile_block,
    tile_offset,
):
    rows, cols = image.shape[1:]
    tiles = tile_block.shape[0]
    sky = lax.axis_size("sky")
    capacity = max(2, tiles // sky)
    taps, basis = row_taps.shape[1], row_taps.shape[0]
    fold = taps // 2 + 1
    visits = visit_weight.shape[0]
    largest = max(b - a for a, b in itertools.pairwise(group_edges(fold)))
    anywhere = pl.BlockSpec(memory_space=pl.ANY)
    vmem = pl.BlockSpec(memory_space=pltpu.VMEM)
    messages = pl.pallas_call(
        functools.partial(window_kernel, capacity),
        out_shape=pltpu.VMEM((sky, capacity * SUB + SUB, cols), jnp.bfloat16),
        in_specs=[anywhere] * 8 + [pl.BlockSpec(memory_space=pltpu.SMEM)],
        out_specs=vmem,
        scratch_shapes=[
            pltpu.VMEM((1, rows, cols), jnp.bfloat16),
            pltpu.VMEM((taps, basis), jnp.bfloat16),
            pltpu.VMEM((taps, basis), jnp.bfloat16),
            pltpu.VMEM((3, 1, basis), jnp.float32),
            pltpu.VMEM((1, visits), jnp.bfloat16),
            pltpu.SMEM((1, 2), jnp.float32),
            pltpu.SMEM((tiles,), jnp.int32),
            pltpu.SMEM((tiles,), jnp.int32),
            pltpu.SemaphoreType.DMA((8,)),
            pltpu.VMEM((rows + 2 * fold, cols), jnp.float32),
            pltpu.VMEM((2 * fold, basis), jnp.float32),
            pltpu.VMEM((3, 2 * fold, cols), jnp.float32),
            pltpu.VMEM((largest * 2 * cols, 2 * cols), jnp.bfloat16),
            pltpu.VMEM((largest * 2 * cols, 2 * cols), jnp.bfloat16),
            pltpu.VMEM(((3 * fold - 1) * (rows // fold), cols), jnp.bfloat16),
            pltpu.VMEM((rows, 2 * cols), jnp.float32),
            pltpu.VMEM((rows + 2 * SUB, cols), jnp.float32),
            pltpu.SMEM((sky * capacity,), jnp.int32),
            pltpu.SMEM((sky * capacity,), jnp.int32),
            pltpu.SMEM((sky,), jnp.int32),
        ],
        compiler_params=pltpu.CompilerParams(vmem_limit_bytes=LARGE_VMEM),
        name="match_warp_pack",
    )(
        *[
            pltpu.with_memory_space_constraint(value, pltpu.HBM)
            for value in (
                image,
                row_taps.T,
                col_taps.T,
                mix_coeff.transpose(1, 0, 2),
                visit_weight.reshape(1, -1),
                shift_frac,
                tile_block,
                tile_offset,
            )
        ],
        ccd_visit,
    )
    order = sorted(range(sky), key=lambda owner: place_of(owner, sky))
    received = lax.all_to_all(
        messages, "sky", split_axis=0, concat_axis=0, axis_index_groups=[order], tiled=True
    )
    coadd, weight_map = pl.pallas_call(
        functools.partial(sky_kernel, capacity),
        out_shape=(
            jax.ShapeDtypeStruct((BLK_DEV * SUB, cols), jnp.float32),
            jax.ShapeDtypeStruct((1, BLK_DEV * SUB), jnp.float32),
        ),
        in_specs=[vmem],
        out_specs=(vmem, vmem),
        compiler_params=pltpu.CompilerParams(vmem_limit_bytes=SMALL_VMEM),
        name="place_normalise",
    )(received)
    return coadd, weight_map.reshape(-1)


def solution(mesh):
    return jax.shard_map(
        on_device,
        mesh=mesh,
        in_specs=(
            P(("groups", "sky"), None, None),
            P(),
            P(),
            P(("groups", "sky"), None, None),
            P(("groups", "sky"), None),
            P(("groups", "sky")),
            P("groups"),
            P(("groups", "sky")),
            P(("groups", "sky")),
        ),
        out_specs=(P(("groups", "sky"), None), P(("groups", "sky"))),
        check_vma=False,
    )
```

```python
import functools
import itertools

import jax
import jax.numpy as jnp
from jax import lax
from jax.experimental import pallas as pl
from jax.experimental.pallas import tpu as pltpu
from jax.sharding import PartitionSpec as P

BLK_DEV = 16
SUB = 8
LARGE_VMEM = 32 * 1024 * 1024
SMALL_VMEM = 16 * 1024 * 1024
EMPTY = -64
TAPS_DOWN = 6


def iota(shape, axis):
    return lax.broadcasted_iota(jnp.int32, shape, axis)


def weight_of(visit_ref, weight_ref):
    values = weight_ref[...].astype(jnp.float32)
    chosen = jnp.where(iota(values.shape, 1) == visit_ref[0], values, 0.0)
    return jnp.sum(chosen, axis=1, keepdims=True)


def lanczos_rows(frac_ref, cols):
    row = iota((2 * SUB, cols), 0)
    tap = jnp.where(row < SUB, row, row - SUB)
    fraction = jnp.where(row < SUB, frac_ref[0, 1], frac_ref[0, 0])
    angles = jnp.pi * ((tap - 2).astype(jnp.float32) - fraction)
    third = angles / 3.0
    kernel = jnp.sin(angles) / angles * (jnp.sin(third) / third)
    kernel = jnp.where(tap < TAPS_DOWN, kernel, 0.0)
    across, down = kernel[:SUB], kernel[SUB:]
    across = across / jnp.sum(across, axis=0, keepdims=True)
    down = down / jnp.sum(down, axis=0, keepdims=True)
    return across, down


def combined_taps(row_ref, col_ref, mix_ref, lifted, base):
    taps, basis = row_ref.shape
    count, cols = base.shape[1:]
    half = taps // 2
    l, s = iota((cols, taps), 0), iota((cols, taps), 1)
    turned = ((s + l == half) | (s + l == half + cols)).astype(jnp.float32).astype(jnp.bfloat16)
    across = jnp.dot(turned, row_ref[...], preferred_element_type=jnp.float32)
    across = across.astype(jnp.bfloat16)
    lifted[0:1] = jnp.zeros((1, basis), jnp.float32)
    lifted[1:] = col_ref[...].astype(jnp.float32)
    down = lifted[...]
    scaled = jnp.concatenate([down * mix_ref[term] for term in range(3)], axis=0)
    high = scaled.astype(jnp.bfloat16)
    low = (scaled - high.astype(jnp.float32)).astype(jnp.bfloat16)
    found = lax.dot_general(
        jnp.concatenate([high, low], axis=0),
        across,
        (((1,), (1,)), ((), ())),
        preferred_element_type=jnp.float32,
    )
    found = found[: 3 * count] + found[3 * count :]
    lane = iota((count, cols), 1)
    lane = jnp.where(lane < cols // 2, lane, lane - cols).astype(jnp.float32)
    base[0] = found[:count] + (2.0 / cols) * lane * found[count : 2 * count]
    base[1] = found[count : 2 * count]
    base[2] = found[2 * count :]


def build_band(base, row, band, first):
    cols = base.shape[2]
    shape = (2 * SUB, cols)
    sub = iota(shape, 0)
    lane = iota(shape, 1)
    lane = jnp.where(lane < cols // 2, lane, lane - cols)
    first_u = (2.0 * sub.astype(jnp.float32) + 1.0) / cols - 1.0

    def spin(term):
        taps = jnp.broadcast_to(base[term, pl.ds(row, 1), :], shape)
        return pltpu.roll(taps, 0, 1, stride=1, stride_axis=0)

    slope = spin(1)
    level = spin(0) + first_u * slope
    rise = spin(2)
    whole = rise.astype(jnp.bfloat16)
    pairs = cols // (2 * SUB)
    for pair in range(pairs):
        shift = 2 * SUB * pair
        value = level + (2.0 * shift / cols) * slope
        other = whole
        if pair == 0 or pair == pairs - 1:
            inside = lane >= 0 if pair == 0 else lane < 2 * SUB
            value = jnp.where(inside, value, 0.0)
            other = jnp.where(inside, rise, 0.0).astype(jnp.bfloat16)
        value = value.astype(jnp.bfloat16)
        if pair:
            value, other = pltpu.roll(value, shift, 1), pltpu.roll(other, shift, 1)
        at = first + shift
        band[at : at + 2 * SUB, :] = jnp.concatenate([value, other], axis=1)


def place_of(owner, owners):
    slow = 1 << ((owners.bit_length() - 1) // 2)
    fast = owners // slow
    return (owner // fast + slow // 2) % slow * fast + (owner + fast // 2) % fast


def group_edges(fold):
    return [0, fold // 8, fold // 2, fold]


def window_kernel(
    capacity,
    image_hbm,
    row_hbm,
    col_hbm,
    mix_hbm,
    weight_hbm,
    frac_hbm,
    block_hbm,
    offset_hbm,
    visit_ref,
    out_ref,
    image_ref,
    row_ref,
    col_ref,
    mix_ref,
    weight_ref,
    frac_ref,
    block_ref,
    offset_ref,
    copied,
    padded,
    lifted,
    base,
    band_a,
    band_b,
    blocks,
    total,
    spread,
    tile_of,
    starts,
    counts,
):
    rows, cols = image_ref.shape[1:]
    fold = row_ref.shape[0] // 2 + 1
    deep = rows // fold
    tiles = block_ref.shape[0]
    owners = out_ref.shape[0]
    data_rows = capacity * SUB
    owned = BLK_DEV * SUB

    pairs = (
        (image_hbm, image_ref),
        (row_hbm, row_ref),
        (col_hbm, col_ref),
        (mix_hbm, mix_ref),
        (frac_hbm, frac_ref),
        (weight_hbm, weight_ref),
        (block_hbm, block_ref),
        (offset_hbm, offset_ref),
    )
    copies = [
        pltpu.make_async_copy(source, target, copied.at[index])
        for index, (source, target) in enumerate(pairs)
    ]
    for copy in copies:
        copy.start()

    @pl.loop(0, owners)
    def _(owner):
        counts[owner] = 0

    if owners * capacity > tiles:

        @pl.loop(0, owners * capacity)
        def _(slot):
            starts[slot] = EMPTY
            tile_of[slot] = 0

    padded[:fold] = jnp.zeros((fold, cols), jnp.float32)
    padded[fold + rows :] = jnp.zeros((fold, cols), jnp.float32)
    spread[:SUB] = jnp.zeros((SUB, cols), jnp.float32)
    spread[SUB + rows :] = jnp.zeros((SUB, cols), jnp.float32)
    for copy in copies[1:4]:
        copy.wait()
    combined_taps(row_ref, col_ref, mix_ref, lifted, base)

    edges = group_edges(fold)
    groups = len(edges) - 1

    def build(group, band):
        for index, r in enumerate(range(edges[group], edges[group + 1])):
            for part in range(2):
                build_band(base, r + part * fold, band, (2 * index + part) * cols)

    held = (band_a, band_b)
    build(0, held[0])
    for copy in copies[:1] + copies[4:]:
        copy.wait()
    padded[fold : fold + rows] = image_ref[0].astype(jnp.float32)
    across, down = lanczos_rows(frac_ref, cols)
    weight = weight_of(visit_ref, weight_ref)

    for index in range(3 * fold - 1):
        blocks[index * deep : (index + 1) * deep, :] = padded[
            pl.ds(index, deep, stride=fold), :
        ].astype(jnp.bfloat16)

    def multiply(group, band):
        parts = []
        for r in range(edges[group], edges[group + 1]):
            for part in range(2):
                first = (r + part * fold) * deep
                parts.append(blocks[first : first + rows, :])
        product = jnp.dot(
            jnp.concatenate(parts, axis=1),
            band[: len(parts) * cols, :],
            preferred_element_type=jnp.float32,
        )
        total[...] = product if group == 0 else total[...] + product

    def assign(tile):
        block = block_ref[tile]
        owner = lax.div(block, BLK_DEV)
        rank = counts[owner]
        counts[owner] = rank + 1
        slot = owner * capacity + rank
        tile_of[slot] = tile
        starts[slot] = (block - owner * BLK_DEV) * SUB + offset_ref[tile]

    for group in range(groups):
        if group + 1 < groups:
            build(group + 1, held[(group + 1) % 2])
        multiply(group, held[group % 2])
        for tile in range(group * tiles // groups, (group + 1) * tiles // groups):
            assign(tile)

    lane = iota((1, cols), 1)
    taps_across = [
        jnp.where((lane + m - 2 >= 0) & (lane + m - 2 < cols), across[m : m + 1], 0.0)
        for m in range(TAPS_DOWN)
    ]
    position = (2 * fold * iota((deep, cols), 0) + 1).astype(jnp.float32) / rows - 1.0
    for phase in range(fold):
        first = phase * deep
        both = total[first : first + deep, :]
        matched = both[:, :cols] + (position + 2.0 * phase / rows) * both[:, cols:]
        result = taps_across[2] * matched
        for m in range(TAPS_DOWN):
            if m != 2:
                result = result + taps_across[m] * pltpu.roll(matched, (2 - m) % cols, 1)
        spread[pl.ds(SUB + phase, deep, stride=fold), :] = result

    sub = iota((SUB, cols), 0)
    wide = iota((SUB, cols), 1)
    segment = wide >> (data_rows.bit_length() - 1)
    lane_row = wide & (SUB - 1)
    lane_slot = (wide >> 3) & (capacity - 1)
    spill_row = wide >> (capacity.bit_length() - 1)
    spill_rows = [jnp.where(wide & (capacity - 1) == c, spill_row, owned) for c in range(capacity)]
    tile_weight = jnp.broadcast_to(weight, (SUB, cols))

    def warped(slot):
        first = tile_of[slot] * SUB + SUB - 2
        result = down[0:1] * spread[pl.ds(first, SUB), :]
        for m in range(1, TAPS_DOWN):
            result = result + down[m : m + 1] * spread[pl.ds(first + m, SUB), :]
        return result

    def message(owner, carry):
        spilled, over = carry
        target = jnp.zeros((SUB, cols), jnp.int32)
        next_spilled = jnp.zeros((SUB, cols), jnp.float32)
        next_over = jnp.zeros((SUB, cols), jnp.float32)
        tiles_here = []
        for c in range(capacity):
            slot = owner * capacity + c
            start = starts[slot]
            past = start + SUB - owned
            tile = warped(slot)
            tiles_here.append(tile)
            target = jnp.where(lane_slot == c, start, target)
            turned = pltpu.roll(tile, start & (SUB - 1), 0)
            next_spilled = next_spilled + jnp.where(sub < past, turned, 0.0)
            next_over = jnp.where(spill_rows[c] < past, tile_weight, next_over)
        meta = jnp.where(segment == 1, (target + lane_row).astype(jnp.float32), tile_weight)
        meta = jnp.where(segment == 0, over, meta)
        tail = jnp.where(sub == SUB - 1, meta, spilled * tile_weight)
        place = place_of(owner, owners)
        out_ref[place, :data_rows, :] = jnp.concatenate(tiles_here, axis=0).astype(jnp.bfloat16)
        out_ref[place, data_rows:, :] = tail.astype(jnp.bfloat16)
        return next_spilled, next_over

    nothing = jnp.zeros((SUB, cols), jnp.float32)
    lax.fori_loop(0, owners, message, (nothing, nothing), unroll=min(owners, 16))


def sky_kernel(capacity, got_ref, coadd_ref, map_ref):
    sources, message_rows, cols = got_ref.shape
    data_rows = capacity * SUB
    owned = coadd_ref.shape[0]
    per_chunk = cols // data_rows
    chunks = sources // per_chunk
    place = iota((chunks, cols), 0)
    wide = iota((chunks, cols), 1)
    row = iota((owned, cols), 0)
    spilled = jnp.zeros((SUB, cols), jnp.float32)
    target = jnp.zeros((chunks, cols), jnp.float32)
    weight = jnp.zeros((chunks, cols), jnp.float32)
    for k in range(per_chunk):
        heads = jnp.zeros((chunks, cols), jnp.float32)
        for chunk in range(chunks):
            tail = got_ref[chunk * per_chunk + k, data_rows:, :].astype(jnp.float32)
            spilled = spilled + tail
            heads = jnp.where(place == chunk, tail[SUB - 1 :], heads)
        here = (wide >= k * data_rows) & (wide < (k + 1) * data_rows)
        target = jnp.where(here, pltpu.roll(heads, (k - 1) * data_rows % cols, 1), target)
        weight = jnp.where(here, pltpu.roll(heads, (k - 2) * data_rows % cols, 1), weight)
    target = target.astype(jnp.int32)
    pieces = [
        jnp.where(row == target[chunk : chunk + 1], weight[chunk : chunk + 1], 0.0)
        for chunk in range(chunks)
    ]
    placement = jnp.concatenate(pieces, axis=1).astype(jnp.bfloat16)
    pixels = got_ref[:, :data_rows, :].reshape(sources * data_rows, cols)
    pixels = jnp.concatenate([pixels, jnp.ones(pixels.shape, jnp.bfloat16)], axis=1)
    sums = jnp.dot(placement, pixels, preferred_element_type=jnp.float32)
    sub = iota((SUB, cols), 0)
    wide = iota((SUB, cols), 1)
    last = sub == SUB - 1
    over = jnp.broadcast_to(spilled[SUB - 1 :], (SUB, cols))
    mine = ((wide >> (capacity.bit_length() - 1)) == sub) & ~last
    over = jnp.sum(jnp.where(mine, over, 0.0), axis=1, keepdims=True)
    rest = jnp.zeros((owned - SUB, cols), jnp.float32)
    pixel_sum = sums[:, :cols] + jnp.concatenate([jnp.where(last, 0.0, spilled), rest], axis=0)
    weight_sum = sums[:, cols:] + jnp.concatenate(
        [jnp.broadcast_to(over, (SUB, cols)), rest], axis=0
    )
    coadd_ref[...] = pixel_sum / jnp.maximum(weight_sum, 1.0)
    diagonal = jnp.where(row == iota((owned, cols), 1), weight_sum, 0.0)
    map_ref[...] = jnp.sum(diagonal, axis=0, keepdims=True)


def on_device(
    image,
    row_taps,
    col_taps,
    mix_coeff,
    shift_frac,
    ccd_visit,
    visit_weight,
    tile_block,
    tile_offset,
):
    rows, cols = image.shape[1:]
    tiles = tile_block.shape[0]
    sky = lax.axis_size("sky")
    capacity = max(2, tiles // sky)
    taps, basis = row_taps.shape[1], row_taps.shape[0]
    fold = taps // 2 + 1
    visits = visit_weight.shape[0]
    largest = max(b - a for a, b in itertools.pairwise(group_edges(fold)))
    anywhere = pl.BlockSpec(memory_space=pl.ANY)
    vmem = pl.BlockSpec(memory_space=pltpu.VMEM)
    messages = pl.pallas_call(
        functools.partial(window_kernel, capacity),
        out_shape=pltpu.VMEM((sky, capacity * SUB + SUB, cols), jnp.bfloat16),
        in_specs=[anywhere] * 8 + [pl.BlockSpec(memory_space=pltpu.SMEM)],
        out_specs=vmem,
        scratch_shapes=[
            pltpu.VMEM((1, rows, cols), jnp.bfloat16),
            pltpu.VMEM((taps, basis), jnp.bfloat16),
            pltpu.VMEM((taps, basis), jnp.bfloat16),
            pltpu.VMEM((3, 1, basis), jnp.float32),
            pltpu.VMEM((1, visits), jnp.bfloat16),
            pltpu.SMEM((1, 2), jnp.float32),
            pltpu.SMEM((tiles,), jnp.int32),
            pltpu.SMEM((tiles,), jnp.int32),
            pltpu.SemaphoreType.DMA((8,)),
            pltpu.VMEM((rows + 2 * fold, cols), jnp.float32),
            pltpu.VMEM((2 * fold, basis), jnp.float32),
            pltpu.VMEM((3, 2 * fold, cols), jnp.float32),
            pltpu.VMEM((largest * 2 * cols, 2 * cols), jnp.bfloat16),
            pltpu.VMEM((largest * 2 * cols, 2 * cols), jnp.bfloat16),
            pltpu.VMEM(((3 * fold - 1) * (rows // fold), cols), jnp.bfloat16),
            pltpu.VMEM((rows, 2 * cols), jnp.float32),
            pltpu.VMEM((rows + 2 * SUB, cols), jnp.float32),
            pltpu.SMEM((sky * capacity,), jnp.int32),
            pltpu.SMEM((sky * capacity,), jnp.int32),
            pltpu.SMEM((sky,), jnp.int32),
        ],
        compiler_params=pltpu.CompilerParams(vmem_limit_bytes=LARGE_VMEM),
        name="match_warp_pack",
    )(
        *[
            pltpu.with_memory_space_constraint(value, pltpu.HBM)
            for value in (
                image,
                row_taps.T,
                col_taps.T,
                mix_coeff.transpose(1, 0, 2),
                visit_weight.reshape(1, -1),
                shift_frac,
                tile_block,
                tile_offset,
            )
        ],
        ccd_visit,
    )
    order = sorted(range(sky), key=lambda owner: place_of(owner, sky))
    received = lax.all_to_all(
        messages, "sky", split_axis=0, concat_axis=0, axis_index_groups=[order], tiled=True
    )
    coadd, weight_map = pl.pallas_call(
        functools.partial(sky_kernel, capacity),
        out_shape=(
            jax.ShapeDtypeStruct((BLK_DEV * SUB, cols), jnp.float32),
            jax.ShapeDtypeStruct((1, BLK_DEV * SUB), jnp.float32),
        ),
        in_specs=[vmem],
        out_specs=(vmem, vmem),
        compiler_params=pltpu.CompilerParams(vmem_limit_bytes=SMALL_VMEM),
        name="place_normalise",
    )(received)
    return coadd, weight_map.reshape(-1)


def solution(mesh):
    return jax.shard_map(
        on_device,
        mesh=mesh,
        in_specs=(
            P(("groups", "sky"), None, None),
            P(),
            P(),
            P(("groups", "sky"), None, None),
            P(("groups", "sky"), None),
            P(("groups", "sky")),
            P("groups"),
            P(("groups", "sky")),
            P(("groups", "sky")),
        ),
        out_specs=(P(("groups", "sky"), None), P(("groups", "sky"))),
        check_vma=False,
    )
```

```python
import functools
import itertools

import jax
import jax.numpy as jnp
from jax import lax
from jax.experimental import pallas as pl
from jax.experimental.pallas import tpu as pltpu
from jax.sharding import PartitionSpec as P

BLK_DEV = 16
SUB = 8
LARGE_VMEM = 32 * 1024 * 1024
SMALL_VMEM = 16 * 1024 * 1024
EMPTY = -64
TAPS_DOWN = 6


def iota(shape, axis):
    return lax.broadcasted_iota(jnp.int32, shape, axis)


def weight_of(visit_ref, weight_ref):
    values = weight_ref[...].astype(jnp.float32)
    chosen = jnp.where(iota(values.shape, 1) == visit_ref[0], values, 0.0)
    return jnp.sum(chosen, axis=1, keepdims=True)


def lanczos_rows(frac_ref, cols):
    row = iota((2 * SUB, cols), 0)
    tap = jnp.where(row < SUB, row, row - SUB)
    fraction = jnp.where(row < SUB, frac_ref[0, 1], frac_ref[0, 0])
    angles = jnp.pi * ((tap - 2).astype(jnp.float32) - fraction)
    third = angles / 3.0
    kernel = jnp.sin(angles) / angles * (jnp.sin(third) / third)
    kernel = jnp.where(tap < TAPS_DOWN, kernel, 0.0)
    across, down = kernel[:SUB], kernel[SUB:]
    across = across / jnp.sum(across, axis=0, keepdims=True)
    down = down / jnp.sum(down, axis=0, keepdims=True)
    return across, down


def combined_taps(row_ref, col_ref, mix_ref, lifted, base):
    taps, basis = row_ref.shape
    count, cols = base.shape[1:]
    half = taps // 2
    l, s = iota((cols, taps), 0), iota((cols, taps), 1)
    turned = ((s + l == half) | (s + l == half + cols)).astype(jnp.float32).astype(jnp.bfloat16)
    across = jnp.dot(turned, row_ref[...], preferred_element_type=jnp.float32)
    across = across.astype(jnp.bfloat16)
    lifted[0:1] = jnp.zeros((1, basis), jnp.float32)
    lifted[1:] = col_ref[...].astype(jnp.float32)
    down = lifted[...]
    scaled = jnp.concatenate([down * mix_ref[term] for term in range(3)], axis=0)
    high = scaled.astype(jnp.bfloat16)
    low = (scaled - high.astype(jnp.float32)).astype(jnp.bfloat16)
    found = lax.dot_general(
        jnp.concatenate([high, low], axis=0),
        across,
        (((1,), (1,)), ((), ())),
        preferred_element_type=jnp.float32,
    )
    found = found[: 3 * count] + found[3 * count :]
    lane = iota((count, cols), 1)
    lane = jnp.where(lane < cols // 2, lane, lane - cols).astype(jnp.float32)
    base[0] = found[:count] + (2.0 / cols) * lane * found[count : 2 * count]
    base[1] = found[count : 2 * count]
    base[2] = found[2 * count :]


def build_band(base, row, band, first):
    cols = base.shape[2]
    shape = (2 * SUB, cols)
    sub = iota(shape, 0)
    lane = iota(shape, 1)
    lane = jnp.where(lane < cols // 2, lane, lane - cols)
    first_u = (2.0 * sub.astype(jnp.float32) + 1.0) / cols - 1.0

    def spin(term):
        taps = jnp.broadcast_to(base[term, pl.ds(row, 1), :], shape)
        return pltpu.roll(taps, 0, 1, stride=1, stride_axis=0)

    slope = spin(1)
    level = spin(0) + first_u * slope
    rise = spin(2)
    whole = rise.astype(jnp.bfloat16)
    pairs = cols // (2 * SUB)
    for pair in range(pairs):
        shift = 2 * SUB * pair
        value = level + (2.0 * shift / cols) * slope
        other = whole
        if pair == 0 or pair == pairs - 1:
            inside = lane >= 0 if pair == 0 else lane < 2 * SUB
            value = jnp.where(inside, value, 0.0)
            other = jnp.where(inside, rise, 0.0).astype(jnp.bfloat16)
        value = value.astype(jnp.bfloat16)
        if pair:
            value, other = pltpu.roll(value, shift, 1), pltpu.roll(other, shift, 1)
        at = first + shift
        band[at : at + 2 * SUB, :] = jnp.concatenate([value, other], axis=1)


def place_of(owner, owners):
    slow = 1 << ((owners.bit_length() - 1) // 2)
    fast = owners // slow
    return (owner // fast + slow // 2) % slow * fast + (owner + fast // 2) % fast


def group_edges(fold):
    return [0, fold // 8, fold // 2, fold]


def window_kernel(
    capacity,
    image_hbm,
    row_hbm,
    col_hbm,
    mix_hbm,
    weight_hbm,
    frac_hbm,
    block_hbm,
    offset_hbm,
    visit_ref,
    out_ref,
    image_ref,
    row_ref,
    col_ref,
    mix_ref,
    weight_ref,
    frac_ref,
    block_ref,
    offset_ref,
    copied,
    padded,
    lifted,
    base,
    band_a,
    band_b,
    blocks,
    total,
    spread,
    tile_of,
    starts,
    counts,
):
    rows, cols = image_ref.shape[1:]
    fold = row_ref.shape[0] // 2 + 1
    deep = rows // fold
    tiles = block_ref.shape[0]
    owners = out_ref.shape[0]
    data_rows = capacity * SUB
    owned = BLK_DEV * SUB

    pairs = (
        (row_hbm, row_ref),
        (col_hbm, col_ref),
        (mix_hbm, mix_ref),
        (image_hbm, image_ref),
        (frac_hbm, frac_ref),
        (weight_hbm, weight_ref),
        (block_hbm, block_ref),
        (offset_hbm, offset_ref),
    )
    copies = [
        pltpu.make_async_copy(source, target, copied.at[index])
        for index, (source, target) in enumerate(pairs)
    ]
    for copy in copies:
        copy.start()

    @pl.loop(0, owners)
    def _(owner):
        counts[owner] = 0

    if owners * capacity > tiles:

        @pl.loop(0, owners * capacity)
        def _(slot):
            starts[slot] = EMPTY
            tile_of[slot] = 0

    padded[:fold] = jnp.zeros((fold, cols), jnp.float32)
    padded[fold + rows :] = jnp.zeros((fold, cols), jnp.float32)
    spread[:SUB] = jnp.zeros((SUB, cols), jnp.float32)
    spread[SUB + rows :] = jnp.zeros((SUB, cols), jnp.float32)
    for copy in copies[:3]:
        copy.wait()
    combined_taps(row_ref, col_ref, mix_ref, lifted, base)
    for copy in copies[3:]:
        copy.wait()
    padded[fold : fold + rows] = image_ref[0].astype(jnp.float32)
    across, down = lanczos_rows(frac_ref, cols)
    weight = weight_of(visit_ref, weight_ref)

    for index in range(3 * fold - 1):
        blocks[index * deep : (index + 1) * deep, :] = padded[
            pl.ds(index, deep, stride=fold), :
        ].astype(jnp.bfloat16)

    edges = group_edges(fold)
    groups = len(edges) - 1

    def build(group, band):
        for index, r in enumerate(range(edges[group], edges[group + 1])):
            for part in range(2):
                build_band(base, r + part * fold, band, (2 * index + part) * cols)

    def multiply(group, band):
        parts = []
        for r in range(edges[group], edges[group + 1]):
            for part in range(2):
                first = (r + part * fold) * deep
                parts.append(blocks[first : first + rows, :])
        product = jnp.dot(
            jnp.concatenate(parts, axis=1),
            band[: len(parts) * cols, :],
            preferred_element_type=jnp.float32,
        )
        total[...] = product if group == 0 else total[...] + product

    def assign(tile):
        block = block_ref[tile]
        owner = lax.div(block, BLK_DEV)
        rank = counts[owner]
        counts[owner] = rank + 1
        slot = owner * capacity + rank
        tile_of[slot] = tile
        starts[slot] = (block - owner * BLK_DEV) * SUB + offset_ref[tile]

    held = (band_a, band_b)
    build(0, held[0])
    for group in range(groups):
        if group + 1 < groups:
            build(group + 1, held[(group + 1) % 2])
        multiply(group, held[group % 2])
        for tile in range(group * tiles // groups, (group + 1) * tiles // groups):
            assign(tile)

    lane = iota((1, cols), 1)
    taps_across = [
        jnp.where((lane + m - 2 >= 0) & (lane + m - 2 < cols), across[m : m + 1], 0.0)
        for m in range(TAPS_DOWN)
    ]
    position = (2 * fold * iota((deep, cols), 0) + 1).astype(jnp.float32) / rows - 1.0
    for phase in range(fold):
        first = phase * deep
        both = total[first : first + deep, :]
        matched = both[:, :cols] + (position + 2.0 * phase / rows) * both[:, cols:]
        result = taps_across[2] * matched
        for m in range(TAPS_DOWN):
            if m != 2:
                result = result + taps_across[m] * pltpu.roll(matched, (2 - m) % cols, 1)
        spread[pl.ds(SUB + phase, deep, stride=fold), :] = result

    sub = iota((SUB, cols), 0)
    wide = iota((SUB, cols), 1)
    segment = wide >> (data_rows.bit_length() - 1)
    lane_row = wide & (SUB - 1)
    lane_slot = (wide >> 3) & (capacity - 1)
    spill_row = wide >> (capacity.bit_length() - 1)
    spill_rows = [jnp.where(wide & (capacity - 1) == c, spill_row, owned) for c in range(capacity)]
    tile_weight = jnp.broadcast_to(weight, (SUB, cols))

    def warped(slot):
        first = tile_of[slot] * SUB + SUB - 2
        result = down[0:1] * spread[pl.ds(first, SUB), :]
        for m in range(1, TAPS_DOWN):
            result = result + down[m : m + 1] * spread[pl.ds(first + m, SUB), :]
        return result

    def message(owner, carry):
        spilled, over = carry
        target = jnp.zeros((SUB, cols), jnp.int32)
        next_spilled = jnp.zeros((SUB, cols), jnp.float32)
        next_over = jnp.zeros((SUB, cols), jnp.float32)
        tiles_here = []
        for c in range(capacity):
            slot = owner * capacity + c
            start = starts[slot]
            past = start + SUB - owned
            tile = warped(slot)
            tiles_here.append(tile)
            target = jnp.where(lane_slot == c, start, target)
            turned = pltpu.roll(tile, start & (SUB - 1), 0)
            next_spilled = next_spilled + jnp.where(sub < past, turned, 0.0)
            next_over = jnp.where(spill_rows[c] < past, tile_weight, next_over)
        meta = jnp.where(segment == 1, (target + lane_row).astype(jnp.float32), tile_weight)
        meta = jnp.where(segment == 0, over, meta)
        tail = jnp.where(sub == SUB - 1, meta, spilled * tile_weight)
        place = place_of(owner, owners)
        out_ref[place, :data_rows, :] = jnp.concatenate(tiles_here, axis=0).astype(jnp.bfloat16)
        out_ref[place, data_rows:, :] = tail.astype(jnp.bfloat16)
        return next_spilled, next_over

    nothing = jnp.zeros((SUB, cols), jnp.float32)
    lax.fori_loop(0, owners, message, (nothing, nothing), unroll=min(owners, 16))


def sky_kernel(capacity, got_ref, coadd_hbm, map_ref, coadd_ref, copied):
    sources, message_rows, cols = got_ref.shape
    data_rows = capacity * SUB
    owned = coadd_ref.shape[0]
    per_chunk = cols // data_rows
    chunks = sources // per_chunk
    place = iota((chunks, cols), 0)
    wide = iota((chunks, cols), 1)
    row = iota((owned, cols), 0)
    spilled = jnp.zeros((SUB, cols), jnp.float32)
    target = jnp.zeros((chunks, cols), jnp.float32)
    weight = jnp.zeros((chunks, cols), jnp.float32)
    for k in range(per_chunk):
        heads = jnp.zeros((chunks, cols), jnp.float32)
        for chunk in range(chunks):
            tail = got_ref[chunk * per_chunk + k, data_rows:, :].astype(jnp.float32)
            spilled = spilled + tail
            heads = jnp.where(place == chunk, tail[SUB - 1 :], heads)
        here = (wide >= k * data_rows) & (wide < (k + 1) * data_rows)
        target = jnp.where(here, pltpu.roll(heads, (k - 1) * data_rows % cols, 1), target)
        weight = jnp.where(here, pltpu.roll(heads, (k - 2) * data_rows % cols, 1), weight)
    target = target.astype(jnp.int32)
    pieces = [
        jnp.where(row == target[chunk : chunk + 1], weight[chunk : chunk + 1], 0.0)
        for chunk in range(chunks)
    ]
    placement = jnp.concatenate(pieces, axis=1).astype(jnp.bfloat16)
    pixels = got_ref[:, :data_rows, :].reshape(sources * data_rows, cols)
    pixels = jnp.concatenate([pixels, jnp.ones(pixels.shape, jnp.bfloat16)], axis=1)
    sums = jnp.dot(placement, pixels, preferred_element_type=jnp.float32)
    sub = iota((SUB, cols), 0)
    wide = iota((SUB, cols), 1)
    last = sub == SUB - 1
    over = jnp.broadcast_to(spilled[SUB - 1 :], (SUB, cols))
    mine = ((wide >> (capacity.bit_length() - 1)) == sub) & ~last
    over = jnp.sum(jnp.where(mine, over, 0.0), axis=1, keepdims=True)
    rest = jnp.zeros((owned - SUB, cols), jnp.float32)
    pixel_sum = sums[:, :cols] + jnp.concatenate([jnp.where(last, 0.0, spilled), rest], axis=0)
    weight_sum = sums[:, cols:] + jnp.concatenate(
        [jnp.broadcast_to(over, (SUB, cols)), rest], axis=0
    )
    copies = []
    for index in range(2):
        part = slice(index * owned // 2, (index + 1) * owned // 2)
        coadd_ref[part, :] = pixel_sum[part] / jnp.maximum(weight_sum[part], 1.0)
        copies.append(
            pltpu.make_async_copy(
                coadd_ref.at[part, :], coadd_hbm.at[part, :], copied.at[index]
            )
        )
        copies[-1].start()
    diagonal = jnp.where(row == iota((owned, cols), 1), weight_sum, 0.0)
    map_ref[...] = jnp.sum(diagonal, axis=0, keepdims=True)
    for copy in copies:
        copy.wait()


def on_device(
    image,
    row_taps,
    col_taps,
    mix_coeff,
    shift_frac,
    ccd_visit,
    visit_weight,
    tile_block,
    tile_offset,
):
    rows, cols = image.shape[1:]
    tiles = tile_block.shape[0]
    sky = lax.axis_size("sky")
    capacity = max(2, tiles // sky)
    taps, basis = row_taps.shape[1], row_taps.shape[0]
    fold = taps // 2 + 1
    visits = visit_weight.shape[0]
    largest = max(b - a for a, b in itertools.pairwise(group_edges(fold)))
    anywhere = pl.BlockSpec(memory_space=pl.ANY)
    vmem = pl.BlockSpec(memory_space=pltpu.VMEM)
    messages = pl.pallas_call(
        functools.partial(window_kernel, capacity),
        out_shape=pltpu.VMEM((sky, capacity * SUB + SUB, cols), jnp.bfloat16),
        in_specs=[anywhere] * 8 + [pl.BlockSpec(memory_space=pltpu.SMEM)],
        out_specs=vmem,
        scratch_shapes=[
            pltpu.VMEM((1, rows, cols), jnp.bfloat16),
            pltpu.VMEM((taps, basis), jnp.bfloat16),
            pltpu.VMEM((taps, basis), jnp.bfloat16),
            pltpu.VMEM((3, 1, basis), jnp.float32),
            pltpu.VMEM((1, visits), jnp.bfloat16),
            pltpu.SMEM((1, 2), jnp.float32),
            pltpu.SMEM((tiles,), jnp.int32),
            pltpu.SMEM((tiles,), jnp.int32),
            pltpu.SemaphoreType.DMA((8,)),
            pltpu.VMEM((rows + 2 * fold, cols), jnp.float32),
            pltpu.VMEM((2 * fold, basis), jnp.float32),
            pltpu.VMEM((3, 2 * fold, cols), jnp.float32),
            pltpu.VMEM((largest * 2 * cols, 2 * cols), jnp.bfloat16),
            pltpu.VMEM((largest * 2 * cols, 2 * cols), jnp.bfloat16),
            pltpu.VMEM(((3 * fold - 1) * (rows // fold), cols), jnp.bfloat16),
            pltpu.VMEM((rows, 2 * cols), jnp.float32),
            pltpu.VMEM((rows + 2 * SUB, cols), jnp.float32),
            pltpu.SMEM((sky * capacity,), jnp.int32),
            pltpu.SMEM((sky * capacity,), jnp.int32),
            pltpu.SMEM((sky,), jnp.int32),
        ],
        compiler_params=pltpu.CompilerParams(vmem_limit_bytes=LARGE_VMEM),
        name="match_warp_pack",
    )(
        *[
            pltpu.with_memory_space_constraint(value, pltpu.HBM)
            for value in (
                image,
                row_taps.T,
                col_taps.T,
                mix_coeff.transpose(1, 0, 2),
                visit_weight.reshape(1, -1),
                shift_frac,
                tile_block,
                tile_offset,
            )
        ],
        ccd_visit,
    )
    order = sorted(range(sky), key=lambda owner: place_of(owner, sky))
    received = lax.all_to_all(
        messages, "sky", split_axis=0, concat_axis=0, axis_index_groups=[order], tiled=True
    )
    coadd, weight_map = pl.pallas_call(
        functools.partial(sky_kernel, capacity),
        out_shape=(
            jax.ShapeDtypeStruct((BLK_DEV * SUB, cols), jnp.float32),
            jax.ShapeDtypeStruct((1, BLK_DEV * SUB), jnp.float32),
        ),
        in_specs=[vmem],
        out_specs=(anywhere, vmem),
        scratch_shapes=[
            pltpu.VMEM((BLK_DEV * SUB, cols), jnp.float32),
            pltpu.SemaphoreType.DMA((2,)),
        ],
        compiler_params=pltpu.CompilerParams(vmem_limit_bytes=SMALL_VMEM),
        name="place_normalise",
    )(received)
    return coadd, weight_map.reshape(-1)


def solution(mesh):
    return jax.shard_map(
        on_device,
        mesh=mesh,
        in_specs=(
            P(("groups", "sky"), None, None),
            P(),
            P(),
            P(("groups", "sky"), None, None),
            P(("groups", "sky"), None),
            P(("groups", "sky")),
            P("groups"),
            P(("groups", "sky")),
            P(("groups", "sky")),
        ),
        out_specs=(P(("groups", "sky"), None), P(("groups", "sky"))),
        check_vma=False,
    )
```

```python
import functools
import itertools

import jax
import jax.numpy as jnp
from jax import lax
from jax.experimental import pallas as pl
from jax.experimental.pallas import tpu as pltpu
from jax.sharding import PartitionSpec as P

BLK_DEV = 16
SUB = 8
LARGE_VMEM = 32 * 1024 * 1024
SMALL_VMEM = 16 * 1024 * 1024
EMPTY = -64
TAPS_DOWN = 6


def iota(shape, axis):
    return lax.broadcasted_iota(jnp.int32, shape, axis)


def weight_of(visit_ref, weight_ref):
    values = weight_ref[...].astype(jnp.float32)
    chosen = jnp.where(iota(values.shape, 1) == visit_ref[0], values, 0.0)
    return jnp.sum(chosen, axis=1, keepdims=True)


def lanczos_rows(frac_ref, cols):
    row = iota((2 * SUB, cols), 0)
    tap = jnp.where(row < SUB, row, row - SUB)
    fraction = jnp.where(row < SUB, frac_ref[0, 1], frac_ref[0, 0])
    angles = jnp.pi * ((tap - 2).astype(jnp.float32) - fraction)
    third = angles / 3.0
    kernel = jnp.sin(angles) / angles * (jnp.sin(third) / third)
    kernel = jnp.where(tap < TAPS_DOWN, kernel, 0.0)
    across, down = kernel[:SUB], kernel[SUB:]
    across = across / jnp.sum(across, axis=0, keepdims=True)
    down = down / jnp.sum(down, axis=0, keepdims=True)
    return across, down


def combined_taps(row_ref, col_ref, mix_ref, lifted, base):
    taps, basis = row_ref.shape
    count, cols = base.shape[1:]
    half = taps // 2
    l, s = iota((cols, taps), 0), iota((cols, taps), 1)
    turned = ((s + l == half) | (s + l == half + cols)).astype(jnp.float32).astype(jnp.bfloat16)
    across = jnp.dot(turned, row_ref[...], preferred_element_type=jnp.float32)
    across = across.astype(jnp.bfloat16)
    lifted[0:1] = jnp.zeros((1, basis), jnp.float32)
    lifted[1:] = col_ref[...].astype(jnp.float32)
    down = lifted[...]
    scaled = jnp.concatenate([down * mix_ref[term] for term in range(3)], axis=0)
    high = scaled.astype(jnp.bfloat16)
    low = (scaled - high.astype(jnp.float32)).astype(jnp.bfloat16)
    found = lax.dot_general(
        jnp.concatenate([high, low], axis=0),
        across,
        (((1,), (1,)), ((), ())),
        preferred_element_type=jnp.float32,
    )
    found = found[: 3 * count] + found[3 * count :]
    lane = iota((count, cols), 1)
    lane = jnp.where(lane < cols // 2, lane, lane - cols).astype(jnp.float32)
    base[0] = found[:count] + (2.0 / cols) * lane * found[count : 2 * count]
    base[1] = found[count : 2 * count]
    base[2] = found[2 * count :]


def build_band(base, row, band, first):
    cols = base.shape[2]
    shape = (2 * SUB, cols)
    sub = iota(shape, 0)
    lane = iota(shape, 1)
    lane = jnp.where(lane < cols // 2, lane, lane - cols)
    first_u = (2.0 * sub.astype(jnp.float32) + 1.0) / cols - 1.0

    def spin(term):
        taps = jnp.broadcast_to(base[term, pl.ds(row, 1), :], shape)
        return pltpu.roll(taps, 0, 1, stride=1, stride_axis=0)

    slope = spin(1)
    level = spin(0) + first_u * slope
    rise = spin(2)
    whole = rise.astype(jnp.bfloat16)
    pairs = cols // (2 * SUB)
    for pair in range(pairs):
        shift = 2 * SUB * pair
        value = level + (2.0 * shift / cols) * slope
        other = whole
        if pair == 0 or pair == pairs - 1:
            inside = lane >= 0 if pair == 0 else lane < 2 * SUB
            value = jnp.where(inside, value, 0.0)
            other = jnp.where(inside, rise, 0.0).astype(jnp.bfloat16)
        value = value.astype(jnp.bfloat16)
        if pair:
            value, other = pltpu.roll(value, shift, 1), pltpu.roll(other, shift, 1)
        at = first + shift
        band[at : at + 2 * SUB, :] = jnp.concatenate([value, other], axis=1)


def place_of(owner, owners):
    slow = 1 << ((owners.bit_length() - 1) // 2)
    fast = owners // slow
    return (owner // fast + slow // 2) % slow * fast + (owner + fast // 2) % fast


def group_edges(fold):
    return [0, fold // 8, fold // 2, fold]


def window_kernel(
    capacity,
    image_hbm,
    row_hbm,
    col_hbm,
    mix_hbm,
    weight_hbm,
    frac_hbm,
    block_hbm,
    offset_hbm,
    visit_ref,
    out_ref,
    image_ref,
    row_ref,
    col_ref,
    mix_ref,
    weight_ref,
    frac_ref,
    block_ref,
    offset_ref,
    copied,
    padded,
    lifted,
    base,
    band_a,
    band_b,
    blocks,
    total,
    spread,
    tile_of,
    starts,
    counts,
):
    rows, cols = image_ref.shape[1:]
    fold = row_ref.shape[0] // 2 + 1
    deep = rows // fold
    tiles = block_ref.shape[0]
    owners = out_ref.shape[0]
    data_rows = capacity * SUB
    owned = BLK_DEV * SUB

    pairs = (
        (row_hbm, row_ref),
        (col_hbm, col_ref),
        (mix_hbm, mix_ref),
        (image_hbm, image_ref),
        (frac_hbm, frac_ref),
        (weight_hbm, weight_ref),
        (block_hbm, block_ref),
        (offset_hbm, offset_ref),
    )
    copies = [
        pltpu.make_async_copy(source, target, copied.at[index])
        for index, (source, target) in enumerate(pairs)
    ]
    for copy in copies:
        copy.start()

    @pl.loop(0, owners)
    def _(owner):
        counts[owner] = 0

    if owners * capacity > tiles:

        @pl.loop(0, owners * capacity)
        def _(slot):
            starts[slot] = EMPTY
            tile_of[slot] = 0

    padded[:fold] = jnp.zeros((fold, cols), jnp.float32)
    padded[fold + rows :] = jnp.zeros((fold, cols), jnp.float32)
    spread[:SUB] = jnp.zeros((SUB, cols), jnp.float32)
    spread[SUB + rows :] = jnp.zeros((SUB, cols), jnp.float32)
    for copy in copies[:3]:
        copy.wait()
    combined_taps(row_ref, col_ref, mix_ref, lifted, base)
    for copy in copies[3:]:
        copy.wait()
    padded[fold : fold + rows] = image_ref[0].astype(jnp.float32)
    across, down = lanczos_rows(frac_ref, cols)
    weight = weight_of(visit_ref, weight_ref)

    for index in range(3 * fold - 1):
        blocks[index * deep : (index + 1) * deep, :] = padded[
            pl.ds(index, deep, stride=fold), :
        ].astype(jnp.bfloat16)

    edges = group_edges(fold)
    groups = len(edges) - 1

    def build(group, band):
        for index, r in enumerate(range(edges[group], edges[group + 1])):
            for part in range(2):
                build_band(base, r + part * fold, band, (2 * index + part) * cols)

    def multiply(group, band):
        parts = []
        for r in range(edges[group], edges[group + 1]):
            for part in range(2):
                first = (r + part * fold) * deep
                parts.append(blocks[first : first + rows, :])
        product = jnp.dot(
            jnp.concatenate(parts, axis=1),
            band[: len(parts) * cols, :],
            preferred_element_type=jnp.float32,
        )
        total[...] = product if group == 0 else total[...] + product

    def assign(tile):
        block = block_ref[tile]
        owner = lax.div(block, BLK_DEV)
        rank = counts[owner]
        counts[owner] = rank + 1
        slot = owner * capacity + rank
        tile_of[slot] = tile
        starts[slot] = (block - owner * BLK_DEV) * SUB + offset_ref[tile]

    held = (band_a, band_b)
    build(0, held[0])
    for group in range(groups):
        if group + 1 < groups:
            build(group + 1, held[(group + 1) % 2])
        multiply(group, held[group % 2])
        for tile in range(group * tiles // groups, (group + 1) * tiles // groups):
            assign(tile)

    lane = iota((1, cols), 1)
    taps_across = [
        jnp.where((lane + m - 2 >= 0) & (lane + m - 2 < cols), across[m : m + 1], 0.0)
        for m in range(TAPS_DOWN)
    ]
    position = (2 * fold * iota((deep, cols), 0) + 1).astype(jnp.float32) / rows - 1.0
    for phase in range(fold):
        first = phase * deep
        both = total[first : first + deep, :]
        matched = both[:, :cols] + (position + 2.0 * phase / rows) * both[:, cols:]
        result = taps_across[2] * matched
        for m in range(TAPS_DOWN):
            if m != 2:
                result = result + taps_across[m] * pltpu.roll(matched, (2 - m) % cols, 1)
        spread[pl.ds(SUB + phase, deep, stride=fold), :] = result

    sub = iota((SUB, cols), 0)
    wide = iota((SUB, cols), 1)
    segment = wide >> (data_rows.bit_length() - 1)
    lane_row = wide & (SUB - 1)
    lane_slot = (wide >> 3) & (capacity - 1)
    spill_row = wide >> (capacity.bit_length() - 1)
    spill_rows = [jnp.where(wide & (capacity - 1) == c, spill_row, owned) for c in range(capacity)]
    tile_weight = jnp.broadcast_to(weight, (SUB, cols))

    def warped(slot):
        first = tile_of[slot] * SUB + SUB - 2
        result = down[0:1] * spread[pl.ds(first, SUB), :]
        for m in range(1, TAPS_DOWN):
            result = result + down[m : m + 1] * spread[pl.ds(first + m, SUB), :]
        return result

    def message(owner, carry):
        spilled, over = carry
        target = jnp.zeros((SUB, cols), jnp.int32)
        next_spilled = jnp.zeros((SUB, cols), jnp.float32)
        next_over = jnp.zeros((SUB, cols), jnp.float32)
        tiles_here = []
        for c in range(capacity):
            slot = owner * capacity + c
            start = starts[slot]
            past = start + SUB - owned
            tile = warped(slot)
            tiles_here.append(tile)
            target = jnp.where(lane_slot == c, start, target)
            turned = pltpu.roll(tile, start & (SUB - 1), 0)
            next_spilled = next_spilled + jnp.where(sub < past, turned, 0.0)
            next_over = jnp.where(spill_rows[c] < past, tile_weight, next_over)
        meta = jnp.where(segment == 1, (target + lane_row).astype(jnp.float32), tile_weight)
        meta = jnp.where(segment == 0, over, meta)
        tail = jnp.where(sub == SUB - 1, meta, spilled * tile_weight)
        place = place_of(owner, owners)
        out_ref[place, :data_rows, :] = jnp.concatenate(tiles_here, axis=0).astype(jnp.bfloat16)
        out_ref[place, data_rows:, :] = tail.astype(jnp.bfloat16)
        return next_spilled, next_over

    nothing = jnp.zeros((SUB, cols), jnp.float32)
    lax.fori_loop(0, owners, message, (nothing, nothing), unroll=min(owners, 16))


def sky_kernel(capacity, got_ref, coadd_ref, map_ref):
    sources, message_rows, cols = got_ref.shape
    data_rows = capacity * SUB
    owned = coadd_ref.shape[0]
    per_chunk = cols // data_rows
    chunks = sources // per_chunk
    place = iota((chunks, cols), 0)
    wide = iota((chunks, cols), 1)
    row = iota((owned, cols), 0)
    spilled = jnp.zeros((SUB, cols), jnp.float32)
    target = jnp.zeros((chunks, cols), jnp.float32)
    weight = jnp.zeros((chunks, cols), jnp.float32)
    for k in range(per_chunk):
        heads = jnp.zeros((chunks, cols), jnp.float32)
        for chunk in range(chunks):
            tail = got_ref[chunk * per_chunk + k, data_rows:, :].astype(jnp.float32)
            spilled = spilled + tail
            heads = jnp.where(place == chunk, tail[SUB - 1 :], heads)
        here = (wide >= k * data_rows) & (wide < (k + 1) * data_rows)
        target = jnp.where(here, pltpu.roll(heads, (k - 1) * data_rows % cols, 1), target)
        weight = jnp.where(here, pltpu.roll(heads, (k - 2) * data_rows % cols, 1), weight)
    target = target.astype(jnp.int32)
    pieces = [
        jnp.where(row == target[chunk : chunk + 1], weight[chunk : chunk + 1], 0.0)
        for chunk in range(chunks)
    ]
    placement = jnp.concatenate(pieces, axis=1).astype(jnp.bfloat16)
    pixels = got_ref[:, :data_rows, :].reshape(sources * data_rows, cols)
    pixels = jnp.concatenate([pixels, jnp.ones(pixels.shape, jnp.bfloat16)], axis=1)
    sums = jnp.dot(placement, pixels, preferred_element_type=jnp.float32)
    sub = iota((SUB, cols), 0)
    wide = iota((SUB, cols), 1)
    last = sub == SUB - 1
    over = jnp.broadcast_to(spilled[SUB - 1 :], (SUB, cols))
    mine = ((wide >> (capacity.bit_length() - 1)) == sub) & ~last
    over = jnp.sum(jnp.where(mine, over, 0.0), axis=1, keepdims=True)
    rest = jnp.zeros((owned - SUB, cols), jnp.float32)
    pixel_sum = sums[:, :cols] + jnp.concatenate([jnp.where(last, 0.0, spilled), rest], axis=0)
    weight_sum = sums[:, cols:] + jnp.concatenate(
        [jnp.broadcast_to(over, (SUB, cols)), rest], axis=0
    )
    coadd_ref[...] = pixel_sum / jnp.maximum(weight_sum, 1.0)
    diagonal = jnp.where(row == iota((owned, cols), 1), weight_sum, 0.0)
    map_ref[...] = jnp.sum(diagonal, axis=0, keepdims=True)


def on_device(
    image,
    row_taps,
    col_taps,
    mix_coeff,
    shift_frac,
    ccd_visit,
    visit_weight,
    tile_block,
    tile_offset,
):
    rows, cols = image.shape[1:]
    tiles = tile_block.shape[0]
    sky = lax.axis_size("sky")
    capacity = max(2, tiles // sky)
    taps, basis = row_taps.shape[1], row_taps.shape[0]
    fold = taps // 2 + 1
    visits = visit_weight.shape[0]
    largest = max(b - a for a, b in itertools.pairwise(group_edges(fold)))
    anywhere = pl.BlockSpec(memory_space=pl.ANY)
    vmem = pl.BlockSpec(memory_space=pltpu.VMEM)
    messages = pl.pallas_call(
        functools.partial(window_kernel, capacity),
        out_shape=pltpu.VMEM((sky, capacity * SUB + SUB, cols), jnp.bfloat16),
        in_specs=[anywhere] * 8 + [pl.BlockSpec(memory_space=pltpu.SMEM)],
        out_specs=vmem,
        scratch_shapes=[
            pltpu.VMEM((1, rows, cols), jnp.bfloat16),
            pltpu.VMEM((taps, basis), jnp.bfloat16),
            pltpu.VMEM((taps, basis), jnp.bfloat16),
            pltpu.VMEM((3, 1, basis), jnp.float32),
            pltpu.VMEM((1, visits), jnp.bfloat16),
            pltpu.SMEM((1, 2), jnp.float32),
            pltpu.SMEM((tiles,), jnp.int32),
            pltpu.SMEM((tiles,), jnp.int32),
            pltpu.SemaphoreType.DMA((8,)),
            pltpu.VMEM((rows + 2 * fold, cols), jnp.float32),
            pltpu.VMEM((2 * fold, basis), jnp.float32),
            pltpu.VMEM((3, 2 * fold, cols), jnp.float32),
            pltpu.VMEM((largest * 2 * cols, 2 * cols), jnp.bfloat16),
            pltpu.VMEM((largest * 2 * cols, 2 * cols), jnp.bfloat16),
            pltpu.VMEM(((3 * fold - 1) * (rows // fold), cols), jnp.bfloat16),
            pltpu.VMEM((rows, 2 * cols), jnp.float32),
            pltpu.VMEM((rows + 2 * SUB, cols), jnp.float32),
            pltpu.SMEM((sky * capacity,), jnp.int32),
            pltpu.SMEM((sky * capacity,), jnp.int32),
            pltpu.SMEM((sky,), jnp.int32),
        ],
        compiler_params=pltpu.CompilerParams(vmem_limit_bytes=LARGE_VMEM),
        name="match_warp_pack",
    )(
        *[
            pltpu.with_memory_space_constraint(value, pltpu.HBM)
            for value in (
                image,
                row_taps.T,
                col_taps.T,
                mix_coeff.transpose(1, 0, 2),
                visit_weight.reshape(1, -1),
                shift_frac,
                tile_block,
                tile_offset,
            )
        ],
        ccd_visit,
    )
    order = sorted(range(sky), key=lambda owner: place_of(owner, sky))
    received = lax.all_to_all(
        messages, "sky", split_axis=0, concat_axis=0, axis_index_groups=[order], tiled=True
    )
    coadd, weight_map = pl.pallas_call(
        functools.partial(sky_kernel, capacity),
        out_shape=(
            jax.ShapeDtypeStruct((BLK_DEV * SUB, cols), jnp.float32),
            jax.ShapeDtypeStruct((1, BLK_DEV * SUB), jnp.float32),
        ),
        in_specs=[vmem],
        out_specs=(vmem, vmem),
        compiler_params=pltpu.CompilerParams(vmem_limit_bytes=SMALL_VMEM),
        name="place_normalise",
    )(received)
    return coadd, weight_map.reshape(-1)


def solution(mesh):
    return jax.shard_map(
        on_device,
        mesh=mesh,
        in_specs=(
            P(("groups", "sky"), None, None),
            P(),
            P(),
            P(("groups", "sky"), None, None),
            P(("groups", "sky"), None),
            P(("groups", "sky")),
            P("groups"),
            P(("groups", "sky")),
            P(("groups", "sky")),
        ),
        out_specs=(P(("groups", "sky"), None), P(("groups", "sky"))),
        check_vma=False,
    )
```

```python
import functools
import itertools

import jax
import jax.numpy as jnp
from jax import lax
from jax.experimental import pallas as pl
from jax.experimental.pallas import tpu as pltpu
from jax.sharding import PartitionSpec as P

BLK_DEV = 16
SUB = 8
LARGE_VMEM = 32 * 1024 * 1024
SMALL_VMEM = 16 * 1024 * 1024
EMPTY = -64
TAPS_DOWN = 6


def iota(shape, axis):
    return lax.broadcasted_iota(jnp.int32, shape, axis)


def weight_of(visit_ref, weight_ref):
    values = weight_ref[...].astype(jnp.float32)
    chosen = jnp.where(iota(values.shape, 1) == visit_ref[0], values, 0.0)
    return jnp.sum(chosen, axis=1, keepdims=True)


def lanczos_rows(frac_ref, cols):
    row = iota((2 * SUB, cols), 0)
    tap = jnp.where(row < SUB, row, row - SUB)
    fraction = jnp.where(row < SUB, frac_ref[0, 1], frac_ref[0, 0])
    angles = jnp.pi * ((tap - 2).astype(jnp.float32) - fraction)
    third = angles / 3.0
    kernel = jnp.sin(angles) / angles * (jnp.sin(third) / third)
    kernel = jnp.where(tap < TAPS_DOWN, kernel, 0.0)
    across, down = kernel[:SUB], kernel[SUB:]
    across = across / jnp.sum(across, axis=0, keepdims=True)
    down = down / jnp.sum(down, axis=0, keepdims=True)
    return across, down


def combined_taps(row_ref, col_ref, mix_ref, lifted, base):
    taps, basis = row_ref.shape
    count, cols = base.shape[1:]
    half = taps // 2
    l, s = iota((cols, taps), 0), iota((cols, taps), 1)
    turned = ((s + l == half) | (s + l == half + cols)).astype(jnp.float32).astype(jnp.bfloat16)
    across = jnp.dot(turned, row_ref[...], preferred_element_type=jnp.float32)
    across = across.astype(jnp.bfloat16)
    lifted[0:1] = jnp.zeros((1, basis), jnp.float32)
    lifted[1:] = col_ref[...].astype(jnp.float32)
    down = lifted[...]
    scaled = jnp.concatenate([down * mix_ref[term] for term in range(3)], axis=0)
    high = scaled.astype(jnp.bfloat16)
    low = (scaled - high.astype(jnp.float32)).astype(jnp.bfloat16)
    found = lax.dot_general(
        jnp.concatenate([high, low], axis=0),
        across,
        (((1,), (1,)), ((), ())),
        preferred_element_type=jnp.float32,
    )
    found = found[: 3 * count] + found[3 * count :]
    lane = iota((count, cols), 1)
    lane = jnp.where(lane < cols // 2, lane, lane - cols).astype(jnp.float32)
    base[0] = found[:count] + (2.0 / cols) * lane * found[count : 2 * count]
    base[1] = found[count : 2 * count]
    base[2] = found[2 * count :]


def build_band(base, row, band, first):
    cols = base.shape[2]
    shape = (2 * SUB, cols)
    sub = iota(shape, 0)
    lane = iota(shape, 1)
    lane = jnp.where(lane < cols // 2, lane, lane - cols)
    first_u = (2.0 * sub.astype(jnp.float32) + 1.0) / cols - 1.0

    def spin(term):
        taps = jnp.broadcast_to(base[term, pl.ds(row, 1), :], shape)
        return pltpu.roll(taps, 0, 1, stride=1, stride_axis=0)

    slope = spin(1)
    level = spin(0) + first_u * slope
    rise = spin(2)
    whole = rise.astype(jnp.bfloat16)
    pairs = cols // (2 * SUB)
    for pair in range(pairs):
        shift = 2 * SUB * pair
        value = level + (2.0 * shift / cols) * slope
        other = whole
        if pair == 0 or pair == pairs - 1:
            inside = lane >= 0 if pair == 0 else lane < 2 * SUB
            value = jnp.where(inside, value, 0.0)
            other = jnp.where(inside, rise, 0.0).astype(jnp.bfloat16)
        value = value.astype(jnp.bfloat16)
        if pair:
            value, other = pltpu.roll(value, shift, 1), pltpu.roll(other, shift, 1)
        at = first + shift
        band[at : at + 2 * SUB, :] = jnp.concatenate([value, other], axis=1)


def place_of(owner, owners):
    slow = 1 << ((owners.bit_length() - 1) // 2)
    fast = owners // slow
    return (owner // fast + slow // 2) % slow * fast + (owner + fast // 2) % fast


def group_edges(fold):
    return [0, fold // 4, fold]


def window_kernel(
    capacity,
    image_hbm,
    row_hbm,
    col_hbm,
    mix_hbm,
    weight_hbm,
    frac_hbm,
    block_hbm,
    offset_hbm,
    visit_ref,
    out_ref,
    image_ref,
    row_ref,
    col_ref,
    mix_ref,
    weight_ref,
    frac_ref,
    block_ref,
    offset_ref,
    copied,
    padded,
    lifted,
    base,
    band_a,
    band_b,
    blocks,
    total,
    spread,
    tile_of,
    starts,
    counts,
):
    rows, cols = image_ref.shape[1:]
    fold = row_ref.shape[0] // 2 + 1
    deep = rows // fold
    tiles = block_ref.shape[0]
    owners = out_ref.shape[0]
    data_rows = capacity * SUB
    owned = BLK_DEV * SUB

    pairs = (
        (row_hbm, row_ref),
        (col_hbm, col_ref),
        (mix_hbm, mix_ref),
        (image_hbm, image_ref),
        (frac_hbm, frac_ref),
        (weight_hbm, weight_ref),
        (block_hbm, block_ref),
        (offset_hbm, offset_ref),
    )
    copies = [
        pltpu.make_async_copy(source, target, copied.at[index])
        for index, (source, target) in enumerate(pairs)
    ]
    for copy in copies:
        copy.start()

    @pl.loop(0, owners)
    def _(owner):
        counts[owner] = 0

    if owners * capacity > tiles:

        @pl.loop(0, owners * capacity)
        def _(slot):
            starts[slot] = EMPTY
            tile_of[slot] = 0

    padded[:fold] = jnp.zeros((fold, cols), jnp.float32)
    padded[fold + rows :] = jnp.zeros((fold, cols), jnp.float32)
    spread[:SUB] = jnp.zeros((SUB, cols), jnp.float32)
    spread[SUB + rows :] = jnp.zeros((SUB, cols), jnp.float32)
    for copy in copies[:3]:
        copy.wait()
    combined_taps(row_ref, col_ref, mix_ref, lifted, base)
    for copy in copies[3:]:
        copy.wait()
    padded[fold : fold + rows] = image_ref[0].astype(jnp.float32)
    across, down = lanczos_rows(frac_ref, cols)
    weight = weight_of(visit_ref, weight_ref)

    for index in range(3 * fold - 1):
        blocks[index * deep : (index + 1) * deep, :] = padded[
            pl.ds(index, deep, stride=fold), :
        ].astype(jnp.bfloat16)

    edges = group_edges(fold)
    groups = len(edges) - 1

    def build(group, band):
        for index, r in enumerate(range(edges[group], edges[group + 1])):
            for part in range(2):
                build_band(base, r + part * fold, band, (2 * index + part) * cols)

    def multiply(group, band):
        parts = []
        for r in range(edges[group], edges[group + 1]):
            for part in range(2):
                first = (r + part * fold) * deep
                parts.append(blocks[first : first + rows, :])
        product = jnp.dot(
            jnp.concatenate(parts, axis=1),
            band[: len(parts) * cols, :],
            preferred_element_type=jnp.float32,
        )
        total[...] = product if group == 0 else total[...] + product

    def assign(tile):
        block = block_ref[tile]
        owner = lax.div(block, BLK_DEV)
        rank = counts[owner]
        counts[owner] = rank + 1
        slot = owner * capacity + rank
        tile_of[slot] = tile
        starts[slot] = (block - owner * BLK_DEV) * SUB + offset_ref[tile]

    held = (band_a, band_b)
    build(0, held[0])
    for group in range(groups):
        if group + 1 < groups:
            build(group + 1, held[(group + 1) % 2])
        multiply(group, held[group % 2])
        for tile in range(group * tiles // groups, (group + 1) * tiles // groups):
            assign(tile)

    lane = iota((1, cols), 1)
    taps_across = [
        jnp.where((lane + m - 2 >= 0) & (lane + m - 2 < cols), across[m : m + 1], 0.0)
        for m in range(TAPS_DOWN)
    ]
    position = (2 * fold * iota((deep, cols), 0) + 1).astype(jnp.float32) / rows - 1.0
    for phase in range(fold):
        first = phase * deep
        both = total[first : first + deep, :]
        matched = both[:, :cols] + (position + 2.0 * phase / rows) * both[:, cols:]
        result = taps_across[2] * matched
        for m in range(TAPS_DOWN):
            if m != 2:
                result = result + taps_across[m] * pltpu.roll(matched, (2 - m) % cols, 1)
        spread[pl.ds(SUB + phase, deep, stride=fold), :] = result

    sub = iota((SUB, cols), 0)
    wide = iota((SUB, cols), 1)
    segment = wide >> (data_rows.bit_length() - 1)
    lane_row = wide & (SUB - 1)
    lane_slot = (wide >> 3) & (capacity - 1)
    spill_row = wide >> (capacity.bit_length() - 1)
    spill_rows = [jnp.where(wide & (capacity - 1) == c, spill_row, owned) for c in range(capacity)]
    tile_weight = jnp.broadcast_to(weight, (SUB, cols))

    def warped(slot):
        first = tile_of[slot] * SUB + SUB - 2
        result = down[0:1] * spread[pl.ds(first, SUB), :]
        for m in range(1, TAPS_DOWN):
            result = result + down[m : m + 1] * spread[pl.ds(first + m, SUB), :]
        return result

    def message(owner, carry):
        spilled, over = carry
        target = jnp.zeros((SUB, cols), jnp.int32)
        next_spilled = jnp.zeros((SUB, cols), jnp.float32)
        next_over = jnp.zeros((SUB, cols), jnp.float32)
        tiles_here = []
        for c in range(capacity):
            slot = owner * capacity + c
            start = starts[slot]
            past = start + SUB - owned
            tile = warped(slot)
            tiles_here.append(tile)
            target = jnp.where(lane_slot == c, start, target)
            turned = pltpu.roll(tile, start & (SUB - 1), 0)
            next_spilled = next_spilled + jnp.where(sub < past, turned, 0.0)
            next_over = jnp.where(spill_rows[c] < past, tile_weight, next_over)
        meta = jnp.where(segment == 1, (target + lane_row).astype(jnp.float32), tile_weight)
        meta = jnp.where(segment == 0, over, meta)
        tail = jnp.where(sub == SUB - 1, meta, spilled * tile_weight)
        place = place_of(owner, owners)
        out_ref[place, :data_rows, :] = jnp.concatenate(tiles_here, axis=0).astype(jnp.bfloat16)
        out_ref[place, data_rows:, :] = tail.astype(jnp.bfloat16)
        return next_spilled, next_over

    nothing = jnp.zeros((SUB, cols), jnp.float32)
    lax.fori_loop(0, owners, message, (nothing, nothing), unroll=min(owners, 16))


def sky_kernel(capacity, got_ref, coadd_ref, map_ref):
    sources, message_rows, cols = got_ref.shape
    data_rows = capacity * SUB
    owned = coadd_ref.shape[0]
    per_chunk = cols // data_rows
    chunks = sources // per_chunk
    place = iota((chunks, cols), 0)
    wide = iota((chunks, cols), 1)
    row = iota((owned, cols), 0)
    spilled = jnp.zeros((SUB, cols), jnp.float32)
    target = jnp.zeros((chunks, cols), jnp.float32)
    weight = jnp.zeros((chunks, cols), jnp.float32)
    for k in range(per_chunk):
        heads = jnp.zeros((chunks, cols), jnp.float32)
        for chunk in range(chunks):
            tail = got_ref[chunk * per_chunk + k, data_rows:, :].astype(jnp.float32)
            spilled = spilled + tail
            heads = jnp.where(place == chunk, tail[SUB - 1 :], heads)
        here = (wide >= k * data_rows) & (wide < (k + 1) * data_rows)
        target = jnp.where(here, pltpu.roll(heads, (k - 1) * data_rows % cols, 1), target)
        weight = jnp.where(here, pltpu.roll(heads, (k - 2) * data_rows % cols, 1), weight)
    target = target.astype(jnp.int32)
    pieces = [
        jnp.where(row == target[chunk : chunk + 1], weight[chunk : chunk + 1], 0.0)
        for chunk in range(chunks)
    ]
    placement = jnp.concatenate(pieces, axis=1).astype(jnp.bfloat16)
    pixels = got_ref[:, :data_rows, :].reshape(sources * data_rows, cols)
    pixels = jnp.concatenate([pixels, jnp.ones(pixels.shape, jnp.bfloat16)], axis=1)
    sums = jnp.dot(placement, pixels, preferred_element_type=jnp.float32)
    sub = iota((SUB, cols), 0)
    wide = iota((SUB, cols), 1)
    last = sub == SUB - 1
    over = jnp.broadcast_to(spilled[SUB - 1 :], (SUB, cols))
    mine = ((wide >> (capacity.bit_length() - 1)) == sub) & ~last
    over = jnp.sum(jnp.where(mine, over, 0.0), axis=1, keepdims=True)
    rest = jnp.zeros((owned - SUB, cols), jnp.float32)
    pixel_sum = sums[:, :cols] + jnp.concatenate([jnp.where(last, 0.0, spilled), rest], axis=0)
    weight_sum = sums[:, cols:] + jnp.concatenate(
        [jnp.broadcast_to(over, (SUB, cols)), rest], axis=0
    )
    coadd_ref[...] = pixel_sum / jnp.maximum(weight_sum, 1.0)
    diagonal = jnp.where(row == iota((owned, cols), 1), weight_sum, 0.0)
    map_ref[...] = jnp.sum(diagonal, axis=0, keepdims=True)


def on_device(
    image,
    row_taps,
    col_taps,
    mix_coeff,
    shift_frac,
    ccd_visit,
    visit_weight,
    tile_block,
    tile_offset,
):
    rows, cols = image.shape[1:]
    tiles = tile_block.shape[0]
    sky = lax.axis_size("sky")
    capacity = max(2, tiles // sky)
    taps, basis = row_taps.shape[1], row_taps.shape[0]
    fold = taps // 2 + 1
    visits = visit_weight.shape[0]
    largest = max(b - a for a, b in itertools.pairwise(group_edges(fold)))
    anywhere = pl.BlockSpec(memory_space=pl.ANY)
    vmem = pl.BlockSpec(memory_space=pltpu.VMEM)
    messages = pl.pallas_call(
        functools.partial(window_kernel, capacity),
        out_shape=pltpu.VMEM((sky, capacity * SUB + SUB, cols), jnp.bfloat16),
        in_specs=[anywhere] * 8 + [pl.BlockSpec(memory_space=pltpu.SMEM)],
        out_specs=vmem,
        scratch_shapes=[
            pltpu.VMEM((1, rows, cols), jnp.bfloat16),
            pltpu.VMEM((taps, basis), jnp.bfloat16),
            pltpu.VMEM((taps, basis), jnp.bfloat16),
            pltpu.VMEM((3, 1, basis), jnp.float32),
            pltpu.VMEM((1, visits), jnp.bfloat16),
            pltpu.SMEM((1, 2), jnp.float32),
            pltpu.SMEM((tiles,), jnp.int32),
            pltpu.SMEM((tiles,), jnp.int32),
            pltpu.SemaphoreType.DMA((8,)),
            pltpu.VMEM((rows + 2 * fold, cols), jnp.float32),
            pltpu.VMEM((2 * fold, basis), jnp.float32),
            pltpu.VMEM((3, 2 * fold, cols), jnp.float32),
            pltpu.VMEM((largest * 2 * cols, 2 * cols), jnp.bfloat16),
            pltpu.VMEM((largest * 2 * cols, 2 * cols), jnp.bfloat16),
            pltpu.VMEM(((3 * fold - 1) * (rows // fold), cols), jnp.bfloat16),
            pltpu.VMEM((rows, 2 * cols), jnp.float32),
            pltpu.VMEM((rows + 2 * SUB, cols), jnp.float32),
            pltpu.SMEM((sky * capacity,), jnp.int32),
            pltpu.SMEM((sky * capacity,), jnp.int32),
            pltpu.SMEM((sky,), jnp.int32),
        ],
        compiler_params=pltpu.CompilerParams(vmem_limit_bytes=LARGE_VMEM),
        name="match_warp_pack",
    )(
        *[
            pltpu.with_memory_space_constraint(value, pltpu.HBM)
            for value in (
                image,
                row_taps.T,
                col_taps.T,
                mix_coeff.transpose(1, 0, 2),
                visit_weight.reshape(1, -1),
                shift_frac,
                tile_block,
                tile_offset,
            )
        ],
        ccd_visit,
    )
    order = sorted(range(sky), key=lambda owner: place_of(owner, sky))
    received = lax.all_to_all(
        messages, "sky", split_axis=0, concat_axis=0, axis_index_groups=[order], tiled=True
    )
    coadd, weight_map = pl.pallas_call(
        functools.partial(sky_kernel, capacity),
        out_shape=(
            jax.ShapeDtypeStruct((BLK_DEV * SUB, cols), jnp.float32),
            jax.ShapeDtypeStruct((1, BLK_DEV * SUB), jnp.float32),
        ),
        in_specs=[vmem],
        out_specs=(vmem, vmem),
        compiler_params=pltpu.CompilerParams(vmem_limit_bytes=SMALL_VMEM),
        name="place_normalise",
    )(received)
    return coadd, weight_map.reshape(-1)


def solution(mesh):
    return jax.shard_map(
        on_device,
        mesh=mesh,
        in_specs=(
            P(("groups", "sky"), None, None),
            P(),
            P(),
            P(("groups", "sky"), None, None),
            P(("groups", "sky"), None),
            P(("groups", "sky")),
            P("groups"),
            P(("groups", "sky")),
            P(("groups", "sky")),
        ),
        out_specs=(P(("groups", "sky"), None), P(("groups", "sky"))),
        check_vma=False,
    )
```
